32 devices in a mesh: batch: 8 (over y, x, core), seq: 4 (over z).
Axes of the slice: x: 2, y: 2, z: 4, core: 2. Of those that a mesh axis runs over, the one named last changes fastest.
Arguments:
- tokens: bfloat16 [32, 1024, 768], P('batch', 'seq'), may hold values from -6 to 6
- norm1_gain: bfloat16 [768], replicated, may hold values from 0.5 to 1.5
- w_query: bfloat16 [768, 768], replicated, may hold values from -0.078125 to 0.078125
- w_key: bfloat16 [768, 768], replicated, may hold values from -0.078125 to 0.078125
- w_value: bfloat16 [768, 768], replicated, may hold values from -0.21875 to 0.21875
- rel_bias: bfloat16 [32, 12], replicated, may hold values from -4 to 4
- w_output: bfloat16 [768, 768], replicated, may hold values from -0.875 to 0.875
- norm2_gain: bfloat16 [768], replicated, may hold values from 0.5 to 1.5
- w_in: bfloat16 [768, 3072], replicated, may hold values from -0.21875 to 0.21875
- w_out: bfloat16 [3072, 768], replicated, may hold values from -0.15625 to 0.15625
- final_gain: bfloat16 [768], replicated, may hold values from 0.5 to 1.5
- w_proj: bfloat16 [768, 768], replicated, may hold values from -0.21875 to 0.21875
- lengths: int32 [32, 16], P('batch'), may hold values from 1 to 256, 1024 in all within a row
- partner: int32 [512], P('batch'), may hold values from 0 to 511, as said below
- cotangent: bfloat16 [32, 1024, 768], P('batch', 'seq'), may hold values from -6 to 6
Outputs:
- block_out: bfloat16 [32, 1024, 768], P('batch', 'seq')
- embeddings: float32 [512, 768], P('batch')
- sentence_loss: float32 [512], P('batch')
- tokens_grad: float32 [32, 1024, 768], P('batch', 'seq')
- norm1_gain_grad: float32 [768], replicated
- query_grad: float32 [768, 768], P('seq', 'batch')
- key_grad: float32 [768, 768], P('seq', 'batch')
- value_grad: float32 [768, 768], P('seq', 'batch')
- rel_bias_grad: float32 [32, 12], replicated
- output_grad: float32 [768, 768], P('seq', 'batch')
- norm2_gain_grad: float32 [768], replicated
- in_grad: float32 [768, 3072], P('seq', 'batch')
- out_grad: float32 [3072, 768], P('seq', 'batch')
- final_gain_grad: float32 [768], replicated
- proj_grad: float32 [768, 768], P('seq', 'batch')
The draws below stay inside these ranges and needn't reach their ends.
Inputs may be any that keep to these rules, and one draw needn't show every extreme that they name: Each row's 16 lengths sum to 1024, and every row's longest sentence has exactly 256 tokens. Pairs are mutual and never a sentence with itself: partner[partner[i]] == i and partner[i] != i.
All inputs are finite; a program needn't handle non-finite values.
Results may differ from the reference program's by a relative error of at most 0.017.
Values may be sent and summed in bfloat16 or wider, within the bound.
No kernel may reach another device: no remote copies, remote signals or barrier semaphores. Data moves between devices by JAX's collectives and lax.ppermute only.
A program may use at most 320 MiB of HBM per device.

```python
import math
import jax
import jax.numpy as jnp
import numpy as np
from jax import lax

D = 768
HEADS = 12
HEAD_DIM = 64
FF = 3072
BUCKETS = 32
SHARD_TOK = 256
SEGS = 16
ROW_LEN = 1024
ROWS = 32
SENT = 512


def draw_partner(key, part):
    key = jax.random.fold_in(key, 7)
    shuffled = jax.random.permutation(key, SENT).astype(jnp.int32)
    leaders = shuffled[0::2]
    followers = shuffled[1::2]
    paired = jnp.zeros((SENT,), jnp.int32)
    paired = paired.at[leaders].set(followers).at[followers].set(leaders)
    return paired


def levels(own_key, shape, shards, low, top_value):
    gain = 1.0
    for dim, blocks in shards:
        steps = jax.random.uniform(jax.random.fold_in(jax.random.fold_in(own_key, 6), dim), (blocks,), jnp.float32, low / len(shards), top_value / len(shards))
        gain = gain * jnp.repeat(jnp.exp(steps), shape[dim] // blocks).reshape((-1,) + (1,) * (len(shape) - 1 - dim))
    return gain


def length_profile(amount, total, reach, skew):
    weights = [(1 << 20) // math.isqrt(standing ** skew) + 1 for standing in range(2, amount + 1)]
    surplus, given = total - reach - (amount - 1), [1] * (amount - 1)
    while surplus > 0:
        free = [i for i in range(amount - 1) if given[i] < reach]
        mass, remaining = sum([weights[i] for i in free]), surplus
        for i in free:
            more = min(reach - given[i], max(1, remaining * weights[i] // mass), surplus)
            given[i] = given[i] + more
            surplus = surplus - more
    return np.array([reach] + given)


def ragged_sizes(rng, count, total, most, slope):
    if count == 2:
        one = jax.random.randint(rng, (), max(1, total - most), min(most, total - 1) + 1)
        return jnp.stack([one, total - one])
    tallies = jnp.asarray(length_profile(count, total, most, slope), jnp.int32)
    couples = (count - 1) // 2
    donor, receiver = tallies[1:1 + 2 * couples:2], tallies[2:2 + 2 * couples:2]
    margin = jnp.minimum(donor - 1, most - receiver)
    passed = jax.random.randint(jax.random.fold_in(rng, 1), (couples,), 0, 1 << 20) % (margin + 1)
    tallies = tallies.at[1:1 + 2 * couples:2].set(donor - passed).at[2:2 + 2 * couples:2].set(receiver + passed)
    return tallies[jax.random.permutation(jax.random.fold_in(rng, 2), count)]


def centred(rng, shape, spread, limit, cuts=(), kind=jnp.bfloat16):
    values = jax.random.normal(rng, shape, jnp.float32) * spread
    if len(cuts) > 0:
        values = levels(rng, shape, cuts, -0.22, 0.18) * values
    return jnp.clip(values, min=-limit, max=limit).astype(kind)


def setup_inputs(seed: int = 0) -> dict:
    streams_of = jax.random.split(jax.random.key(seed), 16)
    tokens = centred(streams_of[0], (ROWS, ROW_LEN, D), 1.0, 6.0, ((0, 8), (1, 4)))
    norm1_gain = jnp.clip(1.0 + 0.1 * jax.random.normal(streams_of[1], (D,), jnp.float32), 0.5, 1.5).astype(jnp.bfloat16)
    w_query = centred(streams_of[2], (D, D), (8 * D) ** -0.5, 0.078125)
    w_key = centred(streams_of[3], (D, D), (8 * D) ** -0.5, 0.078125)
    w_value = centred(streams_of[4], (D, D), D ** -0.5, 0.21875)
    rel_bias = centred(streams_of[5], (BUCKETS, HEADS), 1.0, 4.0)
    w_output = centred(streams_of[6], (D, D), (D // 16) ** -0.5, 0.875)
    norm2_gain = jnp.clip(1.0 + 0.1 * jax.random.normal(streams_of[7], (D,), jnp.float32), 0.5, 1.5).astype(jnp.bfloat16)
    w_in = centred(streams_of[8], (D, FF), D ** -0.5, 0.21875)
    w_out = centred(streams_of[9], (FF, D), (FF // 2) ** -0.5, 0.15625)
    final_gain = jnp.clip(1.0 + 0.1 * jax.random.normal(streams_of[10], (D,), jnp.float32), 0.5, 1.5).astype(jnp.bfloat16)
    w_proj = centred(streams_of[11], (D, D), D ** -0.5, 0.21875)
    lengths = jax.vmap(lambda own: ragged_sizes(own, SEGS, ROW_LEN, SHARD_TOK, 2))(jax.random.split(streams_of[12], ROWS)).reshape((ROWS, SEGS)).astype(jnp.int32)
    partner = draw_partner(jax.random.fold_in(streams_of[15], 71), 0)
    cotangent = centred(streams_of[14], (ROWS, ROW_LEN, D), 1.0, 6.0, ((0, 8), (1, 4)))
    return {"tokens": tokens, "norm1_gain": norm1_gain, "w_query": w_query, "w_key": w_key, "w_value": w_value, "rel_bias": rel_bias, "w_output": w_output, "norm2_gain": norm2_gain, "w_in": w_in, "w_out": w_out, "final_gain": final_gain, "w_proj": w_proj, "lengths": lengths, "partner": partner, "cotangent": cotangent}


EPS = 1e-06
NEGATIVE = -1e+30
SHARPNESS = 50.0
THRESHOLDS = (12, 16, 23, 32, 46, 64, 91)

@jax.custom_vjp
def low(v):
    return lax.optimization_barrier(v.astype(jnp.bfloat16)).astype(jnp.float32)

@jax.custom_vjp
def low_back(v):
    return v

def low_keep(v):
    return (low(v), None)

def low_pass(kept, grad):
    return (grad,)

def back_keep(v):
    return (v, None)

def back_low(kept, grad):
    return (low(grad),)
low.defvjp(low_keep, low_pass)
low_back.defvjp(back_keep, back_low)

def bucket_of(offset):
    distance = jnp.abs(offset)
    beyond = jnp.zeros_like(distance)
    for threshold in THRESHOLDS:
        beyond = beyond + (distance >= threshold).astype(jnp.int32)
    within = jnp.where(distance < 8, distance, 8 + beyond)
    return within + 16 * (offset > 0).astype(jnp.int32)

def segment_of(seg_ends, where_pos):
    return lax.optimization_barrier(jnp.sum((seg_ends[:, None, :] <= where_pos[None, :, None]).astype(jnp.int32), axis=-1))

def matmul_hi(left, right):
    return jnp.dot(left, right, precision=lax.Precision.HIGHEST)

def rms_scale(values):
    return lax.rsqrt(lax.optimization_barrier(jnp.mean(values * values, axis=-1, keepdims=True)) + EPS)

def reference(tokens, norm1_gain, w_query, w_key, w_value, rel_bias, w_output, norm2_gain, w_in, w_out, final_gain, w_proj, lengths, partner, cotangent):
    row_count = tokens.shape[0]
    row_len = tokens.shape[1]
    places = jnp.arange(row_len, dtype=jnp.int32)
    seg_ends = jnp.cumsum(lengths, axis=1)
    segments = segment_of(seg_ends, places)
    member = (segments[:, :, None] == jnp.arange(SEGS, dtype=jnp.int32)[None, None, :]).astype(jnp.float32)
    buckets = bucket_of(places[None, :] - places[:, None])
    counts = lengths.astype(jnp.float32)
    sent_count = row_count * SEGS
    columns = jnp.arange(sent_count, dtype=jnp.int32)
    is_target = columns[None, :] == partner[:, None]
    is_self = columns[None, :] == columns[:, None]

    def forward(inputs, gain_one, wq_f, wk_f, wv_f, table, wo_f, gain_two, win_f, wout_f, gain_fin, wp_f):
        flat_in = inputs.reshape(-1, D)
        normed_one = low(flat_in * rms_scale(flat_in) * gain_one)
        queries = low_back(low(matmul_hi(normed_one, wq_f)))
        keys_proj = low_back(low(matmul_hi(normed_one, wk_f)))
        values_proj = low_back(low(matmul_hi(normed_one, wv_f)))
        bias_grid = jnp.transpose(jnp.take(table, buckets, axis=0), (2, 0, 1))

        def one_row(pieces):
            row_q, row_k, row_v, row_seg = pieces
            head_q = row_q.reshape(row_len, HEADS, HEAD_DIM)
            head_k = row_k.reshape(row_len, HEADS, HEAD_DIM)
            head_v = row_v.reshape(row_len, HEADS, HEAD_DIM)
            raw_dot = low_back(jnp.einsum('ihe,jhe->hij', head_q, head_k, precision=lax.Precision.HIGHEST))
            same_seg = row_seg[:, None] == row_seg[None, :]
            scores = jnp.where(same_seg[None], raw_dot + bias_grid, NEGATIVE)
            row_peak = lax.optimization_barrier(jnp.max(scores, axis=-1, keepdims=True))
            powers = jnp.exp(scores - row_peak)
            soft_probs = low(powers / lax.optimization_barrier(jnp.sum(powers, axis=-1, keepdims=True)))
            result = jnp.einsum('hij,jhe->ihe', soft_probs, head_v, precision=lax.Precision.HIGHEST)
            return result.reshape(row_len, D)
        attended = lax.map(jax.checkpoint(one_row), (queries.reshape(row_count, row_len, D), keys_proj.reshape(row_count, row_len, D), values_proj.reshape(row_count, row_len, D), segments))
        attended = low_back(low(attended.reshape(-1, D)))
        after_attn = flat_in + low_back(matmul_hi(attended, wo_f))
        normed_two = low(after_attn * rms_scale(after_attn) * gain_two)
        pre_act = low_back(matmul_hi(normed_two, win_f))
        act_out = low(jax.nn.gelu(pre_act, approximate=True))
        total_out = after_attn + low_back(matmul_hi(act_out, wout_f))
        block_val = low(total_out)
        final_norm = block_val * rms_scale(block_val) * gain_fin
        pooled = jnp.einsum('rts,rtd->rsd', member, final_norm.reshape(row_count, row_len, D), precision=lax.Precision.HIGHEST)
        pooled = (pooled / counts[:, :, None]).reshape(sent_count, D)
        raw_emb = matmul_hi(pooled, wp_f)
        embedded = raw_emb * lax.rsqrt(lax.optimization_barrier(jnp.sum(raw_emb * raw_emb, axis=-1, keepdims=True)) + EPS)
        logits = SHARPNESS * jnp.einsum('nd,md->nm', embedded, embedded, precision=lax.Precision.HIGHEST)
        logits = jnp.where(is_self, NEGATIVE, logits)
        row_peak = lax.optimization_barrier(jnp.max(logits, axis=-1, keepdims=True))
        log_total = row_peak[:, 0] + jnp.log(lax.optimization_barrier(jnp.sum(jnp.exp(logits - row_peak), axis=-1)))
        sent_loss = log_total - lax.optimization_barrier(jnp.sum(jnp.where(is_target, logits, 0.0), axis=-1))
        return ((block_val, sent_loss), embedded)
    primals = tuple((item.astype(jnp.float32) for item in (tokens, norm1_gain, w_query, w_key, w_value, rel_bias, w_output, norm2_gain, w_in, w_out, final_gain, w_proj)))
    outputs, backward, embedded = jax.vjp(forward, *primals, has_aux=True)
    block_val, sent_loss = outputs
    grads = backward((cotangent.astype(jnp.float32).reshape(-1, D), jnp.ones_like(sent_loss)))
    return (block_val.astype(jnp.bfloat16).reshape(tokens.shape), embedded, sent_loss, grads[0].reshape(tokens.shape), grads[1], grads[2], grads[3], grads[4], grads[5], grads[6], grads[7], grads[8], grads[9], grads[10], grads[11])
```

```python
import functools

import jax
import jax.numpy as jnp
from jax import lax
from jax.experimental import pallas as pl
from jax.experimental.pallas import tpu as pltpu
from jax.sharding import PartitionSpec as P

EPS = 1e-06
NEGATIVE = -1e30
SHARPNESS = 50.0
THRESHOLDS = (12, 16, 23, 32, 46, 64, 91)
HIGHEST = lax.Precision.HIGHEST
BF = jnp.bfloat16
F32 = jnp.float32
VMEM_BYTES = 60 * 1024 * 1024
GELU_A = 0.7978845608028654
GELU_B = 0.044715


def dot_nn(left, right):
    return lax.dot_general(left, right, (((1,), (0,)), ((), ())), preferred_element_type=F32)


def dot_nt(left, right):
    return lax.dot_general(left, right, (((1,), (1,)), ((), ())), preferred_element_type=F32)


def dot_tn(left, right):
    return lax.dot_general(left, right, (((0,), (0,)), ((), ())), preferred_element_type=F32)


def rms_scale(values):
    return lax.rsqrt(jnp.mean(values * values, axis=-1, keepdims=True) + EPS)


def rms_back(values, scale, grad_normed):
    inner = jnp.mean(grad_normed * values, axis=-1, keepdims=True)
    return scale * (grad_normed - values * (scale * scale * inner))


def split_bf(values):
    high = values.astype(BF)
    return high, (values - high.astype(F32)).astype(BF)


def bucket_of(offset):
    distance = jnp.abs(offset)
    beyond = jnp.zeros_like(distance)
    for threshold in THRESHOLDS:
        beyond = beyond + (distance >= threshold).astype(jnp.int32)
    within = jnp.where(distance < 8, distance, 8 + beyond)
    return within + 16 * (offset > 0).astype(jnp.int32)


def wrapped_offsets(shape, axis, size):
    place = lax.broadcasted_iota(jnp.int32, shape, axis)
    return jnp.where(place < size, place, place - 2 * size)


def full(shape):
    return pl.BlockSpec(shape, lambda *_: (0,) * len(shape), pipeline_mode=pl.Buffered(1))


def row_spec(shape, first=0):
    return pl.BlockSpec(
        (1,) + tuple(shape), lambda step, *_: (step + first,) + (0,) * len(shape)
    )


def params(limit=VMEM_BYTES):
    return pltpu.CompilerParams(
        vmem_limit_bytes=limit, dimension_semantics=("arbitrary",)
    )


def bias_kernel(size, table_ref, out_ref):
    buckets, heads = table_ref.shape
    hot = (
        lax.broadcasted_iota(jnp.int32, (buckets, 2 * size), 0)
        == bucket_of(wrapped_offsets((buckets, 2 * size), 1, size))
    ).astype(BF)
    by_offset = dot_tn(table_ref[...], hot)
    for head in range(heads):
        line = jnp.broadcast_to(by_offset[head : head + 1, :], (size, 2 * size))
        out_ref[head] = pltpu.roll(line, 0, 1, stride=1, stride_axis=0).astype(BF)


def bias_tables(rel_bias, size):
    heads = rel_bias.shape[1]
    return pl.pallas_call(
        functools.partial(bias_kernel, size),
        out_shape=jax.ShapeDtypeStruct((heads, size, 2 * size), BF),
        compiler_params=pltpu.CompilerParams(vmem_limit_bytes=VMEM_BYTES),
    )(rel_bias)


def bias_grad_kernel(acc_ref, out_ref):
    heads, size, width = acc_ref.shape
    buckets = out_ref.shape[0]
    hot = (
        lax.broadcasted_iota(jnp.int32, (width, buckets), 1)
        == bucket_of(wrapped_offsets((width, buckets), 0, size))
    ).astype(F32)
    lines = []
    for head in range(heads):
        rows = acc_ref[head]
        count = size
        while count > 1:
            count = count // 2
            rows = rows[:count] + pltpu.roll(rows[count:], width - count, 1)
        lines.append(rows)
    table = jnp.concatenate(lines, axis=0)
    out_ref[...] = lax.dot_general(
        hot, table, (((0,), (1,)), ((), ())), preferred_element_type=F32, precision=HIGHEST
    )


def bias_grad(acc, buckets):
    return pl.pallas_call(
        bias_grad_kernel,
        out_shape=jax.ShapeDtypeStruct((buckets, acc.shape[0]), F32),
        compiler_params=pltpu.CompilerParams(vmem_limit_bytes=VMEM_BYTES),
    )(acc)


def row_masks(lengths_ref, place_ref, row, size):
    slots = lengths_ref.shape[1]
    base = place_ref[0] * size
    col_pos = base + lax.broadcasted_iota(jnp.int32, (size, 1), 0)
    row_pos = base + lax.broadcasted_iota(jnp.int32, (1, size), 1)
    seg_col = jnp.zeros((size, 1), jnp.int32)
    seg_own = jnp.zeros((1, size), jnp.int32)
    seg_low = jnp.zeros((1, size), jnp.int32)
    seg_high = jnp.zeros((1, size), jnp.int32)
    end = jnp.int32(0)
    for slot in range(slots):
        end = end + lengths_ref[row, slot]
        seg_col = seg_col + (end <= col_pos).astype(jnp.int32)
        seg_own = seg_own + (end <= row_pos).astype(jnp.int32)
        seg_low = seg_low + (end <= row_pos - size).astype(jnp.int32)
        seg_high = seg_high + (end <= row_pos + size).astype(jnp.int32)
    seg_low = jnp.where(row_pos < size, -1, seg_low)
    upper = lax.broadcasted_iota(jnp.int32, (size, size), 1) > lax.broadcasted_iota(
        jnp.int32, (size, size), 0
    )
    own = (seg_col == seg_own).astype(F32)
    above = upper.astype(F32)
    low = (seg_col == seg_low).astype(F32) * above
    high = (seg_col == seg_high).astype(F32) * (1.0 - above)
    return seg_col, seg_own, own, low, high


def forward_kernel(
    first,
    lengths_ref,
    place_ref,
    own_ref,
    low_ref,
    high_ref,
    gain1_ref,
    gain2_ref,
    gainf_ref,
    wq_ref,
    wk_ref,
    wv_ref,
    wo_ref,
    win_ref,
    wout_ref,
    bias_ref,
    block_ref,
    pooled_ref,
    n1_ref,
    q_ref,
    k_ref,
    v_ref,
    p_ref,
    att_ref,
    after_ref,
    n2_ref,
    act_ref,
    dact_ref,
    mask_ref,
):
    size, dim = own_ref.shape[1:]
    heads = bias_ref.shape[0]
    pairs = heads // 2
    lanes = dim // pairs
    hidden = win_ref.shape[1]
    slots = pooled_ref.shape[1]
    row = pl.program_id(0) + first
    seg_col, seg_own, own, low, high = row_masks(lengths_ref, place_ref, row, size)
    mask_ref[0] = own.astype(BF)
    mask_ref[1] = low.astype(BF)
    mask_ref[2] = high.astype(BF)
    gain1 = gain1_ref[...].astype(F32)
    for part, source in enumerate((low_ref, own_ref, high_ref)):
        x = source[0].astype(F32)
        n1_ref[0, part] = (x * rms_scale(x) * gain1).astype(BF)
    q_ref[0] = dot_nn(n1_ref[0, 1], wq_ref[...]).astype(BF)
    for part in range(3):
        k_ref[0, part] = dot_nn(n1_ref[0, part], wk_ref[...]).astype(BF)
        v_ref[0, part] = dot_nn(n1_ref[0, part], wv_ref[...]).astype(BF)
    first_half = lax.broadcasted_iota(jnp.int32, (1, lanes), 1) < lanes // 2
    for pair in range(pairs):
        cols = slice(pair * lanes, (pair + 1) * lanes)
        q_pair = q_ref[0, :, cols]
        halves = []
        for half in range(2):
            head = 2 * pair + half
            keep = first_half if half == 0 else jnp.logical_not(first_half)
            q_head = jnp.where(keep, q_pair, jnp.zeros_like(q_pair))
            own_on = mask_ref[0].astype(F32) > 0
            low_on = mask_ref[1].astype(F32) > 0
            high_on = mask_ref[2].astype(F32) > 0
            s_own = dot_nt(q_head, k_ref[0, 1, :, cols]) + bias_ref[head, :, :size].astype(F32)
            s_low = dot_nt(q_head, k_ref[0, 0, :, cols])
            s_high = dot_nt(q_head, k_ref[0, 2, :, cols])
            s_alt = jnp.where(low_on, s_low, s_high) + bias_ref[head, :, size:].astype(F32)
            scores = jnp.where(
                own_on, s_own, jnp.where(low_on | high_on, s_alt, NEGATIVE)
            )
            peak = jnp.max(scores, axis=-1, keepdims=True)
            powers = jnp.exp(scores - peak)
            inverse = 1.0 / jnp.sum(powers, axis=-1, keepdims=True)
            probs = (powers * inverse).astype(BF)
            p_ref[0, head] = probs
            mixed = dot_nn(probs * mask_ref[1], v_ref[0, 0, :, cols])
            mixed += dot_nn(probs * mask_ref[0], v_ref[0, 1, :, cols])
            mixed += dot_nn(probs * mask_ref[2], v_ref[0, 2, :, cols])
            halves.append(mixed)
        att_ref[0, :, cols] = jnp.where(first_half, halves[0], halves[1]).astype(BF)
    after = own_ref[0].astype(F32) + dot_nn(att_ref[0], wo_ref[...])
    after_ref[0] = after
    n2_ref[0] = (after * rms_scale(after) * gain2_ref[...].astype(F32)).astype(BF)
    total = after
    chunk = dim
    for start in range(0, hidden, chunk):
        cols = slice(start, start + chunk)
        pre = dot_nn(n2_ref[0], win_ref[:, cols])
        square = pre * pre
        gate = 0.5 + 0.5 * jnp.tanh(pre * (GELU_A + (GELU_A * GELU_B) * square))
        act = pre * gate
        slope = gate + act * (1.0 - gate) * (2 * GELU_A + (6 * GELU_A * GELU_B) * square)
        act_ref[0, :, cols] = act.astype(BF)
        dact_ref[0, :, cols] = slope.astype(BF)
        total = total + dot_nn(act_ref[0, :, cols], wout_ref[cols, :])
    block = total.astype(BF)
    block_ref[0] = block
    out = block.astype(F32)
    final = out * rms_scale(out) * gainf_ref[...].astype(F32)
    member = (lax.broadcasted_iota(jnp.int32, (slots, size), 0) == seg_own).astype(BF)
    high_part, low_part = split_bf(final)
    pooled_ref[0] = dot_nn(member, high_part) + dot_nn(member, low_part)


def forward(first, count, lengths, place, own, low, high, gains, weights, bias):
    size, dim = own.shape[1:]
    heads = bias.shape[0]
    slots = lengths.shape[1]
    hidden = weights[4].shape[1]
    outs = (
        ((size, dim), BF),
        ((slots, dim), F32),
        ((3, size, dim), BF),
        ((size, dim), BF),
        ((3, size, dim), BF),
        ((3, size, dim), BF),
        ((heads, size, size), BF),
        ((size, dim), BF),
        ((size, dim), F32),
        ((size, dim), BF),
        ((size, hidden), BF),
        ((size, hidden), BF),
    )
    constants = tuple(gains) + tuple(weights) + (bias,)
    return pl.pallas_call(
        functools.partial(forward_kernel, first),
        grid_spec=pltpu.PrefetchScalarGridSpec(
            num_scalar_prefetch=2,
            grid=(count,),
            in_specs=[row_spec((size, dim), first)]
            + [row_spec((size, dim), 0)] * 2
            + [full(item.shape) for item in constants],
            out_specs=[row_spec(shape) for shape, _ in outs],
            scratch_shapes=[pltpu.VMEM((3, size, size), BF)],
        ),
        out_shape=[jax.ShapeDtypeStruct((count,) + shape, kind) for shape, kind in outs],
        compiler_params=params(),
        name="forward_rows",
    )(lengths, place, own, low, high, *constants)


def feed_back_kernel(
    lengths_ref,
    place_ref,
    block_ref,
    after_ref,
    cot_ref,
    pool_ref,
    dact_ref,
    gain2_ref,
    gainf_ref,
    wo_ref,
    win_ref,
    wout_ref,
    branch_ref,
    pre_ref,
    gafter_ref,
    gmix_ref,
    gains_ref,
):
    size, dim = block_ref.shape[1:]
    hidden = win_ref.shape[1]
    slots = pool_ref.shape[1]
    row = pl.program_id(0)
    base = place_ref[0] * size
    col_pos = base + lax.broadcasted_iota(jnp.int32, (size, 1), 0)
    seg_col = jnp.zeros((size, 1), jnp.int32)
    end = jnp.int32(0)
    for slot in range(slots):
        end = end + lengths_ref[row, slot]
        seg_col = seg_col + (end <= col_pos).astype(jnp.int32)
    member = (lax.broadcasted_iota(jnp.int32, (size, slots), 1) == seg_col).astype(BF)
    high_part, low_part = split_bf(pool_ref[0])
    g_final = dot_nn(member, high_part) + dot_nn(member, low_part)
    out = block_ref[0].astype(F32)
    scale = rms_scale(out)
    gain_f = jnp.sum(g_final * out * scale, axis=0, keepdims=True)
    g_out = rms_back(out, scale, g_final * gainf_ref[...].astype(F32)) + cot_ref[0].astype(F32)
    branch_ref[0] = g_out.astype(BF)
    g_n2 = jnp.zeros((size, dim), F32)
    chunk = dim
    for start in range(0, hidden, chunk):
        cols = slice(start, start + chunk)
        g_hidden = dot_nt(branch_ref[0], wout_ref[cols, :])
        pre_ref[0, :, cols] = (g_hidden * dact_ref[0, :, cols].astype(F32)).astype(BF)
        g_n2 = g_n2 + dot_nt(pre_ref[0, :, cols], win_ref[:, cols])
    after = after_ref[0]
    scale = rms_scale(after)
    gain_2 = jnp.sum(g_n2 * after * scale, axis=0, keepdims=True)
    g_after = g_out + rms_back(after, scale, g_n2 * gain2_ref[...].astype(F32))
    gafter_ref[0] = g_after
    gmix_ref[0] = dot_nt(g_after.astype(BF), wo_ref[...]).astype(BF)

    @pl.when(row == 0)
    def _():
        gains_ref[...] = jnp.zeros_like(gains_ref)

    gains_ref[0:1, :] += gain_f
    gains_ref[1:2, :] += gain_2


def feed_back(lengths, place, block, after, cot, pool, dact, gains, weights):
    count, size, dim = block.shape
    slots = lengths.shape[1]
    hidden = dact.shape[2]
    outs = (
        ((size, dim), BF),
        ((size, hidden), BF),
        ((size, dim), F32),
        ((size, dim), BF),
    )
    constants = tuple(gains) + tuple(weights)
    return pl.pallas_call(
        feed_back_kernel,
        grid_spec=pltpu.PrefetchScalarGridSpec(
            num_scalar_prefetch=2,
            grid=(count,),
            in_specs=[row_spec((size, dim))] * 3
            + [row_spec((slots, dim)), row_spec((size, hidden))]
            + [full(item.shape) for item in constants],
            out_specs=[row_spec(shape) for shape, _ in outs]
            + [pl.BlockSpec((8, dim), lambda *_: (0, 0))],
        ),
        out_shape=[jax.ShapeDtypeStruct((count,) + shape, kind) for shape, kind in outs]
        + [jax.ShapeDtypeStruct((8, dim), F32)],
        compiler_params=params(),
        name="feed_back_rows",
    )(lengths, place, block, after, cot, pool, dact, *constants)


def weight_grad_kernel(left_ref, right_ref, out_ref):
    out_ref[...] = dot_tn(left_ref[...].astype(BF), right_ref[...].astype(BF)).astype(BF)


def weight_grad(left, right, tile):
    depth, rows = left.shape
    cols = right.shape[1]
    return pl.pallas_call(
        weight_grad_kernel,
        grid=(rows // tile,),
        in_specs=[
            pl.BlockSpec((depth, tile), lambda step: (0, step)),
            pl.BlockSpec((depth, cols), lambda step: (0, 0), pipeline_mode=pl.Buffered(1)),
        ],
        out_specs=pl.BlockSpec((tile, cols), lambda step: (step, 0)),
        out_shape=jax.ShapeDtypeStruct((rows, cols), BF),
        compiler_params=params(),
        name="weight_grad",
    )(left, right)


def attend_back_kernel(
    lengths_ref,
    place_ref,
    own_ref,
    low_ref,
    high_ref,
    q_ref,
    k_ref,
    v_ref,
    p_ref,
    gmix_ref,
    gafter_ref,
    gain1_ref,
    wq_ref,
    wk_ref,
    wv_ref,
    dq_ref,
    dk_ref,
    dv_ref,
    part_ref,
    halo_ref,
    acc_ref,
    gains_ref,
    mask_ref,
):
    size, dim = own_ref.shape[1:]
    heads = p_ref.shape[1]
    pairs = heads // 2
    lanes = dim // pairs
    row = pl.program_id(0)
    _, _, own, low, high = row_masks(lengths_ref, place_ref, row, size)
    mask_ref[0] = low.astype(BF)
    mask_ref[1] = own.astype(BF)
    mask_ref[2] = high.astype(BF)

    @pl.when(row == 0)
    def _():
        acc_ref[...] = jnp.zeros_like(acc_ref)
        gains_ref[...] = jnp.zeros_like(gains_ref)

    first_half = lax.broadcasted_iota(jnp.int32, (1, lanes), 1) < lanes // 2
    for pair in range(pairs):
        cols = slice(pair * lanes, (pair + 1) * lanes)
        q_pair = q_ref[0, :, cols]
        o_pair = gmix_ref[0, :, cols]
        zero = jnp.zeros_like(q_pair)
        d_q = []
        d_k = [None] * 3
        d_v = [None] * 3
        for half in range(2):
            head = 2 * pair + half
            keep = first_half if half == 0 else jnp.logical_not(first_half)
            q_head = jnp.where(keep, q_pair, zero)
            o_head = jnp.where(keep, o_pair, zero)
            own_on = mask_ref[1].astype(F32) > 0
            low_on = mask_ref[0].astype(F32) > 0
            g_low = dot_nt(o_head, v_ref[0, 0, :, cols])
            g_own = dot_nt(o_head, v_ref[0, 1, :, cols])
            g_high = dot_nt(o_head, v_ref[0, 2, :, cols])
            g_probs = jnp.where(own_on, g_own, jnp.where(low_on, g_low, g_high))
            probs = p_ref[0, head]
            wide = probs.astype(F32)
            product = wide * g_probs
            inner = jnp.sum(product, axis=-1, keepdims=True)
            g_scores = product - wide * inner
            on_own = jnp.where(own_on, g_scores, 0.0)
            acc_ref[head, :, :size] += on_own
            acc_ref[head, :, size:] += g_scores - on_own
            rounded = g_scores.astype(BF)
            total = None
            for part in range(3):
                piece = rounded * mask_ref[part]
                term = dot_nn(piece, k_ref[0, part, :, cols])
                total = term if total is None else total + term
                term = dot_tn(piece, q_head)
                d_k[part] = term if d_k[part] is None else d_k[part] + term
                term = dot_tn(probs * mask_ref[part], o_head)
                d_v[part] = term if d_v[part] is None else d_v[part] + term
            d_q.append(total)
        dq_ref[0, :, cols] = jnp.where(first_half, d_q[0], d_q[1]).astype(BF)
        for part in range(3):
            dk_ref[0, part, :, cols] = d_k[part].astype(BF)
            dv_ref[0, part, :, cols] = d_v[part].astype(BF)

    gain1 = gain1_ref[...].astype(F32)
    gain_1 = jnp.zeros((1, dim), F32)
    for part, source in enumerate((low_ref, own_ref, high_ref)):
        x = source[0].astype(F32)
        scale = rms_scale(x)
        g_norm = dot_nt(dk_ref[0, part], wk_ref[...]) + dot_nt(dv_ref[0, part], wv_ref[...])
        if part == 1:
            g_norm = g_norm + dot_nt(dq_ref[0], wq_ref[...])
        gain_1 = gain_1 + jnp.sum(g_norm * x * scale, axis=0, keepdims=True)
        g_x = rms_back(x, scale, g_norm * gain1)
        if part == 1:
            part_ref[0] = gafter_ref[0] + g_x
        else:
            halo_ref[0, part // 2] = g_x.astype(BF)
    gains_ref[0:1, :] += gain_1


def attend_back(lengths, place, own, low, high, q, k, v, p, gmix, gafter, gain1, weights):
    count, size, dim = own.shape
    heads = p.shape[1]
    outs = (
        ((size, dim), BF),
        ((3, size, dim), BF),
        ((3, size, dim), BF),
        ((size, dim), F32),
        ((2, size, dim), BF),
    )
    constants = (gain1,) + tuple(weights)
    return pl.pallas_call(
        attend_back_kernel,
        grid_spec=pltpu.PrefetchScalarGridSpec(
            num_scalar_prefetch=2,
            grid=(count,),
            in_specs=[row_spec((size, dim))] * 4
            + [row_spec((3, size, dim))] * 2
            + [row_spec((heads, size, size))]
            + [row_spec((size, dim))] * 2
            + [full(item.shape) for item in constants],
            out_specs=[row_spec(shape) for shape, _ in outs]
            + [
                pl.BlockSpec((heads, size, 2 * size), lambda *_: (0, 0, 0)),
                pl.BlockSpec((8, dim), lambda *_: (0, 0)),
            ],
            scratch_shapes=[pltpu.VMEM((3, size, size), BF)],
        ),
        out_shape=[jax.ShapeDtypeStruct((count,) + shape, kind) for shape, kind in outs]
        + [
            jax.ShapeDtypeStruct((heads, size, 2 * size), F32),
            jax.ShapeDtypeStruct((8, dim), F32),
        ],
        compiler_params=params(),
        name="attend_back_rows",
    )(lengths, place, own, low, high, q, k, v, p, gmix, gafter, *constants)


def flip(block, axis, bit):
    count = lax.axis_size(axis)
    return lax.ppermute(block, axis, [(i, i ^ bit) for i in range(count)])


def sum_along(block, axis):
    bit = 1
    while bit < lax.axis_size(axis):
        block = block + flip(block, axis, bit)
        bit *= 2
    return block


def gather_along(block, axis):
    bits = []
    bit = 1
    while bit < lax.axis_size(axis):
        bits.append(bit)
        bit *= 2
    place = lax.axis_index(axis)
    block = block[None]
    for bit in reversed(bits):
        other = flip(block, axis, bit)
        upper = (place // bit) % 2 == 1
        block = jnp.stack([jnp.where(upper, other, block), jnp.where(upper, block, other)], axis=1)
        block = block.reshape((-1,) + block.shape[2:])
    count = block.shape[0]
    order = []
    for index in range(count):
        where_at = 0
        for level, bit in enumerate(bits):
            if index & bit:
                where_at += count >> (level + 1)
        order.append(where_at)
    return jnp.concatenate([block[i] for i in order], axis=0)


def contrast(pooled, w_proj, partner):
    proj = w_proj.astype(F32)
    raw = jnp.dot(pooled, proj, precision=HIGHEST)
    inv_norm = lax.rsqrt(jnp.sum(raw * raw, axis=-1, keepdims=True) + EPS)
    embedded = raw * inv_norm
    everyone = lax.all_gather(embedded, "batch", axis=0, tiled=True)
    own_count = embedded.shape[0]
    total = everyone.shape[0]
    own_index = lax.axis_index("batch") * own_count + jnp.arange(own_count, dtype=jnp.int32)
    columns = jnp.arange(total, dtype=jnp.int32)

    def lse_of(rows, index):
        logits = SHARPNESS * jnp.einsum("nd,md->nm", rows, everyone, precision=HIGHEST)
        logits = jnp.where(columns[None, :] == index[:, None], NEGATIVE, logits)
        peak = jnp.max(logits, axis=-1, keepdims=True)
        return peak[:, 0] + jnp.log(jnp.sum(jnp.exp(logits - peak), axis=-1))

    if total <= 1024:
        lse_all = lse_of(everyone, columns)
    else:
        lse_all = lax.map(
            lambda pieces: lse_of(pieces[0], pieces[1]),
            (everyone.reshape(-1, 512, everyone.shape[1]), columns.reshape(-1, 512)),
        ).reshape(-1)
    logits = SHARPNESS * jnp.einsum("nd,md->nm", embedded, everyone, precision=HIGHEST)
    is_self = columns[None, :] == own_index[:, None]
    logits = jnp.where(is_self, NEGATIVE, logits)
    peak = jnp.max(logits, axis=-1, keepdims=True)
    lse_own = peak[:, 0] + jnp.log(jnp.sum(jnp.exp(logits - peak), axis=-1))
    is_target = columns[None, :] == partner[:, None]
    picked = jnp.sum(jnp.where(is_target, logits, 0.0), axis=-1)
    loss = lse_own - picked
    both = SHARPNESS * (
        jnp.exp(logits - lse_own[:, None])
        + jnp.exp(logits - lse_all[None, :])
        - 2.0 * is_target.astype(F32)
    )
    grad_emb = jnp.dot(both, everyone, precision=HIGHEST)
    grad_raw = inv_norm * (
        grad_emb - embedded * jnp.sum(embedded * grad_emb, axis=-1, keepdims=True)
    )
    grad_pooled = jnp.einsum("ne,de->nd", grad_raw, proj, precision=HIGHEST)
    return embedded, loss, grad_raw, grad_pooled


def shards(
    tokens,
    norm1_gain,
    w_query,
    w_key,
    w_value,
    rel_bias,
    w_output,
    norm2_gain,
    w_in,
    w_out,
    final_gain,
    w_proj,
    lengths,
    partner,
    cotangent,
):
    rows, size, dim = tokens.shape
    slots = lengths.shape[1]
    toks = rows * size
    seq_count = lax.axis_size("seq")
    seq_place = lax.axis_index("seq")
    place = seq_place.astype(jnp.int32).reshape(1)
    up = [(i, i + 1) for i in range(seq_count - 1)]
    down = [(i + 1, i) for i in range(seq_count - 1)]
    gain1 = norm1_gain.reshape(1, dim)
    gain2 = norm2_gain.reshape(1, dim)
    gainf = final_gain.reshape(1, dim)

    x_low = lax.ppermute(tokens, "seq", up)
    x_high = lax.ppermute(tokens, "seq", down)
    bias = bias_tables(rel_bias, size)
    (block, partial, n1, q, k, v, p, att, after, n2, act, dact) = forward(
        0,
        rows,
        lengths,
        place,
        tokens,
        x_low,
        x_high,
        (gain1, gain2, gainf),
        (w_query, w_key, w_value, w_output, w_in, w_out),
        bias,
    )
    pooled_sum = sum_along(partial, "seq")
    counts = lengths.astype(F32)[:, :, None]
    pooled = (pooled_sum / counts).reshape(rows * slots, dim)
    embedded, loss, grad_raw, grad_pooled = contrast(pooled, w_proj, partner)
    lead_only = (seq_place == 0).astype(F32)
    grad_proj = jnp.einsum("ne,nd->ed", lead_only * grad_raw, pooled, precision=HIGHEST)
    pool_grad = grad_pooled.reshape(rows, slots, dim) / counts

    g_branch, g_pre, g_after, g_mix, gains_a = feed_back(
        lengths,
        place,
        block,
        after,
        cotangent,
        pool_grad,
        dact,
        (gain2, gainf),
        (w_output, w_in, w_out),
    )
    flat = lambda array: array.reshape(-1, array.shape[-1])
    t_in = weight_grad(flat(g_pre), flat(n2), 768)
    t_out = weight_grad(flat(g_branch), flat(act), 256)
    t_output = weight_grad(flat(g_after), flat(att), 768)
    dq, dk, dv, part, halo, acc, gains_b = attend_back(
        lengths,
        place,
        tokens,
        x_low,
        x_high,
        q,
        k,
        v,
        p,
        g_mix,
        g_after,
        gain1,
        (w_query, w_key, w_value),
    )
    from_above = lax.ppermute(halo[:, 0], "seq", down)
    from_below = lax.ppermute(halo[:, 1], "seq", up)
    t_query = weight_grad(flat(dq), flat(n1[:, 1]), 768)
    t_key = weight_grad(flat(dk), flat(n1), 768)
    t_value = weight_grad(flat(dv), flat(n1), 768)
    grad_tokens = part + from_above.astype(F32) + from_below.astype(F32)
    grad_rel = bias_grad(acc, rel_bias.shape[0])

    batch_count = lax.axis_size("batch")

    def reduce(array):
        return lax.psum_scatter(array, "batch", scatter_dimension=0, tiled=True)

    def finish(array):
        mine = lax.psum_scatter(array, "seq", scatter_dimension=1, tiled=True)
        return mine.T.astype(F32)

    s_in = finish(reduce(t_in))
    s_out = finish(reduce(t_out))
    small = [
        finish(reduce(item.astype(BF)))
        for item in (t_query, t_key, t_value, t_output, grad_proj)
    ]
    sums = lax.psum((gains_b[0], gains_a[1], gains_a[0], grad_rel), ("batch", "seq"))
    return (
        block,
        embedded,
        loss,
        grad_tokens,
        sums[0],
        small[0],
        small[1],
        small[2],
        sums[3],
        small[3],
        sums[1],
        s_in,
        s_out,
        sums[2],
        small[4],
    )


def solution(mesh):
    tok = P("batch", "seq", None)
    mat = P("seq", "batch")
    return jax.shard_map(
        shards,
        mesh=mesh,
        in_specs=(tok,) + (P(),) * 11 + (P("batch", None), P("batch"), tok),
        out_specs=(
            tok,
            P("batch", None),
            P("batch"),
            tok,
            P(),
            mat,
            mat,
            mat,
            P(),
            mat,
            P(),
            mat,
            mat,
            P(),
            mat,
        ),
        check_vma=False,
    )
```

```python
import functools

import jax
import jax.numpy as jnp
from jax import lax
from jax.experimental import pallas as pl
from jax.experimental.pallas import tpu as pltpu
from jax.sharding import PartitionSpec as P

EPS = 1e-06
NEGATIVE = -1e30
SHARPNESS = 50.0
THRESHOLDS = (12, 16, 23, 32, 46, 64, 91)
HIGHEST = lax.Precision.HIGHEST
BF = jnp.bfloat16
F32 = jnp.float32
VMEM_BYTES = 60 * 1024 * 1024
GELU_A = 0.7978845608028654
GELU_B = 0.044715


def dot_nn(left, right):
    return lax.dot_general(left, right, (((1,), (0,)), ((), ())), preferred_element_type=F32)


def dot_nt(left, right):
    return lax.dot_general(left, right, (((1,), (1,)), ((), ())), preferred_element_type=F32)


def dot_tn(left, right):
    return lax.dot_general(left, right, (((0,), (0,)), ((), ())), preferred_element_type=F32)


def rms_scale(values):
    return lax.rsqrt(jnp.mean(values * values, axis=-1, keepdims=True) + EPS)


def rms_back(values, scale, grad_normed):
    inner = jnp.mean(grad_normed * values, axis=-1, keepdims=True)
    return scale * (grad_normed - values * (scale * scale * inner))


def split_bf(values):
    high = values.astype(BF)
    return high, (values - high.astype(F32)).astype(BF)


def bucket_of(offset):
    distance = jnp.abs(offset)
    beyond = jnp.zeros_like(distance)
    for threshold in THRESHOLDS:
        beyond = beyond + (distance >= threshold).astype(jnp.int32)
    within = jnp.where(distance < 8, distance, 8 + beyond)
    return within + 16 * (offset > 0).astype(jnp.int32)


def wrapped_offsets(shape, axis, size):
    place = lax.broadcasted_iota(jnp.int32, shape, axis)
    return jnp.where(place < size, place, place - 2 * size)


def full(shape):
    return pl.BlockSpec(shape, lambda *_: (0,) * len(shape), pipeline_mode=pl.Buffered(1))


def row_spec(shape, first=0):
    return pl.BlockSpec(
        (1,) + tuple(shape), lambda step, *_: (step + first,) + (0,) * len(shape)
    )


def cost(products, moved, exps=0):
    return pl.CostEstimate(flops=2 * products, bytes_accessed=moved, transcendentals=exps)


def params(limit=VMEM_BYTES):
    return pltpu.CompilerParams(
        vmem_limit_bytes=limit, dimension_semantics=("arbitrary",)
    )


def bias_kernel(size, table_ref, out_ref):
    buckets, heads = table_ref.shape
    hot = (
        lax.broadcasted_iota(jnp.int32, (buckets, 2 * size), 0)
        == bucket_of(wrapped_offsets((buckets, 2 * size), 1, size))
    ).astype(BF)
    by_offset = dot_tn(table_ref[...], hot)
    for head in range(heads):
        line = jnp.broadcast_to(by_offset[head : head + 1, :], (size, 2 * size))
        out_ref[head] = pltpu.roll(line, 0, 1, stride=1, stride_axis=0).astype(BF)


def bias_tables(rel_bias, size):
    heads = rel_bias.shape[1]
    return pl.pallas_call(
        functools.partial(bias_kernel, size),
        out_shape=jax.ShapeDtypeStruct((heads, size, 2 * size), BF),
        compiler_params=pltpu.CompilerParams(vmem_limit_bytes=VMEM_BYTES),
    )(rel_bias)


def bias_grad_kernel(*refs):
    acc_refs, out_ref = refs[:-1], refs[-1]
    group, size, width = acc_refs[0].shape
    buckets = out_ref.shape[2]
    hot = (
        lax.broadcasted_iota(jnp.int32, (width, buckets), 1)
        == bucket_of(wrapped_offsets((width, buckets), 0, width // 2))
    ).astype(BF)
    for head in range(group):
        rows = sum(acc_ref[head] for acc_ref in acc_refs)
        count = size
        while count > 8:
            count = count // 2
            rows = rows[:count] + pltpu.roll(rows[count:], width - count, 1)
        place = lax.broadcasted_iota(jnp.int32, rows.shape, 0)
        for bit in (4, 2, 1):
            rows = jnp.where((place & bit) > 0, pltpu.roll(rows, width - bit, 1), rows)
        first, rest = split_bf(rows)
        second, third = split_bf(rows - first.astype(F32))
        out_ref[head] = dot_nn(first, hot) + dot_nn(second, hot) + dot_nn(third, hot)


def bias_grad(accs, buckets):
    heads, count, width = accs[0].shape
    group = max(size for size in (1, 2, 3, 4) if heads % size == 0)
    out = pl.pallas_call(
        bias_grad_kernel,
        grid=(heads // group,),
        in_specs=[pl.BlockSpec((group, count, width), lambda step: (step, 0, 0))] * len(accs),
        out_specs=pl.BlockSpec((group, 8, buckets), lambda step: (step, 0, 0)),
        out_shape=jax.ShapeDtypeStruct((heads, 8, buckets), F32),
        compiler_params=params(),
        name="bias_grad",
    )(*accs)
    return jnp.sum(out, axis=1).T


def row_masks(lengths_ref, place_ref, row, size):
    slots = lengths_ref.shape[1]
    base = place_ref[0] * size
    col_pos = base + lax.broadcasted_iota(jnp.int32, (size, 1), 0)
    row_pos = base + lax.broadcasted_iota(jnp.int32, (1, size), 1)
    seg_col = jnp.zeros((size, 1), jnp.int32)
    seg_own = jnp.zeros((1, size), jnp.int32)
    seg_low = jnp.zeros((1, size), jnp.int32)
    seg_high = jnp.zeros((1, size), jnp.int32)
    end = jnp.int32(0)
    for slot in range(slots):
        end = end + lengths_ref[row, slot]
        seg_col = seg_col + (end <= col_pos).astype(jnp.int32)
        seg_own = seg_own + (end <= row_pos).astype(jnp.int32)
        seg_low = seg_low + (end <= row_pos - size).astype(jnp.int32)
        seg_high = seg_high + (end <= row_pos + size).astype(jnp.int32)
    seg_low = jnp.where(row_pos < size, -1, seg_low)
    upper = lax.broadcasted_iota(jnp.int32, (size, size), 1) > lax.broadcasted_iota(
        jnp.int32, (size, size), 0
    )
    own = (seg_col == seg_own).astype(F32)
    above = upper.astype(F32)
    low = (seg_col == seg_low).astype(F32) * above
    high = (seg_col == seg_high).astype(F32) * (1.0 - above)
    return seg_col, seg_own, own, low, high


def forward_kernel(
    first,
    lengths_ref,
    place_ref,
    own_ref,
    low_ref,
    high_ref,
    gain1_ref,
    gain2_ref,
    gainf_ref,
    wq_ref,
    wk_ref,
    wv_ref,
    wo_ref,
    win_ref,
    wout_ref,
    bias_ref,
    block_ref,
    pooled_ref,
    n1_ref,
    q_ref,
    k_ref,
    v_ref,
    p_ref,
    att_ref,
    after_ref,
    n2_ref,
    act_ref,
    dact_ref,
    mask_ref,
):
    size, dim = own_ref.shape[1:]
    heads = bias_ref.shape[0]
    pairs = heads // 2
    lanes = dim // pairs
    hidden = win_ref.shape[1]
    slots = pooled_ref.shape[1]
    row = pl.program_id(0) + first
    seg_col, seg_own, own, low, high = row_masks(lengths_ref, place_ref, row, size)
    mask_ref[0] = own.astype(BF)
    mask_ref[1] = low.astype(BF)
    mask_ref[2] = high.astype(BF)
    gain1 = gain1_ref[...].astype(F32)
    for part, source in enumerate((low_ref, own_ref, high_ref)):
        x = source[0].astype(F32)
        n1_ref[0, part] = (x * rms_scale(x) * gain1).astype(BF)
    q_ref[0] = dot_nn(n1_ref[0, 1], wq_ref[...]).astype(BF)
    for part in range(3):
        k_ref[0, part] = dot_nn(n1_ref[0, part], wk_ref[...]).astype(BF)
        v_ref[0, part] = dot_nn(n1_ref[0, part], wv_ref[...]).astype(BF)
    first_half = lax.broadcasted_iota(jnp.int32, (1, lanes), 1) < lanes // 2
    for pair in range(pairs):
        cols = slice(pair * lanes, (pair + 1) * lanes)
        q_pair = q_ref[0, :, cols]
        halves = []
        for half in range(2):
            head = 2 * pair + half
            keep = first_half if half == 0 else jnp.logical_not(first_half)
            q_head = jnp.where(keep, q_pair, jnp.zeros_like(q_pair))
            own_on = mask_ref[0].astype(F32) > 0
            low_on = mask_ref[1].astype(F32) > 0
            high_on = mask_ref[2].astype(F32) > 0
            s_own = dot_nt(q_head, k_ref[0, 1, :, cols]) + bias_ref[head, :, :size].astype(F32)
            s_low = dot_nt(q_head, k_ref[0, 0, :, cols])
            s_high = dot_nt(q_head, k_ref[0, 2, :, cols])
            s_alt = jnp.where(low_on, s_low, s_high) + bias_ref[head, :, size:].astype(F32)
            scores = jnp.where(
                own_on, s_own, jnp.where(low_on | high_on, s_alt, NEGATIVE)
            )
            peak = jnp.max(scores, axis=-1, keepdims=True)
            powers = jnp.exp(scores - peak)
            inverse = 1.0 / jnp.sum(powers, axis=-1, keepdims=True)
            probs = (powers * inverse).astype(BF)
            p_ref[0, head] = probs
            mixed = dot_nn(probs * mask_ref[1], v_ref[0, 0, :, cols])
            mixed += dot_nn(probs * mask_ref[0], v_ref[0, 1, :, cols])
            mixed += dot_nn(probs * mask_ref[2], v_ref[0, 2, :, cols])
            halves.append(mixed)
        att_ref[0, :, cols] = jnp.where(first_half, halves[0], halves[1]).astype(BF)
    after = own_ref[0].astype(F32) + dot_nn(att_ref[0], wo_ref[...])
    after_ref[0] = after
    n2_ref[0] = (after * rms_scale(after) * gain2_ref[...].astype(F32)).astype(BF)
    total = after
    chunk = dim
    for start in range(0, hidden, chunk):
        cols = slice(start, start + chunk)
        pre = dot_nn(n2_ref[0], win_ref[:, cols])
        square = pre * pre
        gate = 0.5 + 0.5 * jnp.tanh(pre * (GELU_A + (GELU_A * GELU_B) * square))
        act = pre * gate
        slope = gate + act * (1.0 - gate) * (2 * GELU_A + (6 * GELU_A * GELU_B) * square)
        act_ref[0, :, cols] = act.astype(BF)
        dact_ref[0, :, cols] = slope.astype(BF)
        total = total + dot_nn(act_ref[0, :, cols], wout_ref[cols, :])
    block = total.astype(BF)
    block_ref[0] = block
    out = block.astype(F32)
    final = out * rms_scale(out) * gainf_ref[...].astype(F32)
    member = (lax.broadcasted_iota(jnp.int32, (slots, size), 0) == seg_own).astype(BF)
    high_part, low_part = split_bf(final)
    pooled_ref[0] = dot_nn(member, high_part) + dot_nn(member, low_part)


def forward(first, count, lengths, place, own, low, high, gains, weights, bias):
    size, dim = own.shape[1:]
    heads = bias.shape[0]
    slots = lengths.shape[1]
    hidden = weights[4].shape[1]
    outs = (
        ((size, dim), BF),
        ((slots, dim), F32),
        ((3, size, dim), BF),
        ((size, dim), BF),
        ((3, size, dim), BF),
        ((3, size, dim), BF),
        ((heads, size, size), BF),
        ((size, dim), BF),
        ((size, dim), F32),
        ((size, dim), BF),
        ((size, hidden), BF),
        ((size, hidden), BF),
    )
    constants = tuple(gains) + tuple(weights) + (bias,)
    return pl.pallas_call(
        functools.partial(forward_kernel, first),
        grid_spec=pltpu.PrefetchScalarGridSpec(
            num_scalar_prefetch=2,
            grid=(count,),
            in_specs=[row_spec((size, dim), first)]
            + [row_spec((size, dim), 0)] * 2
            + [full(item.shape) for item in constants],
            out_specs=[row_spec(shape) for shape, _ in outs],
            scratch_shapes=[pltpu.VMEM((3, size, size), BF)],
        ),
        out_shape=[jax.ShapeDtypeStruct((count,) + shape, kind) for shape, kind in outs],
        compiler_params=params(),
        cost_estimate=cost(
            count * size * dim * (8 * dim + 2 * hidden + 36 * size),
            count * size * (hidden * 4 + dim * 40),
            count * heads * size * size,
        ),
        name="forward_rows",
    )(lengths, place, own, low, high, *constants)


def store_split(core, value, refs, count, first=0):
    if len(refs) == 1:
        refs[0][first : first + value.shape[0], :] = value
        return
    groups = value.shape[0] // (2 * count)
    for group in range(groups):
        even = value[2 * group * count : (2 * group + 1) * count]
        odd = value[(2 * group + 1) * count : (2 * group + 2) * count]

        @pl.when(core == 0)
        def _():
            refs[0][group, first : first + count, :] = even
            refs[1][group, first : first + count, :] = odd

        @pl.when(core != 0)
        def _():
            refs[0][group, first : first + count, :] = odd
            refs[1][group, first : first + count, :] = even


def feed_back_kernel(
    rows,
    parts,
    lengths_ref,
    place_ref,
    block_ref,
    after_ref,
    cot_ref,
    att_ref,
    n2_ref,
    act_ref,
    dact_ref,
    pool_ref,
    graw_ref,
    pooled_ref,
    gain2_ref,
    gainf_ref,
    wo_ref,
    win_ref,
    wout_ref,
    gafter_ref,
    gmix_ref,
    gains_ref,
    *rest,
):
    split = len(rest) == 12
    per = 2 if split else 1
    in_refs, out_refs, small_refs = (rest[i * per : (i + 1) * per] for i in range(3))
    branch_all, pre_all, act_all, n2_all, att_all, gatt_all = rest[3 * per :]
    size, dim = block_ref.shape[1:]
    hidden = win_ref.shape[1]
    slots = pool_ref.shape[1]
    step = pl.program_id(0)
    tiles = hidden // dim
    core = place_ref[1]

    @pl.when(step < rows)
    def _():
        here = pl.ds(pl.multiple_of(step * size, size), size)
        base = place_ref[0] * size
        col_pos = base + lax.broadcasted_iota(jnp.int32, (size, 1), 0)
        seg_col = jnp.zeros((size, 1), jnp.int32)
        end = jnp.int32(0)
        for slot in range(slots):
            end = end + lengths_ref[step, slot]
            seg_col = seg_col + (end <= col_pos).astype(jnp.int32)
        member = (lax.broadcasted_iota(jnp.int32, (size, slots), 1) == seg_col).astype(BF)
        high_part, low_part = split_bf(pool_ref[0])
        g_final = dot_nn(member, high_part) + dot_nn(member, low_part)
        out = block_ref[0].astype(F32)
        scale = rms_scale(out)
        gain_f = jnp.sum(g_final * out * scale, axis=0, keepdims=True)
        g_out = rms_back(out, scale, g_final * gainf_ref[...].astype(F32))
        g_out = g_out + cot_ref[0].astype(F32)
        branch = g_out.astype(BF)
        branch_all[here, :] = branch
        n2_all[here, :] = n2_ref[0]
        att_all[here, :] = att_ref[0]
        g_n2 = jnp.zeros((size, dim), F32)
        for start in range(0, hidden, dim):
            cols = slice(start, start + dim)
            g_hidden = dot_nt(branch, wout_ref[cols, :])
            g_pre = (g_hidden * dact_ref[0, :, cols].astype(F32)).astype(BF)
            pre_all[here, cols] = g_pre
            act_all[here, cols] = act_ref[0, :, cols]
            g_n2 = g_n2 + dot_nt(g_pre, win_ref[:, cols])
        after = after_ref[0]
        scale = rms_scale(after)
        gain_2 = jnp.sum(g_n2 * after * scale, axis=0, keepdims=True)
        g_after = g_out + rms_back(after, scale, g_n2 * gain2_ref[...].astype(F32))
        gafter_ref[0] = g_after
        g_att = g_after.astype(BF)
        gatt_all[here, :] = g_att
        gmix_ref[0] = dot_nt(g_att, wo_ref[...]).astype(BF)

        @pl.when(step == 0)
        def _():
            gains_ref[...] = jnp.zeros_like(gains_ref)

        gains_ref[0:1, :] += gain_f
        gains_ref[1:2, :] += gain_2

    @pl.when((step >= rows) & (step < rows + tiles))
    def _():
        cols = pl.ds(pl.multiple_of((step - rows) * dim, dim), dim)
        value = dot_tn(branch_all[...], act_all[:, cols]).astype(BF)
        store_split(core, value, out_refs, dim // parts)

    @pl.when((step >= rows + tiles) & (step < rows + 2 * tiles))
    def _():
        cols = pl.ds(pl.multiple_of((step - rows - tiles) * dim, dim), dim)
        value = dot_tn(pre_all[:, cols], n2_all[...]).astype(BF)
        store_split(core, value, in_refs, hidden // parts)

    @pl.when(step == rows + 2 * tiles)
    def _():
        value = dot_tn(gatt_all[...], att_all[...]).astype(BF)
        store_split(core, value, small_refs, dim // parts)
        left_high, left_low = split_bf(graw_ref[...])
        right_high, right_low = split_bf(pooled_ref[...])
        value = dot_tn(left_high, right_high)
        value += dot_tn(left_high, right_low) + dot_tn(left_low, right_high)
        first = dim // parts if split else dim
        store_split(core, value.astype(BF), small_refs, dim // parts, first)


def feed_back(parts, lengths, place, block, after, cot, att, n2, act, dact, pool, graw, pooled, gains, weights):
    rows, size, dim = block.shape
    slots = lengths.shape[1]
    hidden = dact.shape[2]
    tiles = hidden // dim
    toks = rows * size
    split = (dim // parts) % 16 == 0 and dim % (2 * hidden // parts) == 0
    per_row = lambda shape: pl.BlockSpec(
        (1,) + shape, lambda step, *_: (jnp.minimum(step, rows - 1),) + (0,) * len(shape)
    )
    during = lambda step, first: jnp.clip(step - first, 0, tiles - 1)
    if split:
        groups = parts // 2
        wide = hidden // parts
        inner = dim // (2 * wide)
        narrow = dim // parts
        in_specs = [pl.BlockSpec((inner, wide, dim), lambda step, *_: (during(step, rows + tiles), 0, 0))] * 2
        out_specs = [pl.BlockSpec((groups, narrow, dim), lambda step, *_: (0, during(step, rows), 0))] * 2
        small_specs = [full((groups, 2 * narrow, dim))] * 2
        shapes = [(groups, wide, dim)] * 2 + [(groups, tiles * narrow, dim)] * 2 + [(groups, 2 * narrow, dim)] * 2
    else:
        in_specs = [pl.BlockSpec((dim, dim), lambda step, *_: (during(step, rows + tiles), 0))]
        out_specs = [pl.BlockSpec((dim, dim), lambda step, *_: (during(step, rows), 0))]
        small_specs = [full((2 * dim, dim))]
        shapes = [(hidden, dim), (tiles * dim, dim), (2 * dim, dim)]
    constants = (graw, pooled) + tuple(gains) + tuple(weights)
    outs = pl.pallas_call(
        functools.partial(feed_back_kernel, rows, parts),
        grid_spec=pltpu.PrefetchScalarGridSpec(
            num_scalar_prefetch=2,
            grid=(rows + 2 * tiles + 1,),
            in_specs=[per_row((size, dim))] * 5
            + [per_row((size, hidden))] * 2
            + [per_row((slots, dim))]
            + [full(item.shape) for item in constants],
            out_specs=[per_row((size, dim))] * 2
            + [full((8, dim))]
            + in_specs
            + out_specs
            + small_specs,
            scratch_shapes=[
                pltpu.VMEM((toks, dim), BF),
                pltpu.VMEM((toks, hidden), BF),
                pltpu.VMEM((toks, hidden), BF),
                pltpu.VMEM((toks, dim), BF),
                pltpu.VMEM((toks, dim), BF),
                pltpu.VMEM((toks, dim), BF),
            ],
        ),
        out_shape=[
            jax.ShapeDtypeStruct((rows, size, dim), F32),
            jax.ShapeDtypeStruct((rows, size, dim), BF),
            jax.ShapeDtypeStruct((8, dim), F32),
        ]
        + [jax.ShapeDtypeStruct(shape, BF) for shape in shapes],
        compiler_params=params(),
        cost_estimate=cost(
            toks * dim * (4 * hidden + 2 * dim), toks * (hidden * 4 + dim * 20) + 8 * hidden * dim
        ),
        name="feed_back_rows",
    )(lengths, place, block, after, cot, att, n2, act, dact, pool, *constants)
    if split:
        mine, theirs = outs[3::2], outs[4::2]
    else:
        whole = [
            outs[3].reshape(parts, hidden // parts, dim),
            outs[4].reshape(tiles, parts, dim // parts, dim).transpose(1, 0, 2, 3),
            outs[5].reshape(2, parts, dim // parts, dim).transpose(1, 0, 2, 3),
        ]
        mine, theirs = split_core(whole)
    return outs[0], outs[1], outs[2], mine, theirs


def split_core(blocks):
    core = (lax.axis_index("batch") % 2).astype(jnp.int32)
    pairs = [item.reshape((item.shape[0] // 2, 2, -1, item.shape[-1])) for item in blocks]
    pick = lambda item, place: lax.dynamic_index_in_dim(item, place, 1, keepdims=False)
    return [pick(item, core) for item in pairs], [pick(item, 1 - core) for item in pairs]


def attend_grad_kernel(parts, place_ref, n1_ref, dq_ref, dk_ref, dv_ref, *rest):
    refs, sums = rest[:-3], rest[-3:]
    size, dim = dq_ref.shape[1:]
    step = pl.program_id(0)
    flat = lambda ref: ref[0].reshape(3 * size, dim)
    terms = (
        dot_tn(dq_ref[0], n1_ref[0, 1]),
        dot_tn(flat(dk_ref), flat(n1_ref)),
        dot_tn(flat(dv_ref), flat(n1_ref)),
    )
    last = pl.num_programs(0) - 1
    for index, term in enumerate(terms):

        @pl.when(step == 0)
        def _():
            sums[index][...] = term

        @pl.when(step > 0)
        def _():
            sums[index][...] += term

    @pl.when(step == last)
    def _():
        for index in range(3):
            width = dim // parts if len(refs) == 2 else dim
            value = sums[index][...].astype(BF)
            store_split(place_ref[1], value, refs, dim // parts, index * width)


def attend_grad(parts, place, n1, dq, dk, dv):
    rows, size, dim = dq.shape
    narrow = dim // parts
    split = narrow % 16 == 0
    shape = (parts // 2, 3 * narrow, dim) if split else (3 * dim, dim)
    copies = 2 if split else 1
    outs = pl.pallas_call(
        functools.partial(attend_grad_kernel, parts),
        grid_spec=pltpu.PrefetchScalarGridSpec(
            num_scalar_prefetch=1,
            grid=(rows,),
            in_specs=[
                row_spec((3, size, dim)),
                row_spec((size, dim)),
                row_spec((3, size, dim)),
                row_spec((3, size, dim)),
            ],
            out_specs=[full(shape)] * copies,
            scratch_shapes=[pltpu.VMEM((dim, dim), F32)] * 3,
        ),
        out_shape=[jax.ShapeDtypeStruct(shape, BF)] * copies,
        compiler_params=params(),
        cost_estimate=cost(rows * size * dim * dim * 7, rows * size * dim * 26),
        name="attend_grad",
    )(place, n1, dq, dk, dv)
    if split:
        return outs[0], outs[1]
    mine, theirs = split_core([outs[0].reshape(3, parts, narrow, dim).transpose(1, 0, 2, 3)])
    return mine[0], theirs[0]


def attend_back_kernel(
    first,
    lengths_ref,
    place_ref,
    own_ref,
    low_ref,
    high_ref,
    q_ref,
    k_ref,
    v_ref,
    p_ref,
    gmix_ref,
    gafter_ref,
    gain1_ref,
    wq_ref,
    wk_ref,
    wv_ref,
    *rest,
):
    dq_ref, dk_ref, dv_ref, part_ref, to_low_ref, to_high_ref, acc_ref, gains_ref, mask_ref = rest[-9:]
    size, dim = own_ref.shape[1:]
    heads = p_ref.shape[1]
    pairs = heads // 2
    lanes = dim // pairs
    row = pl.program_id(0)
    _, _, own, low, high = row_masks(lengths_ref, place_ref, row + first, size)
    mask_ref[0] = low.astype(BF)
    mask_ref[1] = own.astype(BF)
    mask_ref[2] = high.astype(BF)

    @pl.when(row == 0)
    def _():
        acc_ref[...] = jnp.zeros_like(acc_ref)
        gains_ref[...] = jnp.zeros_like(gains_ref)

    first_half = lax.broadcasted_iota(jnp.int32, (1, lanes), 1) < lanes // 2
    for pair in range(pairs):
        cols = slice(pair * lanes, (pair + 1) * lanes)
        q_pair = q_ref[0, :, cols]
        o_pair = gmix_ref[0, :, cols]
        zero = jnp.zeros_like(q_pair)
        d_q = []
        d_k = [None] * 3
        d_v = [None] * 3
        for half in range(2):
            head = 2 * pair + half
            keep = first_half if half == 0 else jnp.logical_not(first_half)
            q_head = jnp.where(keep, q_pair, zero)
            o_head = jnp.where(keep, o_pair, zero)
            own_on = mask_ref[1].astype(F32) > 0
            low_on = mask_ref[0].astype(F32) > 0
            g_low = dot_nt(o_head, v_ref[0, 0, :, cols])
            g_own = dot_nt(o_head, v_ref[0, 1, :, cols])
            g_high = dot_nt(o_head, v_ref[0, 2, :, cols])
            g_probs = jnp.where(own_on, g_own, jnp.where(low_on, g_low, g_high))
            probs = p_ref[0, head]
            wide = probs.astype(F32)
            product = wide * g_probs
            inner = jnp.sum(product, axis=-1, keepdims=True)
            g_scores = product - wide * inner
            on_own = jnp.where(own_on, g_scores, 0.0)
            off_own = g_scores - on_own
            half_size = size // 2
            acc_ref[head, :, :half_size] += on_own[:half_size, :half_size] + on_own[half_size:, half_size:]
            acc_ref[head, :, half_size:size] += on_own[:half_size, half_size:] + off_own[half_size:, :half_size]
            acc_ref[head, :, size : size + half_size] += off_own[:half_size, :half_size] + off_own[half_size:, half_size:]
            acc_ref[head, :, size + half_size :] += off_own[:half_size, half_size:] + on_own[half_size:, :half_size]
            rounded = g_scores.astype(BF)
            total = None
            for part in range(3):
                piece = rounded * mask_ref[part]
                term = dot_nn(piece, k_ref[0, part, :, cols])
                total = term if total is None else total + term
                term = dot_tn(piece, q_head)
                d_k[part] = term if d_k[part] is None else d_k[part] + term
                term = dot_tn(probs * mask_ref[part], o_head)
                d_v[part] = term if d_v[part] is None else d_v[part] + term
            d_q.append(total)
        dq_ref[0, :, cols] = jnp.where(first_half, d_q[0], d_q[1]).astype(BF)
        for part in range(3):
            dk_ref[0, part, :, cols] = d_k[part].astype(BF)
            dv_ref[0, part, :, cols] = d_v[part].astype(BF)

    gain1 = gain1_ref[...].astype(F32)
    gain_1 = jnp.zeros((1, dim), F32)
    for part, source in enumerate((low_ref, own_ref, high_ref)):
        x = source[0].astype(F32)
        scale = rms_scale(x)
        g_norm = dot_nt(dk_ref[0, part], wk_ref[...]) + dot_nt(dv_ref[0, part], wv_ref[...])
        if part == 1:
            g_norm = g_norm + dot_nt(dq_ref[0], wq_ref[...])
        gain_1 = gain_1 + jnp.sum(g_norm * x * scale, axis=0, keepdims=True)
        g_x = rms_back(x, scale, g_norm * gain1)
        if part == 1:
            part_ref[0] = gafter_ref[0] + g_x
        else:
            (to_low_ref if part == 0 else to_high_ref)[0] = g_x.astype(BF)
    gains_ref[0:1, :] += gain_1


def attend_back(first, count, earlier, lengths, place, own, low, high, q, k, v, p, gmix, gafter, gain1, weights):
    size, dim = own.shape[1:]
    heads = p.shape[1]
    outs = (
        ((size, dim), BF),
        ((3, size, dim), BF),
        ((3, size, dim), BF),
        ((size, dim), F32),
        ((size, dim), BF),
        ((size, dim), BF),
    )
    constants = (gain1,) + tuple(weights)
    rows = own.shape[0]
    kept = 4
    aliases = {}
    if earlier:
        start = 2 + 9 + len(constants)
        aliases = {start + index: index for index in range(kept)}
    return pl.pallas_call(
        functools.partial(attend_back_kernel, first),
        grid_spec=pltpu.PrefetchScalarGridSpec(
            num_scalar_prefetch=2,
            grid=(count,),
            in_specs=[row_spec((size, dim), first)] * 4
            + [row_spec((3, size, dim), first)] * 2
            + [row_spec((heads, size, size), first)]
            + [row_spec((size, dim), first)] * 2
            + [full(item.shape) for item in constants]
            + [pl.BlockSpec(memory_space=pl.ANY)] * len(earlier),
            out_specs=[row_spec(shape, first) for shape, _ in outs[:kept]]
            + [row_spec(shape) for shape, _ in outs[kept:]]
            + [full((heads, size // 2, 2 * size)), full((8, dim))],
            scratch_shapes=[pltpu.VMEM((3, size, size), BF)],
        ),
        out_shape=[jax.ShapeDtypeStruct((rows,) + shape, kind) for shape, kind in outs[:kept]]
        + [jax.ShapeDtypeStruct((count,) + shape, kind) for shape, kind in outs[kept:]]
        + [
            jax.ShapeDtypeStruct((heads, size // 2, 2 * size), F32),
            jax.ShapeDtypeStruct((8, dim), F32),
        ],
        input_output_aliases=aliases,
        compiler_params=params(),
        cost_estimate=cost(
            count * size * dim * (9 * dim + 128 * size), count * size * dim * 60
        ),
        name="attend_back_rows",
    )(lengths, place, own, low, high, q, k, v, p, gmix, gafter, *constants, *earlier)


def flip(block, axis, bit):
    count = lax.axis_size(axis)
    return lax.ppermute(block, axis, [(i, i ^ bit) for i in range(count)])


def sum_along(block, axis):
    bit = 1
    while bit < lax.axis_size(axis):
        block = block + flip(block, axis, bit)
        bit *= 2
    return block


def bit_places(axis):
    return [1 << level for level in range((lax.axis_size(axis) - 1).bit_length())]


def gather_batch(block):
    place = lax.axis_index("batch")
    bits = bit_places("batch")
    gathered = block[None]
    for bit in reversed(bits):
        other = flip(gathered, "batch", bit)
        upper = (place & bit) > 0
        gathered = jnp.stack(
            [jnp.where(upper, other, gathered), jnp.where(upper, gathered, other)], axis=1
        )
        gathered = gathered.reshape((-1,) + block.shape)
    return gathered.reshape((-1,) + block.shape[1:])


def halve(block, bits, bit):
    axis = bits.index(bit)
    mine = ((lax.axis_index("batch") & bit) > 0).astype(jnp.int32)
    send = lax.dynamic_index_in_dim(block, 1 - mine, axis, keepdims=False)
    keep = lax.dynamic_index_in_dim(block, mine, axis, keepdims=False)
    return keep + flip(send, "batch", bit), [item for item in bits if item != bit]


def after(value, *others):
    return lax.optimization_barrier((value,) + tuple(others))[0]


def stage_kernel(groups, place_ref, *refs):
    ins = refs[: 2 * sum(len(group) for group in groups)]
    outs = refs[len(ins) :]
    taken = 0
    for index, group in enumerate(groups):
        first = 0
        for count in group:
            value = ins[2 * taken][0, 0, 0] + ins[2 * taken + 1][0, 0, 0]
            taken += 1
            for which in range(2):

                @pl.when(pl.program_id(0) == which)
                def _():
                    outs[2 * index + which][0, 0, first : first + count, :] = value

            first += count


def stage(place, groups, bits, pieces):
    columns = groups[0][0][0].shape[-1]
    lead = bits[0][0][0] * bits[0][0][1]
    if any(count % (16 * pieces) or first % count for group in groups for _, _, first, count in group):
        sends, keeps = [], []
        for index, group in enumerate(groups):
            before, behind = bits[index][0]
            total = jnp.concatenate(
                [(kept + arrived)[..., first : first + count, :].reshape(-1, count, columns)
                 for kept, arrived, first, count in group],
                axis=1,
            ).reshape(before, 2, behind, -1, columns)
            pick = lambda which: lax.dynamic_index_in_dim(total, which, 1, keepdims=False)
            sends.append(pick(1 - place[index]).reshape(lead, 1, -1, columns))
            keeps.append(pick(place[index]).reshape(lead, 1, -1, columns))
        return sends, keeps
    in_specs, operands, out_specs, shapes = [], [], [], []
    for index, group in enumerate(groups):
        before, behind = bits[index][0]
        total = 0

        def place_of(half, step, chunk, places, index=index, behind=behind):
            mine = places[index]
            where_at = jnp.where(half == 0, 1 - mine, mine)
            return step // behind, where_at, step % behind, chunk

        for kept, arrived, first, count in group:
            rows = count // pieces
            total += rows
            shape = (before, 2, behind) + kept.shape[-2:]

            def index_map(half, step, chunk, places, place_of=place_of, first=first, rows=rows):
                one, two, three, four = place_of(half, step, chunk, places)
                return one, two, three, four + first // rows, 0

            for item in (kept, arrived):
                in_specs.append(pl.BlockSpec((1, 1, 1, rows, columns), index_map))
                operands.append(item.reshape(shape))
        for which in range(2):

            def out_map(half, step, chunk, places, which=which):
                if which == 0:
                    step = jnp.where(half == 0, step, lead - 1)
                    chunk = jnp.where(half == 0, chunk, pieces - 1)
                else:
                    step = jnp.where(half == 1, step, 0)
                    chunk = jnp.where(half == 1, chunk, 0)
                return step, chunk, 0, 0

            out_specs.append(pl.BlockSpec((1, 1, total, columns), out_map))
            shapes.append(jax.ShapeDtypeStruct((lead, pieces, total, columns), BF))
    outs = pl.pallas_call(
        functools.partial(
            stage_kernel, [[count // pieces for _, _, _, count in group] for group in groups]
        ),
        grid_spec=pltpu.PrefetchScalarGridSpec(
            num_scalar_prefetch=1, grid=(2, lead, pieces), in_specs=in_specs, out_specs=out_specs
        ),
        out_shape=shapes,
        compiler_params=pltpu.CompilerParams(
            vmem_limit_bytes=VMEM_BYTES, dimension_semantics=("arbitrary",) * 3
        ),
        name="halving_stage",
    )(place, *operands)
    return outs[0::2], outs[1::2]


class BatchSum:
    def __init__(self, mine, theirs, streams):
        bits = bit_places("batch")
        arrived = [flip(item, "batch", bits[0]) for item in theirs]
        self.groups = [
            [(mine[item], arrived[item], first, rows) for item, first, rows in stream] for stream in streams
        ]
        self.bits = [bits[1:][::-1]] * len(streams)
        self.steps = len(bits) - 1
        self.done = 0

    def hold(self, *others):
        self.groups = [
            [(kept, after(arrived, *others), first, rows) for kept, arrived, first, rows in group]
            for group in self.groups
        ]

    def advance(self):
        moved, bits, places = [], [], []
        me = lax.axis_index("batch")
        for index, left in enumerate(self.bits):
            bit = left[::-1][index % len(left)]
            axis = left.index(bit)
            moved.append(bit)
            places.append(((me & bit) > 0).astype(jnp.int32))
            bits.append(((1 << axis, 1 << (len(left) - 1 - axis)),))
        sends, keeps = stage(jnp.stack(places), self.groups, bits, 1)
        self.groups = [
            [(keep, flip(send, "batch", bit), 0, keep.shape[2])]
            for keep, send, bit in zip(keeps, sends, moved)
        ]
        self.bits = [[item for item in left if item != bit] for left, bit in zip(self.bits, moved)]
        self.done += 1
        return sends

    def total(self):
        return [(kept + arrived).reshape(kept.shape[-2:]) for ((kept, arrived, _, _),) in self.groups]


def pack_kernel(tiles_rows, keep_a, come_a, keep_b, come_b, out_ref):
    groups, _, wide = out_ref.shape
    cols = wide // 2
    rows = tiles_rows // groups
    first = keep_a[...] + come_a[...]
    second = keep_b[...] + come_b[...]
    for group in range(groups):
        here = slice(group * cols, (group + 1) * cols)
        out_ref[group, :, :cols] = first[:, here]
        for part in range(groups):
            out_ref[group, part * rows : (part + 1) * rows, cols:] = second[
                group * rows : (group + 1) * rows, part * cols : (part + 1) * cols
            ]
        out_ref[group, tiles_rows:, cols:] = second[tiles_rows:, here]


def pack(stream_a, stream_b, tiles_rows, groups):
    (keep_a, come_a), (keep_b, come_b) = stream_a, stream_b
    rows, dim = keep_a.shape[-2:]
    flat = lambda item: item.reshape(rows, dim)
    shape = (groups, rows, 2 * dim // groups)
    if tiles_rows // groups % 16 == 0:
        return pl.pallas_call(
            functools.partial(pack_kernel, tiles_rows),
            out_shape=jax.ShapeDtypeStruct(shape, BF),
            compiler_params=pltpu.CompilerParams(vmem_limit_bytes=VMEM_BYTES),
            name="pack_places",
        )(flat(keep_a), flat(come_a), flat(keep_b), flat(come_b))
    first = flat(keep_a + come_a).reshape(rows, groups, -1).transpose(1, 0, 2)
    second = flat(keep_b + come_b)
    out = second[:tiles_rows].reshape(groups, -1, groups, dim // groups).transpose(0, 2, 1, 3)
    out = out.reshape(groups, tiles_rows, -1)
    last = second[tiles_rows:].reshape(-1, groups, dim // groups).transpose(1, 0, 2)
    return jnp.concatenate([first, jnp.concatenate([out, last], axis=1)], axis=2)


def contrast(pooled, w_proj, partner):
    proj = w_proj.astype(F32)
    raw = jnp.dot(pooled, proj, precision=HIGHEST)
    inv_norm = lax.rsqrt(jnp.sum(raw * raw, axis=-1, keepdims=True) + EPS)
    embedded = raw * inv_norm
    everyone = gather_batch(embedded)
    own_count = embedded.shape[0]
    total = everyone.shape[0]
    own_index = lax.axis_index("batch") * own_count + jnp.arange(own_count, dtype=jnp.int32)
    columns = jnp.arange(total, dtype=jnp.int32)

    def lse_of(rows, index):
        logits = SHARPNESS * jnp.einsum("nd,md->nm", rows, everyone, precision=HIGHEST)
        logits = jnp.where(columns[None, :] == index[:, None], NEGATIVE, logits)
        peak = jnp.max(logits, axis=-1, keepdims=True)
        return peak[:, 0] + jnp.log(jnp.sum(jnp.exp(logits - peak), axis=-1))

    if total <= 1024:
        lse_all = lse_of(everyone, columns)
    else:
        lse_all = lax.map(
            lambda pieces: lse_of(pieces[0], pieces[1]),
            (everyone.reshape(-1, 512, everyone.shape[1]), columns.reshape(-1, 512)),
        ).reshape(-1)
    logits = SHARPNESS * jnp.einsum("nd,md->nm", embedded, everyone, precision=HIGHEST)
    is_self = columns[None, :] == own_index[:, None]
    logits = jnp.where(is_self, NEGATIVE, logits)
    peak = jnp.max(logits, axis=-1, keepdims=True)
    lse_own = peak[:, 0] + jnp.log(jnp.sum(jnp.exp(logits - peak), axis=-1))
    is_target = columns[None, :] == partner[:, None]
    picked = jnp.sum(jnp.where(is_target, logits, 0.0), axis=-1)
    loss = lse_own - picked
    both = SHARPNESS * (
        jnp.exp(logits - lse_own[:, None])
        + jnp.exp(logits - lse_all[None, :])
        - 2.0 * is_target.astype(F32)
    )
    grad_emb = jnp.dot(both, everyone, precision=HIGHEST)
    grad_raw = inv_norm * (
        grad_emb - embedded * jnp.sum(embedded * grad_emb, axis=-1, keepdims=True)
    )
    grad_pooled = jnp.einsum("ne,de->nd", grad_raw, proj, precision=HIGHEST)
    return embedded, loss, grad_raw, grad_pooled


def shards(
    tokens,
    norm1_gain,
    w_query,
    w_key,
    w_value,
    rel_bias,
    w_output,
    norm2_gain,
    w_in,
    w_out,
    final_gain,
    w_proj,
    lengths,
    partner,
    cotangent,
):
    rows, size, dim = tokens.shape
    slots = lengths.shape[1]
    toks = rows * size
    seq_count = lax.axis_size("seq")
    seq_place = lax.axis_index("seq")
    place = seq_place.astype(jnp.int32).reshape(1)
    up = [(i, i + 1) for i in range(seq_count - 1)]
    down = [(i + 1, i) for i in range(seq_count - 1)]
    gain1 = norm1_gain.reshape(1, dim)
    gain2 = norm2_gain.reshape(1, dim)
    gainf = final_gain.reshape(1, dim)

    x_low = lax.ppermute(tokens, "seq", up)
    x_high = lax.ppermute(tokens, "seq", down)
    bias = bias_tables(rel_bias, size)
    (block, partial, n1, q, k, v, p, att, after_attn, n2, act, dact) = forward(
        0,
        rows,
        lengths,
        place,
        tokens,
        x_low,
        x_high,
        (gain1, gain2, gainf),
        (w_query, w_key, w_value, w_output, w_in, w_out),
        bias,
    )
    pooled_sum = sum_along(partial, "seq")
    counts = lengths.astype(F32)[:, :, None]
    pooled = (pooled_sum / counts).reshape(rows * slots, dim)
    embedded, loss, grad_raw, grad_pooled = contrast(pooled, w_proj, partner)
    lead_only = (seq_place == 0).astype(F32)
    pool_grad = grad_pooled.reshape(rows, slots, dim) / counts
    batch_count = lax.axis_size("batch")
    place = jnp.stack([seq_place, lax.axis_index("batch") % 2]).astype(jnp.int32)

    g_after, g_mix, gains_a, mine, theirs = feed_back(
        batch_count,
        lengths,
        place,
        block,
        after_attn,
        cotangent,
        att,
        n2,
        act,
        dact,
        pool_grad,
        lead_only * grad_raw,
        pooled,
        (gain2, gainf),
        (w_output, w_in, w_out),
    )
    hidden = w_in.shape[1]
    width = dim // batch_count
    tiles = hidden // dim
    wide = hidden // batch_count
    feed_sum = BatchSum(
        mine,
        theirs,
        (((0, 0, wide), (2, 0, width)), ((1, 0, tiles * width), (2, width, width))),
    )
    segments = [(0, 1), (1, rows - 2), (rows - 1, 1)] if rows > 2 else [(0, rows)]
    halves, from_above, from_below = [], [], []
    earlier = ()
    for first, count in segments:
        if halves and feed_sum.done < feed_sum.steps:
            place = after(place, *feed_sum.advance())
        if len(halves) > 1:
            place = after(place, from_above[-2], from_below[-2])
        halves.append(
            attend_back(
                first,
                count,
                earlier,
                lengths,
                place,
                tokens,
                x_low,
                x_high,
                q,
                k,
                v,
                p,
                g_mix,
                g_after,
                gain1,
                (w_query, w_key, w_value),
            )
        )
        earlier = tuple(halves[-1][:4])
        feed_sum.hold(halves[-1][7])
        from_above.append(lax.ppermute(halves[-1][4], "seq", down))
        from_below.append(lax.ppermute(halves[-1][5], "seq", up))
    dq, dk, dv, part = earlier
    while feed_sum.done < feed_sum.steps:
        place = after(place, *feed_sum.advance())

    def by_columns(array):
        return array.reshape(array.shape[0], seq_count, -1).transpose(1, 0, 2)

    feed_part = pack(
        *[(group[0][0], group[0][1]) for group in feed_sum.groups], tiles * width, seq_count
    )
    grad_rel = bias_grad([item[6] for item in halves], rel_bias.shape[0])
    gain1_grad = sum(item[7][0] for item in halves)
    small = jnp.concatenate([gain1_grad, gains_a[1], gains_a[0], grad_rel.reshape(-1)])
    small = jnp.pad(small, (0, -small.shape[0] % 1024)).reshape(-1, 128)
    seq_bits = bit_places("seq")
    batch_bits = bit_places("batch")
    arrived = flip(small, "seq", seq_bits[0])
    place = after(place, feed_part, small, *from_above, *from_below)
    attend_mine, attend_theirs = attend_grad(batch_count, place, n1, dq, dk, dv)
    feed_done = lax.psum_scatter(feed_part, "seq", scatter_dimension=0, tiled=True)[0]
    half = 3 * width // 2
    attend_sum = BatchSum([attend_mine], [attend_theirs], (((0, 0, half),), ((0, half, 3 * width - half),)))
    small = after(small, attend_mine) + arrived
    arrived = flip(small, "batch", batch_bits[0])
    attend_sum.hold(arrived)
    for bit in batch_bits[1:]:
        sends = attend_sum.advance()
        small = after(small, *sends) + arrived
        arrived = flip(small, "batch", bit)
        attend_sum.hold(arrived)
    attend_parts = by_columns(jnp.concatenate(attend_sum.total(), axis=0))
    small = after(small, attend_parts) + arrived
    attend_done = lax.dynamic_index_in_dim(attend_parts, seq_place, 0, keepdims=False).astype(F32)
    for distance in range(1, seq_count):
        route = [(i, (i + distance) % seq_count) for i in range(seq_count)]
        target = (seq_place + distance) % seq_count
        send = lax.dynamic_index_in_dim(attend_parts, target, 0, keepdims=False)
        attend_done = attend_done + lax.ppermute(send, "seq", route).astype(F32)
    for bit in seq_bits[1:]:
        small = small + flip(small, "seq", bit)
    small = small.reshape(-1)
    gain_sums = [small[i * dim : (i + 1) * dim] for i in range(3)]
    rel_sum = small[3 * dim : 3 * dim + rel_bias.size].reshape(rel_bias.shape)

    grad_tokens = (
        part
        + jnp.concatenate(from_above, axis=0).astype(F32)
        + jnp.concatenate(from_below, axis=0).astype(F32)
    )
    turn = lambda array: array.T.astype(F32)
    cols = dim // seq_count
    s_in = turn(feed_done[:wide, :cols])
    s_output = turn(feed_done[wide:, :cols])
    s_out = feed_done[:-width, cols:].reshape(seq_count, width, cols)
    s_out = s_out.transpose(0, 2, 1).reshape(dim, width).astype(F32)
    s_proj = turn(feed_done[-width:, cols:])
    s_attend = [turn(attend_done[i * width : (i + 1) * width]) for i in range(3)]
    return (
        block,
        embedded,
        loss,
        grad_tokens,
        gain_sums[0],
        s_attend[0],
        s_attend[1],
        s_attend[2],
        rel_sum,
        s_output,
        gain_sums[1],
        s_in,
        s_out,
        gain_sums[2],
        s_proj,
    )


def solution(mesh):
    tok = P("batch", "seq", None)
    mat = P("seq", "batch")
    return jax.shard_map(
        shards,
        mesh=mesh,
        in_specs=(tok,) + (P(),) * 11 + (P("batch", None), P("batch"), tok),
        out_specs=(
            tok,
            P("batch", None),
            P("batch"),
            tok,
            P(),
            mat,
            mat,
            mat,
            P(),
            mat,
            P(),
            mat,
            mat,
            P(),
            mat,
        ),
        check_vma=False,
    )
```

```python
import functools

import jax
import jax.numpy as jnp
from jax import lax
from jax.experimental import pallas as pl
from jax.experimental.pallas import tpu as pltpu
from jax.sharding import PartitionSpec as P

EPS = 1e-06
NEGATIVE = -1e30
SHARPNESS = 50.0
THRESHOLDS = (12, 16, 23, 32, 46, 64, 91)
HIGHEST = lax.Precision.HIGHEST
BF = jnp.bfloat16
F32 = jnp.float32
VMEM_BYTES = 60 * 1024 * 1024
GELU_A = 0.7978845608028654
GELU_B = 0.044715


def dot_nn(left, right):
    return lax.dot_general(left, right, (((1,), (0,)), ((), ())), preferred_element_type=F32)


def dot_nt(left, right):
    return lax.dot_general(left, right, (((1,), (1,)), ((), ())), preferred_element_type=F32)


def dot_tn(left, right):
    return lax.dot_general(left, right, (((0,), (0,)), ((), ())), preferred_element_type=F32)


def rms_scale(values):
    return lax.rsqrt(jnp.mean(values * values, axis=-1, keepdims=True) + EPS)


def rms_back(values, scale, grad_normed):
    inner = jnp.mean(grad_normed * values, axis=-1, keepdims=True)
    return scale * (grad_normed - values * (scale * scale * inner))


def split_bf(values):
    high = values.astype(BF)
    return high, (values - high.astype(F32)).astype(BF)


def bucket_of(offset):
    distance = jnp.abs(offset)
    beyond = jnp.zeros_like(distance)
    for threshold in THRESHOLDS:
        beyond = beyond + (distance >= threshold).astype(jnp.int32)
    within = jnp.where(distance < 8, distance, 8 + beyond)
    return within + 16 * (offset > 0).astype(jnp.int32)


def wrapped_offsets(shape, axis, size):
    place = lax.broadcasted_iota(jnp.int32, shape, axis)
    return jnp.where(place < size, place, place - 2 * size)


def full(shape):
    return pl.BlockSpec(shape, lambda *_: (0,) * len(shape), pipeline_mode=pl.Buffered(1))


def row_spec(shape, first=0):
    return pl.BlockSpec(
        (1,) + tuple(shape), lambda step, *_: (step + first,) + (0,) * len(shape)
    )


def cost(products, moved, exps=0):
    return pl.CostEstimate(flops=2 * products, bytes_accessed=moved, transcendentals=exps)


def params(limit=VMEM_BYTES):
    return pltpu.CompilerParams(
        vmem_limit_bytes=limit, dimension_semantics=("arbitrary",)
    )


def bias_kernel(size, table_ref, out_ref):
    buckets, heads = table_ref.shape
    hot = (
        lax.broadcasted_iota(jnp.int32, (buckets, 2 * size), 0)
        == bucket_of(-wrapped_offsets((buckets, 2 * size), 1, size))
    ).astype(BF)
    by_offset = dot_tn(table_ref[...], hot)
    for head in range(heads):
        line = jnp.broadcast_to(by_offset[head : head + 1, :], (size, 2 * size))
        out_ref[head] = pltpu.roll(line, 0, 1, stride=1, stride_axis=0).astype(BF)


def bias_tables(rel_bias, size):
    heads = rel_bias.shape[1]
    return pl.pallas_call(
        functools.partial(bias_kernel, size),
        out_shape=jax.ShapeDtypeStruct((heads, size, 2 * size), BF),
        compiler_params=pltpu.CompilerParams(vmem_limit_bytes=VMEM_BYTES),
    )(rel_bias)


def bias_grad_kernel(*refs):
    acc_refs, out_ref = refs[:-1], refs[-1]
    group, size, width = acc_refs[0].shape
    buckets = out_ref.shape[2]
    hot = (
        lax.broadcasted_iota(jnp.int32, (width, buckets), 1)
        == bucket_of(-wrapped_offsets((width, buckets), 0, width // 2))
    ).astype(BF)
    for head in range(group):
        rows = sum(acc_ref[head] for acc_ref in acc_refs)
        count = size
        while count > 8:
            count = count // 2
            rows = rows[:count] + pltpu.roll(rows[count:], width - count, 1)
        place = lax.broadcasted_iota(jnp.int32, rows.shape, 0)
        for bit in (4, 2, 1):
            rows = jnp.where((place & bit) > 0, pltpu.roll(rows, width - bit, 1), rows)
        first, rest = split_bf(rows)
        second, third = split_bf(rows - first.astype(F32))
        out_ref[head] = dot_nn(first, hot) + dot_nn(second, hot) + dot_nn(third, hot)


def bias_grad(accs, buckets):
    heads, count, width = accs[0].shape
    group = max(size for size in (1, 2, 3, 4) if heads % size == 0)
    out = pl.pallas_call(
        bias_grad_kernel,
        grid=(heads // group,),
        in_specs=[pl.BlockSpec((group, count, width), lambda step: (step, 0, 0))] * len(accs),
        out_specs=pl.BlockSpec((group, 8, buckets), lambda step: (step, 0, 0)),
        out_shape=jax.ShapeDtypeStruct((heads, 8, buckets), F32),
        compiler_params=params(),
        name="bias_grad",
    )(*accs)
    return jnp.sum(out, axis=1).T


class Row:
    def __init__(self, lengths_ref, place_ref, row, size):
        slots = lengths_ref.shape[1]
        base = place_ref[0] * size
        col_pos = base + lax.broadcasted_iota(jnp.int32, (size, 1), 0)
        row_pos = base + lax.broadcasted_iota(jnp.int32, (1, size), 1)
        zero = jnp.int32(0)
        before, first, last, beyond = zero, zero, zero, zero
        col_own = jnp.zeros((size, 1), jnp.int32)
        col_low = jnp.zeros((size, 1), jnp.int32)
        col_high = jnp.zeros((size, 1), jnp.int32)
        row_own = jnp.zeros((1, size), jnp.int32)
        end = zero
        passed = lambda end, place: (end <= place).astype(jnp.int32)
        for slot in range(slots):
            end = end + lengths_ref[row, slot]
            before += passed(end, base - 1)
            first += passed(end, base)
            last += passed(end, base + size - 1)
            beyond += passed(end, base + size)
            col_own += passed(end, col_pos)
            col_low += passed(end, col_pos - size)
            col_high += passed(end, col_pos + size)
            row_own += passed(end, row_pos)
        before = jnp.where(base == 0, -1, before)
        col_low = jnp.where(col_pos < size, -1, col_low)
        self.row_own = row_own
        self.in_low = col_own == before
        self.in_high = col_own == beyond
        self.slot_low = col_low == first
        self.slot_high = col_high == last
        key = lax.broadcasted_iota(jnp.int32, (size, size), 0)
        query = lax.broadcasted_iota(jnp.int32, (size, size), 1)
        self.own = col_own == row_own
        self.alt = ((col_low == row_own) & (key > query)) | ((col_high == row_own) & (key < query))


def store_group_masks(row, ref):
    _, _, size, lanes = ref.shape
    first = lax.broadcasted_iota(jnp.int32, (1, lanes), 1) < lanes // 2
    low = row.in_low.astype(F32)
    high = row.in_high.astype(F32)
    for part, group in enumerate((low, 1.0 - low - high, high)):
        ref[0, part] = jnp.where(first, group, 0.0).astype(BF)
        ref[1, part] = jnp.where(first, 0.0, group).astype(BF)


def by_group(pair, ref, half):
    return jnp.concatenate([pair * ref[half, part] for part in range(3)], axis=1)


def fold_rows(row, first, wide):
    lanes = wide[0].shape[1] // 3
    parts = [
        jnp.where(first, wide[0][:, here], wide[1][:, here])
        for here in (slice(part * lanes, (part + 1) * lanes) for part in range(3))
    ]
    return jnp.where(row.in_low, parts[0], jnp.where(row.in_high, parts[2], parts[1]))


def own_kernel(x_ref, gain1_ref, wq_ref, wk_ref, wv_ref, out_ref):
    x = x_ref[0].astype(F32)
    out_ref[0, 3] = (x * rms_scale(x) * gain1_ref[...].astype(F32)).astype(BF)
    for index, weight_ref in enumerate((wq_ref, wk_ref, wv_ref)):
        out_ref[0, index] = dot_nn(out_ref[0, 3], weight_ref[...]).astype(BF)


def own_projections(tokens, gain1, weights):
    rows, size, dim = tokens.shape
    constants = (gain1,) + tuple(weights)
    return pl.pallas_call(
        own_kernel,
        grid=(rows,),
        in_specs=[row_spec((size, dim))] + [full(item.shape) for item in constants],
        out_specs=row_spec((4, size, dim)),
        out_shape=jax.ShapeDtypeStruct((rows, 4, size, dim), BF),
        compiler_params=params(),
        cost_estimate=cost(3 * rows * size * dim * dim, rows * size * dim * 10),
        name="own_projections",
    )(tokens, *constants)


def row_sentences(lengths_ref, place_ref, row, size):
    where_pos = place_ref[0] * size + lax.broadcasted_iota(jnp.int32, (1, size), 1)
    found = jnp.zeros((1, size), jnp.int32)
    end = jnp.int32(0)
    for slot in range(lengths_ref.shape[1]):
        end = end + lengths_ref[row, slot]
        found = found + (end <= where_pos).astype(jnp.int32)
    return found


def forward_kernel(
    rows,
    lengths_ref,
    place_ref,
    x_ref,
    low_ref,
    high_ref,
    own_ref,
    gains_ref,
    wk_ref,
    wv_ref,
    bias_ref,
    win_ref,
    wout_ref,
    wo_hbm,
    block_ref,
    pooled_ref,
    edge_ref,
    p_ref,
    att_ref,
    act_ref,
    after_hbm,
    n2_hbm,
    mask_ref,
    group_ref,
    att_all,
    after_all,
    after_low,
    n2_all,
    total_ref,
    wo_ref,
    sems,
):
    size, dim = x_ref.shape[1:]
    heads = bias_ref.shape[0]
    pairs = heads // 2
    lanes = dim // pairs
    slots = pooled_ref.shape[1]
    step = pl.program_id(0)
    copies = [
        pltpu.make_async_copy(after_low, after_hbm, sems.at[0]),
        pltpu.make_async_copy(n2_all, n2_hbm, sems.at[1]),
    ]
    wo_copy = pltpu.make_async_copy(wo_hbm, wo_ref, sems.at[2])

    @pl.when(step == 0)
    def _():
        wo_copy.start()

    @pl.when(step < rows)
    def _():
        here = pl.ds(pl.multiple_of(step * size, size), size)
        row = Row(lengths_ref, place_ref, step, size)
        mask_ref[0] = jnp.where(row.own, 0.0, NEGATIVE).astype(BF)
        mask_ref[1] = jnp.where(row.alt, 0.0, NEGATIVE).astype(BF)
        store_group_masks(row, group_ref)
        gain1 = gains_ref[0:1, :].astype(F32)
        own = x_ref[0].astype(F32)
        after_all[here, :] = own
        own = own * rms_scale(own) * gain1
        for part, (source, slot) in enumerate(((low_ref, row.slot_low), (high_ref, row.slot_high))):
            x = source[0].astype(F32)
            edge_ref[0, 4 + part] = jnp.where(slot, x * rms_scale(x) * gain1, own).astype(BF)
        edges = edge_ref[0, 4:].reshape(2 * size, dim)
        first_half = lax.broadcasted_iota(jnp.int32, (1, lanes), 1) < lanes // 2
        for index, weight_ref in enumerate((wk_ref, wv_ref)):
            value = dot_nn(edges, weight_ref[...]).astype(BF)
            edge_ref[0, 2 * index : 2 * index + 2] = value.reshape(2, size, dim)
        for pair in range(pairs):
            cols = slice(pair * lanes, (pair + 1) * lanes)
            keys, values = key_groups(own_ref, edge_ref, cols)
            halves = []
            for half in range(2):
                head = 2 * pair + half
                scores = dot_nt(keys, by_group(own_ref[0, 0, :, cols], group_ref, half))
                bias = jnp.maximum(
                    bias_ref[head, :, :size] + mask_ref[0], bias_ref[head, :, size:] + mask_ref[1]
                )
                scores = scores + bias.astype(F32)
                peak = jnp.max(scores, axis=0, keepdims=True)
                powers = jnp.exp(scores - peak)
                inverse = 1.0 / jnp.sum(powers, axis=0, keepdims=True)
                probs = (powers * inverse).astype(BF)
                p_ref[0, head] = probs
                halves.append(dot_tn(probs, values))
            mixed = fold_rows(row, first_half, halves).astype(BF)
            att_ref[0, :, cols] = mixed
            att_all[here, cols] = mixed

    @pl.when(step == rows)
    def _():
        wo_copy.wait()
        after = after_all[...] + dot_nn(att_all[...], wo_ref[...])
        after_low[...] = after.astype(BF)
        total_ref[...] = after
        n2_all[...] = (after * rms_scale(after) * gains_ref[1:2, :].astype(F32)).astype(BF)
        for copy in copies:
            copy.start()

    @pl.when(step >= rows)
    def _():
        pre = dot_nn(n2_all[...], win_ref[...])
        square = pre * pre
        gate = 0.5 + 0.5 * jnp.tanh(pre * (GELU_A + (GELU_A * GELU_B) * square))
        act = pre * gate
        slope = gate + act * (1.0 - gate) * (2 * GELU_A + (6 * GELU_A * GELU_B) * square)
        act_ref[0] = act.astype(BF)
        act_ref[1] = slope.astype(BF)
        total_ref[...] += dot_nn(act_ref[0], wout_ref[...])

    @pl.when(step == pl.num_programs(0) - 1)
    def _():
        gainf = gains_ref[2:3, :].astype(F32)
        for row in range(rows):
            here = slice(row * size, (row + 1) * size)
            block = total_ref[here, :].astype(BF)
            block_ref[row] = block
            out = block.astype(F32)
            final = out * rms_scale(out) * gainf
            found = row_sentences(lengths_ref, place_ref, row, size)
            member = (lax.broadcasted_iota(jnp.int32, (slots, size), 0) == found).astype(BF)
            high_part, low_part = split_bf(final)
            pooled_ref[row] = dot_nn(member, high_part) + dot_nn(member, low_part)
        for copy in copies:
            copy.wait()


def key_groups(own_ref, edge_ref, cols):
    return [
        jnp.concatenate(
            [edge_ref[0, 2 * index, :, cols], own_ref[0, 1 + index, :, cols], edge_ref[0, 2 * index + 1, :, cols]],
            axis=1,
        )
        for index in range(2)
    ]


def forward(lengths, place, tokens, low, high, own, gains, weights, bias):
    rows, size, dim = tokens.shape
    heads = bias.shape[0]
    slots = lengths.shape[1]
    wk, wv, wo, win, wout = weights
    hidden = win.shape[1]
    tiles = hidden // dim
    toks = rows * size
    per_row = lambda shape: pl.BlockSpec(
        (1,) + shape, lambda step, *_: (jnp.minimum(step, rows - 1),) + (0,) * len(shape)
    )
    tile = lambda step: jnp.maximum(step - rows, 0)
    constants = (gains, wk, wv, bias)
    anywhere = pl.BlockSpec(memory_space=pl.ANY)
    out_of = lambda shape, kind=BF: jax.ShapeDtypeStruct(shape, kind)
    return pl.pallas_call(
        functools.partial(forward_kernel, rows),
        grid_spec=pltpu.PrefetchScalarGridSpec(
            num_scalar_prefetch=2,
            grid=(rows + tiles,),
            in_specs=[per_row((size, dim))] * 3
            + [per_row((3, size, dim))]
            + [full(item.shape) for item in constants]
            + [
                pl.BlockSpec((dim, dim), lambda step, *_: (0, tile(step))),
                pl.BlockSpec((dim, dim), lambda step, *_: (tile(step), 0)),
                anywhere,
            ],
            out_specs=[
                full((rows, size, dim)),
                full((rows, slots, dim)),
                per_row((6, size, dim)),
                per_row((heads, size, size)),
                per_row((size, dim)),
                pl.BlockSpec((2, toks, dim), lambda step, *_: (0, 0, tile(step))),
                anywhere,
                anywhere,
            ],
            scratch_shapes=[
                pltpu.VMEM((2, size, size), BF),
                pltpu.VMEM((2, 3, size, 2 * dim // heads), BF),
                pltpu.VMEM((toks, dim), BF),
                pltpu.VMEM((toks, dim), F32),
                pltpu.VMEM((toks, dim), BF),
                pltpu.VMEM((toks, dim), BF),
                pltpu.VMEM((toks, dim), F32),
                pltpu.VMEM((dim, dim), BF),
                pltpu.SemaphoreType.DMA((3,)),
            ],
        ),
        out_shape=[
            out_of((rows, size, dim)),
            out_of((rows, slots, dim), F32),
            out_of((rows, 6, size, dim)),
            out_of((rows, heads, size, size)),
            out_of((rows, size, dim)),
            out_of((2, toks, hidden)),
            out_of((toks, dim)),
            out_of((toks, dim)),
        ],
        compiler_params=params(),
        cost_estimate=cost(
            toks * dim * (5 * dim + 2 * hidden + 36 * size),
            toks * (hidden * 4 + dim * 40),
            rows * heads * size * size,
        ),
        name="forward",
    )(lengths, place, tokens, low, high, own, *constants, win, wout, wo)


def store_split(core, value, refs, count, first=0):
    if len(refs) == 1:
        refs[0][first : first + value.shape[0], :] = value
        return
    groups = value.shape[0] // (2 * count)
    for group in range(groups):
        even = value[2 * group * count : (2 * group + 1) * count]
        odd = value[(2 * group + 1) * count : (2 * group + 2) * count]

        refs[0][group, first : first + count, :] = jnp.where(core == 0, even, odd)
        refs[1][group, first : first + count, :] = jnp.where(core == 0, odd, even)


def feed_back_kernel(
    rows,
    parts,
    lengths_ref,
    place_ref,
    block_ref,
    cot_ref,
    pool_ref,
    graw_ref,
    pooled_ref,
    gain_ref,
    act_ref,
    win_ref,
    wout_ref,
    after_hbm,
    n2_hbm,
    att_hbm,
    wo_hbm,
    back_ref,
    gains_ref,
    *rest,
):
    split = len(rest) == 14
    per = 2 if split else 1
    in_refs, out_refs, small_refs = (rest[i * per : (i + 1) * per] for i in range(3))
    gout_ref, branch_ref, gn2_ref, after_ref, n2_ref, att_ref, wo_ref, sems = rest[3 * per :]
    _, size, dim = block_ref.shape
    toks = rows * size
    slots = pool_ref.shape[1]
    step = pl.program_id(0)
    tiles = pl.num_programs(0) - 1
    core = place_ref[1]
    copies = [
        pltpu.make_async_copy(n2_hbm, n2_ref, sems.at[0]),
        pltpu.make_async_copy(after_hbm, after_ref, sems.at[1]),
        pltpu.make_async_copy(att_hbm, att_ref, sems.at[2]),
        pltpu.make_async_copy(wo_hbm, wo_ref, sems.at[3]),
    ]

    @pl.when(step == 0)
    def _():
        for copy in copies:
            copy.start()
        gainf = gain_ref[2:3, :].astype(F32)
        gain_f = jnp.zeros((1, dim), F32)
        for row in range(rows):
            here = slice(row * size, (row + 1) * size)
            found = row_sentences(lengths_ref, place_ref, row, size)
            member = (lax.broadcasted_iota(jnp.int32, (slots, size), 0) == found).astype(BF)
            high_part, low_part = split_bf(pool_ref[row])
            g_final = dot_tn(member, high_part) + dot_tn(member, low_part)
            out = block_ref[row].astype(F32)
            scale = rms_scale(out)
            gain_f = gain_f + jnp.sum(g_final * out * scale, axis=0, keepdims=True)
            g_out = rms_back(out, scale, g_final * gainf) + cot_ref[row].astype(F32)
            gout_ref[here, :] = g_out
            branch_ref[here, :] = g_out.astype(BF)
        gains_ref[...] = jnp.zeros_like(gains_ref)
        gains_ref[0:1, :] = gain_f
        copies[0].wait()

    @pl.when(step < tiles)
    def _():
        value = dot_tn(branch_ref[...], act_ref[0]).astype(BF)
        store_split(core, value, out_refs, dim // parts)
        g_hidden = dot_nt(branch_ref[...], wout_ref[...])
        g_pre = (g_hidden * act_ref[1].astype(F32)).astype(BF)
        value = dot_tn(g_pre, n2_ref[...]).astype(BF)
        store_split(core, value, in_refs, tiles * dim // parts)
        part = dot_nt(g_pre, win_ref[...])

        @pl.when(step == 0)
        def _():
            gn2_ref[...] = part

        @pl.when(step > 0)
        def _():
            gn2_ref[...] += part

    @pl.when(step == tiles)
    def _():
        for copy in copies[1:]:
            copy.wait()
        gain2 = gain_ref[1:2, :].astype(F32)
        gain_2 = jnp.zeros((1, dim), F32)
        for row in range(rows):
            here = slice(row * size, (row + 1) * size)
            after = after_ref[here, :].astype(F32)
            g_n2 = gn2_ref[here, :]
            scale = rms_scale(after)
            gain_2 = gain_2 + jnp.sum(g_n2 * after * scale, axis=0, keepdims=True)
            g_after = gout_ref[here, :] + rms_back(after, scale, g_n2 * gain2)
            back_ref[row, 1] = g_after.astype(BF)
            branch_ref[here, :] = g_after.astype(BF)
        gains_ref[1:2, :] = gain_2
        g_mix = dot_nt(branch_ref[...], wo_ref[...]).astype(BF)
        for row in range(rows):
            back_ref[row, 0] = g_mix[row * size : (row + 1) * size]
        value = dot_tn(branch_ref[...], att_ref[...].reshape(toks, dim)).astype(BF)
        store_split(core, value, small_refs, dim // parts)
        left_high, left_low = split_bf(graw_ref[...])
        right_high, right_low = split_bf(pooled_ref[...])
        value = dot_tn(left_high, right_high)
        value += dot_tn(left_high, right_low) + dot_tn(left_low, right_high)
        first = dim // parts if split else dim
        store_split(core, value.astype(BF), small_refs, dim // parts, first)


def feed_back(parts, lengths, place, block, after, cot, att, n2, act, pool, graw, pooled, gains, weights):
    rows, size, dim = block.shape
    hidden = act.shape[2]
    tiles = hidden // dim
    toks = rows * size
    wo, win, wout = weights
    split = (dim // parts) % 16 == 0 and dim % (2 * hidden // parts) == 0
    tile = lambda step: jnp.minimum(step, tiles - 1)
    if split:
        groups = parts // 2
        wide = hidden // parts
        inner = dim // (2 * wide)
        narrow = dim // parts
        in_specs = [pl.BlockSpec((inner, wide, dim), lambda step, *_: (tile(step), 0, 0))] * 2
        out_specs = [pl.BlockSpec((groups, narrow, dim), lambda step, *_: (0, tile(step), 0))] * 2
        small_specs = [full((groups, 2 * narrow, dim))] * 2
        shapes = [(groups, wide, dim)] * 2 + [(groups, tiles * narrow, dim)] * 2 + [(groups, 2 * narrow, dim)] * 2
    else:
        in_specs = [pl.BlockSpec((dim, dim), lambda step, *_: (tile(step), 0))]
        out_specs = [pl.BlockSpec((dim, dim), lambda step, *_: (tile(step), 0))]
        small_specs = [full((2 * dim, dim))]
        shapes = [(hidden, dim), (tiles * dim, dim), (2 * dim, dim)]
    constants = (block, cot, pool, graw, pooled, gains)
    outs = pl.pallas_call(
        functools.partial(feed_back_kernel, rows, parts),
        grid_spec=pltpu.PrefetchScalarGridSpec(
            num_scalar_prefetch=2,
            grid=(tiles + 1,),
            in_specs=[full(item.shape) for item in constants]
            + [
                pl.BlockSpec((2, toks, dim), lambda step, *_: (0, 0, tile(step))),
                pl.BlockSpec((dim, dim), lambda step, *_: (0, tile(step))),
                pl.BlockSpec((dim, dim), lambda step, *_: (tile(step), 0)),
            ]
            + [pl.BlockSpec(memory_space=pl.ANY)] * 4,
            out_specs=[full((rows, 2, size, dim)), full((8, dim))]
            + in_specs
            + out_specs
            + small_specs,
            scratch_shapes=[
                pltpu.VMEM((toks, dim), F32),
                pltpu.VMEM((toks, dim), BF),
                pltpu.VMEM((toks, dim), F32),
                pltpu.VMEM((toks, dim), BF),
                pltpu.VMEM((toks, dim), BF),
                pltpu.VMEM((rows, size, dim), BF),
                pltpu.VMEM((dim, dim), BF),
                pltpu.SemaphoreType.DMA((4,)),
            ],
        ),
        out_shape=[
            jax.ShapeDtypeStruct((rows, 2, size, dim), BF),
            jax.ShapeDtypeStruct((8, dim), F32),
        ]
        + [jax.ShapeDtypeStruct(shape, BF) for shape in shapes],
        compiler_params=params(),
        cost_estimate=cost(
            toks * dim * (4 * hidden + 2 * dim), toks * (hidden * 4 + dim * 20) + 8 * hidden * dim
        ),
        name="feed_back",
    )(lengths, place, *constants, act, win, wout, after, n2, att, wo)
    if split:
        mine, theirs = outs[2::2], outs[3::2]
    else:
        whole = [
            outs[2].reshape(parts, hidden // parts, dim),
            outs[3].reshape(tiles, parts, dim // parts, dim).transpose(1, 0, 2, 3),
            outs[4].reshape(2, parts, dim // parts, dim).transpose(1, 0, 2, 3),
        ]
        mine, theirs = split_core(whole)
    return outs[0], outs[1], mine, theirs


def split_core(blocks):
    core = (lax.axis_index("batch") % 2).astype(jnp.int32)
    pairs = [item.reshape((item.shape[0] // 2, 2, -1, item.shape[-1])) for item in blocks]
    pick = lambda item, place: lax.dynamic_index_in_dim(item, place, 1, keepdims=False)
    return [pick(item, core) for item in pairs], [pick(item, 1 - core) for item in pairs]


def attend_grad_kernel(parts, place_ref, n1_ref, own_ref, edge_hbm, n1_edge_hbm, *rest):
    refs, (edge_ref, n1_edge_ref, sems) = rest[:-3], rest[-3:]
    rows, _, size, dim = own_ref.shape
    step = pl.program_id(0)
    width = dim // parts if len(refs) == 2 else dim
    flat = lambda ref: ref[...].reshape(-1, dim)
    n1_copy = pltpu.make_async_copy(n1_edge_hbm.at[:, 4:6], n1_edge_ref, sems.at[0])
    copies = [
        pltpu.make_async_copy(
            edge_hbm.at[:, 3 + 2 * index : 5 + 2 * index], edge_ref.at[index], sems.at[1 + index]
        )
        for index in range(2)
    ]

    @pl.when(step == 0)
    def _():
        n1_copy.start()
        for copy in copies:
            copy.start()
        value = dot_tn(flat(own_ref), flat(n1_ref)).astype(BF)
        store_split(place_ref[1], value, refs, dim // parts, 0)
        n1_copy.wait()

    for index in range(2):

        @pl.when(step == 1 + index)
        def _():
            copies[index].wait()
            value = dot_tn(flat(own_ref), flat(n1_ref)) + dot_tn(flat(edge_ref.at[index]), flat(n1_edge_ref))
            store_split(place_ref[1], value.astype(BF), refs, dim // parts, (1 + index) * width)


def attend_grad(parts, place, own, edges, grads):
    rows, _, size, dim = own.shape
    narrow = dim // parts
    split = narrow % 16 == 0
    shape = (parts // 2, 3 * narrow, dim) if split else (3 * dim, dim)
    copies = 2 if split else 1
    outs = pl.pallas_call(
        functools.partial(attend_grad_kernel, parts),
        grid_spec=pltpu.PrefetchScalarGridSpec(
            num_scalar_prefetch=1,
            grid=(3,),
            in_specs=[
                pl.BlockSpec((rows, 1, size, dim), lambda step, *_: (0, 3, 0, 0)),
                pl.BlockSpec((rows, 1, size, dim), lambda step, *_: (0, step, 0, 0)),
                pl.BlockSpec(memory_space=pl.ANY),
                pl.BlockSpec(memory_space=pl.ANY),
            ],
            out_specs=[full(shape)] * copies,
            scratch_shapes=[
                pltpu.VMEM((2, rows, 2, size, dim), BF),
                pltpu.VMEM((rows, 2, size, dim), BF),
                pltpu.SemaphoreType.DMA((3,)),
            ],
        ),
        out_shape=[jax.ShapeDtypeStruct(shape, BF)] * copies,
        compiler_params=params(),
        cost_estimate=cost(rows * size * dim * dim * 7, rows * size * dim * 26),
        name="attend_grad",
    )(place, own, grads, grads, edges)
    if split:
        return outs[0], outs[1]
    mine, theirs = split_core([outs[0].reshape(3, parts, narrow, dim).transpose(1, 0, 2, 3)])
    return mine[0], theirs[0]


def attend_back_kernel(
    first,
    lengths_ref,
    place_ref,
    own_ref,
    low_ref,
    high_ref,
    qkv_ref,
    edge_ref,
    p_ref,
    back_ref,
    gain_ref,
    wq_ref,
    wk_ref,
    wv_ref,
    *rest,
):
    grad_ref, part_ref, to_low_ref, to_high_ref, acc_ref, gains_ref, mask_ref, group_ref = rest[-8:]
    size, dim = own_ref.shape[1:]
    heads = p_ref.shape[1]
    pairs = heads // 2
    lanes = dim // pairs
    step = pl.program_id(0)
    row = Row(lengths_ref, place_ref, step + first, size)
    mask_ref[...] = row.own.astype(F32)

    @pl.when(step == 0)
    def _():
        acc_ref[...] = jnp.zeros_like(acc_ref)
        gains_ref[...] = jnp.zeros_like(gains_ref)

    first_half = lax.broadcasted_iota(jnp.int32, (1, lanes), 1) < lanes // 2
    store_group_masks(row, group_ref)
    half_size = size // 2
    for pair in range(pairs):
        cols = slice(pair * lanes, (pair + 1) * lanes)
        keys, values = key_groups(qkv_ref, edge_ref, cols)
        q_groups = [by_group(qkv_ref[0, 0, :, cols], group_ref, half) for half in range(2)]
        o_groups = [by_group(back_ref[0, 0, :, cols], group_ref, half) for half in range(2)]
        d_q, scores_pair = [], []
        for half in range(2):
            head = 2 * pair + half
            g_probs = dot_nt(values, o_groups[half])
            full_probs = p_ref[0, head].astype(F32)
            product = full_probs * g_probs
            inner = jnp.sum(product, axis=0, keepdims=True)
            g_scores = product - full_probs * inner
            on_own = g_scores * mask_ref[...]
            off_own = g_scores - on_own
            acc_ref[head, :, :half_size] += on_own[:half_size, :half_size] + on_own[half_size:, half_size:]
            acc_ref[head, :, half_size:size] += on_own[:half_size, half_size:] + off_own[half_size:, :half_size]
            acc_ref[head, :, size : size + half_size] += off_own[:half_size, :half_size] + off_own[half_size:, half_size:]
            acc_ref[head, :, size + half_size :] += off_own[:half_size, half_size:] + on_own[half_size:, :half_size]
            scores_pair.append(g_scores.astype(BF))
            d_q.append(dot_tn(scores_pair[-1], keys))
        grad_ref[0, 0, :, cols] = fold_rows(row, first_half, d_q).astype(BF)
        probs_pair = [p_ref[0, 2 * pair], p_ref[0, 2 * pair + 1]]
        for index, (left, right) in enumerate(((scores_pair, q_groups), (probs_pair, o_groups))):
            value = dot_nn(jnp.concatenate(left, axis=1), jnp.concatenate(right, axis=0)).astype(BF)
            grad_ref[0, 3 + 2 * index, :, cols] = value[:, :lanes]
            grad_ref[0, 1 + index, :, cols] = value[:, lanes : 2 * lanes]
            grad_ref[0, 4 + 2 * index, :, cols] = value[:, 2 * lanes :]

    gain1 = gain_ref[0:1, :].astype(F32)
    g_whole = None
    for index, weight_ref in enumerate((wk_ref, wv_ref)):
        edge_grad = grad_ref[0, 3 + 2 * index : 5 + 2 * index].reshape(2 * size, dim)
        left = jnp.concatenate([edge_grad, grad_ref[0, 1 + index]], axis=0)
        term = dot_nt(left, weight_ref[...])
        g_whole = term if g_whole is None else g_whole + term
    zero = jnp.zeros((size, dim), F32)
    g_low = jnp.where(row.slot_low, g_whole[:size], zero)
    g_high = jnp.where(row.slot_high, g_whole[size : 2 * size], zero)
    g_own = g_whole[2 * size :] + (g_whole[:size] - g_low) + (g_whole[size : 2 * size] - g_high)
    g_own = g_own + dot_nt(grad_ref[0, 0], wq_ref[...])
    gain_1 = jnp.zeros((1, dim), F32)
    for source, g_norm, out_ref in (
        (low_ref, g_low, to_low_ref),
        (own_ref, g_own, part_ref),
        (high_ref, g_high, to_high_ref),
    ):
        x = source[0].astype(F32)
        scale = rms_scale(x)
        gain_1 = gain_1 + jnp.sum(g_norm * x * scale, axis=0, keepdims=True)
        g_x = rms_back(x, scale, g_norm * gain1)
        if out_ref is part_ref:
            g_x = g_x + back_ref[0, 1].astype(F32)
        out_ref[0] = g_x.astype(BF)
    gains_ref[0:1, :] += gain_1


def attend_back(first, count, earlier, lengths, place, x, low, high, own, edges, p, back, gains, weights):
    rows, size, dim = x.shape
    heads = p.shape[1]
    constants = (gains,) + tuple(weights)
    kept = 2
    aliases = {}
    if earlier:
        start = 2 + 7 + len(constants)
        aliases = {start + index: index for index in range(kept)}
    return pl.pallas_call(
        functools.partial(attend_back_kernel, first),
        grid_spec=pltpu.PrefetchScalarGridSpec(
            num_scalar_prefetch=2,
            grid=(count,),
            in_specs=[row_spec((size, dim), first)] * 3
            + [row_spec((3, size, dim), first), row_spec((4, size, dim), first)]
            + [row_spec((heads, size, size), first), row_spec((2, size, dim), first)]
            + [full(item.shape) for item in constants]
            + [pl.BlockSpec(memory_space=pl.ANY)] * len(earlier),
            out_specs=[
                row_spec((7, size, dim), first),
                row_spec((size, dim), first),
                row_spec((size, dim)),
                row_spec((size, dim)),
            ]
            + [full((heads, size // 2, 2 * size)), full((8, dim))],
            scratch_shapes=[
                pltpu.VMEM((size, size), F32),
                pltpu.VMEM((2, 3, size, 2 * dim // heads), BF),
            ],
        ),
        out_shape=[
            jax.ShapeDtypeStruct((rows, 7, size, dim), BF),
            jax.ShapeDtypeStruct((rows, size, dim), BF),
            jax.ShapeDtypeStruct((count, size, dim), BF),
            jax.ShapeDtypeStruct((count, size, dim), BF),
            jax.ShapeDtypeStruct((heads, size // 2, 2 * size), F32),
            jax.ShapeDtypeStruct((8, dim), F32),
        ],
        input_output_aliases=aliases,
        compiler_params=params(),
        cost_estimate=cost(
            count * size * dim * (9 * dim + 128 * size), count * size * dim * 60
        ),
        name="attend_back_rows",
    )(lengths, place, x, low, high, own, edges, p, back, *constants, *earlier)


def flip(block, axis, bit):
    count = lax.axis_size(axis)
    return lax.ppermute(block, axis, [(i, i ^ bit) for i in range(count)])


def sum_along(block, axis):
    bit = 1
    while bit < lax.axis_size(axis):
        block = block + flip(block, axis, bit)
        bit *= 2
    return block


def bit_places(axis):
    return [1 << level for level in range((lax.axis_size(axis) - 1).bit_length())]


def gather_batch(block):
    place = lax.axis_index("batch")
    bits = bit_places("batch")
    gathered = block[None]
    for bit in reversed(bits):
        other = flip(gathered, "batch", bit)
        upper = (place & bit) > 0
        gathered = jnp.stack(
            [jnp.where(upper, other, gathered), jnp.where(upper, gathered, other)], axis=1
        )
        gathered = gathered.reshape((-1,) + block.shape)
    return gathered.reshape((-1,) + block.shape[1:])


def halve(block, bits, bit):
    axis = bits.index(bit)
    mine = ((lax.axis_index("batch") & bit) > 0).astype(jnp.int32)
    send = lax.dynamic_index_in_dim(block, 1 - mine, axis, keepdims=False)
    keep = lax.dynamic_index_in_dim(block, mine, axis, keepdims=False)
    return keep + flip(send, "batch", bit), [item for item in bits if item != bit]


def after(value, *others):
    return lax.optimization_barrier((value,) + tuple(others))[0]


def stage_kernel(groups, place_ref, *refs):
    ins = refs[: 2 * sum(len(group) for group in groups)]
    outs = refs[len(ins) :]
    taken = 0
    for index, group in enumerate(groups):
        first = 0
        for count in group:
            value = ins[2 * taken][0, 0, 0] + ins[2 * taken + 1][0, 0, 0]
            taken += 1
            for which in range(2):

                @pl.when(pl.program_id(0) == which)
                def _():
                    outs[2 * index + which][0, 0, first : first + count, :] = value

            first += count


def stage(place, groups, bits, pieces):
    columns = groups[0][0][0].shape[-1]
    lead = bits[0][0][0] * bits[0][0][1]
    if any(count % (16 * pieces) or first % count for group in groups for _, _, first, count in group):
        sends, keeps = [], []
        for index, group in enumerate(groups):
            before, behind = bits[index][0]
            total = jnp.concatenate(
                [(kept + arrived)[..., first : first + count, :].reshape(-1, count, columns)
                 for kept, arrived, first, count in group],
                axis=1,
            ).reshape(before, 2, behind, -1, columns)
            pick = lambda which: lax.dynamic_index_in_dim(total, which, 1, keepdims=False)
            sends.append(pick(1 - place[index]).reshape(lead, 1, -1, columns))
            keeps.append(pick(place[index]).reshape(lead, 1, -1, columns))
        return sends, keeps
    in_specs, operands, out_specs, shapes = [], [], [], []
    for index, group in enumerate(groups):
        before, behind = bits[index][0]
        total = 0

        def place_of(half, step, chunk, places, index=index, behind=behind):
            mine = places[index]
            where_at = jnp.where(half == 0, 1 - mine, mine)
            return step // behind, where_at, step % behind, chunk

        for kept, arrived, first, count in group:
            rows = count // pieces
            total += rows
            shape = (before, 2, behind) + kept.shape[-2:]

            def index_map(half, step, chunk, places, place_of=place_of, first=first, rows=rows):
                one, two, three, four = place_of(half, step, chunk, places)
                return one, two, three, four + first // rows, 0

            for item in (kept, arrived):
                in_specs.append(pl.BlockSpec((1, 1, 1, rows, columns), index_map))
                operands.append(item.reshape(shape))
        for which in range(2):

            def out_map(half, step, chunk, places, which=which):
                if which == 0:
                    step = jnp.where(half == 0, step, lead - 1)
                    chunk = jnp.where(half == 0, chunk, pieces - 1)
                else:
                    step = jnp.where(half == 1, step, 0)
                    chunk = jnp.where(half == 1, chunk, 0)
                return step, chunk, 0, 0

            out_specs.append(pl.BlockSpec((1, 1, total, columns), out_map))
            shapes.append(jax.ShapeDtypeStruct((lead, pieces, total, columns), BF))
    outs = pl.pallas_call(
        functools.partial(
            stage_kernel, [[count // pieces for _, _, _, count in group] for group in groups]
        ),
        grid_spec=pltpu.PrefetchScalarGridSpec(
            num_scalar_prefetch=1, grid=(2, lead, pieces), in_specs=in_specs, out_specs=out_specs
        ),
        out_shape=shapes,
        compiler_params=pltpu.CompilerParams(
            vmem_limit_bytes=VMEM_BYTES, dimension_semantics=("arbitrary",) * 3
        ),
        name="halving_stage",
    )(place, *operands)
    return outs[0::2], outs[1::2]


class BatchSum:
    def __init__(self, mine, theirs, streams):
        bits = bit_places("batch")
        arrived = [flip(item, "batch", bits[0]) for item in theirs]
        self.groups = [
            [(mine[item], arrived[item], first, rows) for item, first, rows in stream] for stream in streams
        ]
        self.bits = [bits[1:][::-1]] * len(streams)
        self.steps = len(bits) - 1
        self.done = 0

    def hold(self, *others):
        self.groups = [
            [(kept, after(arrived, *others), first, rows) for kept, arrived, first, rows in group]
            for group in self.groups
        ]

    def advance(self):
        moved, bits, places = [], [], []
        me = lax.axis_index("batch")
        for index, left in enumerate(self.bits):
            bit = left[::-1][index % len(left)]
            axis = left.index(bit)
            moved.append(bit)
            places.append(((me & bit) > 0).astype(jnp.int32))
            bits.append(((1 << axis, 1 << (len(left) - 1 - axis)),))
        sends, keeps = stage(jnp.stack(places), self.groups, bits, 1)
        self.groups = [
            [(keep, flip(send, "batch", bit), 0, keep.shape[2])]
            for keep, send, bit in zip(keeps, sends, moved)
        ]
        self.bits = [[item for item in left if item != bit] for left, bit in zip(self.bits, moved)]
        self.done += 1
        return sends

    def total(self):
        return [(kept + arrived).reshape(kept.shape[-2:]) for ((kept, arrived, _, _),) in self.groups]


def pack_kernel(tiles_rows, keep_a, come_a, keep_b, come_b, out_ref):
    groups, _, wide = out_ref.shape
    cols = wide // 2
    rows = tiles_rows // groups
    first = keep_a[...] + come_a[...]
    second = keep_b[...] + come_b[...]
    for group in range(groups):
        here = slice(group * cols, (group + 1) * cols)
        out_ref[group, :, :cols] = first[:, here]
        for part in range(groups):
            out_ref[group, part * rows : (part + 1) * rows, cols:] = second[
                group * rows : (group + 1) * rows, part * cols : (part + 1) * cols
            ]
        out_ref[group, tiles_rows:, cols:] = second[tiles_rows:, here]


def pack(stream_a, stream_b, tiles_rows, groups):
    (keep_a, come_a), (keep_b, come_b) = stream_a, stream_b
    rows, dim = keep_a.shape[-2:]
    flat = lambda item: item.reshape(rows, dim)
    shape = (groups, rows, 2 * dim // groups)
    if tiles_rows // groups % 16 == 0:
        return pl.pallas_call(
            functools.partial(pack_kernel, tiles_rows),
            out_shape=jax.ShapeDtypeStruct(shape, BF),
            compiler_params=pltpu.CompilerParams(vmem_limit_bytes=VMEM_BYTES),
            name="pack_places",
        )(flat(keep_a), flat(come_a), flat(keep_b), flat(come_b))
    first = flat(keep_a + come_a).reshape(rows, groups, -1).transpose(1, 0, 2)
    second = flat(keep_b + come_b)
    out = second[:tiles_rows].reshape(groups, -1, groups, dim // groups).transpose(0, 2, 1, 3)
    out = out.reshape(groups, tiles_rows, -1)
    last = second[tiles_rows:].reshape(-1, groups, dim // groups).transpose(1, 0, 2)
    return jnp.concatenate([first, jnp.concatenate([out, last], axis=1)], axis=2)


def contrast(pooled, w_proj, partner):
    proj = w_proj.astype(F32)
    raw = jnp.dot(pooled, proj, precision=HIGHEST)
    inv_norm = lax.rsqrt(jnp.sum(raw * raw, axis=-1, keepdims=True) + EPS)
    embedded = raw * inv_norm
    everyone = gather_batch(embedded)
    own_count = embedded.shape[0]
    total = everyone.shape[0]
    own_index = lax.axis_index("batch") * own_count + jnp.arange(own_count, dtype=jnp.int32)
    columns = jnp.arange(total, dtype=jnp.int32)

    def lse_of(rows, index):
        logits = SHARPNESS * jnp.einsum("nd,md->nm", rows, everyone, precision=HIGHEST)
        logits = jnp.where(columns[None, :] == index[:, None], NEGATIVE, logits)
        peak = jnp.max(logits, axis=-1, keepdims=True)
        return peak[:, 0] + jnp.log(jnp.sum(jnp.exp(logits - peak), axis=-1))

    if total <= 1024:
        lse_all = lse_of(everyone, columns)
    else:
        lse_all = lax.map(
            lambda pieces: lse_of(pieces[0], pieces[1]),
            (everyone.reshape(-1, 512, everyone.shape[1]), columns.reshape(-1, 512)),
        ).reshape(-1)
    logits = SHARPNESS * jnp.einsum("nd,md->nm", embedded, everyone, precision=HIGHEST)
    is_self = columns[None, :] == own_index[:, None]
    logits = jnp.where(is_self, NEGATIVE, logits)
    peak = jnp.max(logits, axis=-1, keepdims=True)
    lse_own = peak[:, 0] + jnp.log(jnp.sum(jnp.exp(logits - peak), axis=-1))
    is_target = columns[None, :] == partner[:, None]
    picked = jnp.sum(jnp.where(is_target, logits, 0.0), axis=-1)
    loss = lse_own - picked
    both = SHARPNESS * (
        jnp.exp(logits - lse_own[:, None])
        + jnp.exp(logits - lse_all[None, :])
        - 2.0 * is_target.astype(F32)
    )
    grad_emb = jnp.dot(both, everyone, precision=HIGHEST)
    grad_raw = inv_norm * (
        grad_emb - embedded * jnp.sum(embedded * grad_emb, axis=-1, keepdims=True)
    )
    grad_pooled = jnp.einsum("ne,de->nd", grad_raw, proj, precision=HIGHEST)
    return embedded, loss, grad_raw, grad_pooled


def shards(
    tokens,
    norm1_gain,
    w_query,
    w_key,
    w_value,
    rel_bias,
    w_output,
    norm2_gain,
    w_in,
    w_out,
    final_gain,
    w_proj,
    lengths,
    partner,
    cotangent,
):
    rows, size, dim = tokens.shape
    slots = lengths.shape[1]
    toks = rows * size
    seq_count = lax.axis_size("seq")
    seq_place = lax.axis_index("seq")
    place = seq_place.astype(jnp.int32).reshape(1)
    up = [(i, i + 1) for i in range(seq_count - 1)]
    down = [(i + 1, i) for i in range(seq_count - 1)]
    gains = jnp.stack([norm1_gain, norm2_gain, final_gain])

    x_low = lax.ppermute(tokens, "seq", up)
    x_high = lax.ppermute(tokens, "seq", down)
    bias = bias_tables(rel_bias, size)
    own = own_projections(tokens, norm1_gain.reshape(1, dim), (w_query, w_key, w_value))
    block, partial, edges, p, att, act, after_attn, n2 = forward(
        lengths,
        place,
        tokens,
        x_low,
        x_high,
        own,
        gains,
        (w_key, w_value, w_output, w_in, w_out),
        bias,
    )
    pooled_sum = sum_along(partial, "seq")
    counts = lengths.astype(F32)[:, :, None]
    pooled = (pooled_sum / counts).reshape(rows * slots, dim)
    embedded, loss, grad_raw, grad_pooled = contrast(pooled, w_proj, partner)
    lead_only = (seq_place == 0).astype(F32)
    pool_grad = grad_pooled.reshape(rows, slots, dim) / counts
    batch_count = lax.axis_size("batch")
    place = jnp.stack([seq_place, lax.axis_index("batch") % 2]).astype(jnp.int32)

    back, gains_a, mine, theirs = feed_back(
        batch_count,
        lengths,
        place,
        block,
        after_attn,
        cotangent,
        att,
        n2,
        act,
        pool_grad,
        lead_only * grad_raw,
        pooled,
        gains,
        (w_output, w_in, w_out),
    )
    hidden = w_in.shape[1]
    width = dim // batch_count
    tiles = hidden // dim
    wide = hidden // batch_count
    feed_sum = BatchSum(
        mine,
        theirs,
        (((0, 0, wide), (2, 0, width)), ((1, 0, tiles * width), (2, width, width))),
    )
    segments = [(0, 1), (1, rows - 2), (rows - 1, 1)] if rows > 2 else [(0, rows)]
    halves, from_above, from_below = [], [], []
    earlier = ()
    for first, count in segments:
        if halves and feed_sum.done < feed_sum.steps:
            place = after(place, *feed_sum.advance())
        if len(halves) > 1:
            place = after(place, from_above[-2], from_below[-2])
        halves.append(
            attend_back(
                first,
                count,
                earlier,
                lengths,
                place,
                tokens,
                x_low,
                x_high,
                own,
                edges,
                p,
                back,
                gains,
                (w_query, w_key, w_value),
            )
        )
        earlier = tuple(halves[-1][:2])
        feed_sum.hold(halves[-1][5])
        from_above.append(lax.ppermute(halves[-1][2], "seq", down))
        from_below.append(lax.ppermute(halves[-1][3], "seq", up))
    grads, part = earlier
    while feed_sum.done < feed_sum.steps:
        place = after(place, *feed_sum.advance())

    def by_columns(array):
        return array.reshape(array.shape[0], seq_count, -1).transpose(1, 0, 2)

    feed_part = pack(
        *[(group[0][0], group[0][1]) for group in feed_sum.groups], tiles * width, seq_count
    )
    grad_rel = bias_grad([item[4] for item in halves], rel_bias.shape[0])
    gain1_grad = sum(item[5][0] for item in halves)
    small = jnp.concatenate([gain1_grad, gains_a[1], gains_a[0], grad_rel.reshape(-1)])
    small = jnp.pad(small, (0, -small.shape[0] % 1024)).reshape(-1, 128)
    seq_bits = bit_places("seq")
    batch_bits = bit_places("batch")
    arrived = flip(small, "seq", seq_bits[0])
    place = after(place, feed_part, small, *from_above, *from_below)
    attend_mine, attend_theirs = attend_grad(batch_count, place, own, edges, grads)
    feed_done = lax.psum_scatter(feed_part, "seq", scatter_dimension=0, tiled=True)[0]
    half = 3 * width // 2
    attend_sum = BatchSum([attend_mine], [attend_theirs], (((0, 0, half),), ((0, half, 3 * width - half),)))
    small = after(small, attend_mine) + arrived
    arrived = flip(small, "batch", batch_bits[0])
    attend_sum.hold(arrived)
    for bit in batch_bits[1:]:
        sends = attend_sum.advance()
        small = after(small, *sends) + arrived
        arrived = flip(small, "batch", bit)
        attend_sum.hold(arrived)
    attend_parts = by_columns(jnp.concatenate(attend_sum.total(), axis=0))
    small = after(small, attend_parts) + arrived
    attend_done = lax.dynamic_index_in_dim(attend_parts, seq_place, 0, keepdims=False).astype(F32)
    for distance in range(1, seq_count):
        route = [(i, (i + distance) % seq_count) for i in range(seq_count)]
        target = (seq_place + distance) % seq_count
        send = lax.dynamic_index_in_dim(attend_parts, target, 0, keepdims=False)
        attend_done = attend_done + lax.ppermute(send, "seq", route).astype(F32)
    for bit in seq_bits[1:]:
        small = small + flip(small, "seq", bit)
    small = small.reshape(-1)
    gain_sums = [small[i * dim : (i + 1) * dim] for i in range(3)]
    rel_sum = small[3 * dim : 3 * dim + rel_bias.size].reshape(rel_bias.shape)

    grad_tokens = (
        part.astype(F32)
        + jnp.concatenate(from_above, axis=0).astype(F32)
        + jnp.concatenate(from_below, axis=0).astype(F32)
    )
    turn = lambda array: array.T.astype(F32)
    cols = dim // seq_count
    s_in = turn(feed_done[:wide, :cols])
    s_output = turn(feed_done[wide:, :cols])
    s_out = feed_done[:-width, cols:].reshape(seq_count, width, cols)
    s_out = s_out.transpose(0, 2, 1).reshape(dim, width).astype(F32)
    s_proj = turn(feed_done[-width:, cols:])
    s_attend = [turn(attend_done[i * width : (i + 1) * width]) for i in range(3)]
    return (
        block,
        embedded,
        loss,
        grad_tokens,
        gain_sums[0],
        s_attend[0],
        s_attend[1],
        s_attend[2],
        rel_sum,
        s_output,
        gain_sums[1],
        s_in,
        s_out,
        gain_sums[2],
        s_proj,
    )


def solution(mesh):
    tok = P("batch", "seq", None)
    mat = P("seq", "batch")
    return jax.shard_map(
        shards,
        mesh=mesh,
        in_specs=(tok,) + (P(),) * 11 + (P("batch", None), P("batch"), tok),
        out_specs=(
            tok,
            P("batch", None),
            P("batch"),
            tok,
            P(),
            mat,
            mat,
            mat,
            P(),
            mat,
            P(),
            mat,
            mat,
            P(),
            mat,
        ),
        check_vma=False,
    )
```

```python
import functools

import jax
import jax.numpy as jnp
from jax import lax
from jax.experimental import pallas as pl
from jax.experimental.pallas import tpu as pltpu
from jax.sharding import PartitionSpec as P

EPS = 1e-06
NEGATIVE = -1e30
SHARPNESS = 50.0
THRESHOLDS = (12, 16, 23, 32, 46, 64, 91)
HIGHEST = lax.Precision.HIGHEST
BF = jnp.bfloat16
F32 = jnp.float32
VMEM_BYTES = 60 * 1024 * 1024
GELU_A = 0.7978845608028654
GELU_B = 0.044715
LANES = 128


def dot_nn(left, right):
    return lax.dot_general(left, right, (((1,), (0,)), ((), ())), preferred_element_type=F32)


def dot_nt(left, right):
    return lax.dot_general(left, right, (((1,), (1,)), ((), ())), preferred_element_type=F32)


def dot_tn(left, right):
    return lax.dot_general(left, right, (((0,), (0,)), ((), ())), preferred_element_type=F32)


def rms_scale(values):
    return lax.rsqrt(jnp.mean(values * values, axis=-1, keepdims=True) + EPS)


def rms_back(values, scale, grad_normed):
    inner = jnp.mean(grad_normed * values, axis=-1, keepdims=True)
    return scale * (grad_normed - values * (scale * scale * inner))


def split_bf(values):
    high = values.astype(BF)
    return high, (values - high.astype(F32)).astype(BF)


def bucket_of(offset):
    distance = jnp.abs(offset)
    beyond = jnp.zeros_like(distance)
    for threshold in THRESHOLDS:
        beyond = beyond + (distance >= threshold).astype(jnp.int32)
    within = jnp.where(distance < 8, distance, 8 + beyond)
    return within + 16 * (offset > 0).astype(jnp.int32)


def wrapped_offsets(shape, axis, size):
    place = lax.broadcasted_iota(jnp.int32, shape, axis)
    return jnp.where(place < size, place, place - 2 * size)


def full(shape):
    return pl.BlockSpec(shape, lambda *_: (0,) * len(shape), pipeline_mode=pl.Buffered(1))


def row_spec(shape, first=0):
    return pl.BlockSpec(
        (1,) + tuple(shape), lambda step, *_: (step + first,) + (0,) * len(shape)
    )


def cost(products, moved, exps=0):
    return pl.CostEstimate(flops=2 * products, bytes_accessed=moved, transcendentals=exps)


def params(limit=VMEM_BYTES):
    return pltpu.CompilerParams(
        vmem_limit_bytes=limit, dimension_semantics=("arbitrary",)
    )


def bias_kernel(size, table_ref, out_ref):
    buckets, heads = table_ref.shape
    hot = (
        lax.broadcasted_iota(jnp.int32, (buckets, 2 * size), 0)
        == bucket_of(-wrapped_offsets((buckets, 2 * size), 1, size))
    ).astype(BF)
    by_offset = dot_tn(table_ref[...], hot)
    for head in range(heads):
        line = jnp.broadcast_to(by_offset[head : head + 1, :], (size, 2 * size))
        out_ref[head] = pltpu.roll(line, 0, 1, stride=1, stride_axis=0).astype(BF)


def bias_tables(rel_bias, size):
    heads = rel_bias.shape[1]
    return pl.pallas_call(
        functools.partial(bias_kernel, size),
        out_shape=jax.ShapeDtypeStruct((heads, size, 2 * size), BF),
        compiler_params=pltpu.CompilerParams(vmem_limit_bytes=VMEM_BYTES),
    )(rel_bias)


def bias_grad_kernel(*refs):
    acc_refs, out_ref = refs[:-1], refs[-1]
    group, size, width = acc_refs[0].shape
    buckets = out_ref.shape[2]
    hot = (
        lax.broadcasted_iota(jnp.int32, (width, buckets), 1)
        == bucket_of(-wrapped_offsets((width, buckets), 0, width // 2))
    ).astype(BF)
    for head in range(group):
        rows = sum(acc_ref[head] for acc_ref in acc_refs)
        count = size
        while count > 8:
            count = count // 2
            rows = rows[:count] + pltpu.roll(rows[count:], width - count, 1)
        place = lax.broadcasted_iota(jnp.int32, rows.shape, 0)
        for bit in (4, 2, 1):
            rows = jnp.where((place & bit) > 0, pltpu.roll(rows, width - bit, 1), rows)
        first, rest = split_bf(rows)
        second, third = split_bf(rows - first.astype(F32))
        out_ref[head] = dot_nn(first, hot) + dot_nn(second, hot) + dot_nn(third, hot)


def bias_grad(accs, buckets):
    heads, count, width = accs[0].shape
    group = max(size for size in (1, 2, 3, 4) if heads % size == 0)
    out = pl.pallas_call(
        bias_grad_kernel,
        grid=(heads // group,),
        in_specs=[pl.BlockSpec((group, count, width), lambda step: (step, 0, 0))] * len(accs),
        out_specs=pl.BlockSpec((group, 8, buckets), lambda step: (step, 0, 0)),
        out_shape=jax.ShapeDtypeStruct((heads, 8, buckets), F32),
        compiler_params=params(),
        name="bias_grad",
    )(*accs)
    return jnp.sum(out, axis=1).T


class Row:
    def __init__(self, lengths_ref, place_ref, row, size):
        slots = lengths_ref.shape[1]
        base = place_ref[0] * size
        pos = base + lax.broadcasted_iota(jnp.int32, (1, size), 1)
        zero = jnp.int32(0)
        before, first, last, beyond = zero, zero, zero, zero
        own = jnp.zeros((1, size), jnp.int32)
        low = jnp.zeros((1, size), jnp.int32)
        high = jnp.zeros((1, size), jnp.int32)
        end = zero
        passed = lambda end, place: (end <= place).astype(jnp.int32)
        for slot in range(slots):
            end = end + lengths_ref[row, slot]
            before += passed(end, base - 1)
            first += passed(end, base)
            last += passed(end, base + size - 1)
            beyond += passed(end, base + size)
            own += passed(end, pos)
            low += passed(end, pos - size)
            high += passed(end, pos + size)
        before = jnp.where(base == 0, -1, before).astype(F32)
        low = jnp.where(pos < size, -1, low).astype(F32)
        own = own.astype(F32)
        col_own, col_low, col_high = (
            jnp.broadcast_to(item, (LANES, size)).T for item in (own, low, high.astype(F32))
        )
        self.in_low = col_own == before
        self.in_high = col_own == beyond.astype(F32)
        self.slot_low = col_low == first.astype(F32)
        self.slot_high = col_high == last.astype(F32)
        key = lax.broadcasted_iota(jnp.int32, (size, size), 0)
        query = lax.broadcasted_iota(jnp.int32, (size, size), 1)
        wide = lambda item: jnp.concatenate([item] * (size // LANES), axis=1)
        self.own = wide(col_own) == own
        self.alt = jnp.where(key > query, wide(col_low), jnp.where(key < query, wide(col_high), -2.0)) == own


def where_tiles(mask, left, right):
    lanes = mask.shape[1]
    return jnp.concatenate(
        [
            jnp.where(mask, left[:, start : start + lanes], right[:, start : start + lanes])
            for start in range(0, left.shape[1], lanes)
        ],
        axis=1,
    )


def store_group_masks(row, ref):
    _, _, size, lanes = ref.shape
    first = lax.broadcasted_iota(jnp.int32, (1, lanes), 1) < lanes // 2
    low = row.in_low.astype(F32)
    high = row.in_high.astype(F32)
    for part, group in enumerate((low, 1.0 - low - high, high)):
        ref[0, part] = jnp.where(first, group, 0.0).astype(BF)
        ref[1, part] = jnp.where(first, 0.0, group).astype(BF)


def by_group(pair, ref, half):
    return jnp.concatenate([pair * ref[half, part] for part in range(3)], axis=1)


def fold_rows(row, first, wide):
    lanes = wide[0].shape[1] // 3
    parts = [
        jnp.where(first, wide[0][:, here], wide[1][:, here])
        for here in (slice(part * lanes, (part + 1) * lanes) for part in range(3))
    ]
    return jnp.where(row.in_low, parts[0], jnp.where(row.in_high, parts[2], parts[1]))


def own_kernel(x_ref, gain1_ref, wq_ref, wk_ref, wv_ref, out_ref):
    x = x_ref[0].astype(F32)
    out_ref[0, 3] = (x * rms_scale(x) * gain1_ref[...].astype(F32)).astype(BF)
    for index, weight_ref in enumerate((wq_ref, wk_ref, wv_ref)):
        out_ref[0, index] = dot_nn(out_ref[0, 3], weight_ref[...]).astype(BF)


def own_projections(tokens, gain1, weights):
    rows, size, dim = tokens.shape
    constants = (gain1,) + tuple(weights)
    return pl.pallas_call(
        own_kernel,
        grid=(rows,),
        in_specs=[row_spec((size, dim))] + [full(item.shape) for item in constants],
        out_specs=row_spec((4, size, dim)),
        out_shape=jax.ShapeDtypeStruct((rows, 4, size, dim), BF),
        compiler_params=params(),
        cost_estimate=cost(3 * rows * size * dim * dim, rows * size * dim * 10),
        name="own_projections",
    )(tokens, *constants)


def row_sentences(lengths_ref, place_ref, row, size):
    where_pos = place_ref[0] * size + lax.broadcasted_iota(jnp.int32, (1, size), 1)
    found = jnp.zeros((1, size), jnp.int32)
    end = jnp.int32(0)
    for slot in range(lengths_ref.shape[1]):
        end = end + lengths_ref[row, slot]
        found = found + (end <= where_pos).astype(jnp.int32)
    return found


def forward_kernel(
    rows,
    lengths_ref,
    place_ref,
    x_ref,
    pair_ref,
    across_ref,
    own_ref,
    gains_ref,
    wk_ref,
    wv_ref,
    bias_ref,
    win_ref,
    wout_ref,
    wo_hbm,
    block_ref,
    pooled_ref,
    edge_ref,
    p_ref,
    att_ref,
    pre_ref,
    after_hbm,
    n2_hbm,
    mask_ref,
    group_ref,
    att_all,
    after_all,
    after_low,
    n2_all,
    total_ref,
    wo_ref,
    sems,
):
    size, dim = x_ref.shape[1:]
    heads = bias_ref.shape[0]
    pairs = heads // 2
    lanes = dim // pairs
    slots = pooled_ref.shape[1]
    step = pl.program_id(0)
    copies = [
        pltpu.make_async_copy(after_low, after_hbm, sems.at[0]),
        pltpu.make_async_copy(n2_all, n2_hbm, sems.at[1]),
    ]
    wo_copy = pltpu.make_async_copy(wo_hbm, wo_ref, sems.at[2])

    @pl.when(step == 0)
    def _():
        wo_copy.start()

    @pl.when(step < rows)
    def _():
        here = pl.ds(pl.multiple_of(step * size, size), size)
        row = Row(lengths_ref, place_ref, step, size)
        mask_ref[0] = jnp.where(row.own, 0.0, NEGATIVE).astype(BF)
        mask_ref[1] = jnp.where(row.alt, 0.0, NEGATIVE).astype(BF)
        store_group_masks(row, group_ref)
        gain1 = gains_ref[0:1, :].astype(F32)
        after_all[here, :] = x_ref[0].astype(F32)
        own = own_ref[0, 3].astype(F32)
        sides = by_side(place_ref, pair_ref[0], across_ref[0])
        for part, (source, slot) in enumerate(zip(sides, (row.slot_low, row.slot_high))):
            x = source.astype(F32)
            edge_ref[0, 4 + part] = where_tiles(slot, x * rms_scale(x) * gain1, own).astype(BF)
        edges = edge_ref[0, 4:].reshape(2 * size, dim)
        first_half = lax.broadcasted_iota(jnp.int32, (1, lanes), 1) < lanes // 2
        for index, weight_ref in enumerate((wk_ref, wv_ref)):
            value = dot_nn(edges, weight_ref[...]).astype(BF)
            edge_ref[0, 2 * index : 2 * index + 2] = value.reshape(2, size, dim)
        for pair in range(pairs):
            cols = slice(pair * lanes, (pair + 1) * lanes)
            keys, values = key_groups(own_ref, edge_ref, cols)
            halves, from_pair, from_across = [], [], []
            for half in range(2):
                head = 2 * pair + half
                scores = dot_nt(keys, by_group(own_ref[0, 0, :, cols], group_ref, half))
                bias = jnp.maximum(
                    bias_ref[head, :, :size] + mask_ref[0], bias_ref[head, :, size:] + mask_ref[1]
                )
                scores = scores + bias.astype(F32)
                peak = jnp.max(scores, axis=0, keepdims=True)
                powers = jnp.exp(scores - peak)
                inverse = 1.0 / jnp.sum(powers, axis=0, keepdims=True)
                probs = (powers * inverse).astype(BF)
                p_ref[0, head] = probs
                halves.append(dot_tn(probs, values))
            mixed = fold_rows(row, first_half, halves).astype(BF)
            att_ref[0, :, cols] = mixed
            att_all[here, cols] = mixed

    @pl.when(step == rows)
    def _():
        wo_copy.wait()
        after = after_all[...] + dot_nn(att_all[...], wo_ref[...])
        after_low[...] = after.astype(BF)
        total_ref[...] = after
        n2_all[...] = (after * rms_scale(after) * gains_ref[1:2, :].astype(F32)).astype(BF)
        for copy in copies:
            copy.start()

    @pl.when(step >= rows)
    def _():
        pre = dot_nn(n2_all[...], win_ref[...])
        square = pre * pre
        gate = 0.5 + 0.5 * jnp.tanh(pre * (GELU_A + (GELU_A * GELU_B) * square))
        pre_ref[...] = pre.astype(BF)
        total_ref[...] += dot_nn((pre * gate).astype(BF), wout_ref[...])

    @pl.when(step == pl.num_programs(0) - 1)
    def _():
        gainf = gains_ref[2:3, :].astype(F32)
        for row in range(rows):
            here = slice(row * size, (row + 1) * size)
            block = total_ref[here, :].astype(BF)
            block_ref[row] = block
            out = block.astype(F32)
            final = out * rms_scale(out) * gainf
            found = row_sentences(lengths_ref, place_ref, row, size)
            member = (lax.broadcasted_iota(jnp.int32, (slots, size), 0) == found).astype(BF)
            high_part, low_part = split_bf(final)
            pooled_ref[row] = dot_nn(member, high_part) + dot_nn(member, low_part)
        for copy in copies:
            copy.wait()


def by_side(place_ref, pair, across):
    odd = place_ref[0] % 2 == 1
    return jnp.where(odd, pair, across), jnp.where(odd, across, pair)


def key_groups(own_ref, edge_ref, cols):
    return [
        jnp.concatenate(
            [edge_ref[0, 2 * index, :, cols], own_ref[0, 1 + index, :, cols], edge_ref[0, 2 * index + 1, :, cols]],
            axis=1,
        )
        for index in range(2)
    ]


def forward(lengths, place, tokens, low, high, own, gains, weights, bias):
    rows, size, dim = tokens.shape
    heads = bias.shape[0]
    slots = lengths.shape[1]
    wk, wv, wo, win, wout = weights
    hidden = win.shape[1]
    tiles = hidden // dim
    toks = rows * size
    per_row = lambda shape: pl.BlockSpec(
        (1,) + shape, lambda step, *_: (jnp.minimum(step, rows - 1),) + (0,) * len(shape)
    )
    tile = lambda step: jnp.maximum(step - rows, 0)
    constants = (gains, wk, wv, bias)
    anywhere = pl.BlockSpec(memory_space=pl.ANY)
    out_of = lambda shape, kind=BF: jax.ShapeDtypeStruct(shape, kind)
    return pl.pallas_call(
        functools.partial(forward_kernel, rows),
        grid_spec=pltpu.PrefetchScalarGridSpec(
            num_scalar_prefetch=2,
            grid=(rows + tiles,),
            in_specs=[per_row((size, dim))] * 3
            + [per_row((4, size, dim))]
            + [full(item.shape) for item in constants]
            + [
                pl.BlockSpec((dim, dim), lambda step, *_: (0, tile(step))),
                pl.BlockSpec((dim, dim), lambda step, *_: (tile(step), 0)),
                anywhere,
            ],
            out_specs=[
                full((rows, size, dim)),
                full((rows, slots, dim)),
                per_row((6, size, dim)),
                per_row((heads, size, size)),
                per_row((size, dim)),
                pl.BlockSpec((toks, dim), lambda step, *_: (0, tile(step))),
                anywhere,
                anywhere,
            ],
            scratch_shapes=[
                pltpu.VMEM((2, size, size), BF),
                pltpu.VMEM((2, 3, size, 2 * dim // heads), BF),
                pltpu.VMEM((toks, dim), BF),
                pltpu.VMEM((toks, dim), F32),
                pltpu.VMEM((toks, dim), BF),
                pltpu.VMEM((toks, dim), BF),
                pltpu.VMEM((toks, dim), F32),
                pltpu.VMEM((dim, dim), BF),
                pltpu.SemaphoreType.DMA((3,)),
            ],
        ),
        out_shape=[
            out_of((rows, size, dim)),
            out_of((rows, slots, dim), F32),
            out_of((rows, 6, size, dim)),
            out_of((rows, heads, size, size)),
            out_of((rows, size, dim)),
            out_of((toks, hidden)),
            out_of((toks, dim)),
            out_of((toks, dim)),
        ],
        compiler_params=params(),
        cost_estimate=cost(
            toks * dim * (5 * dim + 2 * hidden + 36 * size),
            toks * (hidden * 4 + dim * 40),
            rows * heads * size * size,
        ),
        name="forward",
    )(lengths, place, tokens, low, high, own, *constants, win, wout, wo)


def store_split(core, value, refs, count, first=0):
    if len(refs) == 1:
        refs[0][first : first + value.shape[0], :] = value
        return
    groups = value.shape[0] // (2 * count)
    for group in range(groups):
        even = value[2 * group * count : (2 * group + 1) * count]
        odd = value[(2 * group + 1) * count : (2 * group + 2) * count]

        refs[0][group, first : first + count, :] = jnp.where(core == 0, even, odd)
        refs[1][group, first : first + count, :] = jnp.where(core == 0, odd, even)


def feed_back_kernel(
    rows,
    parts,
    lengths_ref,
    place_ref,
    block_ref,
    cot_ref,
    pool_ref,
    graw_ref,
    pooled_ref,
    gain_ref,
    pre_ref,
    win_ref,
    wout_ref,
    after_hbm,
    n2_hbm,
    att_hbm,
    wo_hbm,
    back_ref,
    gains_ref,
    *rest,
):
    split = len(rest) == 14
    per = 2 if split else 1
    in_refs, out_refs, small_refs = (rest[i * per : (i + 1) * per] for i in range(3))
    gout_ref, branch_ref, gn2_ref, after_ref, n2_ref, att_ref, wo_ref, sems = rest[3 * per :]
    _, size, dim = block_ref.shape
    toks = rows * size
    slots = pool_ref.shape[1]
    step = pl.program_id(0)
    tiles = pl.num_programs(0) - 1
    core = place_ref[1]
    copies = [
        pltpu.make_async_copy(n2_hbm, n2_ref, sems.at[0]),
        pltpu.make_async_copy(after_hbm, after_ref, sems.at[1]),
        pltpu.make_async_copy(att_hbm, att_ref, sems.at[2]),
        pltpu.make_async_copy(wo_hbm, wo_ref, sems.at[3]),
    ]

    @pl.when(step == 0)
    def _():
        for copy in copies:
            copy.start()
        gainf = gain_ref[2:3, :].astype(F32)
        gain_f = jnp.zeros((1, dim), F32)
        for row in range(rows):
            here = slice(row * size, (row + 1) * size)
            found = row_sentences(lengths_ref, place_ref, row, size)
            member = (lax.broadcasted_iota(jnp.int32, (slots, size), 0) == found).astype(BF)
            high_part, low_part = split_bf(pool_ref[row])
            g_final = dot_tn(member, high_part) + dot_tn(member, low_part)
            out = block_ref[row].astype(F32)
            scale = rms_scale(out)
            gain_f = gain_f + jnp.sum(g_final * out * scale, axis=0, keepdims=True)
            g_out = rms_back(out, scale, g_final * gainf) + cot_ref[row].astype(F32)
            gout_ref[here, :] = g_out
            branch_ref[here, :] = g_out.astype(BF)
        gains_ref[...] = jnp.zeros_like(gains_ref)
        gains_ref[0:1, :] = gain_f
        copies[0].wait()

    @pl.when(step < tiles)
    def _():
        g_hidden = dot_nt(branch_ref[...], wout_ref[...])
        pre = pre_ref[...].astype(F32)
        square = pre * pre
        gate = 0.5 + 0.5 * jnp.tanh(pre * (GELU_A + (GELU_A * GELU_B) * square))
        act = pre * gate
        value = dot_tn(branch_ref[...], act.astype(BF)).astype(BF)
        store_split(core, value, out_refs, dim // parts)
        slope = gate + act * (1.0 - gate) * (2 * GELU_A + (6 * GELU_A * GELU_B) * square)
        g_pre = (g_hidden * slope).astype(BF)
        value = dot_tn(g_pre, n2_ref[...]).astype(BF)
        store_split(core, value, in_refs, tiles * dim // parts)
        part = dot_nt(g_pre, win_ref[...])

        @pl.when(step == 0)
        def _():
            gn2_ref[...] = part

        @pl.when(step > 0)
        def _():
            gn2_ref[...] += part

    @pl.when(step == tiles)
    def _():
        for copy in copies[1:]:
            copy.wait()
        gain2 = gain_ref[1:2, :].astype(F32)
        gain_2 = jnp.zeros((1, dim), F32)
        for row in range(rows):
            here = slice(row * size, (row + 1) * size)
            after = after_ref[here, :].astype(F32)
            g_n2 = gn2_ref[here, :]
            scale = rms_scale(after)
            gain_2 = gain_2 + jnp.sum(g_n2 * after * scale, axis=0, keepdims=True)
            g_after = gout_ref[here, :] + rms_back(after, scale, g_n2 * gain2)
            back_ref[row, 1] = g_after.astype(BF)
            branch_ref[here, :] = g_after.astype(BF)
        gains_ref[1:2, :] = gain_2
        g_mix = dot_nt(branch_ref[...], wo_ref[...]).astype(BF)
        for row in range(rows):
            back_ref[row, 0] = g_mix[row * size : (row + 1) * size]
        value = dot_tn(branch_ref[...], att_ref[...].reshape(toks, dim)).astype(BF)
        store_split(core, value, small_refs, dim // parts)
        left_high, left_low = split_bf(jnp.where(place_ref[0] == 0, graw_ref[...], 0.0))
        right_high, right_low = split_bf(pooled_ref[...])
        value = dot_tn(left_high, right_high)
        value += dot_tn(left_high, right_low) + dot_tn(left_low, right_high)
        first = dim // parts if split else dim
        store_split(core, value.astype(BF), small_refs, dim // parts, first)


def feed_back(parts, lengths, place, block, after, cot, att, n2, pre, pool, graw, pooled, gains, weights):
    rows, size, dim = block.shape
    hidden = pre.shape[1]
    tiles = hidden // dim
    toks = rows * size
    wo, win, wout = weights
    split = (dim // parts) % 16 == 0 and dim % (2 * hidden // parts) == 0
    tile = lambda step: jnp.minimum(step, tiles - 1)
    if split:
        groups = parts // 2
        wide = hidden // parts
        inner = dim // (2 * wide)
        narrow = dim // parts
        in_specs = [pl.BlockSpec((inner, wide, dim), lambda step, *_: (tile(step), 0, 0))] * 2
        out_specs = [pl.BlockSpec((groups, narrow, dim), lambda step, *_: (0, tile(step), 0))] * 2
        small_specs = [full((groups, 2 * narrow, dim))] * 2
        shapes = [(groups, wide, dim)] * 2 + [(groups, tiles * narrow, dim)] * 2 + [(groups, 2 * narrow, dim)] * 2
    else:
        in_specs = [pl.BlockSpec((dim, dim), lambda step, *_: (tile(step), 0))]
        out_specs = [pl.BlockSpec((dim, dim), lambda step, *_: (tile(step), 0))]
        small_specs = [full((2 * dim, dim))]
        shapes = [(hidden, dim), (tiles * dim, dim), (2 * dim, dim)]
    constants = (block, cot, pool, graw, pooled, gains)
    outs = pl.pallas_call(
        functools.partial(feed_back_kernel, rows, parts),
        grid_spec=pltpu.PrefetchScalarGridSpec(
            num_scalar_prefetch=2,
            grid=(tiles + 1,),
            in_specs=[full(item.shape) for item in constants]
            + [
                pl.BlockSpec((toks, dim), lambda step, *_: (0, tile(step))),
                pl.BlockSpec((dim, dim), lambda step, *_: (0, tile(step))),
                pl.BlockSpec((dim, dim), lambda step, *_: (tile(step), 0)),
            ]
            + [pl.BlockSpec(memory_space=pl.ANY)] * 4,
            out_specs=[full((rows, 2, size, dim)), full((8, dim))]
            + in_specs
            + out_specs
            + small_specs,
            scratch_shapes=[
                pltpu.VMEM((toks, dim), F32),
                pltpu.VMEM((toks, dim), BF),
                pltpu.VMEM((toks, dim), F32),
                pltpu.VMEM((toks, dim), BF),
                pltpu.VMEM((toks, dim), BF),
                pltpu.VMEM((rows, size, dim), BF),
                pltpu.VMEM((dim, dim), BF),
                pltpu.SemaphoreType.DMA((4,)),
            ],
        ),
        out_shape=[
            jax.ShapeDtypeStruct((rows, 2, size, dim), BF),
            jax.ShapeDtypeStruct((8, dim), F32),
        ]
        + [jax.ShapeDtypeStruct(shape, BF) for shape in shapes],
        compiler_params=params(),
        cost_estimate=cost(
            toks * dim * (4 * hidden + 2 * dim), toks * (hidden * 4 + dim * 20) + 8 * hidden * dim
        ),
        name="feed_back",
    )(lengths, place, *constants, pre, win, wout, after, n2, att, wo)
    if split:
        mine, theirs = outs[2::2], outs[3::2]
    else:
        whole = [
            outs[2].reshape(parts, hidden // parts, dim),
            outs[3].reshape(tiles, parts, dim // parts, dim).transpose(1, 0, 2, 3),
            outs[4].reshape(2, parts, dim // parts, dim).transpose(1, 0, 2, 3),
        ]
        mine, theirs = split_core(whole)
    return outs[0], outs[1], mine, theirs


def split_core(blocks):
    core = (lax.axis_index("batch") % 2).astype(jnp.int32)
    pairs = [item.reshape((item.shape[0] // 2, 2, -1, item.shape[-1])) for item in blocks]
    pick = lambda item, place: lax.dynamic_index_in_dim(item, place, 1, keepdims=False)
    return [pick(item, core) for item in pairs], [pick(item, 1 - core) for item in pairs]


def attend_grad_kernel(parts, place_ref, n1_ref, own_ref, edge_hbm, n1_edge_hbm, *rest):
    refs, (edge_ref, n1_edge_ref, sems) = rest[:-3], rest[-3:]
    rows, _, size, dim = own_ref.shape
    step = pl.program_id(0)
    width = dim // parts if len(refs) == 2 else dim
    flat = lambda ref: ref[...].reshape(-1, dim)
    n1_copy = pltpu.make_async_copy(n1_edge_hbm.at[:, 4:6], n1_edge_ref, sems.at[0])
    copies = [
        pltpu.make_async_copy(
            edge_hbm.at[:, 3 + 2 * index : 5 + 2 * index], edge_ref.at[index], sems.at[1 + index]
        )
        for index in range(2)
    ]

    @pl.when(step == 0)
    def _():
        n1_copy.start()
        for copy in copies:
            copy.start()
        value = dot_tn(flat(own_ref), flat(n1_ref)).astype(BF)
        store_split(place_ref[1], value, refs, dim // parts, 0)
        n1_copy.wait()

    for index in range(2):

        @pl.when(step == 1 + index)
        def _():
            copies[index].wait()
            value = dot_tn(flat(own_ref), flat(n1_ref)) + dot_tn(flat(edge_ref.at[index]), flat(n1_edge_ref))
            store_split(place_ref[1], value.astype(BF), refs, dim // parts, (1 + index) * width)


def attend_grad(parts, place, own, edges, grads):
    rows, _, size, dim = own.shape
    narrow = dim // parts
    split = narrow % 16 == 0
    shape = (parts // 2, 3 * narrow, dim) if split else (3 * dim, dim)
    copies = 2 if split else 1
    outs = pl.pallas_call(
        functools.partial(attend_grad_kernel, parts),
        grid_spec=pltpu.PrefetchScalarGridSpec(
            num_scalar_prefetch=1,
            grid=(3,),
            in_specs=[
                pl.BlockSpec((rows, 1, size, dim), lambda step, *_: (0, 3, 0, 0)),
                pl.BlockSpec((rows, 1, size, dim), lambda step, *_: (0, step, 0, 0)),
                pl.BlockSpec(memory_space=pl.ANY),
                pl.BlockSpec(memory_space=pl.ANY),
            ],
            out_specs=[full(shape)] * copies,
            scratch_shapes=[
                pltpu.VMEM((2, rows, 2, size, dim), BF),
                pltpu.VMEM((rows, 2, size, dim), BF),
                pltpu.SemaphoreType.DMA((3,)),
            ],
        ),
        out_shape=[jax.ShapeDtypeStruct(shape, BF)] * copies,
        compiler_params=params(),
        cost_estimate=cost(rows * size * dim * dim * 7, rows * size * dim * 26),
        name="attend_grad",
    )(place, own, grads, grads, edges)
    if split:
        return outs[0], outs[1]
    mine, theirs = split_core([outs[0].reshape(3, parts, narrow, dim).transpose(1, 0, 2, 3)])
    return mine[0], theirs[0]


def attend_back_kernel(
    first,
    lengths_ref,
    place_ref,
    own_ref,
    pair_ref,
    across_ref,
    qkv_ref,
    edge_ref,
    p_ref,
    back_ref,
    gain_ref,
    wq_ref,
    wk_ref,
    wv_ref,
    *rest,
):
    grad_ref, part_ref, to_pair_ref, to_across_ref, acc_ref, gains_ref, mask_ref, group_ref = rest[-8:]
    size, dim = own_ref.shape[1:]
    heads = p_ref.shape[1]
    pairs = heads // 2
    lanes = dim // pairs
    step = pl.program_id(0)
    row = Row(lengths_ref, place_ref, step + first, size)
    mask_ref[...] = row.own.astype(F32)

    @pl.when(step == 0)
    def _():
        acc_ref[...] = jnp.zeros_like(acc_ref)
        gains_ref[...] = jnp.zeros_like(gains_ref)

    first_half = lax.broadcasted_iota(jnp.int32, (1, lanes), 1) < lanes // 2
    store_group_masks(row, group_ref)
    half_size = size // 2
    for pair in range(pairs):
        cols = slice(pair * lanes, (pair + 1) * lanes)
        keys, values = key_groups(qkv_ref, edge_ref, cols)
        q_groups = [by_group(qkv_ref[0, 0, :, cols], group_ref, half) for half in range(2)]
        o_groups = [by_group(back_ref[0, 0, :, cols], group_ref, half) for half in range(2)]
        d_q, scores_pair = [], []
        for half in range(2):
            head = 2 * pair + half
            g_probs = dot_nt(values, o_groups[half])
            full_probs = p_ref[0, head].astype(F32)
            product = full_probs * g_probs
            inner = jnp.sum(product, axis=0, keepdims=True)
            g_scores = product - full_probs * inner
            on_own = g_scores * mask_ref[...]
            off_own = g_scores - on_own
            acc_ref[head, :, :half_size] += on_own[:half_size, :half_size] + on_own[half_size:, half_size:]
            acc_ref[head, :, half_size:size] += on_own[:half_size, half_size:] + off_own[half_size:, :half_size]
            acc_ref[head, :, size : size + half_size] += off_own[:half_size, :half_size] + off_own[half_size:, half_size:]
            acc_ref[head, :, size + half_size :] += off_own[:half_size, half_size:] + on_own[half_size:, :half_size]
            scores_pair.append(g_scores.astype(BF))
            d_q.append(dot_tn(scores_pair[-1], keys))
        grad_ref[0, 0, :, cols] = fold_rows(row, first_half, d_q).astype(BF)
        probs_pair = [p_ref[0, 2 * pair], p_ref[0, 2 * pair + 1]]
        for index, (left, right) in enumerate(((scores_pair, q_groups), (probs_pair, o_groups))):
            value = dot_nn(jnp.concatenate(left, axis=1), jnp.concatenate(right, axis=0)).astype(BF)
            grad_ref[0, 3 + 2 * index, :, cols] = value[:, :lanes]
            grad_ref[0, 1 + index, :, cols] = value[:, lanes : 2 * lanes]
            grad_ref[0, 4 + 2 * index, :, cols] = value[:, 2 * lanes :]

    gain1 = gain_ref[0:1, :].astype(F32)
    g_whole = None
    for index, weight_ref in enumerate((wk_ref, wv_ref)):
        edge_grad = grad_ref[0, 3 + 2 * index : 5 + 2 * index].reshape(2 * size, dim)
        left = jnp.concatenate([edge_grad, grad_ref[0, 1 + index]], axis=0)
        term = dot_nt(left, weight_ref[...])
        g_whole = term if g_whole is None else g_whole + term
    zero = jnp.zeros((size, dim), F32)
    g_low = where_tiles(row.slot_low, g_whole[:size], zero)
    g_high = where_tiles(row.slot_high, g_whole[size : 2 * size], zero)
    g_own = g_whole[2 * size :] + (g_whole[:size] - g_low) + (g_whole[size : 2 * size] - g_high)
    g_own = g_own + dot_nt(grad_ref[0, 0], wq_ref[...])
    gain_1 = jnp.zeros((1, dim), F32)
    low, high = by_side(place_ref, pair_ref[0], across_ref[0])
    results = []
    for source, g_norm in ((own_ref[0], g_own), (low, g_low), (high, g_high)):
        x = source.astype(F32)
        scale = rms_scale(x)
        gain_1 = gain_1 + jnp.sum(g_norm * x * scale, axis=0, keepdims=True)
        results.append(rms_back(x, scale, g_norm * gain1))
    part_ref[0] = (results[0] + back_ref[0, 1].astype(F32)).astype(BF)
    odd = place_ref[0] % 2 == 1
    to_pair_ref[0] = jnp.where(odd, results[1], results[2]).astype(BF)
    to_across_ref[0] = jnp.where(odd, results[2], results[1]).astype(BF)
    gains_ref[0:1, :] += gain_1


def attend_back(first, count, halo, earlier, lengths, place, x, low, high, own, edges, p, back, gains, weights):
    rows, size, dim = x.shape
    heads = p.shape[1]
    constants = (gains,) + tuple(weights)
    start = 2 + 7 + len(constants)
    aliases = {start + index: index for index in range(len(earlier))}
    return pl.pallas_call(
        functools.partial(attend_back_kernel, first),
        grid_spec=pltpu.PrefetchScalarGridSpec(
            num_scalar_prefetch=2,
            grid=(count,),
            in_specs=[row_spec((size, dim), first)] * 3
            + [row_spec((3, size, dim), first), row_spec((4, size, dim), first)]
            + [row_spec((heads, size, size), first), row_spec((2, size, dim), first)]
            + [full(item.shape) for item in constants]
            + [pl.BlockSpec(memory_space=pl.ANY)] * len(earlier),
            out_specs=[
                row_spec((7, size, dim), first),
                row_spec((size, dim), first),
                row_spec((size, dim), first - halo[0]),
                row_spec((size, dim), first - halo[0]),
            ]
            + [full((heads, size // 2, 2 * size)), full((8, dim))],
            scratch_shapes=[
                pltpu.VMEM((size, size), F32),
                pltpu.VMEM((2, 3, size, 2 * dim // heads), BF),
            ],
        ),
        out_shape=[
            jax.ShapeDtypeStruct((rows, 7, size, dim), BF),
            jax.ShapeDtypeStruct((rows, size, dim), BF),
            jax.ShapeDtypeStruct((halo[1], size, dim), BF),
            jax.ShapeDtypeStruct((halo[1], size, dim), BF),
            jax.ShapeDtypeStruct((heads, size // 2, 2 * size), F32),
            jax.ShapeDtypeStruct((8, dim), F32),
        ],
        input_output_aliases=aliases,
        compiler_params=params(),
        cost_estimate=cost(
            count * size * dim * (9 * dim + 128 * size), count * size * dim * 60
        ),
        name="attend_back_rows",
    )(lengths, place, x, low, high, own, edges, p, back, *constants, *earlier)


def flip(block, axis, bit):
    count = lax.axis_size(axis)
    return lax.ppermute(block, axis, [(i, i ^ bit) for i in range(count)])


def sum_along(block, axis):
    bit = 1
    while bit < lax.axis_size(axis):
        block = block + flip(block, axis, bit)
        bit *= 2
    return block


def bit_places(axis):
    return [1 << level for level in range((lax.axis_size(axis) - 1).bit_length())]


def gather_batch(block):
    place = lax.axis_index("batch")
    bits = bit_places("batch")
    gathered = block[None]
    for bit in reversed(bits):
        other = flip(gathered, "batch", bit)
        upper = (place & bit) > 0
        gathered = jnp.stack(
            [jnp.where(upper, other, gathered), jnp.where(upper, gathered, other)], axis=1
        )
        gathered = gathered.reshape((-1,) + block.shape)
    return gathered.reshape((-1,) + block.shape[1:])


def halve(block, bits, bit):
    axis = bits.index(bit)
    mine = ((lax.axis_index("batch") & bit) > 0).astype(jnp.int32)
    send = lax.dynamic_index_in_dim(block, 1 - mine, axis, keepdims=False)
    keep = lax.dynamic_index_in_dim(block, mine, axis, keepdims=False)
    return keep + flip(send, "batch", bit), [item for item in bits if item != bit]


def after(value, *others):
    return lax.optimization_barrier((value,) + tuple(others))[0]


def stage_kernel(groups, place_ref, *refs):
    ins = refs[: 2 * sum(len(group) for group in groups)]
    outs = refs[len(ins) :]
    taken = 0
    for index, group in enumerate(groups):
        first = 0
        for count in group:
            value = ins[2 * taken][0, 0, 0] + ins[2 * taken + 1][0, 0, 0]
            taken += 1
            for which in range(2):

                @pl.when(pl.program_id(0) == which)
                def _():
                    outs[2 * index + which][0, 0, first : first + count, :] = value

            first += count


def stage(place, groups, bits, pieces):
    columns = groups[0][0][0].shape[-1]
    lead = bits[0][0][0] * bits[0][0][1]
    if any(count % (16 * pieces) or first % count for group in groups for _, _, first, count in group):
        sends, keeps = [], []
        for index, group in enumerate(groups):
            before, behind = bits[index][0]
            total = jnp.concatenate(
                [(kept + arrived)[..., first : first + count, :].reshape(-1, count, columns)
                 for kept, arrived, first, count in group],
                axis=1,
            ).reshape(before, 2, behind, -1, columns)
            pick = lambda which: lax.dynamic_index_in_dim(total, which, 1, keepdims=False)
            sends.append(pick(1 - place[index]).reshape(lead, 1, -1, columns))
            keeps.append(pick(place[index]).reshape(lead, 1, -1, columns))
        return sends, keeps
    in_specs, operands, out_specs, shapes = [], [], [], []
    for index, group in enumerate(groups):
        before, behind = bits[index][0]
        total = 0

        def place_of(half, step, chunk, places, index=index, behind=behind):
            mine = places[index]
            where_at = jnp.where(half == 0, 1 - mine, mine)
            return step // behind, where_at, step % behind, chunk

        for kept, arrived, first, count in group:
            rows = count // pieces
            total += rows
            shape = (before, 2, behind) + kept.shape[-2:]

            def index_map(half, step, chunk, places, place_of=place_of, first=first, rows=rows):
                one, two, three, four = place_of(half, step, chunk, places)
                return one, two, three, four + first // rows, 0

            for item in (kept, arrived):
                in_specs.append(pl.BlockSpec((1, 1, 1, rows, columns), index_map))
                operands.append(item.reshape(shape))
        for which in range(2):

            def out_map(half, step, chunk, places, which=which):
                if which == 0:
                    step = jnp.where(half == 0, step, lead - 1)
                    chunk = jnp.where(half == 0, chunk, pieces - 1)
                else:
                    step = jnp.where(half == 1, step, 0)
                    chunk = jnp.where(half == 1, chunk, 0)
                return step, chunk, 0, 0

            out_specs.append(pl.BlockSpec((1, 1, total, columns), out_map))
            shapes.append(jax.ShapeDtypeStruct((lead, pieces, total, columns), BF))
    outs = pl.pallas_call(
        functools.partial(
            stage_kernel, [[count // pieces for _, _, _, count in group] for group in groups]
        ),
        grid_spec=pltpu.PrefetchScalarGridSpec(
            num_scalar_prefetch=1, grid=(2, lead, pieces), in_specs=in_specs, out_specs=out_specs
        ),
        out_shape=shapes,
        compiler_params=pltpu.CompilerParams(
            vmem_limit_bytes=VMEM_BYTES, dimension_semantics=("arbitrary",) * 3
        ),
        name="halving_stage",
    )(place, *operands)
    return outs[0::2], outs[1::2]


class BatchSum:
    def __init__(self, mine, theirs, streams):
        bits = bit_places("batch")
        arrived = [flip(item, "batch", bits[0]) for item in theirs]
        self.groups = [
            [(mine[item], arrived[item], first, rows) for item, first, rows in stream] for stream in streams
        ]
        self.bits = [bits[1:][::-1]] * len(streams)
        self.steps = len(bits) - 1
        self.done = 0

    def hold(self, *others):
        self.groups = [
            [(kept, after(arrived, *others), first, rows) for kept, arrived, first, rows in group]
            for group in self.groups
        ]

    def advance(self):
        moved, bits, places = [], [], []
        me = lax.axis_index("batch")
        for index, left in enumerate(self.bits):
            bit = left[::-1][index % len(left)]
            axis = left.index(bit)
            moved.append(bit)
            places.append(((me & bit) > 0).astype(jnp.int32))
            bits.append(((1 << axis, 1 << (len(left) - 1 - axis)),))
        sends, keeps = stage(jnp.stack(places), self.groups, bits, 1)
        self.groups = [
            [(keep, flip(send, "batch", bit), 0, keep.shape[2])]
            for keep, send, bit in zip(keeps, sends, moved)
        ]
        self.bits = [[item for item in left if item != bit] for left, bit in zip(self.bits, moved)]
        self.done += 1
        return sends

    def total(self):
        return [(kept + arrived).reshape(kept.shape[-2:]) for ((kept, arrived, _, _),) in self.groups]


def pack_kernel(tiles_rows, keep_a, come_a, keep_b, come_b, out_ref):
    groups, _, wide = out_ref.shape
    cols = wide // 2
    rows = tiles_rows // groups
    first = keep_a[...] + come_a[...]
    second = keep_b[...] + come_b[...]
    for group in range(groups):
        here = slice(group * cols, (group + 1) * cols)
        out_ref[group, :, :cols] = first[:, here]
        for part in range(groups):
            out_ref[group, part * rows : (part + 1) * rows, cols:] = second[
                group * rows : (group + 1) * rows, part * cols : (part + 1) * cols
            ]
        out_ref[group, tiles_rows:, cols:] = second[tiles_rows:, here]


def pack(stream_a, stream_b, tiles_rows, groups):
    (keep_a, come_a), (keep_b, come_b) = stream_a, stream_b
    rows, dim = keep_a.shape[-2:]
    flat = lambda item: item.reshape(rows, dim)
    shape = (groups, rows, 2 * dim // groups)
    if tiles_rows // groups % 16 == 0:
        return pl.pallas_call(
            functools.partial(pack_kernel, tiles_rows),
            out_shape=jax.ShapeDtypeStruct(shape, BF),
            compiler_params=pltpu.CompilerParams(vmem_limit_bytes=VMEM_BYTES),
            name="pack_places",
        )(flat(keep_a), flat(come_a), flat(keep_b), flat(come_b))
    first = flat(keep_a + come_a).reshape(rows, groups, -1).transpose(1, 0, 2)
    second = flat(keep_b + come_b)
    out = second[:tiles_rows].reshape(groups, -1, groups, dim // groups).transpose(0, 2, 1, 3)
    out = out.reshape(groups, tiles_rows, -1)
    last = second[tiles_rows:].reshape(-1, groups, dim // groups).transpose(1, 0, 2)
    return jnp.concatenate([first, jnp.concatenate([out, last], axis=1)], axis=2)


def columns_kernel(keep_a, come_a, keep_b, come_b, out_ref):
    groups, rows, cols = out_ref.shape
    half = keep_a.shape[0]
    first = keep_a[...] + come_a[...]
    second = keep_b[...] + come_b[...]
    for group in range(groups):
        here = slice(group * cols, (group + 1) * cols)
        out_ref[group, :half, :] = first[:, here]
        out_ref[group, half:, :] = second[:, here]


def pack_columns(streams, groups):
    rows, dim = streams[0][0].shape[-2:]
    pieces = [item.reshape(rows, dim) for keep, come in streams for item in (keep, come)]
    if rows % 16:
        total = jnp.concatenate([pieces[0] + pieces[1], pieces[2] + pieces[3]], axis=0)
        return total.reshape(2 * rows, groups, -1).transpose(1, 0, 2)
    return pl.pallas_call(
        columns_kernel,
        out_shape=jax.ShapeDtypeStruct((groups, 2 * rows, dim // groups), BF),
        compiler_params=pltpu.CompilerParams(vmem_limit_bytes=VMEM_BYTES),
        name="pack_columns",
    )(*pieces)


def split_dot(dot, left, right):
    return dot(left[0], right[0]) + (dot(left[0], right[1]) + dot(left[1], right[0]))


def embed_kernel(sum_ref, more_ref, count_ref, proj_ref, pooled_ref, emb_ref, inverse_ref):
    pooled = (sum_ref[...] + more_ref[...]) / count_ref[...]
    high, low = split_bf(pooled)
    raw = dot_nn(high, proj_ref[...]) + dot_nn(low, proj_ref[...])
    inverse = lax.rsqrt(jnp.sum(raw * raw, axis=-1, keepdims=True) + EPS)
    pooled_ref[...] = pooled
    emb_ref[...] = raw * inverse
    inverse_ref[...] = jnp.broadcast_to(inverse, inverse_ref.shape)


def embed(sums, more, counts, w_proj):
    own, dim = sums.shape
    shapes = ((own, dim), (own, dim), (own, LANES))
    return pl.pallas_call(
        embed_kernel,
        out_shape=[jax.ShapeDtypeStruct(shape, F32) for shape in shapes],
        compiler_params=pltpu.CompilerParams(vmem_limit_bytes=VMEM_BYTES),
        name="embed",
    )(sums, more, counts, w_proj)


def contrast_kernel(
    place_ref,
    own_ref,
    x_ref,
    y_ref,
    xy_ref,
    other_ref,
    inverse_ref,
    partner_ref,
    count_ref,
    proj_ref,
    loss_ref,
    graw_ref,
    pool_ref,
    all_ref,
    logit_ref,
):
    own, dim = own_ref.shape
    total = all_ref.shape[0]
    me = place_ref[0]
    rows_of = lambda place: pl.ds(pl.multiple_of(place * own, own), own)
    for step, ref in enumerate((own_ref, x_ref, y_ref, xy_ref)):
        place = jnp.bitwise_xor(me, 2 * step)
        all_ref[rows_of(place), :] = ref[...]
        all_ref[rows_of(jnp.bitwise_xor(place, 1)), :] = other_ref[step]
    everyone = split_bf(all_ref[...])
    logits = SHARPNESS * split_dot(dot_nt, everyone, everyone)
    row = lax.broadcasted_iota(jnp.int32, (total, total), 0)
    column = lax.broadcasted_iota(jnp.int32, (total, total), 1)
    logits = jnp.where(row == column, NEGATIVE, logits)
    logit_ref[...] = logits
    peak = jnp.max(logits, axis=0, keepdims=True)
    lse_all = peak + jnp.log(jnp.sum(jnp.exp(logits - peak), axis=0, keepdims=True))
    mine = logit_ref[rows_of(me), :]
    peak = jnp.max(mine, axis=1, keepdims=True)
    lse_own = peak + jnp.log(jnp.sum(jnp.exp(mine - peak), axis=1, keepdims=True))
    target = (lax.broadcasted_iota(jnp.int32, (own, total), 1) == partner_ref[...]).astype(F32)
    loss = lse_own - jnp.sum(jnp.where(target > 0, mine, 0.0), axis=1, keepdims=True)
    loss_ref[...] = jnp.broadcast_to(loss, loss_ref.shape)
    both = SHARPNESS * (jnp.exp(mine - lse_own) + jnp.exp(mine - lse_all) - 2.0 * target)
    grad = split_dot(dot_nn, split_bf(both), everyone)
    emb = own_ref[...]
    grad = inverse_ref[:, :1] * (grad - emb * jnp.sum(emb * grad, axis=1, keepdims=True))
    graw_ref[...] = grad
    high, low = split_bf(grad)
    pool_ref[...] = (dot_nt(high, proj_ref[...]) + dot_nt(low, proj_ref[...])) / count_ref[...]


def contrast_near(embedded, inverse, partner, counts, w_proj):
    own, dim = embedded.shape
    total = own * lax.axis_size("batch")
    parts = [embedded] + [flip(embedded, "batch", bits) for bits in (2, 4, 6)]
    other = flip(jnp.stack(parts), "batch", 1)
    me = lax.axis_index("batch").astype(jnp.int32).reshape(1)
    constants = (*parts, other, inverse, partner.reshape(own, 1), counts, w_proj)
    loss, graw, pool = pl.pallas_call(
        contrast_kernel,
        grid_spec=pltpu.PrefetchScalarGridSpec(
            num_scalar_prefetch=1,
            grid=(1,),
            in_specs=[full(item.shape) for item in constants],
            out_specs=[full((own, LANES)), full((own, dim)), full((own, dim))],
            scratch_shapes=[pltpu.VMEM((total, dim), F32), pltpu.VMEM((total, total), F32)],
        ),
        out_shape=[
            jax.ShapeDtypeStruct((own, LANES), F32),
            jax.ShapeDtypeStruct((own, dim), F32),
            jax.ShapeDtypeStruct((own, dim), F32),
        ],
        compiler_params=params(),
        name="contrast",
    )(me, *constants)
    return loss[:, 0], graw, pool


def finish_kernel(count, width, *refs):
    total = sum(ref[...].astype(F32) for ref in refs[:-count])
    for index, ref in enumerate(refs[-count:]):
        ref[...] = total[index * width : (index + 1) * width, :].T


def finish(pieces, count, width):
    cols = pieces[0].shape[1]
    return pl.pallas_call(
        functools.partial(finish_kernel, count, width),
        out_shape=[jax.ShapeDtypeStruct((cols, width), F32)] * count,
        compiler_params=pltpu.CompilerParams(vmem_limit_bytes=VMEM_BYTES),
        name="finish",
    )(*pieces)


def contrast(embedded, inv_norm, w_proj, partner):
    proj = w_proj.astype(F32)
    everyone = gather_batch(embedded)
    own_count = embedded.shape[0]
    total = everyone.shape[0]
    own_index = lax.axis_index("batch") * own_count + jnp.arange(own_count, dtype=jnp.int32)
    columns = jnp.arange(total, dtype=jnp.int32)

    def lse_of(rows, index):
        logits = SHARPNESS * jnp.einsum("nd,md->nm", rows, everyone, precision=HIGHEST)
        logits = jnp.where(columns[None, :] == index[:, None], NEGATIVE, logits)
        peak = jnp.max(logits, axis=-1, keepdims=True)
        return peak[:, 0] + jnp.log(jnp.sum(jnp.exp(logits - peak), axis=-1))

    if total <= 1024:
        lse_all = lse_of(everyone, columns)
    else:
        lse_all = lax.map(
            lambda pieces: lse_of(pieces[0], pieces[1]),
            (everyone.reshape(-1, 512, everyone.shape[1]), columns.reshape(-1, 512)),
        ).reshape(-1)
    logits = SHARPNESS * jnp.einsum("nd,md->nm", embedded, everyone, precision=HIGHEST)
    is_self = columns[None, :] == own_index[:, None]
    logits = jnp.where(is_self, NEGATIVE, logits)
    peak = jnp.max(logits, axis=-1, keepdims=True)
    lse_own = peak[:, 0] + jnp.log(jnp.sum(jnp.exp(logits - peak), axis=-1))
    is_target = columns[None, :] == partner[:, None]
    picked = jnp.sum(jnp.where(is_target, logits, 0.0), axis=-1)
    loss = lse_own - picked
    both = SHARPNESS * (
        jnp.exp(logits - lse_own[:, None])
        + jnp.exp(logits - lse_all[None, :])
        - 2.0 * is_target.astype(F32)
    )
    grad_emb = jnp.dot(both, everyone, precision=HIGHEST)
    grad_raw = inv_norm * (
        grad_emb - embedded * jnp.sum(embedded * grad_emb, axis=-1, keepdims=True)
    )
    grad_pooled = jnp.einsum("ne,de->nd", grad_raw, proj, precision=HIGHEST)
    return loss, grad_raw, grad_pooled


def shards(
    tokens,
    norm1_gain,
    w_query,
    w_key,
    w_value,
    rel_bias,
    w_output,
    norm2_gain,
    w_in,
    w_out,
    final_gain,
    w_proj,
    lengths,
    partner,
    cotangent,
):
    rows, size, dim = tokens.shape
    slots = lengths.shape[1]
    toks = rows * size
    seq_count = lax.axis_size("seq")
    seq_place = lax.axis_index("seq")
    place = seq_place.astype(jnp.int32).reshape(1)
    pairs = [(i, i ^ 1) for i in range(seq_count)]
    across = [(i, i - 1 if i % 2 == 0 else i + 1) for i in range(1, seq_count - 1)]
    gains = jnp.stack([norm1_gain, norm2_gain, final_gain])

    x_pair = lax.ppermute(tokens, "seq", pairs)
    x_across = lax.ppermute(tokens, "seq", across)
    bias = bias_tables(rel_bias, size)
    own = own_projections(tokens, norm1_gain.reshape(1, dim), (w_query, w_key, w_value))
    block, partial, edges, p, att, pre, after_attn, n2 = forward(
        lengths,
        place,
        tokens,
        x_pair,
        x_across,
        own,
        gains,
        (w_key, w_value, w_output, w_in, w_out),
        bias,
    )
    counts = lengths.astype(F32).reshape(rows * slots, 1)
    partial = partial.reshape(rows * slots, dim)
    seq_bits = bit_places("seq")
    for bit in seq_bits[:-1]:
        partial = partial + flip(partial, "seq", bit)
    pooled, embedded, inverse = embed(partial, flip(partial, "seq", seq_bits[-1]), counts, w_proj)
    if lax.axis_size("batch") == 8:
        loss, grad_raw, pool_grad = contrast_near(embedded, inverse, partner, counts, w_proj)
    else:
        loss, grad_raw, grad_pooled = contrast(embedded, inverse[:, :1], w_proj, partner)
        pool_grad = grad_pooled / counts
    pool_grad = pool_grad.reshape(rows, slots, dim)
    batch_count = lax.axis_size("batch")
    place = jnp.stack([seq_place, lax.axis_index("batch") % 2]).astype(jnp.int32)

    back, gains_a, mine, theirs = feed_back(
        batch_count,
        lengths,
        place,
        block,
        after_attn,
        cotangent,
        att,
        n2,
        pre,
        pool_grad,
        grad_raw,
        pooled,
        gains,
        (w_output, w_in, w_out),
    )
    hidden = w_in.shape[1]
    width = dim // batch_count
    tiles = hidden // dim
    wide = hidden // batch_count
    feed_sum = BatchSum(
        mine,
        theirs,
        (((0, 0, wide), (2, 0, width)), ((1, 0, tiles * width), (2, width, width))),
    )
    segments = [(0, 1), (1, rows - 2), (rows - 1, 1)] if rows > 2 else [(0, rows)]
    halves, from_pair, from_across = [], [], []
    earlier = ()
    for first, count in segments:
        if halves and feed_sum.done < feed_sum.steps:
            place = after(place, *feed_sum.advance())
        halves.append(
            attend_back(
                first,
                count,
                (0, rows - 1) if first + count < rows else (first, count),
                earlier,
                lengths,
                place,
                tokens,
                x_pair,
                x_across,
                own,
                edges,
                p,
                back,
                gains,
                (w_query, w_key, w_value),
            )
        )
        feed_sum.hold(halves[-1][5])
        earlier = tuple(halves[-1][:4])
        if first + count >= rows - 1:
            from_pair.append(lax.ppermute(halves[-1][2], "seq", pairs))
            from_across.append(lax.ppermute(halves[-1][3], "seq", across))
            earlier = earlier[:2]
    grads, part = earlier
    while feed_sum.done < feed_sum.steps:
        place = after(place, *feed_sum.advance())

    feed_part = pack(
        *[(group[0][0], group[0][1]) for group in feed_sum.groups], tiles * width, seq_count
    )
    grad_rel = bias_grad([item[4] for item in halves], rel_bias.shape[0])
    gain1_grad = sum(item[5][0] for item in halves)
    small = jnp.concatenate([gain1_grad, gains_a[1], gains_a[0], grad_rel.reshape(-1)])
    small = jnp.pad(small, (0, -small.shape[0] % 1024)).reshape(-1, 128)
    batch_bits = bit_places("batch")
    arrived = flip(small, "seq", seq_bits[0])
    place = after(place, feed_part, small, *from_pair, *from_across)
    attend_mine, attend_theirs = attend_grad(batch_count, place, own, edges, grads)
    feed_done = lax.psum_scatter(feed_part, "seq", scatter_dimension=0, tiled=True)[0]
    half = 3 * width // 2
    attend_sum = BatchSum([attend_mine], [attend_theirs], (((0, 0, half),), ((0, half, 3 * width - half),)))
    small = after(small, attend_mine) + arrived
    arrived = flip(small, "batch", batch_bits[0])
    attend_sum.hold(arrived)
    for bit in batch_bits[1:]:
        sends = attend_sum.advance()
        small = after(small, *sends) + arrived
        arrived = flip(small, "batch", bit)
        attend_sum.hold(arrived)
    attend_parts = pack_columns([group[0][:2] for group in attend_sum.groups], seq_count)
    small = after(small, attend_parts) + arrived
    came = [lax.dynamic_index_in_dim(attend_parts, seq_place, 0, keepdims=False)]
    for distance in range(1, seq_count):
        route = [(i, (i + distance) % seq_count) for i in range(seq_count)]
        target = (seq_place + distance) % seq_count
        send = lax.dynamic_index_in_dim(attend_parts, target, 0, keepdims=False)
        came.append(lax.ppermute(send, "seq", route))
    sent = came[0]
    for bit in seq_bits[1:]:
        small = small + flip(small, "seq", bit)
    small = small.reshape(-1)
    gain_sums = [small[i * dim : (i + 1) * dim] for i in range(3)]
    rel_sum = small[3 * dim : 3 * dim + rel_bias.size].reshape(rel_bias.shape)

    grad_tokens = (
        after(part, sent).astype(F32)
        + jnp.concatenate(from_pair, axis=0).astype(F32)
        + jnp.concatenate(from_across, axis=0).astype(F32)
    )
    turn = lambda array: array.T.astype(F32)
    cols = dim // seq_count
    s_in = turn(feed_done[:wide, :cols])
    s_output = turn(feed_done[wide:, :cols])
    s_out = feed_done[:-width, cols:].reshape(seq_count, width, cols)
    s_out = s_out.transpose(0, 2, 1).reshape(dim, width).astype(F32)
    s_proj = turn(feed_done[-width:, cols:])
    came[0] = after(came[0], s_in, s_output, s_out, s_proj, grad_tokens)
    s_attend = finish(came, 3, width)
    return (
        block,
        embedded,
        loss,
        grad_tokens,
        gain_sums[0],
        s_attend[0],
        s_attend[1],
        s_attend[2],
        rel_sum,
        s_output,
        gain_sums[1],
        s_in,
        s_out,
        gain_sums[2],
        s_proj,
    )


def solution(mesh):
    tok = P("batch", "seq", None)
    mat = P("seq", "batch")
    return jax.shard_map(
        shards,
        mesh=mesh,
        in_specs=(tok,) + (P(),) * 11 + (P("batch", None), P("batch"), tok),
        out_specs=(
            tok,
            P("batch", None),
            P("batch"),
            tok,
            P(),
            mat,
            mat,
            mat,
            P(),
            mat,
            P(),
            mat,
            mat,
            P(),
            mat,
        ),
        check_vma=False,
    )
```

```python
import functools

import jax
import jax.numpy as jnp
from jax import lax
from jax.experimental import pallas as pl
from jax.experimental.pallas import tpu as pltpu
from jax.sharding import PartitionSpec as P

EPS = 1e-06
NEGATIVE = -1e30
SHARPNESS = 50.0
THRESHOLDS = (12, 16, 23, 32, 46, 64, 91)
HIGHEST = lax.Precision.HIGHEST
BF = jnp.bfloat16
F32 = jnp.float32
VMEM_BYTES = 60 * 1024 * 1024
GELU_A = 0.7978845608028654
GELU_B = 0.044715
LANES = 128


def dot_nn(left, right):
    return lax.dot_general(left, right, (((1,), (0,)), ((), ())), preferred_element_type=F32)


def dot_nt(left, right):
    return lax.dot_general(left, right, (((1,), (1,)), ((), ())), preferred_element_type=F32)


def dot_tn(left, right):
    return lax.dot_general(left, right, (((0,), (0,)), ((), ())), preferred_element_type=F32)


def rms_scale(values):
    return lax.rsqrt(jnp.mean(values * values, axis=-1, keepdims=True) + EPS)


def rms_back(values, scale, grad_normed):
    inner = jnp.mean(grad_normed * values, axis=-1, keepdims=True)
    return scale * (grad_normed - values * (scale * scale * inner))


def split_bf(values):
    high = values.astype(BF)
    return high, (values - high.astype(F32)).astype(BF)


def bucket_of(offset):
    distance = jnp.abs(offset)
    beyond = jnp.zeros_like(distance)
    for threshold in THRESHOLDS:
        beyond = beyond + (distance >= threshold).astype(jnp.int32)
    within = jnp.where(distance < 8, distance, 8 + beyond)
    return within + 16 * (offset > 0).astype(jnp.int32)


def wrapped_offsets(shape, axis, size):
    place = lax.broadcasted_iota(jnp.int32, shape, axis)
    return jnp.where(place < size, place, place - 2 * size)


def full(shape):
    return pl.BlockSpec(shape, lambda *_: (0,) * len(shape), pipeline_mode=pl.Buffered(1))


def row_spec(shape, first=0):
    return pl.BlockSpec(
        (1,) + tuple(shape), lambda step, *_: (step + first,) + (0,) * len(shape)
    )


def cost(products, moved, exps=0):
    return pl.CostEstimate(flops=2 * products, bytes_accessed=moved, transcendentals=exps)


def params(limit=VMEM_BYTES):
    return pltpu.CompilerParams(
        vmem_limit_bytes=limit, dimension_semantics=("arbitrary",)
    )


def bias_kernel(size, table_ref, out_ref):
    buckets, heads = table_ref.shape
    hot = (
        lax.broadcasted_iota(jnp.int32, (buckets, 2 * size), 0)
        == bucket_of(-wrapped_offsets((buckets, 2 * size), 1, size))
    ).astype(BF)
    by_offset = dot_tn(table_ref[...], hot)
    for head in range(heads):
        line = jnp.broadcast_to(by_offset[head : head + 1, :], (size, 2 * size))
        out_ref[head] = pltpu.roll(line, 0, 1, stride=1, stride_axis=0).astype(BF)


def bias_tables(rel_bias, size):
    heads = rel_bias.shape[1]
    return pl.pallas_call(
        functools.partial(bias_kernel, size),
        out_shape=jax.ShapeDtypeStruct((heads, size, 2 * size), BF),
        compiler_params=pltpu.CompilerParams(vmem_limit_bytes=VMEM_BYTES),
    )(rel_bias)


def fold_offsets(rows):
    count, width = rows.shape
    while count > 8:
        count = count // 2
        rows = rows[:count] + pltpu.roll(rows[count:], width - count, 1)
    return rows


def bias_grad_kernel(heads, *refs):
    acc_refs, out_ref = refs[:-1], refs[-1]
    rows = sum(acc_ref[...] for acc_ref in acc_refs)
    width = rows.shape[1]
    buckets = out_ref.shape[1]
    place = lax.broadcasted_iota(jnp.int32, rows.shape, 0)
    for bit in (4, 2, 1):
        rows = jnp.where((place & bit) > 0, pltpu.roll(rows, width - bit, 1), rows)
    hot = (
        lax.broadcasted_iota(jnp.int32, (width, buckets), 1)
        == bucket_of(-wrapped_offsets((width, buckets), 0, width // 2))
    ).astype(BF)
    first, rest = split_bf(rows)
    second, third = split_bf(rows - first.astype(F32))
    table = dot_nn(first, hot) + dot_nn(second, hot) + dot_nn(third, hot)
    for head in range(heads):
        out_ref[head : head + 1, :] = jnp.sum(table[8 * head : 8 * head + 8], axis=0, keepdims=True)


def bias_grad(accs, buckets):
    heads, _, width = accs[0].shape
    out = pl.pallas_call(
        functools.partial(bias_grad_kernel, heads),
        out_shape=jax.ShapeDtypeStruct((heads, buckets), F32),
        compiler_params=pltpu.CompilerParams(vmem_limit_bytes=VMEM_BYTES),
        name="bias_grad",
    )(*[acc.reshape(heads * 8, width) for acc in accs])
    return out.T


class Row:
    def __init__(self, lengths_ref, place_ref, row, size):
        slots = lengths_ref.shape[1]
        base = place_ref[0] * size
        pos = base + lax.broadcasted_iota(jnp.int32, (1, size), 1)
        zero = jnp.int32(0)
        before, first, last, beyond = zero, zero, zero, zero
        own = jnp.zeros((1, size), jnp.int32)
        low = jnp.zeros((1, size), jnp.int32)
        high = jnp.zeros((1, size), jnp.int32)
        end = zero
        passed = lambda end, place: (end <= place).astype(jnp.int32)
        for slot in range(slots):
            end = end + lengths_ref[row, slot]
            before += passed(end, base - 1)
            first += passed(end, base)
            last += passed(end, base + size - 1)
            beyond += passed(end, base + size)
            own += passed(end, pos)
            low += passed(end, pos - size)
            high += passed(end, pos + size)
        before = jnp.where(base == 0, -1, before).astype(F32)
        low = jnp.where(pos < size, -1, low).astype(F32)
        own = own.astype(F32)
        col_own, col_low, col_high = (
            jnp.broadcast_to(item, (LANES, size)).T for item in (own, low, high.astype(F32))
        )
        self.in_low = col_own == before
        self.in_high = col_own == beyond.astype(F32)
        self.slot_low = col_low == first.astype(F32)
        self.slot_high = col_high == last.astype(F32)
        key = lax.broadcasted_iota(jnp.int32, (size, size), 0)
        query = lax.broadcasted_iota(jnp.int32, (size, size), 1)
        wide = lambda item: jnp.concatenate([item] * (size // LANES), axis=1)
        self.own = wide(col_own) == own
        self.alt = jnp.where(key > query, wide(col_low), jnp.where(key < query, wide(col_high), -2.0)) == own


def where_tiles(mask, left, right):
    lanes = mask.shape[1]
    return jnp.concatenate(
        [
            jnp.where(mask, left[:, start : start + lanes], right[:, start : start + lanes])
            for start in range(0, left.shape[1], lanes)
        ],
        axis=1,
    )


def store_group_masks(row, ref):
    _, _, size, lanes = ref.shape
    first = lax.broadcasted_iota(jnp.int32, (1, lanes), 1) < lanes // 2
    low = row.in_low.astype(F32)
    high = row.in_high.astype(F32)
    for part, group in enumerate((low, 1.0 - low - high, high)):
        ref[0, part] = jnp.where(first, group, 0.0).astype(BF)
        ref[1, part] = jnp.where(first, 0.0, group).astype(BF)


def by_group(pair, ref, half):
    return jnp.concatenate([pair * ref[half, part] for part in range(3)], axis=1)


def fold_rows(row, first, wide):
    lanes = wide[0].shape[1] // 3
    parts = [
        jnp.where(first, wide[0][:, here], wide[1][:, here])
        for here in (slice(part * lanes, (part + 1) * lanes) for part in range(3))
    ]
    return jnp.where(row.in_low, parts[0], jnp.where(row.in_high, parts[2], parts[1]))


def own_kernel(x_ref, gain1_ref, wq_ref, wk_ref, wv_ref, out_ref):
    x = x_ref[0].astype(F32)
    out_ref[0, 3] = (x * rms_scale(x) * gain1_ref[...].astype(F32)).astype(BF)
    for index, weight_ref in enumerate((wq_ref, wk_ref, wv_ref)):
        out_ref[0, index] = dot_nn(out_ref[0, 3], weight_ref[...]).astype(BF)


def own_projections(tokens, gain1, weights):
    rows, size, dim = tokens.shape
    constants = (gain1,) + tuple(weights)
    return pl.pallas_call(
        own_kernel,
        grid=(rows,),
        in_specs=[row_spec((size, dim))] + [full(item.shape) for item in constants],
        out_specs=row_spec((4, size, dim)),
        out_shape=jax.ShapeDtypeStruct((rows, 4, size, dim), BF),
        compiler_params=params(),
        cost_estimate=cost(3 * rows * size * dim * dim, rows * size * dim * 10),
        name="own_projections",
    )(tokens, *constants)


def row_sentences(lengths_ref, place_ref, row, size):
    where_pos = place_ref[0] * size + lax.broadcasted_iota(jnp.int32, (1, size), 1)
    found = jnp.zeros((1, size), jnp.int32)
    end = jnp.int32(0)
    for slot in range(lengths_ref.shape[1]):
        end = end + lengths_ref[row, slot]
        found = found + (end <= where_pos).astype(jnp.int32)
    return found


def forward_kernel(
    rows,
    lengths_ref,
    place_ref,
    x_ref,
    pair_ref,
    across_ref,
    own_ref,
    gains_ref,
    wk_ref,
    wv_ref,
    bias_ref,
    win_ref,
    wout_ref,
    wo_hbm,
    block_ref,
    pooled_ref,
    edge_ref,
    p_ref,
    att_ref,
    pre_ref,
    after_hbm,
    n2_hbm,
    mask_ref,
    group_ref,
    att_all,
    after_all,
    after_low,
    n2_all,
    total_ref,
    wo_ref,
    sems,
):
    size, dim = x_ref.shape[1:]
    heads = bias_ref.shape[0]
    pairs = heads // 2
    lanes = dim // pairs
    slots = pooled_ref.shape[1]
    step = pl.program_id(0)
    copies = [
        pltpu.make_async_copy(after_low, after_hbm, sems.at[0]),
        pltpu.make_async_copy(n2_all, n2_hbm, sems.at[1]),
    ]
    wo_copy = pltpu.make_async_copy(wo_hbm, wo_ref, sems.at[2])

    @pl.when(step == 0)
    def _():
        wo_copy.start()

    @pl.when(step < rows)
    def _():
        here = pl.ds(pl.multiple_of(step * size, size), size)
        row = Row(lengths_ref, place_ref, step, size)
        mask_ref[0] = jnp.where(row.own, 0.0, NEGATIVE).astype(BF)
        mask_ref[1] = jnp.where(row.alt, 0.0, NEGATIVE).astype(BF)
        store_group_masks(row, group_ref)
        gain1 = gains_ref[0:1, :].astype(F32)
        after_all[here, :] = x_ref[0].astype(F32)
        own = own_ref[0, 3].astype(F32)
        sides = by_side(place_ref, pair_ref[0], across_ref[0])
        for part, (source, slot) in enumerate(zip(sides, (row.slot_low, row.slot_high))):
            x = source.astype(F32)
            edge_ref[0, 4 + part] = where_tiles(slot, x * rms_scale(x) * gain1, own).astype(BF)
        edges = edge_ref[0, 4:].reshape(2 * size, dim)
        first_half = lax.broadcasted_iota(jnp.int32, (1, lanes), 1) < lanes // 2
        for index, weight_ref in enumerate((wk_ref, wv_ref)):
            value = dot_nn(edges, weight_ref[...]).astype(BF)
            edge_ref[0, 2 * index : 2 * index + 2] = value.reshape(2, size, dim)
        for pair in range(pairs):
            cols = slice(pair * lanes, (pair + 1) * lanes)
            keys, values = key_groups(own_ref, edge_ref, cols)
            halves, from_pair, from_across = [], [], []
            for half in range(2):
                head = 2 * pair + half
                scores = dot_nt(keys, by_group(own_ref[0, 0, :, cols], group_ref, half))
                bias = jnp.maximum(
                    bias_ref[head, :, :size] + mask_ref[0], bias_ref[head, :, size:] + mask_ref[1]
                )
                scores = scores + bias.astype(F32)
                peak = jnp.max(scores, axis=0, keepdims=True)
                powers = jnp.exp(scores - peak)
                inverse = 1.0 / jnp.sum(powers, axis=0, keepdims=True)
                probs = (powers * inverse).astype(BF)
                p_ref[0, head] = probs
                halves.append(dot_tn(probs, values))
            mixed = fold_rows(row, first_half, halves).astype(BF)
            att_ref[0, :, cols] = mixed
            att_all[here, cols] = mixed

    @pl.when(step == rows)
    def _():
        wo_copy.wait()
        after = after_all[...] + dot_nn(att_all[...], wo_ref[...])
        after_low[...] = after.astype(BF)
        total_ref[...] = after
        n2_all[...] = (after * rms_scale(after) * gains_ref[1:2, :].astype(F32)).astype(BF)
        for copy in copies:
            copy.start()

    @pl.when(step >= rows)
    def _():
        pre = dot_nn(n2_all[...], win_ref[...])
        square = pre * pre
        gate = 0.5 + 0.5 * jnp.tanh(pre * (GELU_A + (GELU_A * GELU_B) * square))
        pre_ref[...] = pre.astype(BF)
        total_ref[...] += dot_nn((pre * gate).astype(BF), wout_ref[...])

    @pl.when(step == pl.num_programs(0) - 1)
    def _():
        gainf = gains_ref[2:3, :].astype(F32)
        for row in range(rows):
            here = slice(row * size, (row + 1) * size)
            block = total_ref[here, :].astype(BF)
            block_ref[row] = block
            out = block.astype(F32)
            final = out * rms_scale(out) * gainf
            found = row_sentences(lengths_ref, place_ref, row, size)
            member = (lax.broadcasted_iota(jnp.int32, (slots, size), 0) == found).astype(BF)
            high_part, low_part = split_bf(final)
            pooled_ref[row] = dot_nn(member, high_part) + dot_nn(member, low_part)
        for copy in copies:
            copy.wait()


def by_side(place_ref, pair, across):
    odd = place_ref[0] % 2 == 1
    return jnp.where(odd, pair, across), jnp.where(odd, across, pair)


def key_groups(own_ref, edge_ref, cols):
    return [
        jnp.concatenate(
            [edge_ref[0, 2 * index, :, cols], own_ref[0, 1 + index, :, cols], edge_ref[0, 2 * index + 1, :, cols]],
            axis=1,
        )
        for index in range(2)
    ]


def forward(lengths, place, tokens, low, high, own, gains, weights, bias):
    rows, size, dim = tokens.shape
    heads = bias.shape[0]
    slots = lengths.shape[1]
    wk, wv, wo, win, wout = weights
    hidden = win.shape[1]
    tiles = hidden // dim
    toks = rows * size
    per_row = lambda shape: pl.BlockSpec(
        (1,) + shape, lambda step, *_: (jnp.minimum(step, rows - 1),) + (0,) * len(shape)
    )
    tile = lambda step: jnp.maximum(step - rows, 0)
    constants = (gains, wk, wv, bias)
    anywhere = pl.BlockSpec(memory_space=pl.ANY)
    out_of = lambda shape, kind=BF: jax.ShapeDtypeStruct(shape, kind)
    return pl.pallas_call(
        functools.partial(forward_kernel, rows),
        grid_spec=pltpu.PrefetchScalarGridSpec(
            num_scalar_prefetch=2,
            grid=(rows + tiles,),
            in_specs=[per_row((size, dim))] * 3
            + [per_row((4, size, dim))]
            + [full(item.shape) for item in constants]
            + [
                pl.BlockSpec((dim, dim), lambda step, *_: (0, tile(step))),
                pl.BlockSpec((dim, dim), lambda step, *_: (tile(step), 0)),
                anywhere,
            ],
            out_specs=[
                full((rows, size, dim)),
                full((rows, slots, dim)),
                per_row((6, size, dim)),
                per_row((heads, size, size)),
                per_row((size, dim)),
                pl.BlockSpec((toks, dim), lambda step, *_: (0, tile(step))),
                anywhere,
                anywhere,
            ],
            scratch_shapes=[
                pltpu.VMEM((2, size, size), BF),
                pltpu.VMEM((2, 3, size, 2 * dim // heads), BF),
                pltpu.VMEM((toks, dim), BF),
                pltpu.VMEM((toks, dim), F32),
                pltpu.VMEM((toks, dim), BF),
                pltpu.VMEM((toks, dim), BF),
                pltpu.VMEM((toks, dim), F32),
                pltpu.VMEM((dim, dim), BF),
                pltpu.SemaphoreType.DMA((3,)),
            ],
        ),
        out_shape=[
            out_of((rows, size, dim)),
            out_of((rows, slots, dim), F32),
            out_of((rows, 6, size, dim)),
            out_of((rows, heads, size, size)),
            out_of((rows, size, dim)),
            out_of((toks, hidden)),
            out_of((toks, dim)),
            out_of((toks, dim)),
        ],
        compiler_params=params(),
        cost_estimate=cost(
            toks * dim * (5 * dim + 2 * hidden + 36 * size),
            toks * (hidden * 4 + dim * 40),
            rows * heads * size * size,
        ),
        name="forward",
    )(lengths, place, tokens, low, high, own, *constants, win, wout, wo)


def store_split(core, value, refs, count, first=0):
    if len(refs) == 1:
        refs[0][first : first + value.shape[0], :] = value
        return
    groups = value.shape[0] // (2 * count)
    for group in range(groups):
        even = value[2 * group * count : (2 * group + 1) * count]
        odd = value[(2 * group + 1) * count : (2 * group + 2) * count]

        refs[0][group, first : first + count, :] = jnp.where(core == 0, even, odd)
        refs[1][group, first : first + count, :] = jnp.where(core == 0, odd, even)


def feed_back_kernel(
    rows,
    parts,
    lengths_ref,
    place_ref,
    block_ref,
    cot_ref,
    pool_ref,
    graw_ref,
    pooled_ref,
    gain_ref,
    pre_ref,
    win_ref,
    wout_ref,
    after_hbm,
    n2_hbm,
    att_hbm,
    wo_hbm,
    back_ref,
    gains_ref,
    *rest,
):
    split = len(rest) == 14
    per = 2 if split else 1
    in_refs, out_refs, small_refs = (rest[i * per : (i + 1) * per] for i in range(3))
    gout_ref, branch_ref, gn2_ref, after_ref, n2_ref, att_ref, wo_ref, sems = rest[3 * per :]
    _, size, dim = block_ref.shape
    toks = rows * size
    slots = pool_ref.shape[1]
    step = pl.program_id(0)
    tiles = pl.num_programs(0) - 1
    core = place_ref[1]
    copies = [
        pltpu.make_async_copy(n2_hbm, n2_ref, sems.at[0]),
        pltpu.make_async_copy(after_hbm, after_ref, sems.at[1]),
        pltpu.make_async_copy(att_hbm, att_ref, sems.at[2]),
        pltpu.make_async_copy(wo_hbm, wo_ref, sems.at[3]),
    ]

    @pl.when(step == 0)
    def _():
        for copy in copies:
            copy.start()
        gainf = gain_ref[2:3, :].astype(F32)
        gain_f = jnp.zeros((1, dim), F32)
        for row in range(rows):
            here = slice(row * size, (row + 1) * size)
            found = row_sentences(lengths_ref, place_ref, row, size)
            member = (lax.broadcasted_iota(jnp.int32, (slots, size), 0) == found).astype(BF)
            high_part, low_part = split_bf(pool_ref[row])
            g_final = dot_tn(member, high_part) + dot_tn(member, low_part)
            out = block_ref[row].astype(F32)
            scale = rms_scale(out)
            gain_f = gain_f + jnp.sum(g_final * out * scale, axis=0, keepdims=True)
            g_out = rms_back(out, scale, g_final * gainf) + cot_ref[row].astype(F32)
            gout_ref[here, :] = g_out
            branch_ref[here, :] = g_out.astype(BF)
        gains_ref[...] = jnp.zeros_like(gains_ref)
        gains_ref[0:1, :] = gain_f
        copies[0].wait()

    @pl.when(step < tiles)
    def _():
        g_hidden = dot_nt(branch_ref[...], wout_ref[...])
        pre = pre_ref[...].astype(F32)
        square = pre * pre
        gate = 0.5 + 0.5 * jnp.tanh(pre * (GELU_A + (GELU_A * GELU_B) * square))
        act = pre * gate
        value = dot_tn(branch_ref[...], act.astype(BF)).astype(BF)
        store_split(core, value, out_refs, dim // parts)
        slope = gate + act * (1.0 - gate) * (2 * GELU_A + (6 * GELU_A * GELU_B) * square)
        g_pre = (g_hidden * slope).astype(BF)
        value = dot_tn(g_pre, n2_ref[...]).astype(BF)
        store_split(core, value, in_refs, tiles * dim // parts)
        part = dot_nt(g_pre, win_ref[...])

        @pl.when(step == 0)
        def _():
            gn2_ref[...] = part

        @pl.when(step > 0)
        def _():
            gn2_ref[...] += part

    @pl.when(step == tiles)
    def _():
        for copy in copies[1:]:
            copy.wait()
        gain2 = gain_ref[1:2, :].astype(F32)
        gain_2 = jnp.zeros((1, dim), F32)
        for row in range(rows):
            here = slice(row * size, (row + 1) * size)
            after = after_ref[here, :].astype(F32)
            g_n2 = gn2_ref[here, :]
            scale = rms_scale(after)
            gain_2 = gain_2 + jnp.sum(g_n2 * after * scale, axis=0, keepdims=True)
            g_after = gout_ref[here, :] + rms_back(after, scale, g_n2 * gain2)
            back_ref[row, 1] = g_after.astype(BF)
            branch_ref[here, :] = g_after.astype(BF)
        gains_ref[1:2, :] = gain_2
        g_mix = dot_nt(branch_ref[...], wo_ref[...]).astype(BF)
        for row in range(rows):
            back_ref[row, 0] = g_mix[row * size : (row + 1) * size]
        value = dot_tn(branch_ref[...], att_ref[...].reshape(toks, dim)).astype(BF)
        store_split(core, value, small_refs, dim // parts)
        left_high, left_low = split_bf(jnp.where(place_ref[0] == 0, graw_ref[...], 0.0))
        right_high, right_low = split_bf(pooled_ref[...])
        value = dot_tn(left_high, right_high)
        value += dot_tn(left_high, right_low) + dot_tn(left_low, right_high)
        first = dim // parts if split else dim
        store_split(core, value.astype(BF), small_refs, dim // parts, first)


def feed_back(parts, lengths, place, block, after, cot, att, n2, pre, pool, graw, pooled, gains, weights):
    rows, size, dim = block.shape
    hidden = pre.shape[1]
    tiles = hidden // dim
    toks = rows * size
    wo, win, wout = weights
    split = (dim // parts) % 16 == 0 and dim % (2 * hidden // parts) == 0
    tile = lambda step: jnp.minimum(step, tiles - 1)
    if split:
        groups = parts // 2
        wide = hidden // parts
        inner = dim // (2 * wide)
        narrow = dim // parts
        in_specs = [pl.BlockSpec((inner, wide, dim), lambda step, *_: (tile(step), 0, 0))] * 2
        out_specs = [pl.BlockSpec((groups, narrow, dim), lambda step, *_: (0, tile(step), 0))] * 2
        small_specs = [full((groups, 2 * narrow, dim))] * 2
        shapes = [(groups, wide, dim)] * 2 + [(groups, tiles * narrow, dim)] * 2 + [(groups, 2 * narrow, dim)] * 2
    else:
        in_specs = [pl.BlockSpec((dim, dim), lambda step, *_: (tile(step), 0))]
        out_specs = [pl.BlockSpec((dim, dim), lambda step, *_: (tile(step), 0))]
        small_specs = [full((2 * dim, dim))]
        shapes = [(hidden, dim), (tiles * dim, dim), (2 * dim, dim)]
    constants = (block, cot, pool, graw, pooled, gains)
    outs = pl.pallas_call(
        functools.partial(feed_back_kernel, rows, parts),
        grid_spec=pltpu.PrefetchScalarGridSpec(
            num_scalar_prefetch=2,
            grid=(tiles + 1,),
            in_specs=[full(item.shape) for item in constants]
            + [
                pl.BlockSpec((toks, dim), lambda step, *_: (0, tile(step))),
                pl.BlockSpec((dim, dim), lambda step, *_: (0, tile(step))),
                pl.BlockSpec((dim, dim), lambda step, *_: (tile(step), 0)),
            ]
            + [pl.BlockSpec(memory_space=pl.ANY)] * 4,
            out_specs=[full((rows, 2, size, dim)), full((8, dim))]
            + in_specs
            + out_specs
            + small_specs,
            scratch_shapes=[
                pltpu.VMEM((toks, dim), F32),
                pltpu.VMEM((toks, dim), BF),
                pltpu.VMEM((toks, dim), F32),
                pltpu.VMEM((toks, dim), BF),
                pltpu.VMEM((toks, dim), BF),
                pltpu.VMEM((rows, size, dim), BF),
                pltpu.VMEM((dim, dim), BF),
                pltpu.SemaphoreType.DMA((4,)),
            ],
        ),
        out_shape=[
            jax.ShapeDtypeStruct((rows, 2, size, dim), BF),
            jax.ShapeDtypeStruct((8, dim), F32),
        ]
        + [jax.ShapeDtypeStruct(shape, BF) for shape in shapes],
        compiler_params=params(),
        cost_estimate=cost(
            toks * dim * (4 * hidden + 2 * dim), toks * (hidden * 4 + dim * 20) + 8 * hidden * dim
        ),
        name="feed_back",
    )(lengths, place, *constants, pre, win, wout, after, n2, att, wo)
    if split:
        mine, theirs = outs[2::2], outs[3::2]
    else:
        whole = [
            outs[2].reshape(parts, hidden // parts, dim),
            outs[3].reshape(tiles, parts, dim // parts, dim).transpose(1, 0, 2, 3),
            outs[4].reshape(2, parts, dim // parts, dim).transpose(1, 0, 2, 3),
        ]
        mine, theirs = split_core(whole)
    return outs[0], outs[1], mine, theirs


def split_core(blocks):
    core = (lax.axis_index("batch") % 2).astype(jnp.int32)
    pairs = [item.reshape((item.shape[0] // 2, 2, -1, item.shape[-1])) for item in blocks]
    pick = lambda item, place: lax.dynamic_index_in_dim(item, place, 1, keepdims=False)
    return [pick(item, core) for item in pairs], [pick(item, 1 - core) for item in pairs]


def attend_grad_kernel(parts, place_ref, n1_ref, own_ref, edge_hbm, n1_edge_hbm, *rest):
    refs, (edge_ref, n1_edge_ref, sems) = rest[:-3], rest[-3:]
    rows, _, size, dim = own_ref.shape
    step = pl.program_id(0)
    width = dim // parts if len(refs) == 2 else dim
    flat = lambda ref: ref[...].reshape(-1, dim)
    n1_copy = pltpu.make_async_copy(n1_edge_hbm.at[:, 4:6], n1_edge_ref, sems.at[0])
    copies = [
        pltpu.make_async_copy(
            edge_hbm.at[:, 3 + 2 * index : 5 + 2 * index], edge_ref.at[index], sems.at[1 + index]
        )
        for index in range(2)
    ]

    @pl.when(step == 0)
    def _():
        n1_copy.start()
        for copy in copies:
            copy.start()
        value = dot_tn(flat(own_ref), flat(n1_ref)).astype(BF)
        store_split(place_ref[1], value, refs, dim // parts, 0)
        n1_copy.wait()

    for index in range(2):

        @pl.when(step == 1 + index)
        def _():
            copies[index].wait()
            value = dot_tn(flat(own_ref), flat(n1_ref)) + dot_tn(flat(edge_ref.at[index]), flat(n1_edge_ref))
            store_split(place_ref[1], value.astype(BF), refs, dim // parts, (1 + index) * width)


def attend_grad(parts, place, own, edges, grads):
    rows, _, size, dim = own.shape
    narrow = dim // parts
    split = narrow % 16 == 0
    shape = (parts // 2, 3 * narrow, dim) if split else (3 * dim, dim)
    copies = 2 if split else 1
    outs = pl.pallas_call(
        functools.partial(attend_grad_kernel, parts),
        grid_spec=pltpu.PrefetchScalarGridSpec(
            num_scalar_prefetch=1,
            grid=(3,),
            in_specs=[
                pl.BlockSpec((rows, 1, size, dim), lambda step, *_: (0, 3, 0, 0)),
                pl.BlockSpec((rows, 1, size, dim), lambda step, *_: (0, step, 0, 0)),
                pl.BlockSpec(memory_space=pl.ANY),
                pl.BlockSpec(memory_space=pl.ANY),
            ],
            out_specs=[full(shape)] * copies,
            scratch_shapes=[
                pltpu.VMEM((2, rows, 2, size, dim), BF),
                pltpu.VMEM((rows, 2, size, dim), BF),
                pltpu.SemaphoreType.DMA((3,)),
            ],
        ),
        out_shape=[jax.ShapeDtypeStruct(shape, BF)] * copies,
        compiler_params=params(),
        cost_estimate=cost(rows * size * dim * dim * 7, rows * size * dim * 26),
        name="attend_grad",
    )(place, own, grads, grads, edges)
    if split:
        return outs[0], outs[1]
    mine, theirs = split_core([outs[0].reshape(3, parts, narrow, dim).transpose(1, 0, 2, 3)])
    return mine[0], theirs[0]


def attend_back_kernel(
    first,
    lengths_ref,
    place_ref,
    own_ref,
    pair_ref,
    across_ref,
    qkv_ref,
    edge_ref,
    p_ref,
    back_ref,
    gain_ref,
    wq_ref,
    wk_ref,
    wv_ref,
    *rest,
):
    grad_ref, part_ref, to_pair_ref, to_across_ref, offset_ref, gains_ref, mask_ref, group_ref, acc_ref = rest[-9:]
    size, dim = own_ref.shape[1:]
    heads = p_ref.shape[1]
    pairs = heads // 2
    lanes = dim // pairs
    step = pl.program_id(0)
    row = Row(lengths_ref, place_ref, step + first, size)
    mask_ref[...] = row.own.astype(F32)

    @pl.when(step == 0)
    def _():
        acc_ref[...] = jnp.zeros_like(acc_ref)
        gains_ref[...] = jnp.zeros_like(gains_ref)

    first_half = lax.broadcasted_iota(jnp.int32, (1, lanes), 1) < lanes // 2
    store_group_masks(row, group_ref)
    half_size = size // 2
    for pair in range(pairs):
        cols = slice(pair * lanes, (pair + 1) * lanes)
        keys, values = key_groups(qkv_ref, edge_ref, cols)
        q_groups = [by_group(qkv_ref[0, 0, :, cols], group_ref, half) for half in range(2)]
        o_groups = [by_group(back_ref[0, 0, :, cols], group_ref, half) for half in range(2)]
        d_q, scores_pair = [], []
        for half in range(2):
            head = 2 * pair + half
            g_probs = dot_nt(values, o_groups[half])
            full_probs = p_ref[0, head].astype(F32)
            product = full_probs * g_probs
            inner = jnp.sum(product, axis=0, keepdims=True)
            g_scores = product - full_probs * inner
            on_own = g_scores * mask_ref[...]
            off_own = g_scores - on_own
            acc_ref[head, :, :half_size] += on_own[:half_size, :half_size] + on_own[half_size:, half_size:]
            acc_ref[head, :, half_size:size] += on_own[:half_size, half_size:] + off_own[half_size:, :half_size]
            acc_ref[head, :, size : size + half_size] += off_own[:half_size, :half_size] + off_own[half_size:, half_size:]
            acc_ref[head, :, size + half_size :] += off_own[:half_size, half_size:] + on_own[half_size:, :half_size]
            scores_pair.append(g_scores.astype(BF))
            d_q.append(dot_tn(scores_pair[-1], keys))
        grad_ref[0, 0, :, cols] = fold_rows(row, first_half, d_q).astype(BF)
        probs_pair = [p_ref[0, 2 * pair], p_ref[0, 2 * pair + 1]]
        for index, (left, right) in enumerate(((scores_pair, q_groups), (probs_pair, o_groups))):
            value = dot_nn(jnp.concatenate(left, axis=1), jnp.concatenate(right, axis=0)).astype(BF)
            grad_ref[0, 3 + 2 * index, :, cols] = value[:, :lanes]
            grad_ref[0, 1 + index, :, cols] = value[:, lanes : 2 * lanes]
            grad_ref[0, 4 + 2 * index, :, cols] = value[:, 2 * lanes :]

    gain1 = gain_ref[0:1, :].astype(F32)
    g_whole = None
    for index, weight_ref in enumerate((wk_ref, wv_ref)):
        edge_grad = grad_ref[0, 3 + 2 * index : 5 + 2 * index].reshape(2 * size, dim)
        left = jnp.concatenate([edge_grad, grad_ref[0, 1 + index]], axis=0)
        term = dot_nt(left, weight_ref[...])
        g_whole = term if g_whole is None else g_whole + term
    zero = jnp.zeros((size, dim), F32)
    g_low = where_tiles(row.slot_low, g_whole[:size], zero)
    g_high = where_tiles(row.slot_high, g_whole[size : 2 * size], zero)
    g_own = g_whole[2 * size :] + (g_whole[:size] - g_low) + (g_whole[size : 2 * size] - g_high)
    g_own = g_own + dot_nt(grad_ref[0, 0], wq_ref[...])
    gain_1 = jnp.zeros((1, dim), F32)
    low, high = by_side(place_ref, pair_ref[0], across_ref[0])
    results = []
    for source, g_norm in ((own_ref[0], g_own), (low, g_low), (high, g_high)):
        x = source.astype(F32)
        scale = rms_scale(x)
        gain_1 = gain_1 + jnp.sum(g_norm * x * scale, axis=0, keepdims=True)
        results.append(rms_back(x, scale, g_norm * gain1))
    part_ref[0] = (results[0] + back_ref[0, 1].astype(F32)).astype(BF)
    odd = place_ref[0] % 2 == 1
    to_pair_ref[0] = jnp.where(odd, results[1], results[2]).astype(BF)
    to_across_ref[0] = jnp.where(odd, results[2], results[1]).astype(BF)
    gains_ref[0:1, :] += gain_1

    @pl.when(step == pl.num_programs(0) - 1)
    def _():
        for head in range(heads):
            offset_ref[head] = fold_offsets(acc_ref[head])


def attend_back(first, count, halo, earlier, lengths, place, x, low, high, own, edges, p, back, gains, weights):
    rows, size, dim = x.shape
    heads = p.shape[1]
    constants = (gains,) + tuple(weights)
    start = 2 + 7 + len(constants)
    aliases = {start + index: index for index in range(len(earlier))}
    return pl.pallas_call(
        functools.partial(attend_back_kernel, first),
        grid_spec=pltpu.PrefetchScalarGridSpec(
            num_scalar_prefetch=2,
            grid=(count,),
            in_specs=[row_spec((size, dim), first)] * 3
            + [row_spec((3, size, dim), first), row_spec((4, size, dim), first)]
            + [row_spec((heads, size, size), first), row_spec((2, size, dim), first)]
            + [full(item.shape) for item in constants]
            + [pl.BlockSpec(memory_space=pl.ANY)] * len(earlier),
            out_specs=[
                row_spec((7, size, dim), first),
                row_spec((size, dim), first),
                row_spec((size, dim), first - halo[0]),
                row_spec((size, dim), first - halo[0]),
            ]
            + [full((heads, 8, 2 * size)), full((8, dim))],
            scratch_shapes=[
                pltpu.VMEM((size, size), F32),
                pltpu.VMEM((2, 3, size, 2 * dim // heads), BF),
                pltpu.VMEM((heads, size // 2, 2 * size), F32),
            ],
        ),
        out_shape=[
            jax.ShapeDtypeStruct((rows, 7, size, dim), BF),
            jax.ShapeDtypeStruct((rows, size, dim), BF),
            jax.ShapeDtypeStruct((halo[1], size, dim), BF),
            jax.ShapeDtypeStruct((halo[1], size, dim), BF),
            jax.ShapeDtypeStruct((heads, 8, 2 * size), F32),
            jax.ShapeDtypeStruct((8, dim), F32),
        ],
        input_output_aliases=aliases,
        compiler_params=params(),
        cost_estimate=cost(
            count * size * dim * (9 * dim + 128 * size), count * size * dim * 60
        ),
        name="attend_back_rows",
    )(lengths, place, x, low, high, own, edges, p, back, *constants, *earlier)


def flip(block, axis, bit):
    count = lax.axis_size(axis)
    return lax.ppermute(block, axis, [(i, i ^ bit) for i in range(count)])


def sum_along(block, axis):
    bit = 1
    while bit < lax.axis_size(axis):
        block = block + flip(block, axis, bit)
        bit *= 2
    return block


def bit_places(axis):
    return [1 << level for level in range((lax.axis_size(axis) - 1).bit_length())]


def gather_batch(block):
    place = lax.axis_index("batch")
    bits = bit_places("batch")
    gathered = block[None]
    for bit in reversed(bits):
        other = flip(gathered, "batch", bit)
        upper = (place & bit) > 0
        gathered = jnp.stack(
            [jnp.where(upper, other, gathered), jnp.where(upper, gathered, other)], axis=1
        )
        gathered = gathered.reshape((-1,) + block.shape)
    return gathered.reshape((-1,) + block.shape[1:])


def halve(block, bits, bit):
    axis = bits.index(bit)
    mine = ((lax.axis_index("batch") & bit) > 0).astype(jnp.int32)
    send = lax.dynamic_index_in_dim(block, 1 - mine, axis, keepdims=False)
    keep = lax.dynamic_index_in_dim(block, mine, axis, keepdims=False)
    return keep + flip(send, "batch", bit), [item for item in bits if item != bit]


def after(value, *others):
    return lax.optimization_barrier((value,) + tuple(others))[0]


def stage_kernel(groups, place_ref, *refs):
    ins = refs[: 2 * sum(len(group) for group in groups)]
    outs = refs[len(ins) :]
    taken = 0
    for index, group in enumerate(groups):
        first = 0
        for count in group:
            value = ins[2 * taken][0, 0, 0] + ins[2 * taken + 1][0, 0, 0]
            taken += 1
            for which in range(2):

                @pl.when(pl.program_id(0) == which)
                def _():
                    outs[2 * index + which][0, 0, first : first + count, :] = value

            first += count


def stage(place, groups, bits, pieces):
    columns = groups[0][0][0].shape[-1]
    lead = bits[0][0][0] * bits[0][0][1]
    if any(count % (16 * pieces) or first % count for group in groups for _, _, first, count in group):
        sends, keeps = [], []
        for index, group in enumerate(groups):
            before, behind = bits[index][0]
            total = jnp.concatenate(
                [(kept + arrived)[..., first : first + count, :].reshape(-1, count, columns)
                 for kept, arrived, first, count in group],
                axis=1,
            ).reshape(before, 2, behind, -1, columns)
            pick = lambda which: lax.dynamic_index_in_dim(total, which, 1, keepdims=False)
            sends.append(pick(1 - place[index]).reshape(lead, 1, -1, columns))
            keeps.append(pick(place[index]).reshape(lead, 1, -1, columns))
        return sends, keeps
    in_specs, operands, out_specs, shapes = [], [], [], []
    for index, group in enumerate(groups):
        before, behind = bits[index][0]
        total = 0

        def place_of(half, step, chunk, places, index=index, behind=behind):
            mine = places[index]
            where_at = jnp.where(half == 0, 1 - mine, mine)
            return step // behind, where_at, step % behind, chunk

        for kept, arrived, first, count in group:
            rows = count // pieces
            total += rows
            shape = (before, 2, behind) + kept.shape[-2:]

            def index_map(half, step, chunk, places, place_of=place_of, first=first, rows=rows):
                one, two, three, four = place_of(half, step, chunk, places)
                return one, two, three, four + first // rows, 0

            for item in (kept, arrived):
                in_specs.append(pl.BlockSpec((1, 1, 1, rows, columns), index_map))
                operands.append(item.reshape(shape))
        for which in range(2):

            def out_map(half, step, chunk, places, which=which):
                if which == 0:
                    step = jnp.where(half == 0, step, lead - 1)
                    chunk = jnp.where(half == 0, chunk, pieces - 1)
                else:
                    step = jnp.where(half == 1, step, 0)
                    chunk = jnp.where(half == 1, chunk, 0)
                return step, chunk, 0, 0

            out_specs.append(pl.BlockSpec((1, 1, total, columns), out_map))
            shapes.append(jax.ShapeDtypeStruct((lead, pieces, total, columns), BF))
    outs = pl.pallas_call(
        functools.partial(
            stage_kernel, [[count // pieces for _, _, _, count in group] for group in groups]
        ),
        grid_spec=pltpu.PrefetchScalarGridSpec(
            num_scalar_prefetch=1, grid=(2, lead, pieces), in_specs=in_specs, out_specs=out_specs
        ),
        out_shape=shapes,
        compiler_params=pltpu.CompilerParams(
            vmem_limit_bytes=VMEM_BYTES, dimension_semantics=("arbitrary",) * 3
        ),
        name="halving_stage",
    )(place, *operands)
    return outs[0::2], outs[1::2]


class BatchSum:
    def __init__(self, mine, theirs, streams):
        bits = bit_places("batch")
        arrived = [flip(item, "batch", bits[0]) for item in theirs]
        self.groups = [
            [(mine[item], arrived[item], first, rows) for item, first, rows in stream] for stream in streams
        ]
        self.bits = [bits[1:][::-1]] * len(streams)
        self.steps = len(bits) - 1
        self.done = 0

    def hold(self, *others):
        self.groups = [
            [(kept, after(arrived, *others), first, rows) for kept, arrived, first, rows in group]
            for group in self.groups
        ]

    def advance(self):
        moved, bits, places = [], [], []
        me = lax.axis_index("batch")
        for index, left in enumerate(self.bits):
            bit = left[::-1][index % len(left)]
            axis = left.index(bit)
            moved.append(bit)
            places.append(((me & bit) > 0).astype(jnp.int32))
            bits.append(((1 << axis, 1 << (len(left) - 1 - axis)),))
        sends, keeps = stage(jnp.stack(places), self.groups, bits, 1)
        self.groups = [
            [(keep, flip(send, "batch", bit), 0, keep.shape[2])]
            for keep, send, bit in zip(keeps, sends, moved)
        ]
        self.bits = [[item for item in left if item != bit] for left, bit in zip(self.bits, moved)]
        self.done += 1
        return sends

    def total(self):
        return [(kept + arrived).reshape(kept.shape[-2:]) for ((kept, arrived, _, _),) in self.groups]


def pack_kernel(tiles_rows, keep_a, come_a, keep_b, come_b, out_ref):
    groups, _, wide = out_ref.shape
    cols = wide // 2
    rows = tiles_rows // groups
    first = keep_a[...] + come_a[...]
    second = keep_b[...] + come_b[...]
    for group in range(groups):
        here = slice(group * cols, (group + 1) * cols)
        out_ref[group, :, :cols] = first[:, here]
        for part in range(groups):
            out_ref[group, part * rows : (part + 1) * rows, cols:] = second[
                group * rows : (group + 1) * rows, part * cols : (part + 1) * cols
            ]
        out_ref[group, tiles_rows:, cols:] = second[tiles_rows:, here]


def pack(stream_a, stream_b, tiles_rows, groups):
    (keep_a, come_a), (keep_b, come_b) = stream_a, stream_b
    rows, dim = keep_a.shape[-2:]
    flat = lambda item: item.reshape(rows, dim)
    shape = (groups, rows, 2 * dim // groups)
    if tiles_rows // groups % 16 == 0:
        return pl.pallas_call(
            functools.partial(pack_kernel, tiles_rows),
            out_shape=jax.ShapeDtypeStruct(shape, BF),
            compiler_params=pltpu.CompilerParams(vmem_limit_bytes=VMEM_BYTES),
            name="pack_places",
        )(flat(keep_a), flat(come_a), flat(keep_b), flat(come_b))
    first = flat(keep_a + come_a).reshape(rows, groups, -1).transpose(1, 0, 2)
    second = flat(keep_b + come_b)
    out = second[:tiles_rows].reshape(groups, -1, groups, dim // groups).transpose(0, 2, 1, 3)
    out = out.reshape(groups, tiles_rows, -1)
    last = second[tiles_rows:].reshape(-1, groups, dim // groups).transpose(1, 0, 2)
    return jnp.concatenate([first, jnp.concatenate([out, last], axis=1)], axis=2)


def columns_kernel(keep_a, come_a, keep_b, come_b, out_ref):
    groups, rows, cols = out_ref.shape
    half = keep_a.shape[0]
    first = keep_a[...] + come_a[...]
    second = keep_b[...] + come_b[...]
    for group in range(groups):
        here = slice(group * cols, (group + 1) * cols)
        out_ref[group, :half, :] = first[:, here]
        out_ref[group, half:, :] = second[:, here]


def pack_columns(streams, groups):
    rows, dim = streams[0][0].shape[-2:]
    pieces = [item.reshape(rows, dim) for keep, come in streams for item in (keep, come)]
    if rows % 16:
        total = jnp.concatenate([pieces[0] + pieces[1], pieces[2] + pieces[3]], axis=0)
        return total.reshape(2 * rows, groups, -1).transpose(1, 0, 2)
    return pl.pallas_call(
        columns_kernel,
        out_shape=jax.ShapeDtypeStruct((groups, 2 * rows, dim // groups), BF),
        compiler_params=pltpu.CompilerParams(vmem_limit_bytes=VMEM_BYTES),
        name="pack_columns",
    )(*pieces)


def split_dot(dot, left, right):
    return dot(left[0], right[0]) + (dot(left[0], right[1]) + dot(left[1], right[0]))


def embed_kernel(sum_ref, more_ref, count_ref, proj_ref, pooled_ref, emb_ref, inverse_ref):
    pooled = (sum_ref[...] + more_ref[...]) / count_ref[...]
    high, low = split_bf(pooled)
    raw = dot_nn(high, proj_ref[...]) + dot_nn(low, proj_ref[...])
    inverse = lax.rsqrt(jnp.sum(raw * raw, axis=-1, keepdims=True) + EPS)
    pooled_ref[...] = pooled
    emb_ref[...] = raw * inverse
    inverse_ref[...] = jnp.broadcast_to(inverse, inverse_ref.shape)


def embed(sums, more, counts, w_proj):
    own, dim = sums.shape
    shapes = ((own, dim), (own, dim), (own, LANES))
    return pl.pallas_call(
        embed_kernel,
        out_shape=[jax.ShapeDtypeStruct(shape, F32) for shape in shapes],
        compiler_params=pltpu.CompilerParams(vmem_limit_bytes=VMEM_BYTES),
        name="embed",
    )(sums, more, counts, w_proj)


def contrast_kernel(
    place_ref,
    own_ref,
    x_ref,
    y_ref,
    xy_ref,
    other_ref,
    inverse_ref,
    partner_ref,
    count_ref,
    proj_ref,
    loss_ref,
    graw_ref,
    pool_ref,
    all_ref,
    logit_ref,
):
    own, dim = own_ref.shape
    total = all_ref.shape[0]
    me = place_ref[0]
    rows_of = lambda place: pl.ds(pl.multiple_of(place * own, own), own)
    for step, ref in enumerate((own_ref, x_ref, y_ref, xy_ref)):
        place = jnp.bitwise_xor(me, 2 * step)
        all_ref[rows_of(place), :] = ref[...]
        all_ref[rows_of(jnp.bitwise_xor(place, 1)), :] = other_ref[step]
    everyone = split_bf(all_ref[...])
    logits = SHARPNESS * split_dot(dot_nt, everyone, everyone)
    row = lax.broadcasted_iota(jnp.int32, (total, total), 0)
    column = lax.broadcasted_iota(jnp.int32, (total, total), 1)
    logits = jnp.where(row == column, NEGATIVE, logits)
    logit_ref[...] = logits
    peak = jnp.max(logits, axis=0, keepdims=True)
    lse_all = peak + jnp.log(jnp.sum(jnp.exp(logits - peak), axis=0, keepdims=True))
    mine = logit_ref[rows_of(me), :]
    peak = jnp.max(mine, axis=1, keepdims=True)
    lse_own = peak + jnp.log(jnp.sum(jnp.exp(mine - peak), axis=1, keepdims=True))
    target = (lax.broadcasted_iota(jnp.int32, (own, total), 1) == partner_ref[...]).astype(F32)
    loss = lse_own - jnp.sum(jnp.where(target > 0, mine, 0.0), axis=1, keepdims=True)
    loss_ref[...] = jnp.broadcast_to(loss, loss_ref.shape)
    both = SHARPNESS * (jnp.exp(mine - lse_own) + jnp.exp(mine - lse_all) - 2.0 * target)
    grad = split_dot(dot_nn, split_bf(both), everyone)
    emb = own_ref[...]
    grad = inverse_ref[:, :1] * (grad - emb * jnp.sum(emb * grad, axis=1, keepdims=True))
    graw_ref[...] = grad
    high, low = split_bf(grad)
    pool_ref[...] = (dot_nt(high, proj_ref[...]) + dot_nt(low, proj_ref[...])) / count_ref[...]


def contrast_near(embedded, inverse, partner, counts, w_proj):
    own, dim = embedded.shape
    total = own * lax.axis_size("batch")
    parts = [embedded] + [flip(embedded, "batch", bits) for bits in (2, 4, 6)]
    other = flip(jnp.stack(parts), "batch", 1)
    me = lax.axis_index("batch").astype(jnp.int32).reshape(1)
    constants = (*parts, other, inverse, partner.reshape(own, 1), counts, w_proj)
    loss, graw, pool = pl.pallas_call(
        contrast_kernel,
        grid_spec=pltpu.PrefetchScalarGridSpec(
            num_scalar_prefetch=1,
            grid=(1,),
            in_specs=[full(item.shape) for item in constants],
            out_specs=[full((own, LANES)), full((own, dim)), full((own, dim))],
            scratch_shapes=[pltpu.VMEM((total, dim), F32), pltpu.VMEM((total, total), F32)],
        ),
        out_shape=[
            jax.ShapeDtypeStruct((own, LANES), F32),
            jax.ShapeDtypeStruct((own, dim), F32),
            jax.ShapeDtypeStruct((own, dim), F32),
        ],
        compiler_params=params(),
        name="contrast",
    )(me, *constants)
    return loss[:, 0], graw, pool


def finish_kernel(count, width, *refs):
    total = sum(ref[...].astype(F32) for ref in refs[:-count])
    for index, ref in enumerate(refs[-count:]):
        ref[...] = total[index * width : (index + 1) * width, :].T


def finish(pieces, count, width):
    cols = pieces[0].shape[1]
    return pl.pallas_call(
        functools.partial(finish_kernel, count, width),
        out_shape=[jax.ShapeDtypeStruct((cols, width), F32)] * count,
        compiler_params=pltpu.CompilerParams(vmem_limit_bytes=VMEM_BYTES),
        name="finish",
    )(*pieces)


def contrast(embedded, inv_norm, w_proj, partner):
    proj = w_proj.astype(F32)
    everyone = gather_batch(embedded)
    own_count = embedded.shape[0]
    total = everyone.shape[0]
    own_index = lax.axis_index("batch") * own_count + jnp.arange(own_count, dtype=jnp.int32)
    columns = jnp.arange(total, dtype=jnp.int32)

    def lse_of(rows, index):
        logits = SHARPNESS * jnp.einsum("nd,md->nm", rows, everyone, precision=HIGHEST)
        logits = jnp.where(columns[None, :] == index[:, None], NEGATIVE, logits)
        peak = jnp.max(logits, axis=-1, keepdims=True)
        return peak[:, 0] + jnp.log(jnp.sum(jnp.exp(logits - peak), axis=-1))

    if total <= 1024:
        lse_all = lse_of(everyone, columns)
    else:
        lse_all = lax.map(
            lambda pieces: lse_of(pieces[0], pieces[1]),
            (everyone.reshape(-1, 512, everyone.shape[1]), columns.reshape(-1, 512)),
        ).reshape(-1)
    logits = SHARPNESS * jnp.einsum("nd,md->nm", embedded, everyone, precision=HIGHEST)
    is_self = columns[None, :] == own_index[:, None]
    logits = jnp.where(is_self, NEGATIVE, logits)
    peak = jnp.max(logits, axis=-1, keepdims=True)
    lse_own = peak[:, 0] + jnp.log(jnp.sum(jnp.exp(logits - peak), axis=-1))
    is_target = columns[None, :] == partner[:, None]
    picked = jnp.sum(jnp.where(is_target, logits, 0.0), axis=-1)
    loss = lse_own - picked
    both = SHARPNESS * (
        jnp.exp(logits - lse_own[:, None])
        + jnp.exp(logits - lse_all[None, :])
        - 2.0 * is_target.astype(F32)
    )
    grad_emb = jnp.dot(both, everyone, precision=HIGHEST)
    grad_raw = inv_norm * (
        grad_emb - embedded * jnp.sum(embedded * grad_emb, axis=-1, keepdims=True)
    )
    grad_pooled = jnp.einsum("ne,de->nd", grad_raw, proj, precision=HIGHEST)
    return loss, grad_raw, grad_pooled


def shards(
    tokens,
    norm1_gain,
    w_query,
    w_key,
    w_value,
    rel_bias,
    w_output,
    norm2_gain,
    w_in,
    w_out,
    final_gain,
    w_proj,
    lengths,
    partner,
    cotangent,
):
    rows, size, dim = tokens.shape
    slots = lengths.shape[1]
    toks = rows * size
    seq_count = lax.axis_size("seq")
    seq_place = lax.axis_index("seq")
    place = seq_place.astype(jnp.int32).reshape(1)
    pairs = [(i, i ^ 1) for i in range(seq_count)]
    across = [(i, i - 1 if i % 2 == 0 else i + 1) for i in range(1, seq_count - 1)]
    gains = jnp.stack([norm1_gain, norm2_gain, final_gain])

    x_pair = lax.ppermute(tokens, "seq", pairs)
    x_across = lax.ppermute(tokens, "seq", across)
    bias = bias_tables(rel_bias, size)
    own = own_projections(tokens, norm1_gain.reshape(1, dim), (w_query, w_key, w_value))
    block, partial, edges, p, att, pre, after_attn, n2 = forward(
        lengths,
        place,
        tokens,
        x_pair,
        x_across,
        own,
        gains,
        (w_key, w_value, w_output, w_in, w_out),
        bias,
    )
    counts = lengths.astype(F32).reshape(rows * slots, 1)
    partial = partial.reshape(rows * slots, dim)
    seq_bits = bit_places("seq")
    for bit in seq_bits[:-1]:
        partial = partial + flip(partial, "seq", bit)
    pooled, embedded, inverse = embed(partial, flip(partial, "seq", seq_bits[-1]), counts, w_proj)
    if lax.axis_size("batch") == 8:
        loss, grad_raw, pool_grad = contrast_near(embedded, inverse, partner, counts, w_proj)
    else:
        loss, grad_raw, grad_pooled = contrast(embedded, inverse[:, :1], w_proj, partner)
        pool_grad = grad_pooled / counts
    pool_grad = pool_grad.reshape(rows, slots, dim)
    batch_count = lax.axis_size("batch")
    place = jnp.stack([seq_place, lax.axis_index("batch") % 2]).astype(jnp.int32)

    back, gains_a, mine, theirs = feed_back(
        batch_count,
        lengths,
        place,
        block,
        after_attn,
        cotangent,
        att,
        n2,
        pre,
        pool_grad,
        grad_raw,
        pooled,
        gains,
        (w_output, w_in, w_out),
    )
    hidden = w_in.shape[1]
    width = dim // batch_count
    tiles = hidden // dim
    wide = hidden // batch_count
    feed_sum = BatchSum(
        mine,
        theirs,
        (((0, 0, wide), (2, 0, width)), ((1, 0, tiles * width), (2, width, width))),
    )
    segments = [(0, 1), (1, rows - 2), (rows - 1, 1)] if rows > 2 else [(0, rows)]
    halves, from_pair, from_across = [], [], []
    earlier = ()
    for first, count in segments:
        if halves and feed_sum.done < feed_sum.steps:
            place = after(place, *feed_sum.advance())
        halves.append(
            attend_back(
                first,
                count,
                (0, rows - 1) if first + count < rows else (first, count),
                earlier,
                lengths,
                place,
                tokens,
                x_pair,
                x_across,
                own,
                edges,
                p,
                back,
                gains,
                (w_query, w_key, w_value),
            )
        )
        feed_sum.hold(halves[-1][5])
        earlier = tuple(halves[-1][:4])
        if first + count >= rows - 1:
            from_pair.append(lax.ppermute(halves[-1][2], "seq", pairs))
            from_across.append(lax.ppermute(halves[-1][3], "seq", across))
            earlier = earlier[:2]
    grads, part = earlier
    while feed_sum.done < feed_sum.steps:
        place = after(place, *feed_sum.advance())

    feed_part = pack(
        *[(group[0][0], group[0][1]) for group in feed_sum.groups], tiles * width, seq_count
    )
    grad_rel = bias_grad([item[4] for item in halves], rel_bias.shape[0])
    gain1_grad = sum(item[5][0] for item in halves)
    small = jnp.concatenate([gain1_grad, gains_a[1], gains_a[0], grad_rel.reshape(-1)])
    small = jnp.pad(small, (0, -small.shape[0] % 1024)).reshape(-1, 128)
    batch_bits = bit_places("batch")
    arrived = flip(small, "seq", seq_bits[0])
    place = after(place, feed_part, small, *from_pair, *from_across)
    attend_mine, attend_theirs = attend_grad(batch_count, place, own, edges, grads)
    feed_done = lax.psum_scatter(feed_part, "seq", scatter_dimension=0, tiled=True)[0]
    half = 3 * width // 2
    attend_sum = BatchSum([attend_mine], [attend_theirs], (((0, 0, half),), ((0, half, 3 * width - half),)))
    small = after(small, attend_mine) + arrived
    arrived = flip(small, "batch", batch_bits[0])
    attend_sum.hold(arrived)
    for bit in batch_bits[1:]:
        sends = attend_sum.advance()
        small = after(small, *sends) + arrived
        arrived = flip(small, "batch", bit)
        attend_sum.hold(arrived)
    attend_parts = pack_columns([group[0][:2] for group in attend_sum.groups], seq_count)
    small = after(small, attend_parts) + arrived
    came = [lax.dynamic_index_in_dim(attend_parts, seq_place, 0, keepdims=False)]
    for distance in range(1, seq_count):
        route = [(i, (i + distance) % seq_count) for i in range(seq_count)]
        target = (seq_place + distance) % seq_count
        send = lax.dynamic_index_in_dim(attend_parts, target, 0, keepdims=False)
        came.append(lax.ppermute(send, "seq", route))
    sent = came[0]
    for bit in seq_bits[1:]:
        small = small + flip(small, "seq", bit)
    small = small.reshape(-1)
    gain_sums = [small[i * dim : (i + 1) * dim] for i in range(3)]
    rel_sum = small[3 * dim : 3 * dim + rel_bias.size].reshape(rel_bias.shape)

    grad_tokens = (
        after(part, sent).astype(F32)
        + jnp.concatenate(from_pair, axis=0).astype(F32)
        + jnp.concatenate(from_across, axis=0).astype(F32)
    )
    turn = lambda array: array.T.astype(F32)
    cols = dim // seq_count
    s_in = turn(feed_done[:wide, :cols])
    s_output = turn(feed_done[wide:, :cols])
    s_out = feed_done[:-width, cols:].reshape(seq_count, width, cols)
    s_out = s_out.transpose(0, 2, 1).reshape(dim, width).astype(F32)
    s_proj = turn(feed_done[-width:, cols:])
    came[0] = after(came[0], s_in, s_output, s_out, s_proj, grad_tokens)
    s_attend = finish(came, 3, width)
    return (
        block,
        embedded,
        loss,
        grad_tokens,
        gain_sums[0],
        s_attend[0],
        s_attend[1],
        s_attend[2],
        rel_sum,
        s_output,
        gain_sums[1],
        s_in,
        s_out,
        gain_sums[2],
        s_proj,
    )


def solution(mesh):
    tok = P("batch", "seq", None)
    mat = P("seq", "batch")
    return jax.shard_map(
        shards,
        mesh=mesh,
        in_specs=(tok,) + (P(),) * 11 + (P("batch", None), P("batch"), tok),
        out_specs=(
            tok,
            P("batch", None),
            P("batch"),
            tok,
            P(),
            mat,
            mat,
            mat,
            P(),
            mat,
            P(),
            mat,
            mat,
            P(),
            mat,
        ),
        check_vma=False,
    )
```

```python
import functools

import jax
import jax.numpy as jnp
from jax import lax
from jax.experimental import pallas as pl
from jax.experimental.pallas import tpu as pltpu
from jax.sharding import PartitionSpec as P

EPS = 1e-06
NEGATIVE = -1e30
SHARPNESS = 50.0
THRESHOLDS = (12, 16, 23, 32, 46, 64, 91)
HIGHEST = lax.Precision.HIGHEST
BF = jnp.bfloat16
F32 = jnp.float32
VMEM_BYTES = 63 * 1024 * 1024
GELU_A = 0.7978845608028654
GELU_B = 0.044715
LANES = 128


def dot_nn(left, right):
    return lax.dot_general(left, right, (((1,), (0,)), ((), ())), preferred_element_type=F32)


def dot_nt(left, right):
    return lax.dot_general(left, right, (((1,), (1,)), ((), ())), preferred_element_type=F32)


def dot_tn(left, right):
    return lax.dot_general(left, right, (((0,), (0,)), ((), ())), preferred_element_type=F32)


def rms_scale(values):
    return lax.rsqrt(jnp.mean(values * values, axis=-1, keepdims=True) + EPS)


def rms_back(values, scale, grad_normed):
    inner = jnp.mean(grad_normed * values, axis=-1, keepdims=True)
    return scale * (grad_normed - values * (scale * scale * inner))


def split_bf(values):
    high = values.astype(BF)
    return high, (values - high.astype(F32)).astype(BF)


def bucket_of(offset):
    distance = jnp.abs(offset)
    beyond = jnp.zeros_like(distance)
    for threshold in THRESHOLDS:
        beyond = beyond + (distance >= threshold).astype(jnp.int32)
    within = jnp.where(distance < 8, distance, 8 + beyond)
    return within + 16 * (offset > 0).astype(jnp.int32)


def wrapped_offsets(shape, axis, size):
    place = lax.broadcasted_iota(jnp.int32, shape, axis)
    return jnp.where(place < size, place, place - 2 * size)


def full(shape):
    return pl.BlockSpec(shape, lambda *_: (0,) * len(shape), pipeline_mode=pl.Buffered(1))


def row_spec(shape, first=0):
    return pl.BlockSpec(
        (1,) + tuple(shape), lambda step, *_: (step + first,) + (0,) * len(shape)
    )


def cost(products, moved, exps=0):
    return pl.CostEstimate(flops=2 * products, bytes_accessed=moved, transcendentals=exps)


def params(limit=VMEM_BYTES):
    return pltpu.CompilerParams(
        vmem_limit_bytes=limit, dimension_semantics=("arbitrary",)
    )


def bias_kernel(size, table_ref, out_ref):
    buckets, heads = table_ref.shape
    hot = (
        lax.broadcasted_iota(jnp.int32, (buckets, 2 * size), 0)
        == bucket_of(-wrapped_offsets((buckets, 2 * size), 1, size))
    ).astype(BF)
    by_offset = dot_tn(table_ref[...], hot)
    for head in range(heads):
        line = jnp.broadcast_to(by_offset[head : head + 1, :], (size, 2 * size))
        out_ref[head] = pltpu.roll(line, 0, 1, stride=1, stride_axis=0).astype(BF)


def bias_tables(rel_bias, size):
    heads = rel_bias.shape[1]
    return pl.pallas_call(
        functools.partial(bias_kernel, size),
        out_shape=jax.ShapeDtypeStruct((heads, size, 2 * size), BF),
        compiler_params=pltpu.CompilerParams(vmem_limit_bytes=VMEM_BYTES),
    )(rel_bias)


def fold_offsets(rows):
    count, width = rows.shape
    while count > 8:
        count = count // 2
        rows = rows[:count] + pltpu.roll(rows[count:], width - count, 1)
    return rows


def bias_grad_kernel(heads, *refs):
    acc_refs, out_ref = refs[:-1], refs[-1]
    rows = sum(acc_ref[...] for acc_ref in acc_refs)
    width = rows.shape[1]
    buckets = out_ref.shape[1]
    place = lax.broadcasted_iota(jnp.int32, rows.shape, 0)
    for bit in (4, 2, 1):
        rows = jnp.where((place & bit) > 0, pltpu.roll(rows, width - bit, 1), rows)
    hot = (
        lax.broadcasted_iota(jnp.int32, (width, buckets), 1)
        == bucket_of(-wrapped_offsets((width, buckets), 0, width // 2))
    ).astype(BF)
    first, rest = split_bf(rows)
    second, third = split_bf(rows - first.astype(F32))
    table = dot_nn(first, hot) + dot_nn(second, hot) + dot_nn(third, hot)
    for head in range(heads):
        out_ref[head : head + 1, :] = jnp.sum(table[8 * head : 8 * head + 8], axis=0, keepdims=True)


def bias_grad(accs, buckets):
    heads, _, width = accs[0].shape
    out = pl.pallas_call(
        functools.partial(bias_grad_kernel, heads),
        out_shape=jax.ShapeDtypeStruct((heads, buckets), F32),
        compiler_params=pltpu.CompilerParams(vmem_limit_bytes=VMEM_BYTES),
        name="bias_grad",
    )(*[acc.reshape(heads * 8, width) for acc in accs])
    return out.T


class Row:
    def __init__(self, lengths_ref, place_ref, row, size):
        slots = lengths_ref.shape[1]
        base = place_ref[0] * size
        pos = base + lax.broadcasted_iota(jnp.int32, (1, size), 1)
        zero = jnp.int32(0)
        before, first, last, beyond = zero, zero, zero, zero
        own = jnp.zeros((1, size), jnp.int32)
        low = jnp.zeros((1, size), jnp.int32)
        high = jnp.zeros((1, size), jnp.int32)
        end = zero
        passed = lambda end, place: (end <= place).astype(jnp.int32)
        for slot in range(slots):
            end = end + lengths_ref[row, slot]
            before += passed(end, base - 1)
            first += passed(end, base)
            last += passed(end, base + size - 1)
            beyond += passed(end, base + size)
            own += passed(end, pos)
            low += passed(end, pos - size)
            high += passed(end, pos + size)
        before = jnp.where(base == 0, -1, before).astype(F32)
        low = jnp.where(pos < size, -1, low).astype(F32)
        own = own.astype(F32)
        col_own, col_low, col_high = (
            jnp.broadcast_to(item, (LANES, size)).T for item in (own, low, high.astype(F32))
        )
        self.in_low = col_own == before
        self.in_high = col_own == beyond.astype(F32)
        self.slot_low = col_low == first.astype(F32)
        self.slot_high = col_high == last.astype(F32)
        key = lax.broadcasted_iota(jnp.int32, (size, size), 0)
        query = lax.broadcasted_iota(jnp.int32, (size, size), 1)
        wide = lambda item: jnp.concatenate([item] * (size // LANES), axis=1)
        self.own = wide(col_own) == own
        self.alt = jnp.where(key > query, wide(col_low), jnp.where(key < query, wide(col_high), -2.0)) == own


def where_tiles(mask, left, right):
    lanes = mask.shape[1]
    return jnp.concatenate(
        [
            jnp.where(mask, left[:, start : start + lanes], right[:, start : start + lanes])
            for start in range(0, left.shape[1], lanes)
        ],
        axis=1,
    )


def store_group_masks(row, ref):
    _, _, size, lanes = ref.shape
    first = lax.broadcasted_iota(jnp.int32, (1, lanes), 1) < lanes // 2
    low = row.in_low.astype(F32)
    high = row.in_high.astype(F32)
    for part, group in enumerate((low, 1.0 - low - high, high)):
        ref[0, part] = jnp.where(first, group, 0.0).astype(BF)
        ref[1, part] = jnp.where(first, 0.0, group).astype(BF)


def by_group(pair, ref, half):
    return jnp.concatenate([pair * ref[half, part] for part in range(3)], axis=1)


def fold_rows(row, first, wide):
    lanes = wide[0].shape[1] // 3
    parts = [
        jnp.where(first, wide[0][:, here], wide[1][:, here])
        for here in (slice(part * lanes, (part + 1) * lanes) for part in range(3))
    ]
    return jnp.where(row.in_low, parts[0], jnp.where(row.in_high, parts[2], parts[1]))


def own_kernel(x_ref, gain1_ref, wq_ref, wk_ref, wv_ref, out_ref):
    x = x_ref[0].astype(F32)
    out_ref[0, 3] = (x * rms_scale(x) * gain1_ref[...].astype(F32)).astype(BF)
    for index, weight_ref in enumerate((wq_ref, wk_ref, wv_ref)):
        out_ref[0, index] = dot_nn(out_ref[0, 3], weight_ref[...]).astype(BF)


def own_projections(tokens, gain1, weights):
    rows, size, dim = tokens.shape
    constants = (gain1,) + tuple(weights)
    return pl.pallas_call(
        own_kernel,
        grid=(rows,),
        in_specs=[row_spec((size, dim))] + [full(item.shape) for item in constants],
        out_specs=row_spec((4, size, dim)),
        out_shape=jax.ShapeDtypeStruct((rows, 4, size, dim), BF),
        compiler_params=params(),
        cost_estimate=cost(3 * rows * size * dim * dim, rows * size * dim * 10),
        name="own_projections",
    )(tokens, *constants)


def row_sentences(lengths_ref, place_ref, row, size):
    where_pos = place_ref[0] * size + lax.broadcasted_iota(jnp.int32, (1, size), 1)
    found = jnp.zeros((1, size), jnp.int32)
    end = jnp.int32(0)
    for slot in range(lengths_ref.shape[1]):
        end = end + lengths_ref[row, slot]
        found = found + (end <= where_pos).astype(jnp.int32)
    return found


def attend_kernel(
    first,
    lengths_ref,
    place_ref,
    pair_ref,
    across_ref,
    own_ref,
    gains_ref,
    wk_ref,
    wv_ref,
    bias_ref,
    *rest,
):
    edge_ref, p_ref, att_ref, mask_ref, group_ref = rest[-5:]
    size, dim = pair_ref.shape[1:]
    heads = bias_ref.shape[0]
    pairs = heads // 2
    lanes = dim // pairs
    row = Row(lengths_ref, place_ref, pl.program_id(0) + first, size)
    mask_ref[0] = jnp.where(row.own, 0.0, NEGATIVE).astype(BF)
    mask_ref[1] = jnp.where(row.alt, 0.0, NEGATIVE).astype(BF)
    store_group_masks(row, group_ref)
    gain1 = gains_ref[0:1, :].astype(F32)
    own = own_ref[0, 3].astype(F32)
    sides = by_side(place_ref, pair_ref[0], across_ref[0])
    for part, (source, slot) in enumerate(zip(sides, (row.slot_low, row.slot_high))):
        x = source.astype(F32)
        edge_ref[0, 4 + part] = where_tiles(slot, x * rms_scale(x) * gain1, own).astype(BF)
    edges = edge_ref[0, 4:].reshape(2 * size, dim)
    first_half = lax.broadcasted_iota(jnp.int32, (1, lanes), 1) < lanes // 2
    for index, weight_ref in enumerate((wk_ref, wv_ref)):
        value = dot_nn(edges, weight_ref[...]).astype(BF)
        edge_ref[0, 2 * index : 2 * index + 2] = value.reshape(2, size, dim)
    for pair in range(pairs):
        cols = slice(pair * lanes, (pair + 1) * lanes)
        keys, values = key_groups(own_ref, edge_ref, cols)
        halves = []
        for half in range(2):
            head = 2 * pair + half
            scores = dot_nt(keys, by_group(own_ref[0, 0, :, cols], group_ref, half))
            bias = jnp.maximum(
                bias_ref[head, :, :size] + mask_ref[0], bias_ref[head, :, size:] + mask_ref[1]
            )
            scores = scores + bias.astype(F32)
            peak = jnp.max(scores, axis=0, keepdims=True)
            powers = jnp.exp(scores - peak)
            inverse = 1.0 / jnp.sum(powers, axis=0, keepdims=True)
            probs = (powers * inverse).astype(BF)
            p_ref[0, head] = probs
            halves.append(dot_tn(probs, values))
        att_ref[0, :, cols] = fold_rows(row, first_half, halves).astype(BF)


def attend(first, earlier, lengths, place, pair, across, own, gains, wk, wv, bias):
    count, size, dim = pair.shape
    rows = own.shape[0]
    heads = bias.shape[0]
    constants = (gains, wk, wv, bias)
    shapes = ((6, size, dim), (heads, size, size), (size, dim))
    start = 2 + 3 + len(constants)
    return pl.pallas_call(
        functools.partial(attend_kernel, first),
        grid_spec=pltpu.PrefetchScalarGridSpec(
            num_scalar_prefetch=2,
            grid=(count,),
            in_specs=[row_spec((size, dim))] * 2
            + [row_spec((4, size, dim), first)]
            + [full(item.shape) for item in constants]
            + [pl.BlockSpec(memory_space=pl.ANY)] * len(earlier),
            out_specs=[row_spec(shape, first) for shape in shapes],
            scratch_shapes=[
                pltpu.VMEM((2, size, size), BF),
                pltpu.VMEM((2, 3, size, 2 * dim // heads), BF),
            ],
        ),
        out_shape=[jax.ShapeDtypeStruct((rows,) + shape, BF) for shape in shapes],
        input_output_aliases={start + index: index for index in range(len(earlier))},
        compiler_params=params(),
        cost_estimate=cost(count * size * dim * (4 * dim + 36 * size), count * size * dim * 40),
        name="attend_rows",
    )(lengths, place, pair, across, own, *constants, *earlier)


def forward_kernel(
    rows,
    lengths_ref,
    place_ref,
    x_ref,
    att_ref,
    gains_ref,
    wo_ref,
    win_ref,
    wout_ref,
    block_ref,
    pooled_ref,
    pre_ref,
    after_hbm,
    n2_hbm,
    after_low,
    n2_all,
    total_ref,
    sems,
):
    _, size, dim = x_ref.shape
    slots = pooled_ref.shape[1]
    toks = rows * size
    step = pl.program_id(0)
    copies = [
        pltpu.make_async_copy(after_low, after_hbm, sems.at[0]),
        pltpu.make_async_copy(n2_all, n2_hbm, sems.at[1]),
    ]

    @pl.when(step == 0)
    def _():
        mixed = dot_nn(att_ref[...].reshape(toks, dim), wo_ref[...])
        after = x_ref[...].reshape(toks, dim).astype(F32) + mixed
        after_low[...] = after.astype(BF)
        total_ref[...] = after
        n2_all[...] = (after * rms_scale(after) * gains_ref[1:2, :].astype(F32)).astype(BF)
        for copy in copies:
            copy.start()

    pre = dot_nn(n2_all[...], win_ref[...])
    square = pre * pre
    gate = 0.5 + 0.5 * jnp.tanh(pre * (GELU_A + (GELU_A * GELU_B) * square))
    pre_ref[...] = pre.astype(BF)
    total_ref[...] += dot_nn((pre * gate).astype(BF), wout_ref[...])

    @pl.when(step == pl.num_programs(0) - 1)
    def _():
        gainf = gains_ref[2:3, :].astype(F32)
        for row in range(rows):
            here = slice(row * size, (row + 1) * size)
            block = total_ref[here, :].astype(BF)
            block_ref[row] = block
            out = block.astype(F32)
            final = out * rms_scale(out) * gainf
            found = row_sentences(lengths_ref, place_ref, row, size)
            member = (lax.broadcasted_iota(jnp.int32, (slots, size), 0) == found).astype(BF)
            high_part, low_part = split_bf(final)
            pooled_ref[row] = dot_nn(member, high_part) + dot_nn(member, low_part)
        for copy in copies:
            copy.wait()


def by_side(place_ref, pair, across):
    odd = place_ref[0] % 2 == 1
    return jnp.where(odd, pair, across), jnp.where(odd, across, pair)


def key_groups(own_ref, edge_ref, cols):
    return [
        jnp.concatenate(
            [edge_ref[0, 2 * index, :, cols], own_ref[0, 1 + index, :, cols], edge_ref[0, 2 * index + 1, :, cols]],
            axis=1,
        )
        for index in range(2)
    ]


def forward(lengths, place, tokens, att, gains, wo, win, wout):
    rows, size, dim = tokens.shape
    slots = lengths.shape[1]
    hidden = win.shape[1]
    toks = rows * size
    constants = (tokens, att, gains, wo)
    anywhere = pl.BlockSpec(memory_space=pl.ANY)
    out_of = lambda shape, kind=BF: jax.ShapeDtypeStruct(shape, kind)
    return pl.pallas_call(
        functools.partial(forward_kernel, rows),
        grid_spec=pltpu.PrefetchScalarGridSpec(
            num_scalar_prefetch=2,
            grid=(hidden // dim,),
            in_specs=[full(item.shape) for item in constants]
            + [
                pl.BlockSpec((dim, dim), lambda step, *_: (0, step)),
                pl.BlockSpec((dim, dim), lambda step, *_: (step, 0)),
            ],
            out_specs=[
                full((rows, size, dim)),
                full((rows, slots, dim)),
                pl.BlockSpec((toks, dim), lambda step, *_: (0, step)),
                anywhere,
                anywhere,
            ],
            scratch_shapes=[
                pltpu.VMEM((toks, dim), BF),
                pltpu.VMEM((toks, dim), BF),
                pltpu.VMEM((toks, dim), F32),
                pltpu.SemaphoreType.DMA((2,)),
            ],
        ),
        out_shape=[
            out_of((rows, size, dim)),
            out_of((rows, slots, dim), F32),
            out_of((toks, hidden)),
            out_of((toks, dim)),
            out_of((toks, dim)),
        ],
        compiler_params=params(),
        cost_estimate=cost(toks * dim * (dim + 2 * hidden), toks * (hidden * 2 + dim * 20)),
        name="feed_forward",
    )(lengths, place, *constants, win, wout)


def store_split(core, value, refs, count, first=0):
    if len(refs) == 1:
        refs[0][first : first + value.shape[0], :] = value
        return
    groups = value.shape[0] // (2 * count)
    for group in range(groups):
        even = value[2 * group * count : (2 * group + 1) * count]
        odd = value[(2 * group + 1) * count : (2 * group + 2) * count]

        refs[0][group, first : first + count, :] = jnp.where(core == 0, even, odd)
        refs[1][group, first : first + count, :] = jnp.where(core == 0, odd, even)


def feed_back_kernel(
    rows,
    parts,
    lengths_ref,
    place_ref,
    block_ref,
    cot_ref,
    pool_ref,
    graw_ref,
    pooled_ref,
    gain_ref,
    pre_ref,
    win_ref,
    wout_ref,
    after_hbm,
    n2_hbm,
    att_hbm,
    wo_hbm,
    back_ref,
    gains_ref,
    *rest,
):
    split = len(rest) == 14
    per = 2 if split else 1
    in_refs, out_refs, small_refs = (rest[i * per : (i + 1) * per] for i in range(3))
    gout_ref, branch_ref, gn2_ref, after_ref, n2_ref, att_ref, wo_ref, sems = rest[3 * per :]
    _, size, dim = block_ref.shape
    toks = rows * size
    slots = pool_ref.shape[1]
    step = pl.program_id(0)
    tiles = pl.num_programs(0) - 1
    core = place_ref[1]
    copies = [
        pltpu.make_async_copy(n2_hbm, n2_ref, sems.at[0]),
        pltpu.make_async_copy(after_hbm, after_ref, sems.at[1]),
        pltpu.make_async_copy(att_hbm, att_ref, sems.at[2]),
        pltpu.make_async_copy(wo_hbm, wo_ref, sems.at[3]),
    ]

    @pl.when(step == 0)
    def _():
        for copy in copies:
            copy.start()
        gainf = gain_ref[2:3, :].astype(F32)
        gain_f = jnp.zeros((1, dim), F32)
        for row in range(rows):
            here = slice(row * size, (row + 1) * size)
            found = row_sentences(lengths_ref, place_ref, row, size)
            member = (lax.broadcasted_iota(jnp.int32, (slots, size), 0) == found).astype(BF)
            high_part, low_part = split_bf(pool_ref[row])
            g_final = dot_tn(member, high_part) + dot_tn(member, low_part)
            out = block_ref[row].astype(F32)
            scale = rms_scale(out)
            gain_f = gain_f + jnp.sum(g_final * out * scale, axis=0, keepdims=True)
            g_out = rms_back(out, scale, g_final * gainf) + cot_ref[row].astype(F32)
            gout_ref[here, :] = g_out
            branch_ref[here, :] = g_out.astype(BF)
        gains_ref[...] = jnp.zeros_like(gains_ref)
        gains_ref[0:1, :] = gain_f
        copies[0].wait()

    @pl.when(step < tiles)
    def _():
        g_hidden = dot_nt(branch_ref[...], wout_ref[...])
        pre = pre_ref[...].astype(F32)
        square = pre * pre
        gate = 0.5 + 0.5 * jnp.tanh(pre * (GELU_A + (GELU_A * GELU_B) * square))
        act = pre * gate
        value = dot_tn(branch_ref[...], act.astype(BF)).astype(BF)
        store_split(core, value, out_refs, dim // parts)
        slope = gate + act * (1.0 - gate) * (2 * GELU_A + (6 * GELU_A * GELU_B) * square)
        g_pre = (g_hidden * slope).astype(BF)
        value = dot_tn(g_pre, n2_ref[...]).astype(BF)
        store_split(core, value, in_refs, tiles * dim // parts)
        part = dot_nt(g_pre, win_ref[...])

        @pl.when(step == 0)
        def _():
            gn2_ref[...] = part

        @pl.when(step > 0)
        def _():
            gn2_ref[...] += part

    @pl.when(step == tiles)
    def _():
        for copy in copies[1:]:
            copy.wait()
        gain2 = gain_ref[1:2, :].astype(F32)
        gain_2 = jnp.zeros((1, dim), F32)
        for row in range(rows):
            here = slice(row * size, (row + 1) * size)
            after = after_ref[here, :].astype(F32)
            g_n2 = gn2_ref[here, :]
            scale = rms_scale(after)
            gain_2 = gain_2 + jnp.sum(g_n2 * after * scale, axis=0, keepdims=True)
            g_after = gout_ref[here, :] + rms_back(after, scale, g_n2 * gain2)
            back_ref[row, 1] = g_after.astype(BF)
            branch_ref[here, :] = g_after.astype(BF)
        gains_ref[1:2, :] = gain_2
        g_mix = dot_nt(branch_ref[...], wo_ref[...]).astype(BF)
        for row in range(rows):
            back_ref[row, 0] = g_mix[row * size : (row + 1) * size]
        value = dot_tn(branch_ref[...], att_ref[...].reshape(toks, dim)).astype(BF)
        store_split(core, value, small_refs, dim // parts)
        left_high, left_low = split_bf(jnp.where(place_ref[0] == 0, graw_ref[...], 0.0))
        right_high, right_low = split_bf(pooled_ref[...])
        value = dot_tn(left_high, right_high)
        value += dot_tn(left_high, right_low) + dot_tn(left_low, right_high)
        first = dim // parts if split else dim
        store_split(core, value.astype(BF), small_refs, dim // parts, first)


def feed_back(parts, lengths, place, block, after, cot, att, n2, pre, pool, graw, pooled, gains, weights):
    rows, size, dim = block.shape
    hidden = pre.shape[1]
    tiles = hidden // dim
    toks = rows * size
    wo, win, wout = weights
    split = (dim // parts) % 16 == 0 and dim % (2 * hidden // parts) == 0
    tile = lambda step: jnp.minimum(step, tiles - 1)
    if split:
        groups = parts // 2
        wide = hidden // parts
        inner = dim // (2 * wide)
        narrow = dim // parts
        in_specs = [pl.BlockSpec((inner, wide, dim), lambda step, *_: (tile(step), 0, 0))] * 2
        out_specs = [pl.BlockSpec((groups, narrow, dim), lambda step, *_: (0, tile(step), 0))] * 2
        small_specs = [full((groups, 2 * narrow, dim))] * 2
        shapes = [(groups, wide, dim)] * 2 + [(groups, tiles * narrow, dim)] * 2 + [(groups, 2 * narrow, dim)] * 2
    else:
        in_specs = [pl.BlockSpec((dim, dim), lambda step, *_: (tile(step), 0))]
        out_specs = [pl.BlockSpec((dim, dim), lambda step, *_: (tile(step), 0))]
        small_specs = [full((2 * dim, dim))]
        shapes = [(hidden, dim), (tiles * dim, dim), (2 * dim, dim)]
    constants = (block, cot, pool, graw, pooled, gains)
    outs = pl.pallas_call(
        functools.partial(feed_back_kernel, rows, parts),
        grid_spec=pltpu.PrefetchScalarGridSpec(
            num_scalar_prefetch=2,
            grid=(tiles + 1,),
            in_specs=[full(item.shape) for item in constants]
            + [
                pl.BlockSpec((toks, dim), lambda step, *_: (0, tile(step))),
                pl.BlockSpec((dim, dim), lambda step, *_: (0, tile(step))),
                pl.BlockSpec((dim, dim), lambda step, *_: (tile(step), 0)),
            ]
            + [pl.BlockSpec(memory_space=pl.ANY)] * 4,
            out_specs=[full((rows, 2, size, dim)), full((8, dim))]
            + in_specs
            + out_specs
            + small_specs,
            scratch_shapes=[
                pltpu.VMEM((toks, dim), F32),
                pltpu.VMEM((toks, dim), BF),
                pltpu.VMEM((toks, dim), F32),
                pltpu.VMEM((toks, dim), BF),
                pltpu.VMEM((toks, dim), BF),
                pltpu.VMEM((rows, size, dim), BF),
                pltpu.VMEM((dim, dim), BF),
                pltpu.SemaphoreType.DMA((4,)),
            ],
        ),
        out_shape=[
            jax.ShapeDtypeStruct((rows, 2, size, dim), BF),
            jax.ShapeDtypeStruct((8, dim), F32),
        ]
        + [jax.ShapeDtypeStruct(shape, BF) for shape in shapes],
        compiler_params=params(),
        cost_estimate=cost(
            toks * dim * (4 * hidden + 2 * dim), toks * (hidden * 4 + dim * 20) + 8 * hidden * dim
        ),
        name="feed_back",
    )(lengths, place, *constants, pre, win, wout, after, n2, att, wo)
    if split:
        mine, theirs = outs[2::2], outs[3::2]
    else:
        whole = [
            outs[2].reshape(parts, hidden // parts, dim),
            outs[3].reshape(tiles, parts, dim // parts, dim).transpose(1, 0, 2, 3),
            outs[4].reshape(2, parts, dim // parts, dim).transpose(1, 0, 2, 3),
        ]
        mine, theirs = split_core(whole)
    return outs[0], outs[1], mine, theirs


def split_core(blocks):
    core = (lax.axis_index("batch") % 2).astype(jnp.int32)
    pairs = [item.reshape((item.shape[0] // 2, 2, -1, item.shape[-1])) for item in blocks]
    pick = lambda item, place: lax.dynamic_index_in_dim(item, place, 1, keepdims=False)
    return [pick(item, core) for item in pairs], [pick(item, 1 - core) for item in pairs]


def attend_grad_kernel(parts, place_ref, n1_ref, own_ref, edge_hbm, n1_edge_hbm, *rest):
    refs, (edge_ref, n1_edge_ref, sems) = rest[:-3], rest[-3:]
    rows, _, size, dim = own_ref.shape
    step = pl.program_id(0)
    width = dim // parts if len(refs) == 2 else dim
    flat = lambda ref: ref[...].reshape(-1, dim)
    n1_copy = pltpu.make_async_copy(n1_edge_hbm.at[:, 4:6], n1_edge_ref, sems.at[0])
    copies = [
        pltpu.make_async_copy(
            edge_hbm.at[:, 3 + 2 * index : 5 + 2 * index], edge_ref.at[index], sems.at[1 + index]
        )
        for index in range(2)
    ]

    @pl.when(step == 0)
    def _():
        n1_copy.start()
        for copy in copies:
            copy.start()
        value = dot_tn(flat(own_ref), flat(n1_ref)).astype(BF)
        store_split(place_ref[1], value, refs, dim // parts, 0)
        n1_copy.wait()

    for index in range(2):

        @pl.when(step == 1 + index)
        def _():
            copies[index].wait()
            value = dot_tn(flat(own_ref), flat(n1_ref)) + dot_tn(flat(edge_ref.at[index]), flat(n1_edge_ref))
            store_split(place_ref[1], value.astype(BF), refs, dim // parts, (1 + index) * width)


def attend_grad(parts, place, own, edges, grads):
    rows, _, size, dim = own.shape
    narrow = dim // parts
    split = narrow % 16 == 0
    shape = (parts // 2, 3 * narrow, dim) if split else (3 * dim, dim)
    copies = 2 if split else 1
    outs = pl.pallas_call(
        functools.partial(attend_grad_kernel, parts),
        grid_spec=pltpu.PrefetchScalarGridSpec(
            num_scalar_prefetch=1,
            grid=(3,),
            in_specs=[
                pl.BlockSpec((rows, 1, size, dim), lambda step, *_: (0, 3, 0, 0)),
                pl.BlockSpec((rows, 1, size, dim), lambda step, *_: (0, step, 0, 0)),
                pl.BlockSpec(memory_space=pl.ANY),
                pl.BlockSpec(memory_space=pl.ANY),
            ],
            out_specs=[full(shape)] * copies,
            scratch_shapes=[
                pltpu.VMEM((2, rows, 2, size, dim), BF),
                pltpu.VMEM((rows, 2, size, dim), BF),
                pltpu.SemaphoreType.DMA((3,)),
            ],
        ),
        out_shape=[jax.ShapeDtypeStruct(shape, BF)] * copies,
        compiler_params=params(),
        cost_estimate=cost(rows * size * dim * dim * 7, rows * size * dim * 26),
        name="attend_grad",
    )(place, own, grads, grads, edges)
    if split:
        return outs[0], outs[1]
    mine, theirs = split_core([outs[0].reshape(3, parts, narrow, dim).transpose(1, 0, 2, 3)])
    return mine[0], theirs[0]


def attend_back_kernel(
    first,
    lengths_ref,
    place_ref,
    own_ref,
    pair_ref,
    across_ref,
    qkv_ref,
    edge_ref,
    p_ref,
    back_ref,
    gain_ref,
    wq_ref,
    wk_ref,
    wv_ref,
    *rest,
):
    grad_ref, part_ref, to_pair_ref, to_across_ref, offset_ref, gains_ref, mask_ref, group_ref, acc_ref = rest[-9:]
    size, dim = own_ref.shape[1:]
    heads = p_ref.shape[1]
    pairs = heads // 2
    lanes = dim // pairs
    step = pl.program_id(0)
    row = Row(lengths_ref, place_ref, step + first, size)
    mask_ref[...] = row.own.astype(F32)

    @pl.when(step == 0)
    def _():
        acc_ref[...] = jnp.zeros_like(acc_ref)
        gains_ref[...] = jnp.zeros_like(gains_ref)

    first_half = lax.broadcasted_iota(jnp.int32, (1, lanes), 1) < lanes // 2
    store_group_masks(row, group_ref)
    half_size = size // 2
    for pair in range(pairs):
        cols = slice(pair * lanes, (pair + 1) * lanes)
        keys, values = key_groups(qkv_ref, edge_ref, cols)
        q_groups = [by_group(qkv_ref[0, 0, :, cols], group_ref, half) for half in range(2)]
        o_groups = [by_group(back_ref[0, 0, :, cols], group_ref, half) for half in range(2)]
        d_q, scores_pair = [], []
        for half in range(2):
            head = 2 * pair + half
            g_probs = dot_nt(values, o_groups[half])
            full_probs = p_ref[0, head].astype(F32)
            product = full_probs * g_probs
            inner = jnp.sum(product, axis=0, keepdims=True)
            g_scores = product - full_probs * inner
            on_own = g_scores * mask_ref[...]
            off_own = g_scores - on_own
            acc_ref[head, :, :half_size] += on_own[:half_size, :half_size] + on_own[half_size:, half_size:]
            acc_ref[head, :, half_size:size] += on_own[:half_size, half_size:] + off_own[half_size:, :half_size]
            acc_ref[head, :, size : size + half_size] += off_own[:half_size, :half_size] + off_own[half_size:, half_size:]
            acc_ref[head, :, size + half_size :] += off_own[:half_size, half_size:] + on_own[half_size:, :half_size]
            scores_pair.append(g_scores.astype(BF))
            d_q.append(dot_tn(scores_pair[-1], keys))
        grad_ref[0, 0, :, cols] = fold_rows(row, first_half, d_q).astype(BF)
        probs_pair = [p_ref[0, 2 * pair], p_ref[0, 2 * pair + 1]]
        for index, (left, right) in enumerate(((scores_pair, q_groups), (probs_pair, o_groups))):
            value = dot_nn(jnp.concatenate(left, axis=1), jnp.concatenate(right, axis=0)).astype(BF)
            grad_ref[0, 3 + 2 * index, :, cols] = value[:, :lanes]
            grad_ref[0, 1 + index, :, cols] = value[:, lanes : 2 * lanes]
            grad_ref[0, 4 + 2 * index, :, cols] = value[:, 2 * lanes :]

    gain1 = gain_ref[0:1, :].astype(F32)
    g_whole = None
    for index, weight_ref in enumerate((wk_ref, wv_ref)):
        edge_grad = grad_ref[0, 3 + 2 * index : 5 + 2 * index].reshape(2 * size, dim)
        left = jnp.concatenate([edge_grad, grad_ref[0, 1 + index]], axis=0)
        term = dot_nt(left, weight_ref[...])
        g_whole = term if g_whole is None else g_whole + term
    zero = jnp.zeros((size, dim), F32)
    g_low = where_tiles(row.slot_low, g_whole[:size], zero)
    g_high = where_tiles(row.slot_high, g_whole[size : 2 * size], zero)
    g_own = g_whole[2 * size :] + (g_whole[:size] - g_low) + (g_whole[size : 2 * size] - g_high)
    g_own = g_own + dot_nt(grad_ref[0, 0], wq_ref[...])
    gain_1 = jnp.zeros((1, dim), F32)
    low, high = by_side(place_ref, pair_ref[0], across_ref[0])
    results = []
    for source, g_norm in ((own_ref[0], g_own), (low, g_low), (high, g_high)):
        x = source.astype(F32)
        scale = rms_scale(x)
        gain_1 = gain_1 + jnp.sum(g_norm * x * scale, axis=0, keepdims=True)
        results.append(rms_back(x, scale, g_norm * gain1))
    part_ref[0] = (results[0] + back_ref[0, 1].astype(F32)).astype(BF)
    odd = place_ref[0] % 2 == 1
    to_pair_ref[0] = jnp.where(odd, results[1], results[2]).astype(BF)
    to_across_ref[0] = jnp.where(odd, results[2], results[1]).astype(BF)
    gains_ref[0:1, :] += gain_1

    @pl.when(step == pl.num_programs(0) - 1)
    def _():
        for head in range(heads):
            offset_ref[head] = fold_offsets(acc_ref[head])


def attend_back(first, count, halo, earlier, lengths, place, x, low, high, own, edges, p, back, gains, weights):
    rows, size, dim = x.shape
    heads = p.shape[1]
    constants = (gains,) + tuple(weights)
    start = 2 + 7 + len(constants)
    aliases = {start + index: index for index in range(len(earlier))}
    return pl.pallas_call(
        functools.partial(attend_back_kernel, first),
        grid_spec=pltpu.PrefetchScalarGridSpec(
            num_scalar_prefetch=2,
            grid=(count,),
            in_specs=[row_spec((size, dim), first)] * 3
            + [row_spec((3, size, dim), first), row_spec((4, size, dim), first)]
            + [row_spec((heads, size, size), first), row_spec((2, size, dim), first)]
            + [full(item.shape) for item in constants]
            + [pl.BlockSpec(memory_space=pl.ANY)] * len(earlier),
            out_specs=[
                row_spec((7, size, dim), first),
                row_spec((size, dim), first),
                row_spec((size, dim), first - halo[0]),
                row_spec((size, dim), first - halo[0]),
            ]
            + [full((heads, 8, 2 * size)), full((8, dim))],
            scratch_shapes=[
                pltpu.VMEM((size, size), F32),
                pltpu.VMEM((2, 3, size, 2 * dim // heads), BF),
                pltpu.VMEM((heads, size // 2, 2 * size), F32),
            ],
        ),
        out_shape=[
            jax.ShapeDtypeStruct((rows, 7, size, dim), BF),
            jax.ShapeDtypeStruct((rows, size, dim), BF),
            jax.ShapeDtypeStruct((halo[1], size, dim), BF),
            jax.ShapeDtypeStruct((halo[1], size, dim), BF),
            jax.ShapeDtypeStruct((heads, 8, 2 * size), F32),
            jax.ShapeDtypeStruct((8, dim), F32),
        ],
        input_output_aliases=aliases,
        compiler_params=params(),
        cost_estimate=cost(
            count * size * dim * (9 * dim + 128 * size), count * size * dim * 60
        ),
        name="attend_back_rows",
    )(lengths, place, x, low, high, own, edges, p, back, *constants, *earlier)


def flip(block, axis, bit):
    count = lax.axis_size(axis)
    return lax.ppermute(block, axis, [(i, i ^ bit) for i in range(count)])


def sum_along(block, axis):
    bit = 1
    while bit < lax.axis_size(axis):
        block = block + flip(block, axis, bit)
        bit *= 2
    return block


def bit_places(axis):
    return [1 << level for level in range((lax.axis_size(axis) - 1).bit_length())]


def gather_batch(block):
    place = lax.axis_index("batch")
    bits = bit_places("batch")
    gathered = block[None]
    for bit in reversed(bits):
        other = flip(gathered, "batch", bit)
        upper = (place & bit) > 0
        gathered = jnp.stack(
            [jnp.where(upper, other, gathered), jnp.where(upper, gathered, other)], axis=1
        )
        gathered = gathered.reshape((-1,) + block.shape)
    return gathered.reshape((-1,) + block.shape[1:])


def halve(block, bits, bit):
    axis = bits.index(bit)
    mine = ((lax.axis_index("batch") & bit) > 0).astype(jnp.int32)
    send = lax.dynamic_index_in_dim(block, 1 - mine, axis, keepdims=False)
    keep = lax.dynamic_index_in_dim(block, mine, axis, keepdims=False)
    return keep + flip(send, "batch", bit), [item for item in bits if item != bit]


def after(value, *others):
    return lax.optimization_barrier((value,) + tuple(others))[0]


def stage_kernel(groups, place_ref, *refs):
    ins = refs[: 2 * sum(len(group) for group in groups)]
    outs = refs[len(ins) :]
    taken = 0
    for index, group in enumerate(groups):
        first = 0
        for count in group:
            value = ins[2 * taken][0, 0, 0] + ins[2 * taken + 1][0, 0, 0]
            taken += 1
            for which in range(2):

                @pl.when(pl.program_id(0) == which)
                def _():
                    outs[2 * index + which][0, 0, first : first + count, :] = value

            first += count


def stage(place, groups, bits, pieces):
    columns = groups[0][0][0].shape[-1]
    lead = bits[0][0][0] * bits[0][0][1]
    if any(count % (16 * pieces) or first % count for group in groups for _, _, first, count in group):
        sends, keeps = [], []
        for index, group in enumerate(groups):
            before, behind = bits[index][0]
            total = jnp.concatenate(
                [(kept + arrived)[..., first : first + count, :].reshape(-1, count, columns)
                 for kept, arrived, first, count in group],
                axis=1,
            ).reshape(before, 2, behind, -1, columns)
            pick = lambda which: lax.dynamic_index_in_dim(total, which, 1, keepdims=False)
            sends.append(pick(1 - place[index]).reshape(lead, 1, -1, columns))
            keeps.append(pick(place[index]).reshape(lead, 1, -1, columns))
        return sends, keeps
    in_specs, operands, out_specs, shapes = [], [], [], []
    for index, group in enumerate(groups):
        before, behind = bits[index][0]
        total = 0

        def place_of(half, step, chunk, places, index=index, behind=behind):
            mine = places[index]
            where_at = jnp.where(half == 0, 1 - mine, mine)
            return step // behind, where_at, step % behind, chunk

        for kept, arrived, first, count in group:
            rows = count // pieces
            total += rows
            shape = (before, 2, behind) + kept.shape[-2:]

            def index_map(half, step, chunk, places, place_of=place_of, first=first, rows=rows):
                one, two, three, four = place_of(half, step, chunk, places)
                return one, two, three, four + first // rows, 0

            for item in (kept, arrived):
                in_specs.append(pl.BlockSpec((1, 1, 1, rows, columns), index_map))
                operands.append(item.reshape(shape))
        for which in range(2):

            def out_map(half, step, chunk, places, which=which):
                if which == 0:
                    step = jnp.where(half == 0, step, lead - 1)
                    chunk = jnp.where(half == 0, chunk, pieces - 1)
                else:
                    step = jnp.where(half == 1, step, 0)
                    chunk = jnp.where(half == 1, chunk, 0)
                return step, chunk, 0, 0

            out_specs.append(pl.BlockSpec((1, 1, total, columns), out_map))
            shapes.append(jax.ShapeDtypeStruct((lead, pieces, total, columns), BF))
    outs = pl.pallas_call(
        functools.partial(
            stage_kernel, [[count // pieces for _, _, _, count in group] for group in groups]
        ),
        grid_spec=pltpu.PrefetchScalarGridSpec(
            num_scalar_prefetch=1, grid=(2, lead, pieces), in_specs=in_specs, out_specs=out_specs
        ),
        out_shape=shapes,
        compiler_params=pltpu.CompilerParams(
            vmem_limit_bytes=VMEM_BYTES, dimension_semantics=("arbitrary",) * 3
        ),
        name="halving_stage",
    )(place, *operands)
    return outs[0::2], outs[1::2]


class BatchSum:
    def __init__(self, mine, theirs, streams):
        bits = bit_places("batch")
        arrived = [flip(item, "batch", bits[0]) for item in theirs]
        self.groups = [
            [(mine[item], arrived[item], first, rows) for item, first, rows in stream] for stream in streams
        ]
        self.bits = [bits[1:][::-1]] * len(streams)
        self.steps = len(bits) - 1
        self.done = 0

    def hold(self, *others):
        self.groups = [
            [(kept, after(arrived, *others), first, rows) for kept, arrived, first, rows in group]
            for group in self.groups
        ]

    def advance(self):
        moved, bits, places = [], [], []
        me = lax.axis_index("batch")
        for index, left in enumerate(self.bits):
            bit = left[::-1][index % len(left)]
            axis = left.index(bit)
            moved.append(bit)
            places.append(((me & bit) > 0).astype(jnp.int32))
            bits.append(((1 << axis, 1 << (len(left) - 1 - axis)),))
        sends, keeps = stage(jnp.stack(places), self.groups, bits, 1)
        self.groups = [
            [(keep, flip(send, "batch", bit), 0, keep.shape[2])]
            for keep, send, bit in zip(keeps, sends, moved)
        ]
        self.bits = [[item for item in left if item != bit] for left, bit in zip(self.bits, moved)]
        self.done += 1
        return sends

    def total(self):
        return [(kept + arrived).reshape(kept.shape[-2:]) for ((kept, arrived, _, _),) in self.groups]


def pack_kernel(tiles_rows, keep_a, come_a, keep_b, come_b, out_ref):
    groups, _, wide = out_ref.shape
    cols = wide // 2
    rows = tiles_rows // groups
    first = keep_a[...] + come_a[...]
    second = keep_b[...] + come_b[...]
    for group in range(groups):
        here = slice(group * cols, (group + 1) * cols)
        out_ref[group, :, :cols] = first[:, here]
        for part in range(groups):
            out_ref[group, part * rows : (part + 1) * rows, cols:] = second[
                group * rows : (group + 1) * rows, part * cols : (part + 1) * cols
            ]
        out_ref[group, tiles_rows:, cols:] = second[tiles_rows:, here]


def pack(stream_a, stream_b, tiles_rows, groups):
    (keep_a, come_a), (keep_b, come_b) = stream_a, stream_b
    rows, dim = keep_a.shape[-2:]
    flat = lambda item: item.reshape(rows, dim)
    shape = (groups, rows, 2 * dim // groups)
    if tiles_rows // groups % 16 == 0:
        return pl.pallas_call(
            functools.partial(pack_kernel, tiles_rows),
            out_shape=jax.ShapeDtypeStruct(shape, BF),
            compiler_params=pltpu.CompilerParams(vmem_limit_bytes=VMEM_BYTES),
            name="pack_places",
        )(flat(keep_a), flat(come_a), flat(keep_b), flat(come_b))
    first = flat(keep_a + come_a).reshape(rows, groups, -1).transpose(1, 0, 2)
    second = flat(keep_b + come_b)
    out = second[:tiles_rows].reshape(groups, -1, groups, dim // groups).transpose(0, 2, 1, 3)
    out = out.reshape(groups, tiles_rows, -1)
    last = second[tiles_rows:].reshape(-1, groups, dim // groups).transpose(1, 0, 2)
    return jnp.concatenate([first, jnp.concatenate([out, last], axis=1)], axis=2)


def columns_kernel(keep_a, come_a, keep_b, come_b, out_ref):
    groups, rows, cols = out_ref.shape
    half = keep_a.shape[0]
    first = keep_a[...] + come_a[...]
    second = keep_b[...] + come_b[...]
    for group in range(groups):
        here = slice(group * cols, (group + 1) * cols)
        out_ref[group, :half, :] = first[:, here]
        out_ref[group, half:, :] = second[:, here]


def pack_columns(streams, groups):
    rows, dim = streams[0][0].shape[-2:]
    pieces = [item.reshape(rows, dim) for keep, come in streams for item in (keep, come)]
    if rows % 16:
        total = jnp.concatenate([pieces[0] + pieces[1], pieces[2] + pieces[3]], axis=0)
        return total.reshape(2 * rows, groups, -1).transpose(1, 0, 2)
    return pl.pallas_call(
        columns_kernel,
        out_shape=jax.ShapeDtypeStruct((groups, 2 * rows, dim // groups), BF),
        compiler_params=pltpu.CompilerParams(vmem_limit_bytes=VMEM_BYTES),
        name="pack_columns",
    )(*pieces)


def split_dot(dot, left, right):
    return dot(left[0], right[0]) + (dot(left[0], right[1]) + dot(left[1], right[0]))


def embed_kernel(sum_ref, more_ref, count_ref, proj_ref, pooled_ref, emb_ref, inverse_ref):
    pooled = (sum_ref[...] + more_ref[...]) / count_ref[...]
    high, low = split_bf(pooled)
    raw = dot_nn(high, proj_ref[...]) + dot_nn(low, proj_ref[...])
    inverse = lax.rsqrt(jnp.sum(raw * raw, axis=-1, keepdims=True) + EPS)
    pooled_ref[...] = pooled
    emb_ref[...] = raw * inverse
    inverse_ref[...] = jnp.broadcast_to(inverse, inverse_ref.shape)


def embed(sums, more, counts, w_proj):
    own, dim = sums.shape
    shapes = ((own, dim), (own, dim), (own, LANES))
    return pl.pallas_call(
        embed_kernel,
        out_shape=[jax.ShapeDtypeStruct(shape, F32) for shape in shapes],
        compiler_params=pltpu.CompilerParams(vmem_limit_bytes=VMEM_BYTES),
        name="embed",
    )(sums, more, counts, w_proj)


def contrast_kernel(
    place_ref,
    own_ref,
    x_ref,
    y_ref,
    xy_ref,
    other_ref,
    inverse_ref,
    partner_ref,
    count_ref,
    proj_ref,
    loss_ref,
    graw_ref,
    pool_ref,
    all_ref,
    logit_ref,
):
    own, dim = own_ref.shape
    total = all_ref.shape[0]
    me = place_ref[0]
    rows_of = lambda place: pl.ds(pl.multiple_of(place * own, own), own)
    for step, ref in enumerate((own_ref, x_ref, y_ref, xy_ref)):
        place = jnp.bitwise_xor(me, 2 * step)
        all_ref[rows_of(place), :] = ref[...]
        all_ref[rows_of(jnp.bitwise_xor(place, 1)), :] = other_ref[step]
    everyone = split_bf(all_ref[...])
    logits = SHARPNESS * split_dot(dot_nt, everyone, everyone)
    row = lax.broadcasted_iota(jnp.int32, (total, total), 0)
    column = lax.broadcasted_iota(jnp.int32, (total, total), 1)
    logits = jnp.where(row == column, NEGATIVE, logits)
    logit_ref[...] = logits
    peak = jnp.max(logits, axis=0, keepdims=True)
    lse_all = peak + jnp.log(jnp.sum(jnp.exp(logits - peak), axis=0, keepdims=True))
    mine = logit_ref[rows_of(me), :]
    peak = jnp.max(mine, axis=1, keepdims=True)
    lse_own = peak + jnp.log(jnp.sum(jnp.exp(mine - peak), axis=1, keepdims=True))
    target = (lax.broadcasted_iota(jnp.int32, (own, total), 1) == partner_ref[...]).astype(F32)
    loss = lse_own - jnp.sum(jnp.where(target > 0, mine, 0.0), axis=1, keepdims=True)
    loss_ref[...] = jnp.broadcast_to(loss, loss_ref.shape)
    both = SHARPNESS * (jnp.exp(mine - lse_own) + jnp.exp(mine - lse_all) - 2.0 * target)
    grad = split_dot(dot_nn, split_bf(both), everyone)
    emb = own_ref[...]
    grad = inverse_ref[:, :1] * (grad - emb * jnp.sum(emb * grad, axis=1, keepdims=True))
    graw_ref[...] = grad
    high, low = split_bf(grad)
    pool_ref[...] = (dot_nt(high, proj_ref[...]) + dot_nt(low, proj_ref[...])) / count_ref[...]


def contrast_near(embedded, inverse, partner, counts, w_proj):
    own, dim = embedded.shape
    total = own * lax.axis_size("batch")
    parts = [embedded] + [flip(embedded, "batch", bits) for bits in (2, 4, 6)]
    other = flip(jnp.stack(parts), "batch", 1)
    me = lax.axis_index("batch").astype(jnp.int32).reshape(1)
    constants = (*parts, other, inverse, partner.reshape(own, 1), counts, w_proj)
    loss, graw, pool = pl.pallas_call(
        contrast_kernel,
        grid_spec=pltpu.PrefetchScalarGridSpec(
            num_scalar_prefetch=1,
            grid=(1,),
            in_specs=[full(item.shape) for item in constants],
            out_specs=[full((own, LANES)), full((own, dim)), full((own, dim))],
            scratch_shapes=[pltpu.VMEM((total, dim), F32), pltpu.VMEM((total, total), F32)],
        ),
        out_shape=[
            jax.ShapeDtypeStruct((own, LANES), F32),
            jax.ShapeDtypeStruct((own, dim), F32),
            jax.ShapeDtypeStruct((own, dim), F32),
        ],
        compiler_params=params(),
        name="contrast",
    )(me, *constants)
    return loss[:, 0], graw, pool


def finish_kernel(count, width, *refs):
    total = sum(ref[...].astype(F32) for ref in refs[:-count])
    for index, ref in enumerate(refs[-count:]):
        ref[...] = total[index * width : (index + 1) * width, :].T


def finish(pieces, count, width):
    cols = pieces[0].shape[1]
    return pl.pallas_call(
        functools.partial(finish_kernel, count, width),
        out_shape=[jax.ShapeDtypeStruct((cols, width), F32)] * count,
        compiler_params=pltpu.CompilerParams(vmem_limit_bytes=VMEM_BYTES),
        name="finish",
    )(*pieces)


def contrast(embedded, inv_norm, w_proj, partner):
    proj = w_proj.astype(F32)
    everyone = gather_batch(embedded)
    own_count = embedded.shape[0]
    total = everyone.shape[0]
    own_index = lax.axis_index("batch") * own_count + jnp.arange(own_count, dtype=jnp.int32)
    columns = jnp.arange(total, dtype=jnp.int32)

    def lse_of(rows, index):
        logits = SHARPNESS * jnp.einsum("nd,md->nm", rows, everyone, precision=HIGHEST)
        logits = jnp.where(columns[None, :] == index[:, None], NEGATIVE, logits)
        peak = jnp.max(logits, axis=-1, keepdims=True)
        return peak[:, 0] + jnp.log(jnp.sum(jnp.exp(logits - peak), axis=-1))

    if total <= 1024:
        lse_all = lse_of(everyone, columns)
    else:
        lse_all = lax.map(
            lambda pieces: lse_of(pieces[0], pieces[1]),
            (everyone.reshape(-1, 512, everyone.shape[1]), columns.reshape(-1, 512)),
        ).reshape(-1)
    logits = SHARPNESS * jnp.einsum("nd,md->nm", embedded, everyone, precision=HIGHEST)
    is_self = columns[None, :] == own_index[:, None]
    logits = jnp.where(is_self, NEGATIVE, logits)
    peak = jnp.max(logits, axis=-1, keepdims=True)
    lse_own = peak[:, 0] + jnp.log(jnp.sum(jnp.exp(logits - peak), axis=-1))
    is_target = columns[None, :] == partner[:, None]
    picked = jnp.sum(jnp.where(is_target, logits, 0.0), axis=-1)
    loss = lse_own - picked
    both = SHARPNESS * (
        jnp.exp(logits - lse_own[:, None])
        + jnp.exp(logits - lse_all[None, :])
        - 2.0 * is_target.astype(F32)
    )
    grad_emb = jnp.dot(both, everyone, precision=HIGHEST)
    grad_raw = inv_norm * (
        grad_emb - embedded * jnp.sum(embedded * grad_emb, axis=-1, keepdims=True)
    )
    grad_pooled = jnp.einsum("ne,de->nd", grad_raw, proj, precision=HIGHEST)
    return loss, grad_raw, grad_pooled


def shards(
    tokens,
    norm1_gain,
    w_query,
    w_key,
    w_value,
    rel_bias,
    w_output,
    norm2_gain,
    w_in,
    w_out,
    final_gain,
    w_proj,
    lengths,
    partner,
    cotangent,
):
    rows, size, dim = tokens.shape
    slots = lengths.shape[1]
    toks = rows * size
    seq_count = lax.axis_size("seq")
    seq_place = lax.axis_index("seq")
    place = seq_place.astype(jnp.int32).reshape(1)
    pairs = [(i, i ^ 1) for i in range(seq_count)]
    across = [(i, i - 1 if i % 2 == 0 else i + 1) for i in range(1, seq_count - 1)]
    gains = jnp.stack([norm1_gain, norm2_gain, final_gain])

    half_rows = rows // 2 if rows > 1 else rows
    bounds = [(first, min(first + half_rows, rows)) for first in range(0, rows, half_rows)]
    sides = []
    for first, last in bounds:
        piece = tokens[first:last]
        if sides:
            piece = after(piece, *sides[-1])
        sides.append((lax.ppermute(piece, "seq", pairs), lax.ppermute(piece, "seq", across)))
    bias = bias_tables(rel_bias, size)
    own = own_projections(tokens, norm1_gain.reshape(1, dim), (w_query, w_key, w_value))
    attended = ()
    for (first, _), (pair_part, across_part) in zip(bounds, sides):
        attended = tuple(
            attend(
                first, attended, lengths, place, pair_part, across_part, own, gains, w_key, w_value, bias
            )
        )
    edges, p, att = attended
    block, partial, pre, after_attn, n2 = forward(
        lengths, place, tokens, att, gains, w_output, w_in, w_out
    )
    x_pair, x_across = (
        jnp.concatenate([side[index] for side in sides], axis=0) for index in range(2)
    )
    counts = lengths.astype(F32).reshape(rows * slots, 1)
    partial = partial.reshape(rows * slots, dim)
    seq_bits = bit_places("seq")
    for bit in seq_bits[:-1]:
        partial = partial + flip(partial, "seq", bit)
    arrived = flip(partial, "seq", seq_bits[-1])
    partial = after(partial, x_pair, x_across)
    pooled, embedded, inverse = embed(partial, arrived, counts, w_proj)
    if lax.axis_size("batch") == 8:
        loss, grad_raw, pool_grad = contrast_near(embedded, inverse, partner, counts, w_proj)
    else:
        loss, grad_raw, grad_pooled = contrast(embedded, inverse[:, :1], w_proj, partner)
        pool_grad = grad_pooled / counts
    pool_grad = pool_grad.reshape(rows, slots, dim)
    batch_count = lax.axis_size("batch")
    place = jnp.stack([seq_place, lax.axis_index("batch") % 2]).astype(jnp.int32)

    back, gains_a, mine, theirs = feed_back(
        batch_count,
        lengths,
        place,
        block,
        after_attn,
        cotangent,
        att,
        n2,
        pre,
        pool_grad,
        grad_raw,
        pooled,
        gains,
        (w_output, w_in, w_out),
    )
    hidden = w_in.shape[1]
    width = dim // batch_count
    tiles = hidden // dim
    wide = hidden // batch_count
    feed_sum = BatchSum(
        mine,
        theirs,
        (((0, 0, wide), (2, 0, width)), ((1, 0, tiles * width), (2, width, width))),
    )
    segments = [(0, 1), (1, rows - 2), (rows - 1, 1)] if rows > 2 else [(0, rows)]
    halves, from_pair, from_across = [], [], []
    earlier = ()
    for first, count in segments:
        if halves and feed_sum.done < feed_sum.steps:
            place = after(place, *feed_sum.advance())
        halves.append(
            attend_back(
                first,
                count,
                (0, rows - 1) if first + count < rows else (first, count),
                earlier,
                lengths,
                place,
                tokens,
                x_pair,
                x_across,
                own,
                edges,
                p,
                back,
                gains,
                (w_query, w_key, w_value),
            )
        )
        feed_sum.hold(halves[-1][5])
        earlier = tuple(halves[-1][:4])
        if first + count >= rows - 1:
            from_pair.append(lax.ppermute(halves[-1][2], "seq", pairs))
            from_across.append(lax.ppermute(halves[-1][3], "seq", across))
            earlier = earlier[:2]
    grads, part = earlier
    while feed_sum.done < feed_sum.steps:
        place = after(place, *feed_sum.advance())

    feed_part = pack(
        *[(group[0][0], group[0][1]) for group in feed_sum.groups], tiles * width, seq_count
    )
    grad_rel = bias_grad([item[4] for item in halves], rel_bias.shape[0])
    gain1_grad = sum(item[5][0] for item in halves)
    small = jnp.concatenate([gain1_grad, gains_a[1], gains_a[0], grad_rel.reshape(-1)])
    small = jnp.pad(small, (0, -small.shape[0] % 1024)).reshape(-1, 128)
    batch_bits = bit_places("batch")
    arrived = flip(small, "seq", seq_bits[0])
    place = after(place, feed_part, small, *from_pair, *from_across)
    attend_mine, attend_theirs = attend_grad(batch_count, place, own, edges, grads)
    feed_done = lax.psum_scatter(feed_part, "seq", scatter_dimension=0, tiled=True)[0]
    half = 3 * width // 2
    attend_sum = BatchSum([attend_mine], [attend_theirs], (((0, 0, half),), ((0, half, 3 * width - half),)))
    small = after(small, attend_mine) + arrived
    arrived = flip(small, "batch", batch_bits[0])
    attend_sum.hold(arrived)
    for bit in batch_bits[1:]:
        sends = attend_sum.advance()
        small = after(small, *sends) + arrived
        arrived = flip(small, "batch", bit)
        attend_sum.hold(arrived)
    attend_parts = pack_columns([group[0][:2] for group in attend_sum.groups], seq_count)
    small = after(small, attend_parts) + arrived
    came = [lax.dynamic_index_in_dim(attend_parts, seq_place, 0, keepdims=False)]
    for distance in range(1, seq_count):
        route = [(i, (i + distance) % seq_count) for i in range(seq_count)]
        target = (seq_place + distance) % seq_count
        send = lax.dynamic_index_in_dim(attend_parts, target, 0, keepdims=False)
        came.append(lax.ppermute(send, "seq", route))
    sent = came[0]
    for bit in seq_bits[1:]:
        small = small + flip(small, "seq", bit)
    small = small.reshape(-1)
    gain_sums = [small[i * dim : (i + 1) * dim] for i in range(3)]
    rel_sum = small[3 * dim : 3 * dim + rel_bias.size].reshape(rel_bias.shape)

    grad_tokens = (
        after(part, sent).astype(F32)
        + jnp.concatenate(from_pair, axis=0).astype(F32)
        + jnp.concatenate(from_across, axis=0).astype(F32)
    )
    turn = lambda array: array.T.astype(F32)
    cols = dim // seq_count
    s_in = turn(feed_done[:wide, :cols])
    s_output = turn(feed_done[wide:, :cols])
    s_out = feed_done[:-width, cols:].reshape(seq_count, width, cols)
    s_out = s_out.transpose(0, 2, 1).reshape(dim, width).astype(F32)
    s_proj = turn(feed_done[-width:, cols:])
    came[0] = after(came[0], s_in, s_output, s_out, s_proj, grad_tokens)
    s_attend = finish(came, 3, width)
    return (
        block,
        embedded,
        loss,
        grad_tokens,
        gain_sums[0],
        s_attend[0],
        s_attend[1],
        s_attend[2],
        rel_sum,
        s_output,
        gain_sums[1],
        s_in,
        s_out,
        gain_sums[2],
        s_proj,
    )


def solution(mesh):
    tok = P("batch", "seq", None)
    mat = P("seq", "batch")
    return jax.shard_map(
        shards,
        mesh=mesh,
        in_specs=(tok,) + (P(),) * 11 + (P("batch", None), P("batch"), tok),
        out_specs=(
            tok,
            P("batch", None),
            P("batch"),
            tok,
            P(),
            mat,
            mat,
            mat,
            P(),
            mat,
            P(),
            mat,
            mat,
            P(),
            mat,
        ),
        check_vma=False,
    )
```

```python
import functools

import jax
import jax.numpy as jnp
from jax import lax
from jax.experimental import pallas as pl
from jax.experimental.pallas import tpu as pltpu
from jax.sharding import PartitionSpec as P

EPS = 1e-06
NEGATIVE = -1e30
SHARPNESS = 50.0
THRESHOLDS = (12, 16, 23, 32, 46, 64, 91)
HIGHEST = lax.Precision.HIGHEST
BF = jnp.bfloat16
F32 = jnp.float32
VMEM_BYTES = 63 * 1024 * 1024
GELU_A = 0.7978845608028654
GELU_B = 0.044715
LANES = 128


def dot_nn(left, right):
    return lax.dot_general(left, right, (((1,), (0,)), ((), ())), preferred_element_type=F32)


def dot_nt(left, right):
    return lax.dot_general(left, right, (((1,), (1,)), ((), ())), preferred_element_type=F32)


def dot_tn(left, right):
    return lax.dot_general(left, right, (((0,), (0,)), ((), ())), preferred_element_type=F32)


def rms_scale(values):
    return lax.rsqrt(jnp.mean(values * values, axis=-1, keepdims=True) + EPS)


def rms_back(values, scale, grad_normed):
    inner = jnp.mean(grad_normed * values, axis=-1, keepdims=True)
    return scale * (grad_normed - values * (scale * scale * inner))


def split_bf(values):
    high = values.astype(BF)
    return high, (values - high.astype(F32)).astype(BF)


def bucket_of(offset):
    distance = jnp.abs(offset)
    beyond = jnp.zeros_like(distance)
    for threshold in THRESHOLDS:
        beyond = beyond + (distance >= threshold).astype(jnp.int32)
    within = jnp.where(distance < 8, distance, 8 + beyond)
    return within + 16 * (offset > 0).astype(jnp.int32)


def wrapped_offsets(shape, axis, size):
    place = lax.broadcasted_iota(jnp.int32, shape, axis)
    return jnp.where(place < size, place, place - 2 * size)


def full(shape):
    return pl.BlockSpec(shape, lambda *_: (0,) * len(shape), pipeline_mode=pl.Buffered(1))


def row_spec(shape, first=0):
    return pl.BlockSpec(
        (1,) + tuple(shape), lambda step, *_: (step + first,) + (0,) * len(shape)
    )


def cost(products, moved, exps=0):
    return pl.CostEstimate(flops=2 * products, bytes_accessed=moved, transcendentals=exps)


def params(limit=VMEM_BYTES):
    return pltpu.CompilerParams(
        vmem_limit_bytes=limit, dimension_semantics=("arbitrary",)
    )


def bias_kernel(size, table_ref, out_ref):
    buckets, heads = table_ref.shape
    hot = (
        lax.broadcasted_iota(jnp.int32, (buckets, 2 * size), 0)
        == bucket_of(-wrapped_offsets((buckets, 2 * size), 1, size))
    ).astype(BF)
    by_offset = dot_tn(table_ref[...], hot)
    for head in range(heads):
        line = jnp.broadcast_to(by_offset[head : head + 1, :], (size, 2 * size))
        out_ref[head] = pltpu.roll(line, 0, 1, stride=1, stride_axis=0).astype(BF)


def bias_tables(rel_bias, size):
    heads = rel_bias.shape[1]
    return pl.pallas_call(
        functools.partial(bias_kernel, size),
        out_shape=jax.ShapeDtypeStruct((heads, size, 2 * size), BF),
        compiler_params=pltpu.CompilerParams(vmem_limit_bytes=VMEM_BYTES),
    )(rel_bias)


def fold_offsets(rows):
    count, width = rows.shape
    while count > 8:
        count = count // 2
        rows = rows[:count] + pltpu.roll(rows[count:], width - count, 1)
    return rows


def bias_grad_kernel(heads, *refs):
    acc_refs, out_ref = refs[:-1], refs[-1]
    rows = sum(acc_ref[...] for acc_ref in acc_refs)
    width = rows.shape[1]
    buckets = out_ref.shape[1]
    place = lax.broadcasted_iota(jnp.int32, rows.shape, 0)
    for bit in (4, 2, 1):
        rows = jnp.where((place & bit) > 0, pltpu.roll(rows, width - bit, 1), rows)
    hot = (
        lax.broadcasted_iota(jnp.int32, (width, buckets), 1)
        == bucket_of(-wrapped_offsets((width, buckets), 0, width // 2))
    ).astype(BF)
    first, rest = split_bf(rows)
    second, third = split_bf(rows - first.astype(F32))
    table = dot_nn(first, hot) + dot_nn(second, hot) + dot_nn(third, hot)
    for head in range(heads):
        out_ref[head : head + 1, :] = jnp.sum(table[8 * head : 8 * head + 8], axis=0, keepdims=True)


def bias_grad(accs, buckets):
    heads, _, width = accs[0].shape
    out = pl.pallas_call(
        functools.partial(bias_grad_kernel, heads),
        out_shape=jax.ShapeDtypeStruct((heads, buckets), F32),
        compiler_params=pltpu.CompilerParams(vmem_limit_bytes=VMEM_BYTES),
        name="bias_grad",
    )(*[acc.reshape(heads * 8, width) for acc in accs])
    return out.T


class Row:
    def __init__(self, lengths_ref, place_ref, row, size):
        slots = lengths_ref.shape[1]
        base = place_ref[0] * size
        pos = base + lax.broadcasted_iota(jnp.int32, (1, size), 1)
        zero = jnp.int32(0)
        before, first, last, beyond = zero, zero, zero, zero
        own = jnp.zeros((1, size), jnp.int32)
        low = jnp.zeros((1, size), jnp.int32)
        high = jnp.zeros((1, size), jnp.int32)
        end = zero
        passed = lambda end, place: (end <= place).astype(jnp.int32)
        for slot in range(slots):
            end = end + lengths_ref[row, slot]
            before += passed(end, base - 1)
            first += passed(end, base)
            last += passed(end, base + size - 1)
            beyond += passed(end, base + size)
            own += passed(end, pos)
            low += passed(end, pos - size)
            high += passed(end, pos + size)
        before = jnp.where(base == 0, -1, before).astype(F32)
        low = jnp.where(pos < size, -1, low).astype(F32)
        own = own.astype(F32)
        col_own, col_low, col_high = (
            jnp.broadcast_to(item, (LANES, size)).T for item in (own, low, high.astype(F32))
        )
        self.in_low = col_own == before
        self.in_high = col_own == beyond.astype(F32)
        self.slot_low = col_low == first.astype(F32)
        self.slot_high = col_high == last.astype(F32)
        key = lax.broadcasted_iota(jnp.int32, (size, size), 0)
        query = lax.broadcasted_iota(jnp.int32, (size, size), 1)
        wide = lambda item: jnp.concatenate([item] * (size // LANES), axis=1)
        self.own = wide(col_own) == own
        self.alt = jnp.where(key > query, wide(col_low), jnp.where(key < query, wide(col_high), -2.0)) == own


def where_tiles(mask, left, right):
    lanes = mask.shape[1]
    return jnp.concatenate(
        [
            jnp.where(mask, left[:, start : start + lanes], right[:, start : start + lanes])
            for start in range(0, left.shape[1], lanes)
        ],
        axis=1,
    )


def store_group_masks(row, ref):
    _, _, size, lanes = ref.shape
    first = lax.broadcasted_iota(jnp.int32, (1, lanes), 1) < lanes // 2
    low = row.in_low.astype(F32)
    high = row.in_high.astype(F32)
    for part, group in enumerate((low, 1.0 - low - high, high)):
        ref[0, part] = jnp.where(first, group, 0.0).astype(BF)
        ref[1, part] = jnp.where(first, 0.0, group).astype(BF)


def by_group(pair, ref, half):
    return jnp.concatenate([pair * ref[half, part] for part in range(3)], axis=1)


def fold_rows(row, first, wide):
    lanes = wide[0].shape[1] // 3
    parts = [
        jnp.where(first, wide[0][:, here], wide[1][:, here])
        for here in (slice(part * lanes, (part + 1) * lanes) for part in range(3))
    ]
    return jnp.where(row.in_low, parts[0], jnp.where(row.in_high, parts[2], parts[1]))


def own_kernel(x_ref, gain1_ref, wq_ref, wk_ref, wv_ref, out_ref):
    x = x_ref[0].astype(F32)
    out_ref[0, 3] = (x * rms_scale(x) * gain1_ref[...].astype(F32)).astype(BF)
    for index, weight_ref in enumerate((wq_ref, wk_ref, wv_ref)):
        out_ref[0, index] = dot_nn(out_ref[0, 3], weight_ref[...]).astype(BF)


def own_projections(tokens, gain1, weights):
    rows, size, dim = tokens.shape
    constants = (gain1,) + tuple(weights)
    return pl.pallas_call(
        own_kernel,
        grid=(rows,),
        in_specs=[row_spec((size, dim))] + [full(item.shape) for item in constants],
        out_specs=row_spec((4, size, dim)),
        out_shape=jax.ShapeDtypeStruct((rows, 4, size, dim), BF),
        compiler_params=params(),
        cost_estimate=cost(3 * rows * size * dim * dim, rows * size * dim * 10),
        name="own_projections",
    )(tokens, *constants)


def row_sentences(lengths_ref, place_ref, row, size):
    where_pos = place_ref[0] * size + lax.broadcasted_iota(jnp.int32, (1, size), 1)
    found = jnp.zeros((1, size), jnp.int32)
    end = jnp.int32(0)
    for slot in range(lengths_ref.shape[1]):
        end = end + lengths_ref[row, slot]
        found = found + (end <= where_pos).astype(jnp.int32)
    return found


def attend_kernel(
    first,
    lengths_ref,
    place_ref,
    pair_ref,
    across_ref,
    own_ref,
    gains_ref,
    wk_ref,
    wv_ref,
    bias_hbm,
    *rest,
):
    edge_ref, p_ref, att_ref, mask_ref, group_ref, bias_ref, sem = rest[-7:]
    size, dim = pair_ref.shape[1:]
    copy = pltpu.make_async_copy(bias_hbm, bias_ref, sem)

    @pl.when(pl.program_id(0) == 0)
    def _():
        copy.start()

    heads = bias_ref.shape[0]
    pairs = heads // 2
    lanes = dim // pairs
    row = Row(lengths_ref, place_ref, pl.program_id(0) + first, size)
    mask_ref[0] = jnp.where(row.own, 0.0, NEGATIVE).astype(BF)
    mask_ref[1] = jnp.where(row.alt, 0.0, NEGATIVE).astype(BF)
    store_group_masks(row, group_ref)
    gain1 = gains_ref[0:1, :].astype(F32)
    own = own_ref[0, 3].astype(F32)
    sides = by_side(place_ref, pair_ref[0], across_ref[0])
    for part, (source, slot) in enumerate(zip(sides, (row.slot_low, row.slot_high))):
        x = source.astype(F32)
        edge_ref[0, 4 + part] = where_tiles(slot, x * rms_scale(x) * gain1, own).astype(BF)
    edges = edge_ref[0, 4:].reshape(2 * size, dim)
    first_half = lax.broadcasted_iota(jnp.int32, (1, lanes), 1) < lanes // 2
    for index, weight_ref in enumerate((wk_ref, wv_ref)):
        value = dot_nn(edges, weight_ref[...]).astype(BF)
        edge_ref[0, 2 * index : 2 * index + 2] = value.reshape(2, size, dim)

    @pl.when(pl.program_id(0) == 0)
    def _():
        copy.wait()

    for pair in range(pairs):
        cols = slice(pair * lanes, (pair + 1) * lanes)
        keys, values = key_groups(own_ref, edge_ref, cols)
        halves = []
        for half in range(2):
            head = 2 * pair + half
            scores = dot_nt(keys, by_group(own_ref[0, 0, :, cols], group_ref, half))
            bias = jnp.maximum(
                bias_ref[head, :, :size] + mask_ref[0], bias_ref[head, :, size:] + mask_ref[1]
            )
            scores = scores + bias.astype(F32)
            peak = jnp.max(scores, axis=0, keepdims=True)
            powers = jnp.exp(scores - peak)
            inverse = 1.0 / jnp.sum(powers, axis=0, keepdims=True)
            probs = (powers * inverse).astype(BF)
            p_ref[0, head] = probs
            halves.append(dot_tn(probs, values))
        att_ref[0, :, cols] = fold_rows(row, first_half, halves).astype(BF)


def attend(first, earlier, lengths, place, pair, across, own, gains, wk, wv, bias):
    count, size, dim = pair.shape
    rows = own.shape[0]
    heads = bias.shape[0]
    constants = (gains, wk, wv, bias)
    shapes = ((6, size, dim), (heads, size, size), (size, dim))
    start = 2 + 3 + len(constants)
    return pl.pallas_call(
        functools.partial(attend_kernel, first),
        grid_spec=pltpu.PrefetchScalarGridSpec(
            num_scalar_prefetch=2,
            grid=(count,),
            in_specs=[row_spec((size, dim))] * 2
            + [row_spec((4, size, dim), first)]
            + [full(item.shape) for item in constants[:-1]]
            + [pl.BlockSpec(memory_space=pl.ANY)] * (1 + len(earlier)),
            out_specs=[row_spec(shape, first) for shape in shapes],
            scratch_shapes=[
                pltpu.VMEM((2, size, size), BF),
                pltpu.VMEM((2, 3, size, 2 * dim // heads), BF),
                pltpu.VMEM(bias.shape, BF),
                pltpu.SemaphoreType.DMA,
            ],
        ),
        out_shape=[jax.ShapeDtypeStruct((rows,) + shape, BF) for shape in shapes],
        input_output_aliases={start + index: index for index in range(len(earlier))},
        compiler_params=params(),
        cost_estimate=cost(count * size * dim * (4 * dim + 36 * size), count * size * dim * 40),
        name="attend_rows",
    )(lengths, place, pair, across, own, *constants, *earlier)


def forward_kernel(
    rows,
    lengths_ref,
    place_ref,
    x_ref,
    att_ref,
    gains_ref,
    wo_ref,
    win_ref,
    wout_ref,
    block_ref,
    pooled_ref,
    pre_ref,
    after_hbm,
    n2_hbm,
    after_low,
    n2_all,
    total_ref,
    sems,
):
    _, size, dim = x_ref.shape
    slots = pooled_ref.shape[1]
    toks = rows * size
    step = pl.program_id(0)
    copies = [
        pltpu.make_async_copy(after_low, after_hbm, sems.at[0]),
        pltpu.make_async_copy(n2_all, n2_hbm, sems.at[1]),
    ]

    @pl.when(step == 0)
    def _():
        mixed = dot_nn(att_ref[...].reshape(toks, dim), wo_ref[...])
        after = x_ref[...].reshape(toks, dim).astype(F32) + mixed
        after_low[...] = after.astype(BF)
        total_ref[...] = after
        n2_all[...] = (after * rms_scale(after) * gains_ref[1:2, :].astype(F32)).astype(BF)
        for copy in copies:
            copy.start()

    pre = dot_nn(n2_all[...], win_ref[...])
    square = pre * pre
    gate = 0.5 + 0.5 * jnp.tanh(pre * (GELU_A + (GELU_A * GELU_B) * square))
    pre_ref[...] = pre.astype(BF)
    total_ref[...] += dot_nn((pre * gate).astype(BF), wout_ref[...])

    @pl.when(step == pl.num_programs(0) - 1)
    def _():
        gainf = gains_ref[2:3, :].astype(F32)
        for row in range(rows):
            here = slice(row * size, (row + 1) * size)
            block = total_ref[here, :].astype(BF)
            block_ref[row] = block
            out = block.astype(F32)
            final = out * rms_scale(out) * gainf
            found = row_sentences(lengths_ref, place_ref, row, size)
            member = (lax.broadcasted_iota(jnp.int32, (slots, size), 0) == found).astype(BF)
            high_part, low_part = split_bf(final)
            pooled_ref[row] = dot_nn(member, high_part) + dot_nn(member, low_part)
        for copy in copies:
            copy.wait()


def by_side(place_ref, pair, across):
    odd = place_ref[0] % 2 == 1
    return jnp.where(odd, pair, across), jnp.where(odd, across, pair)


def key_groups(own_ref, edge_ref, cols):
    return [
        jnp.concatenate(
            [edge_ref[0, 2 * index, :, cols], own_ref[0, 1 + index, :, cols], edge_ref[0, 2 * index + 1, :, cols]],
            axis=1,
        )
        for index in range(2)
    ]


def forward(lengths, place, tokens, att, gains, wo, win, wout):
    rows, size, dim = tokens.shape
    slots = lengths.shape[1]
    hidden = win.shape[1]
    toks = rows * size
    constants = (tokens, att, gains, wo)
    anywhere = pl.BlockSpec(memory_space=pl.ANY)
    out_of = lambda shape, kind=BF: jax.ShapeDtypeStruct(shape, kind)
    return pl.pallas_call(
        functools.partial(forward_kernel, rows),
        grid_spec=pltpu.PrefetchScalarGridSpec(
            num_scalar_prefetch=2,
            grid=(hidden // dim,),
            in_specs=[full(item.shape) for item in constants]
            + [
                pl.BlockSpec((dim, dim), lambda step, *_: (0, step)),
                pl.BlockSpec((dim, dim), lambda step, *_: (step, 0)),
            ],
            out_specs=[
                full((rows, size, dim)),
                full((rows, slots, dim)),
                pl.BlockSpec((toks, dim), lambda step, *_: (0, step)),
                anywhere,
                anywhere,
            ],
            scratch_shapes=[
                pltpu.VMEM((toks, dim), BF),
                pltpu.VMEM((toks, dim), BF),
                pltpu.VMEM((toks, dim), F32),
                pltpu.SemaphoreType.DMA((2,)),
            ],
        ),
        out_shape=[
            out_of((rows, size, dim)),
            out_of((rows, slots, dim), F32),
            out_of((toks, hidden)),
            out_of((toks, dim)),
            out_of((toks, dim)),
        ],
        compiler_params=params(),
        cost_estimate=cost(toks * dim * (dim + 2 * hidden), toks * (hidden * 2 + dim * 20)),
        name="feed_forward",
    )(lengths, place, *constants, win, wout)


def store_split(core, value, refs, count, first=0):
    if len(refs) == 1:
        refs[0][first : first + value.shape[0], :] = value
        return
    groups = value.shape[0] // (2 * count)
    for group in range(groups):
        even = value[2 * group * count : (2 * group + 1) * count]
        odd = value[(2 * group + 1) * count : (2 * group + 2) * count]

        refs[0][group, first : first + count, :] = jnp.where(core == 0, even, odd)
        refs[1][group, first : first + count, :] = jnp.where(core == 0, odd, even)


def feed_back_kernel(
    rows,
    parts,
    lengths_ref,
    place_ref,
    block_ref,
    cot_ref,
    pool_ref,
    graw_ref,
    pooled_ref,
    gain_ref,
    pre_ref,
    win_ref,
    wout_ref,
    after_hbm,
    n2_hbm,
    att_hbm,
    wo_hbm,
    back_ref,
    gains_ref,
    *rest,
):
    split = len(rest) == 14
    per = 2 if split else 1
    in_refs, out_refs, small_refs = (rest[i * per : (i + 1) * per] for i in range(3))
    gout_ref, branch_ref, gn2_ref, after_ref, n2_ref, att_ref, wo_ref, sems = rest[3 * per :]
    _, size, dim = block_ref.shape
    toks = rows * size
    slots = pool_ref.shape[1]
    step = pl.program_id(0)
    tiles = pl.num_programs(0) - 1
    core = place_ref[1]
    copies = [
        pltpu.make_async_copy(n2_hbm, n2_ref, sems.at[0]),
        pltpu.make_async_copy(after_hbm, after_ref, sems.at[1]),
        pltpu.make_async_copy(att_hbm, att_ref, sems.at[2]),
        pltpu.make_async_copy(wo_hbm, wo_ref, sems.at[3]),
    ]

    @pl.when(step == 0)
    def _():
        for copy in copies:
            copy.start()
        gainf = gain_ref[2:3, :].astype(F32)
        gain_f = jnp.zeros((1, dim), F32)
        for row in range(rows):
            here = slice(row * size, (row + 1) * size)
            found = row_sentences(lengths_ref, place_ref, row, size)
            member = (lax.broadcasted_iota(jnp.int32, (slots, size), 0) == found).astype(BF)
            high_part, low_part = split_bf(pool_ref[row])
            g_final = dot_tn(member, high_part) + dot_tn(member, low_part)
            out = block_ref[row].astype(F32)
            scale = rms_scale(out)
            gain_f = gain_f + jnp.sum(g_final * out * scale, axis=0, keepdims=True)
            g_out = rms_back(out, scale, g_final * gainf) + cot_ref[row].astype(F32)
            gout_ref[here, :] = g_out
            branch_ref[here, :] = g_out.astype(BF)
        gains_ref[...] = jnp.zeros_like(gains_ref)
        gains_ref[0:1, :] = gain_f
        copies[0].wait()

    @pl.when(step < tiles)
    def _():
        g_hidden = dot_nt(branch_ref[...], wout_ref[...])
        pre = pre_ref[...].astype(F32)
        square = pre * pre
        gate = 0.5 + 0.5 * jnp.tanh(pre * (GELU_A + (GELU_A * GELU_B) * square))
        act = pre * gate
        value = dot_tn(branch_ref[...], act.astype(BF)).astype(BF)
        store_split(core, value, out_refs, dim // parts)
        slope = gate + act * (1.0 - gate) * (2 * GELU_A + (6 * GELU_A * GELU_B) * square)
        g_pre = (g_hidden * slope).astype(BF)
        value = dot_tn(g_pre, n2_ref[...]).astype(BF)
        store_split(core, value, in_refs, tiles * dim // parts)
        part = dot_nt(g_pre, win_ref[...])

        @pl.when(step == 0)
        def _():
            gn2_ref[...] = part

        @pl.when(step > 0)
        def _():
            gn2_ref[...] += part

    @pl.when(step == tiles)
    def _():
        for copy in copies[1:]:
            copy.wait()
        gain2 = gain_ref[1:2, :].astype(F32)
        gain_2 = jnp.zeros((1, dim), F32)
        for row in range(rows):
            here = slice(row * size, (row + 1) * size)
            after = after_ref[here, :].astype(F32)
            g_n2 = gn2_ref[here, :]
            scale = rms_scale(after)
            gain_2 = gain_2 + jnp.sum(g_n2 * after * scale, axis=0, keepdims=True)
            g_after = gout_ref[here, :] + rms_back(after, scale, g_n2 * gain2)
            back_ref[row, 1] = g_after.astype(BF)
            branch_ref[here, :] = g_after.astype(BF)
        gains_ref[1:2, :] = gain_2
        g_mix = dot_nt(branch_ref[...], wo_ref[...]).astype(BF)
        for row in range(rows):
            back_ref[row, 0] = g_mix[row * size : (row + 1) * size]
        value = dot_tn(branch_ref[...], att_ref[...].reshape(toks, dim)).astype(BF)
        store_split(core, value, small_refs, dim // parts)
        left_high, left_low = split_bf(jnp.where(place_ref[0] == 0, graw_ref[...], 0.0))
        right_high, right_low = split_bf(pooled_ref[...])
        value = dot_tn(left_high, right_high)
        value += dot_tn(left_high, right_low) + dot_tn(left_low, right_high)
        first = dim // parts if split else dim
        store_split(core, value.astype(BF), small_refs, dim // parts, first)


def feed_back(parts, lengths, place, block, after, cot, att, n2, pre, pool, graw, pooled, gains, weights):
    rows, size, dim = block.shape
    hidden = pre.shape[1]
    tiles = hidden // dim
    toks = rows * size
    wo, win, wout = weights
    split = (dim // parts) % 16 == 0 and dim % (2 * hidden // parts) == 0
    tile = lambda step: jnp.minimum(step, tiles - 1)
    if split:
        groups = parts // 2
        wide = hidden // parts
        inner = dim // (2 * wide)
        narrow = dim // parts
        in_specs = [pl.BlockSpec((inner, wide, dim), lambda step, *_: (tile(step), 0, 0))] * 2
        out_specs = [pl.BlockSpec((groups, narrow, dim), lambda step, *_: (0, tile(step), 0))] * 2
        small_specs = [full((groups, 2 * narrow, dim))] * 2
        shapes = [(groups, wide, dim)] * 2 + [(groups, tiles * narrow, dim)] * 2 + [(groups, 2 * narrow, dim)] * 2
    else:
        in_specs = [pl.BlockSpec((dim, dim), lambda step, *_: (tile(step), 0))]
        out_specs = [pl.BlockSpec((dim, dim), lambda step, *_: (tile(step), 0))]
        small_specs = [full((2 * dim, dim))]
        shapes = [(hidden, dim), (tiles * dim, dim), (2 * dim, dim)]
    constants = (block, cot, pool, graw, pooled, gains)
    outs = pl.pallas_call(
        functools.partial(feed_back_kernel, rows, parts),
        grid_spec=pltpu.PrefetchScalarGridSpec(
            num_scalar_prefetch=2,
            grid=(tiles + 1,),
            in_specs=[full(item.shape) for item in constants]
            + [
                pl.BlockSpec((toks, dim), lambda step, *_: (0, tile(step))),
                pl.BlockSpec((dim, dim), lambda step, *_: (0, tile(step))),
                pl.BlockSpec((dim, dim), lambda step, *_: (tile(step), 0)),
            ]
            + [pl.BlockSpec(memory_space=pl.ANY)] * 4,
            out_specs=[full((rows, 2, size, dim)), full((8, dim))]
            + in_specs
            + out_specs
            + small_specs,
            scratch_shapes=[
                pltpu.VMEM((toks, dim), F32),
                pltpu.VMEM((toks, dim), BF),
                pltpu.VMEM((toks, dim), F32),
                pltpu.VMEM((toks, dim), BF),
                pltpu.VMEM((toks, dim), BF),
                pltpu.VMEM((rows, size, dim), BF),
                pltpu.VMEM((dim, dim), BF),
                pltpu.SemaphoreType.DMA((4,)),
            ],
        ),
        out_shape=[
            jax.ShapeDtypeStruct((rows, 2, size, dim), BF),
            jax.ShapeDtypeStruct((8, dim), F32),
        ]
        + [jax.ShapeDtypeStruct(shape, BF) for shape in shapes],
        compiler_params=params(),
        cost_estimate=cost(
            toks * dim * (4 * hidden + 2 * dim), toks * (hidden * 4 + dim * 20) + 8 * hidden * dim
        ),
        name="feed_back",
    )(lengths, place, *constants, pre, win, wout, after, n2, att, wo)
    if split:
        mine, theirs = outs[2::2], outs[3::2]
    else:
        whole = [
            outs[2].reshape(parts, hidden // parts, dim),
            outs[3].reshape(tiles, parts, dim // parts, dim).transpose(1, 0, 2, 3),
            outs[4].reshape(2, parts, dim // parts, dim).transpose(1, 0, 2, 3),
        ]
        mine, theirs = split_core(whole)
    return outs[0], outs[1], mine, theirs


def split_core(blocks):
    core = (lax.axis_index("batch") % 2).astype(jnp.int32)
    pairs = [item.reshape((item.shape[0] // 2, 2, -1, item.shape[-1])) for item in blocks]
    pick = lambda item, place: lax.dynamic_index_in_dim(item, place, 1, keepdims=False)
    return [pick(item, core) for item in pairs], [pick(item, 1 - core) for item in pairs]


def attend_grad_kernel(parts, place_ref, n1_ref, own_ref, edge_hbm, n1_edge_hbm, *rest):
    refs, (edge_ref, n1_edge_ref, sems) = rest[:-3], rest[-3:]
    rows, _, size, dim = own_ref.shape
    step = pl.program_id(0)
    width = dim // parts if len(refs) == 2 else dim
    flat = lambda ref: ref[...].reshape(-1, dim)
    n1_copy = pltpu.make_async_copy(n1_edge_hbm.at[:, 4:6], n1_edge_ref, sems.at[0])
    copies = [
        pltpu.make_async_copy(
            edge_hbm.at[:, 3 + 2 * index : 5 + 2 * index], edge_ref.at[index], sems.at[1 + index]
        )
        for index in range(2)
    ]

    @pl.when(step == 0)
    def _():
        n1_copy.start()
        for copy in copies:
            copy.start()
        value = dot_tn(flat(own_ref), flat(n1_ref)).astype(BF)
        store_split(place_ref[1], value, refs, dim // parts, 0)
        n1_copy.wait()

    for index in range(2):

        @pl.when(step == 1 + index)
        def _():
            copies[index].wait()
            value = dot_tn(flat(own_ref), flat(n1_ref)) + dot_tn(flat(edge_ref.at[index]), flat(n1_edge_ref))
            store_split(place_ref[1], value.astype(BF), refs, dim // parts, (1 + index) * width)


def attend_grad(parts, place, own, edges, grads):
    rows, _, size, dim = own.shape
    narrow = dim // parts
    split = narrow % 16 == 0
    shape = (parts // 2, 3 * narrow, dim) if split else (3 * dim, dim)
    copies = 2 if split else 1
    outs = pl.pallas_call(
        functools.partial(attend_grad_kernel, parts),
        grid_spec=pltpu.PrefetchScalarGridSpec(
            num_scalar_prefetch=1,
            grid=(3,),
            in_specs=[
                pl.BlockSpec((rows, 1, size, dim), lambda step, *_: (0, 3, 0, 0)),
                pl.BlockSpec((rows, 1, size, dim), lambda step, *_: (0, step, 0, 0)),
                pl.BlockSpec(memory_space=pl.ANY),
                pl.BlockSpec(memory_space=pl.ANY),
            ],
            out_specs=[full(shape)] * copies,
            scratch_shapes=[
                pltpu.VMEM((2, rows, 2, size, dim), BF),
                pltpu.VMEM((rows, 2, size, dim), BF),
                pltpu.SemaphoreType.DMA((3,)),
            ],
        ),
        out_shape=[jax.ShapeDtypeStruct(shape, BF)] * copies,
        compiler_params=params(),
        cost_estimate=cost(rows * size * dim * dim * 7, rows * size * dim * 26),
        name="attend_grad",
    )(place, own, grads, grads, edges)
    if split:
        return outs[0], outs[1]
    mine, theirs = split_core([outs[0].reshape(3, parts, narrow, dim).transpose(1, 0, 2, 3)])
    return mine[0], theirs[0]


def attend_back_kernel(
    first,
    lengths_ref,
    place_ref,
    own_ref,
    pair_ref,
    across_ref,
    qkv_ref,
    edge_ref,
    p_ref,
    back_ref,
    gain_ref,
    wq_hbm,
    wk_hbm,
    wv_hbm,
    *rest,
):
    grad_ref, part_ref, to_pair_ref, to_across_ref, offset_ref, gains_ref = rest[-11:-5]
    mask_ref, group_ref, acc_ref, weight_ref, sems = rest[-5:]
    copies = [
        pltpu.make_async_copy(source, weight_ref.at[index], sems.at[index])
        for index, source in enumerate((wq_hbm, wk_hbm, wv_hbm))
    ]
    size, dim = own_ref.shape[1:]
    heads = p_ref.shape[1]
    pairs = heads // 2
    lanes = dim // pairs
    step = pl.program_id(0)
    row = Row(lengths_ref, place_ref, step + first, size)
    mask_ref[...] = row.own.astype(F32)

    @pl.when(step == 0)
    def _():
        for copy in copies:
            copy.start()
        acc_ref[...] = jnp.zeros_like(acc_ref)
        gains_ref[...] = jnp.zeros_like(gains_ref)

    first_half = lax.broadcasted_iota(jnp.int32, (1, lanes), 1) < lanes // 2
    store_group_masks(row, group_ref)
    half_size = size // 2
    for pair in range(pairs):
        cols = slice(pair * lanes, (pair + 1) * lanes)
        keys, values = key_groups(qkv_ref, edge_ref, cols)
        q_groups = [by_group(qkv_ref[0, 0, :, cols], group_ref, half) for half in range(2)]
        o_groups = [by_group(back_ref[0, 0, :, cols], group_ref, half) for half in range(2)]
        d_q, scores_pair = [], []
        for half in range(2):
            head = 2 * pair + half
            g_probs = dot_nt(values, o_groups[half])
            full_probs = p_ref[0, head].astype(F32)
            product = full_probs * g_probs
            inner = jnp.sum(product, axis=0, keepdims=True)
            g_scores = product - full_probs * inner
            on_own = g_scores * mask_ref[...]
            off_own = g_scores - on_own
            acc_ref[head, :, :half_size] += on_own[:half_size, :half_size] + on_own[half_size:, half_size:]
            acc_ref[head, :, half_size:size] += on_own[:half_size, half_size:] + off_own[half_size:, :half_size]
            acc_ref[head, :, size : size + half_size] += off_own[:half_size, :half_size] + off_own[half_size:, half_size:]
            acc_ref[head, :, size + half_size :] += off_own[:half_size, half_size:] + on_own[half_size:, :half_size]
            scores_pair.append(g_scores.astype(BF))
            d_q.append(dot_tn(scores_pair[-1], keys))
        grad_ref[0, 0, :, cols] = fold_rows(row, first_half, d_q).astype(BF)
        probs_pair = [p_ref[0, 2 * pair], p_ref[0, 2 * pair + 1]]
        for index, (left, right) in enumerate(((scores_pair, q_groups), (probs_pair, o_groups))):
            value = dot_nn(jnp.concatenate(left, axis=1), jnp.concatenate(right, axis=0)).astype(BF)
            grad_ref[0, 3 + 2 * index, :, cols] = value[:, :lanes]
            grad_ref[0, 1 + index, :, cols] = value[:, lanes : 2 * lanes]
            grad_ref[0, 4 + 2 * index, :, cols] = value[:, 2 * lanes :]

    @pl.when(step == 0)
    def _():
        for copy in copies:
            copy.wait()

    gain1 = gain_ref[0:1, :].astype(F32)
    g_whole = None
    for index in range(2):
        edge_grad = grad_ref[0, 3 + 2 * index : 5 + 2 * index].reshape(2 * size, dim)
        left = jnp.concatenate([edge_grad, grad_ref[0, 1 + index]], axis=0)
        term = dot_nt(left, weight_ref[1 + index])
        g_whole = term if g_whole is None else g_whole + term
    zero = jnp.zeros((size, dim), F32)
    g_low = where_tiles(row.slot_low, g_whole[:size], zero)
    g_high = where_tiles(row.slot_high, g_whole[size : 2 * size], zero)
    g_own = g_whole[2 * size :] + (g_whole[:size] - g_low) + (g_whole[size : 2 * size] - g_high)
    g_own = g_own + dot_nt(grad_ref[0, 0], weight_ref[0])
    gain_1 = jnp.zeros((1, dim), F32)
    low, high = by_side(place_ref, pair_ref[0], across_ref[0])
    results = []
    for source, g_norm in ((own_ref[0], g_own), (low, g_low), (high, g_high)):
        x = source.astype(F32)
        scale = rms_scale(x)
        gain_1 = gain_1 + jnp.sum(g_norm * x * scale, axis=0, keepdims=True)
        results.append(rms_back(x, scale, g_norm * gain1))
    part_ref[0] = (results[0] + back_ref[0, 1].astype(F32)).astype(BF)
    odd = place_ref[0] % 2 == 1
    to_pair_ref[0] = jnp.where(odd, results[1], results[2]).astype(BF)
    to_across_ref[0] = jnp.where(odd, results[2], results[1]).astype(BF)
    gains_ref[0:1, :] += gain_1

    @pl.when(step == pl.num_programs(0) - 1)
    def _():
        for head in range(heads):
            offset_ref[head] = fold_offsets(acc_ref[head])


def attend_back(first, count, halo, earlier, lengths, place, x, low, high, own, edges, p, back, gains, weights):
    rows, size, dim = x.shape
    heads = p.shape[1]
    constants = (gains,) + tuple(weights)
    anywhere = pl.BlockSpec(memory_space=pl.ANY)
    start = 2 + 7 + len(constants)
    aliases = {start + index: index for index in range(len(earlier))}
    return pl.pallas_call(
        functools.partial(attend_back_kernel, first),
        grid_spec=pltpu.PrefetchScalarGridSpec(
            num_scalar_prefetch=2,
            grid=(count,),
            in_specs=[row_spec((size, dim), first)] * 3
            + [row_spec((3, size, dim), first), row_spec((4, size, dim), first)]
            + [row_spec((heads, size, size), first), row_spec((2, size, dim), first)]
            + [full(gains.shape)]
            + [anywhere] * (len(weights) + len(earlier)),
            out_specs=[
                row_spec((7, size, dim), first),
                row_spec((size, dim), first),
                row_spec((size, dim), first - halo[0]),
                row_spec((size, dim), first - halo[0]),
            ]
            + [full((heads, 8, 2 * size)), full((8, dim))],
            scratch_shapes=[
                pltpu.VMEM((size, size), F32),
                pltpu.VMEM((2, 3, size, 2 * dim // heads), BF),
                pltpu.VMEM((heads, size // 2, 2 * size), F32),
                pltpu.VMEM((3, dim, dim), BF),
                pltpu.SemaphoreType.DMA((3,)),
            ],
        ),
        out_shape=[
            jax.ShapeDtypeStruct((rows, 7, size, dim), BF),
            jax.ShapeDtypeStruct((rows, size, dim), BF),
            jax.ShapeDtypeStruct((halo[1], size, dim), BF),
            jax.ShapeDtypeStruct((halo[1], size, dim), BF),
            jax.ShapeDtypeStruct((heads, 8, 2 * size), F32),
            jax.ShapeDtypeStruct((8, dim), F32),
        ],
        input_output_aliases=aliases,
        compiler_params=params(),
        cost_estimate=cost(
            count * size * dim * (9 * dim + 128 * size), count * size * dim * 60
        ),
        name="attend_back_rows",
    )(lengths, place, x, low, high, own, edges, p, back, *constants, *earlier)


def flip(block, axis, bit):
    count = lax.axis_size(axis)
    return lax.ppermute(block, axis, [(i, i ^ bit) for i in range(count)])


def sum_along(block, axis):
    bit = 1
    while bit < lax.axis_size(axis):
        block = block + flip(block, axis, bit)
        bit *= 2
    return block


def bit_places(axis):
    return [1 << level for level in range((lax.axis_size(axis) - 1).bit_length())]


def gather_batch(block):
    place = lax.axis_index("batch")
    bits = bit_places("batch")
    gathered = block[None]
    for bit in reversed(bits):
        other = flip(gathered, "batch", bit)
        upper = (place & bit) > 0
        gathered = jnp.stack(
            [jnp.where(upper, other, gathered), jnp.where(upper, gathered, other)], axis=1
        )
        gathered = gathered.reshape((-1,) + block.shape)
    return gathered.reshape((-1,) + block.shape[1:])


def halve(block, bits, bit):
    axis = bits.index(bit)
    mine = ((lax.axis_index("batch") & bit) > 0).astype(jnp.int32)
    send = lax.dynamic_index_in_dim(block, 1 - mine, axis, keepdims=False)
    keep = lax.dynamic_index_in_dim(block, mine, axis, keepdims=False)
    return keep + flip(send, "batch", bit), [item for item in bits if item != bit]


def after(value, *others):
    return lax.optimization_barrier((value,) + tuple(others))[0]


def stage_kernel(groups, place_ref, *refs):
    ins = refs[: 2 * sum(len(group) for group in groups)]
    outs = refs[len(ins) :]
    taken = 0
    for index, group in enumerate(groups):
        first = 0
        for count in group:
            value = ins[2 * taken][0, 0, 0] + ins[2 * taken + 1][0, 0, 0]
            taken += 1
            for which in range(2):

                @pl.when(pl.program_id(0) == which)
                def _():
                    outs[2 * index + which][0, 0, first : first + count, :] = value

            first += count


def stage(place, groups, bits, pieces):
    columns = groups[0][0][0].shape[-1]
    lead = bits[0][0][0] * bits[0][0][1]
    if any(count % (16 * pieces) or first % count for group in groups for _, _, first, count in group):
        sends, keeps = [], []
        for index, group in enumerate(groups):
            before, behind = bits[index][0]
            total = jnp.concatenate(
                [(kept + arrived)[..., first : first + count, :].reshape(-1, count, columns)
                 for kept, arrived, first, count in group],
                axis=1,
            ).reshape(before, 2, behind, -1, columns)
            pick = lambda which: lax.dynamic_index_in_dim(total, which, 1, keepdims=False)
            sends.append(pick(1 - place[index]).reshape(lead, 1, -1, columns))
            keeps.append(pick(place[index]).reshape(lead, 1, -1, columns))
        return sends, keeps
    in_specs, operands, out_specs, shapes = [], [], [], []
    for index, group in enumerate(groups):
        before, behind = bits[index][0]
        total = 0

        def place_of(half, step, chunk, places, index=index, behind=behind):
            mine = places[index]
            where_at = jnp.where(half == 0, 1 - mine, mine)
            return step // behind, where_at, step % behind, chunk

        for kept, arrived, first, count in group:
            rows = count // pieces
            total += rows
            shape = (before, 2, behind) + kept.shape[-2:]

            def index_map(half, step, chunk, places, place_of=place_of, first=first, rows=rows):
                one, two, three, four = place_of(half, step, chunk, places)
                return one, two, three, four + first // rows, 0

            for item in (kept, arrived):
                in_specs.append(pl.BlockSpec((1, 1, 1, rows, columns), index_map))
                operands.append(item.reshape(shape))
        for which in range(2):

            def out_map(half, step, chunk, places, which=which):
                if which == 0:
                    step = jnp.where(half == 0, step, lead - 1)
                    chunk = jnp.where(half == 0, chunk, pieces - 1)
                else:
                    step = jnp.where(half == 1, step, 0)
                    chunk = jnp.where(half == 1, chunk, 0)
                return step, chunk, 0, 0

            out_specs.append(pl.BlockSpec((1, 1, total, columns), out_map))
            shapes.append(jax.ShapeDtypeStruct((lead, pieces, total, columns), BF))
    outs = pl.pallas_call(
        functools.partial(
            stage_kernel, [[count // pieces for _, _, _, count in group] for group in groups]
        ),
        grid_spec=pltpu.PrefetchScalarGridSpec(
            num_scalar_prefetch=1, grid=(2, lead, pieces), in_specs=in_specs, out_specs=out_specs
        ),
        out_shape=shapes,
        compiler_params=pltpu.CompilerParams(
            vmem_limit_bytes=VMEM_BYTES, dimension_semantics=("arbitrary",) * 3
        ),
        name="halving_stage",
    )(place, *operands)
    return outs[0::2], outs[1::2]


class BatchSum:
    def __init__(self, mine, theirs, streams):
        bits = bit_places("batch")
        arrived = [flip(item, "batch", bits[0]) for item in theirs]
        self.groups = [
            [(mine[item], arrived[item], first, rows) for item, first, rows in stream] for stream in streams
        ]
        self.bits = [bits[1:][::-1]] * len(streams)
        self.steps = len(bits) - 1
        self.done = 0

    def hold(self, *others):
        self.groups = [
            [(kept, after(arrived, *others), first, rows) for kept, arrived, first, rows in group]
            for group in self.groups
        ]

    def advance(self):
        moved, bits, places = [], [], []
        me = lax.axis_index("batch")
        for index, left in enumerate(self.bits):
            bit = left[::-1][index % len(left)]
            axis = left.index(bit)
            moved.append(bit)
            places.append(((me & bit) > 0).astype(jnp.int32))
            bits.append(((1 << axis, 1 << (len(left) - 1 - axis)),))
        sends, keeps = stage(jnp.stack(places), self.groups, bits, 1)
        self.groups = [
            [(keep, flip(send, "batch", bit), 0, keep.shape[2])]
            for keep, send, bit in zip(keeps, sends, moved)
        ]
        self.bits = [[item for item in left if item != bit] for left, bit in zip(self.bits, moved)]
        self.done += 1
        return sends

    def total(self):
        return [(kept + arrived).reshape(kept.shape[-2:]) for ((kept, arrived, _, _),) in self.groups]


def pack_kernel(tiles_rows, keep_a, come_a, keep_b, come_b, out_ref):
    groups, _, wide = out_ref.shape
    cols = wide // 2
    rows = tiles_rows // groups
    first = keep_a[...] + come_a[...]
    second = keep_b[...] + come_b[...]
    for group in range(groups):
        here = slice(group * cols, (group + 1) * cols)
        out_ref[group, :, :cols] = first[:, here]
        for part in range(groups):
            out_ref[group, part * rows : (part + 1) * rows, cols:] = second[
                group * rows : (group + 1) * rows, part * cols : (part + 1) * cols
            ]
        out_ref[group, tiles_rows:, cols:] = second[tiles_rows:, here]


def pack(stream_a, stream_b, tiles_rows, groups):
    (keep_a, come_a), (keep_b, come_b) = stream_a, stream_b
    rows, dim = keep_a.shape[-2:]
    flat = lambda item: item.reshape(rows, dim)
    shape = (groups, rows, 2 * dim // groups)
    if tiles_rows // groups % 16 == 0:
        return pl.pallas_call(
            functools.partial(pack_kernel, tiles_rows),
            out_shape=jax.ShapeDtypeStruct(shape, BF),
            compiler_params=pltpu.CompilerParams(vmem_limit_bytes=VMEM_BYTES),
            name="pack_places",
        )(flat(keep_a), flat(come_a), flat(keep_b), flat(come_b))
    first = flat(keep_a + come_a).reshape(rows, groups, -1).transpose(1, 0, 2)
    second = flat(keep_b + come_b)
    out = second[:tiles_rows].reshape(groups, -1, groups, dim // groups).transpose(0, 2, 1, 3)
    out = out.reshape(groups, tiles_rows, -1)
    last = second[tiles_rows:].reshape(-1, groups, dim // groups).transpose(1, 0, 2)
    return jnp.concatenate([first, jnp.concatenate([out, last], axis=1)], axis=2)


def columns_kernel(keep_a, come_a, keep_b, come_b, out_ref):
    groups, rows, cols = out_ref.shape
    half = keep_a.shape[0]
    first = keep_a[...] + come_a[...]
    second = keep_b[...] + come_b[...]
    for group in range(groups):
        here = slice(group * cols, (group + 1) * cols)
        out_ref[group, :half, :] = first[:, here]
        out_ref[group, half:, :] = second[:, here]


def pack_columns(streams, groups):
    rows, dim = streams[0][0].shape[-2:]
    pieces = [item.reshape(rows, dim) for keep, come in streams for item in (keep, come)]
    if rows % 16:
        total = jnp.concatenate([pieces[0] + pieces[1], pieces[2] + pieces[3]], axis=0)
        return total.reshape(2 * rows, groups, -1).transpose(1, 0, 2)
    return pl.pallas_call(
        columns_kernel,
        out_shape=jax.ShapeDtypeStruct((groups, 2 * rows, dim // groups), BF),
        compiler_params=pltpu.CompilerParams(vmem_limit_bytes=VMEM_BYTES),
        name="pack_columns",
    )(*pieces)


def split_dot(dot, left, right):
    return dot(left[0], right[0]) + (dot(left[0], right[1]) + dot(left[1], right[0]))


def embed_kernel(sum_ref, more_ref, count_ref, proj_ref, pooled_ref, emb_ref, inverse_ref):
    pooled = (sum_ref[...] + more_ref[...]) / count_ref[...]
    high, low = split_bf(pooled)
    raw = dot_nn(high, proj_ref[...]) + dot_nn(low, proj_ref[...])
    inverse = lax.rsqrt(jnp.sum(raw * raw, axis=-1, keepdims=True) + EPS)
    pooled_ref[...] = pooled
    emb_ref[...] = raw * inverse
    inverse_ref[...] = jnp.broadcast_to(inverse, inverse_ref.shape)


def embed(sums, more, counts, w_proj):
    own, dim = sums.shape
    shapes = ((own, dim), (own, dim), (own, LANES))
    return pl.pallas_call(
        embed_kernel,
        out_shape=[jax.ShapeDtypeStruct(shape, F32) for shape in shapes],
        compiler_params=pltpu.CompilerParams(vmem_limit_bytes=VMEM_BYTES),
        name="embed",
    )(sums, more, counts, w_proj)


def contrast_kernel(
    place_ref,
    own_ref,
    x_ref,
    y_ref,
    xy_ref,
    other_ref,
    inverse_ref,
    partner_ref,
    count_ref,
    proj_ref,
    loss_ref,
    graw_ref,
    pool_ref,
    all_ref,
    logit_ref,
):
    own, dim = own_ref.shape
    total = all_ref.shape[0]
    me = place_ref[0]
    rows_of = lambda place: pl.ds(pl.multiple_of(place * own, own), own)
    for step, ref in enumerate((own_ref, x_ref, y_ref, xy_ref)):
        place = jnp.bitwise_xor(me, 2 * step)
        all_ref[rows_of(place), :] = ref[...]
        all_ref[rows_of(jnp.bitwise_xor(place, 1)), :] = other_ref[step]
    everyone = split_bf(all_ref[...])
    logits = SHARPNESS * split_dot(dot_nt, everyone, everyone)
    row = lax.broadcasted_iota(jnp.int32, (total, total), 0)
    column = lax.broadcasted_iota(jnp.int32, (total, total), 1)
    logits = jnp.where(row == column, NEGATIVE, logits)
    logit_ref[...] = logits
    peak = jnp.max(logits, axis=0, keepdims=True)
    lse_all = peak + jnp.log(jnp.sum(jnp.exp(logits - peak), axis=0, keepdims=True))
    mine = logit_ref[rows_of(me), :]
    peak = jnp.max(mine, axis=1, keepdims=True)
    lse_own = peak + jnp.log(jnp.sum(jnp.exp(mine - peak), axis=1, keepdims=True))
    target = (lax.broadcasted_iota(jnp.int32, (own, total), 1) == partner_ref[...]).astype(F32)
    loss = lse_own - jnp.sum(jnp.where(target > 0, mine, 0.0), axis=1, keepdims=True)
    loss_ref[...] = jnp.broadcast_to(loss, loss_ref.shape)
    both = SHARPNESS * (jnp.exp(mine - lse_own) + jnp.exp(mine - lse_all) - 2.0 * target)
    grad = split_dot(dot_nn, split_bf(both), everyone)
    emb = own_ref[...]
    grad = inverse_ref[:, :1] * (grad - emb * jnp.sum(emb * grad, axis=1, keepdims=True))
    graw_ref[...] = grad
    high, low = split_bf(grad)
    pool_ref[...] = (dot_nt(high, proj_ref[...]) + dot_nt(low, proj_ref[...])) / count_ref[...]


def contrast_near(embedded, inverse, partner, counts, w_proj):
    own, dim = embedded.shape
    total = own * lax.axis_size("batch")
    parts = [embedded] + [flip(embedded, "batch", bits) for bits in (2, 4, 6)]
    other = flip(jnp.stack(parts), "batch", 1)
    me = lax.axis_index("batch").astype(jnp.int32).reshape(1)
    constants = (*parts, other, inverse, partner.reshape(own, 1), counts, w_proj)
    loss, graw, pool = pl.pallas_call(
        contrast_kernel,
        grid_spec=pltpu.PrefetchScalarGridSpec(
            num_scalar_prefetch=1,
            grid=(1,),
            in_specs=[full(item.shape) for item in constants],
            out_specs=[full((own, LANES)), full((own, dim)), full((own, dim))],
            scratch_shapes=[pltpu.VMEM((total, dim), F32), pltpu.VMEM((total, total), F32)],
        ),
        out_shape=[
            jax.ShapeDtypeStruct((own, LANES), F32),
            jax.ShapeDtypeStruct((own, dim), F32),
            jax.ShapeDtypeStruct((own, dim), F32),
        ],
        compiler_params=params(),
        name="contrast",
    )(me, *constants)
    return loss[:, 0], graw, pool


def finish_kernel(count, width, *refs):
    total = sum(ref[...].astype(F32) for ref in refs[:-count])
    for index, ref in enumerate(refs[-count:]):
        ref[...] = total[index * width : (index + 1) * width, :].T


def finish(pieces, count, width):
    cols = pieces[0].shape[1]
    return pl.pallas_call(
        functools.partial(finish_kernel, count, width),
        out_shape=[jax.ShapeDtypeStruct((cols, width), F32)] * count,
        compiler_params=pltpu.CompilerParams(vmem_limit_bytes=VMEM_BYTES),
        name="finish",
    )(*pieces)


def contrast(embedded, inv_norm, w_proj, partner):
    proj = w_proj.astype(F32)
    everyone = gather_batch(embedded)
    own_count = embedded.shape[0]
    total = everyone.shape[0]
    own_index = lax.axis_index("batch") * own_count + jnp.arange(own_count, dtype=jnp.int32)
    columns = jnp.arange(total, dtype=jnp.int32)

    def lse_of(rows, index):
        logits = SHARPNESS * jnp.einsum("nd,md->nm", rows, everyone, precision=HIGHEST)
        logits = jnp.where(columns[None, :] == index[:, None], NEGATIVE, logits)
        peak = jnp.max(logits, axis=-1, keepdims=True)
        return peak[:, 0] + jnp.log(jnp.sum(jnp.exp(logits - peak), axis=-1))

    if total <= 1024:
        lse_all = lse_of(everyone, columns)
    else:
        lse_all = lax.map(
            lambda pieces: lse_of(pieces[0], pieces[1]),
            (everyone.reshape(-1, 512, everyone.shape[1]), columns.reshape(-1, 512)),
        ).reshape(-1)
    logits = SHARPNESS * jnp.einsum("nd,md->nm", embedded, everyone, precision=HIGHEST)
    is_self = columns[None, :] == own_index[:, None]
    logits = jnp.where(is_self, NEGATIVE, logits)
    peak = jnp.max(logits, axis=-1, keepdims=True)
    lse_own = peak[:, 0] + jnp.log(jnp.sum(jnp.exp(logits - peak), axis=-1))
    is_target = columns[None, :] == partner[:, None]
    picked = jnp.sum(jnp.where(is_target, logits, 0.0), axis=-1)
    loss = lse_own - picked
    both = SHARPNESS * (
        jnp.exp(logits - lse_own[:, None])
        + jnp.exp(logits - lse_all[None, :])
        - 2.0 * is_target.astype(F32)
    )
    grad_emb = jnp.dot(both, everyone, precision=HIGHEST)
    grad_raw = inv_norm * (
        grad_emb - embedded * jnp.sum(embedded * grad_emb, axis=-1, keepdims=True)
    )
    grad_pooled = jnp.einsum("ne,de->nd", grad_raw, proj, precision=HIGHEST)
    return loss, grad_raw, grad_pooled


def shards(
    tokens,
    norm1_gain,
    w_query,
    w_key,
    w_value,
    rel_bias,
    w_output,
    norm2_gain,
    w_in,
    w_out,
    final_gain,
    w_proj,
    lengths,
    partner,
    cotangent,
):
    rows, size, dim = tokens.shape
    slots = lengths.shape[1]
    toks = rows * size
    seq_count = lax.axis_size("seq")
    seq_place = lax.axis_index("seq")
    place = seq_place.astype(jnp.int32).reshape(1)
    pairs = [(i, i ^ 1) for i in range(seq_count)]
    across = [(i, i - 1 if i % 2 == 0 else i + 1) for i in range(1, seq_count - 1)]
    gains = jnp.stack([norm1_gain, norm2_gain, final_gain])

    half_rows = rows // 2 if rows > 1 else rows
    bounds = [(first, min(first + half_rows, rows)) for first in range(0, rows, half_rows)]
    sides = []
    for first, last in bounds:
        piece = tokens[first:last]
        if sides:
            piece = after(piece, *sides[-1])
        sides.append((lax.ppermute(piece, "seq", pairs), lax.ppermute(piece, "seq", across)))
    bias = bias_tables(rel_bias, size)
    own = own_projections(tokens, norm1_gain.reshape(1, dim), (w_query, w_key, w_value))
    attended = ()
    for (first, _), (pair_part, across_part) in zip(bounds, sides):
        attended = tuple(
            attend(
                first, attended, lengths, place, pair_part, across_part, own, gains, w_key, w_value, bias
            )
        )
    edges, p, att = attended
    block, partial, pre, after_attn, n2 = forward(
        lengths, place, tokens, att, gains, w_output, w_in, w_out
    )
    x_pair, x_across = (
        jnp.concatenate([side[index] for side in sides], axis=0) for index in range(2)
    )
    counts = lengths.astype(F32).reshape(rows * slots, 1)
    partial = partial.reshape(rows * slots, dim)
    seq_bits = bit_places("seq")
    for bit in seq_bits[:-1]:
        partial = partial + flip(partial, "seq", bit)
    arrived = flip(partial, "seq", seq_bits[-1])
    partial = after(partial, x_pair, x_across)
    pooled, embedded, inverse = embed(partial, arrived, counts, w_proj)
    if lax.axis_size("batch") == 8:
        loss, grad_raw, pool_grad = contrast_near(embedded, inverse, partner, counts, w_proj)
    else:
        loss, grad_raw, grad_pooled = contrast(embedded, inverse[:, :1], w_proj, partner)
        pool_grad = grad_pooled / counts
    pool_grad = pool_grad.reshape(rows, slots, dim)
    batch_count = lax.axis_size("batch")
    place = jnp.stack([seq_place, lax.axis_index("batch") % 2]).astype(jnp.int32)

    back, gains_a, mine, theirs = feed_back(
        batch_count,
        lengths,
        place,
        block,
        after_attn,
        cotangent,
        att,
        n2,
        pre,
        pool_grad,
        grad_raw,
        pooled,
        gains,
        (w_output, w_in, w_out),
    )
    hidden = w_in.shape[1]
    width = dim // batch_count
    tiles = hidden // dim
    wide = hidden // batch_count
    feed_sum = BatchSum(
        mine,
        theirs,
        (((0, 0, wide), (2, 0, width)), ((1, 0, tiles * width), (2, width, width))),
    )
    segments = [(0, 1), (1, rows - 2), (rows - 1, 1)] if rows > 2 else [(0, rows)]
    halves, from_pair, from_across = [], [], []
    earlier = ()
    for first, count in segments:
        if halves and feed_sum.done < feed_sum.steps:
            place = after(place, *feed_sum.advance())
        halves.append(
            attend_back(
                first,
                count,
                (0, rows - 1) if first + count < rows else (first, count),
                earlier,
                lengths,
                place,
                tokens,
                x_pair,
                x_across,
                own,
                edges,
                p,
                back,
                gains,
                (w_query, w_key, w_value),
            )
        )
        feed_sum.hold(halves[-1][5])
        earlier = tuple(halves[-1][:4])
        if first + count >= rows - 1:
            from_pair.append(lax.ppermute(halves[-1][2], "seq", pairs))
            from_across.append(lax.ppermute(halves[-1][3], "seq", across))
            earlier = earlier[:2]
    grads, part = earlier
    while feed_sum.done < feed_sum.steps:
        place = after(place, *feed_sum.advance())

    feed_part = pack(
        *[(group[0][0], group[0][1]) for group in feed_sum.groups], tiles * width, seq_count
    )
    grad_rel = bias_grad([item[4] for item in halves], rel_bias.shape[0])
    gain1_grad = sum(item[5][0] for item in halves)
    small = jnp.concatenate([gain1_grad, gains_a[1], gains_a[0], grad_rel.reshape(-1)])
    small = jnp.pad(small, (0, -small.shape[0] % 1024)).reshape(-1, 128)
    batch_bits = bit_places("batch")
    arrived = flip(small, "seq", seq_bits[0])
    place = after(place, feed_part, small, *from_pair, *from_across)
    attend_mine, attend_theirs = attend_grad(batch_count, place, own, edges, grads)
    feed_done = lax.psum_scatter(feed_part, "seq", scatter_dimension=0, tiled=True)[0]
    half = 3 * width // 2
    attend_sum = BatchSum([attend_mine], [attend_theirs], (((0, 0, half),), ((0, half, 3 * width - half),)))
    small = after(small, attend_mine) + arrived
    arrived = flip(small, "batch", batch_bits[0])
    attend_sum.hold(arrived)
    for bit in batch_bits[1:]:
        sends = attend_sum.advance()
        small = after(small, *sends) + arrived
        arrived = flip(small, "batch", bit)
        attend_sum.hold(arrived)
    attend_parts = pack_columns([group[0][:2] for group in attend_sum.groups], seq_count)
    small = after(small, attend_parts) + arrived
    came = [lax.dynamic_index_in_dim(attend_parts, seq_place, 0, keepdims=False)]
    for distance in range(1, seq_count):
        route = [(i, (i + distance) % seq_count) for i in range(seq_count)]
        target = (seq_place + distance) % seq_count
        send = lax.dynamic_index_in_dim(attend_parts, target, 0, keepdims=False)
        came.append(lax.ppermute(send, "seq", route))
    sent = came[0]
    for bit in seq_bits[1:]:
        small = small + flip(small, "seq", bit)
    small = small.reshape(-1)
    gain_sums = [small[i * dim : (i + 1) * dim] for i in range(3)]
    rel_sum = small[3 * dim : 3 * dim + rel_bias.size].reshape(rel_bias.shape)

    grad_tokens = (
        after(part, sent).astype(F32)
        + jnp.concatenate(from_pair, axis=0).astype(F32)
        + jnp.concatenate(from_across, axis=0).astype(F32)
    )
    turn = lambda array: array.T.astype(F32)
    cols = dim // seq_count
    s_in = turn(feed_done[:wide, :cols])
    s_output = turn(feed_done[wide:, :cols])
    s_out = feed_done[:-width, cols:].reshape(seq_count, width, cols)
    s_out = s_out.transpose(0, 2, 1).reshape(dim, width).astype(F32)
    s_proj = turn(feed_done[-width:, cols:])
    came[0] = after(came[0], s_in, s_output, s_out, s_proj, grad_tokens)
    s_attend = finish(came, 3, width)
    return (
        block,
        embedded,
        loss,
        grad_tokens,
        gain_sums[0],
        s_attend[0],
        s_attend[1],
        s_attend[2],
        rel_sum,
        s_output,
        gain_sums[1],
        s_in,
        s_out,
        gain_sums[2],
        s_proj,
    )


def solution(mesh):
    tok = P("batch", "seq", None)
    mat = P("seq", "batch")
    return jax.shard_map(
        shards,
        mesh=mesh,
        in_specs=(tok,) + (P(),) * 11 + (P("batch", None), P("batch"), tok),
        out_specs=(
            tok,
            P("batch", None),
            P("batch"),
            tok,
            P(),
            mat,
            mat,
            mat,
            P(),
            mat,
            P(),
            mat,
            mat,
            P(),
            mat,
        ),
        check_vma=False,
    )
```

```python
import functools

import jax
import jax.numpy as jnp
from jax import lax
from jax.experimental import pallas as pl
from jax.experimental.pallas import tpu as pltpu
from jax.sharding import PartitionSpec as P

EPS = 1e-06
NEGATIVE = -1e30
SHARPNESS = 50.0
THRESHOLDS = (12, 16, 23, 32, 46, 64, 91)
HIGHEST = lax.Precision.HIGHEST
BF = jnp.bfloat16
F32 = jnp.float32
VMEM_BYTES = 63 * 1024 * 1024
GELU_A = 0.7978845608028654
GELU_B = 0.044715
LANES = 128


def dot_nn(left, right):
    return lax.dot_general(left, right, (((1,), (0,)), ((), ())), preferred_element_type=F32)


def dot_nt(left, right):
    return lax.dot_general(left, right, (((1,), (1,)), ((), ())), preferred_element_type=F32)


def dot_tn(left, right):
    return lax.dot_general(left, right, (((0,), (0,)), ((), ())), preferred_element_type=F32)


def rms_scale(values):
    return lax.rsqrt(jnp.mean(values * values, axis=-1, keepdims=True) + EPS)


def rms_back(values, scale, grad_normed):
    inner = jnp.mean(grad_normed * values, axis=-1, keepdims=True)
    return scale * (grad_normed - values * (scale * scale * inner))


def split_bf(values):
    high = values.astype(BF)
    return high, (values - high.astype(F32)).astype(BF)


def bucket_of(offset):
    distance = jnp.abs(offset)
    beyond = jnp.zeros_like(distance)
    for threshold in THRESHOLDS:
        beyond = beyond + (distance >= threshold).astype(jnp.int32)
    within = jnp.where(distance < 8, distance, 8 + beyond)
    return within + 16 * (offset > 0).astype(jnp.int32)


def wrapped_offsets(shape, axis, size):
    place = lax.broadcasted_iota(jnp.int32, shape, axis)
    return jnp.where(place < size, place, place - 2 * size)


def full(shape):
    return pl.BlockSpec(shape, lambda *_: (0,) * len(shape), pipeline_mode=pl.Buffered(1))


def row_spec(shape, first=0):
    return pl.BlockSpec(
        (1,) + tuple(shape), lambda step, *_: (step + first,) + (0,) * len(shape)
    )


def cost(products, moved, exps=0):
    return pl.CostEstimate(flops=2 * products, bytes_accessed=moved, transcendentals=exps)


def params(limit=VMEM_BYTES):
    return pltpu.CompilerParams(
        vmem_limit_bytes=limit, dimension_semantics=("arbitrary",)
    )


def bias_kernel(size, table_ref, out_ref):
    buckets, heads = table_ref.shape
    hot = (
        lax.broadcasted_iota(jnp.int32, (buckets, 2 * size), 0)
        == bucket_of(-wrapped_offsets((buckets, 2 * size), 1, size))
    ).astype(BF)
    by_offset = dot_tn(table_ref[...], hot)
    for head in range(heads):
        line = jnp.broadcast_to(by_offset[head : head + 1, :], (size, 2 * size))
        out_ref[head] = pltpu.roll(line, 0, 1, stride=1, stride_axis=0).astype(BF)


def bias_tables(rel_bias, size):
    heads = rel_bias.shape[1]
    return pl.pallas_call(
        functools.partial(bias_kernel, size),
        out_shape=jax.ShapeDtypeStruct((heads, size, 2 * size), BF),
        compiler_params=pltpu.CompilerParams(vmem_limit_bytes=VMEM_BYTES),
    )(rel_bias)


def fold_offsets(heads):
    count, width = heads[0].shape
    while count > 8:
        count = count // 2
        heads = [rows[:count] + pltpu.roll(rows[count:], width - count, 1) for rows in heads]
    return heads


def bias_grad_kernel(heads, *refs):
    acc_refs, out_ref = refs[:-1], refs[-1]
    rows = sum(acc_ref[...] for acc_ref in acc_refs)
    width = rows.shape[1]
    buckets = out_ref.shape[1]
    place = lax.broadcasted_iota(jnp.int32, rows.shape, 0)
    for bit in (4, 2, 1):
        rows = jnp.where((place & bit) > 0, pltpu.roll(rows, width - bit, 1), rows)
    hot = (
        lax.broadcasted_iota(jnp.int32, (width, buckets), 1)
        == bucket_of(-wrapped_offsets((width, buckets), 0, width // 2))
    ).astype(BF)
    first, rest = split_bf(rows)
    second, third = split_bf(rows - first.astype(F32))
    table = dot_nn(first, hot) + dot_nn(second, hot) + dot_nn(third, hot)
    for head in range(heads):
        out_ref[head : head + 1, :] = jnp.sum(table[8 * head : 8 * head + 8], axis=0, keepdims=True)


def bias_grad(accs, buckets):
    heads, _, width = accs[0].shape
    out = pl.pallas_call(
        functools.partial(bias_grad_kernel, heads),
        out_shape=jax.ShapeDtypeStruct((heads, buckets), F32),
        compiler_params=pltpu.CompilerParams(vmem_limit_bytes=VMEM_BYTES),
        name="bias_grad",
    )(*[acc.reshape(heads * 8, width) for acc in accs])
    return out.T


class Row:
    def __init__(self, lengths_ref, place_ref, row, size):
        slots = lengths_ref.shape[1]
        base = place_ref[0] * size
        pos = base + lax.broadcasted_iota(jnp.int32, (1, size), 1)
        zero = jnp.int32(0)
        before, first, last, beyond = zero, zero, zero, zero
        own = jnp.zeros((1, size), jnp.int32)
        low = jnp.zeros((1, size), jnp.int32)
        high = jnp.zeros((1, size), jnp.int32)
        end = zero
        passed = lambda end, place: (end <= place).astype(jnp.int32)
        for slot in range(slots):
            end = end + lengths_ref[row, slot]
            before += passed(end, base - 1)
            first += passed(end, base)
            last += passed(end, base + size - 1)
            beyond += passed(end, base + size)
            own += passed(end, pos)
            low += passed(end, pos - size)
            high += passed(end, pos + size)
        before = jnp.where(base == 0, -1, before).astype(F32)
        low = jnp.where(pos < size, -1, low).astype(F32)
        own = own.astype(F32)
        col_own, col_low, col_high = (
            jnp.broadcast_to(item, (LANES, size)).T for item in (own, low, high.astype(F32))
        )
        self.in_low = col_own == before
        self.in_high = col_own == beyond.astype(F32)
        self.slot_low = col_low == first.astype(F32)
        self.slot_high = col_high == last.astype(F32)
        key = lax.broadcasted_iota(jnp.int32, (size, size), 0)
        query = lax.broadcasted_iota(jnp.int32, (size, size), 1)
        wide = lambda item: jnp.concatenate([item] * (size // LANES), axis=1)
        self.own = wide(col_own) == own
        self.alt = jnp.where(key > query, wide(col_low), jnp.where(key < query, wide(col_high), -2.0)) == own


def where_tiles(mask, left, right):
    lanes = mask.shape[1]
    return jnp.concatenate(
        [
            jnp.where(mask, left[:, start : start + lanes], right[:, start : start + lanes])
            for start in range(0, left.shape[1], lanes)
        ],
        axis=1,
    )


def store_group_masks(row, ref):
    _, _, size, lanes = ref.shape
    first = lax.broadcasted_iota(jnp.int32, (1, lanes), 1) < lanes // 2
    low = row.in_low.astype(F32)
    high = row.in_high.astype(F32)
    for part, group in enumerate((low, 1.0 - low - high, high)):
        ref[0, part] = jnp.where(first, group, 0.0).astype(BF)
        ref[1, part] = jnp.where(first, 0.0, group).astype(BF)


def by_group(pair, ref, half):
    return jnp.concatenate([pair * ref[half, part] for part in range(3)], axis=1)


def fold_rows(row, first, wide):
    lanes = wide[0].shape[1] // 3
    parts = [
        jnp.where(first, wide[0][:, here], wide[1][:, here])
        for here in (slice(part * lanes, (part + 1) * lanes) for part in range(3))
    ]
    return jnp.where(row.in_low, parts[0], jnp.where(row.in_high, parts[2], parts[1]))


def own_kernel(x_ref, gain1_ref, wq_ref, wk_ref, wv_ref, out_ref):
    x = x_ref[0].astype(F32)
    out_ref[0, 3] = (x * rms_scale(x) * gain1_ref[...].astype(F32)).astype(BF)
    for index, weight_ref in enumerate((wq_ref, wk_ref, wv_ref)):
        out_ref[0, index] = dot_nn(out_ref[0, 3], weight_ref[...]).astype(BF)


def own_projections(tokens, gain1, weights):
    rows, size, dim = tokens.shape
    constants = (gain1,) + tuple(weights)
    return pl.pallas_call(
        own_kernel,
        grid=(rows,),
        in_specs=[row_spec((size, dim))] + [full(item.shape) for item in constants],
        out_specs=row_spec((4, size, dim)),
        out_shape=jax.ShapeDtypeStruct((rows, 4, size, dim), BF),
        compiler_params=params(),
        cost_estimate=cost(3 * rows * size * dim * dim, rows * size * dim * 10),
        name="own_projections",
    )(tokens, *constants)


def row_sentences(lengths_ref, place_ref, row, size):
    where_pos = place_ref[0] * size + lax.broadcasted_iota(jnp.int32, (1, size), 1)
    found = jnp.zeros((1, size), jnp.int32)
    end = jnp.int32(0)
    for slot in range(lengths_ref.shape[1]):
        end = end + lengths_ref[row, slot]
        found = found + (end <= where_pos).astype(jnp.int32)
    return found


def attend_kernel(
    first,
    lengths_ref,
    place_ref,
    pair_ref,
    across_ref,
    own_ref,
    gains_ref,
    wk_ref,
    wv_ref,
    bias_hbm,
    *rest,
):
    edge_ref, p_ref, att_ref, mask_ref, group_ref, bias_ref, sem = rest[-7:]
    size, dim = pair_ref.shape[1:]
    copy = pltpu.make_async_copy(bias_hbm, bias_ref, sem)

    @pl.when(pl.program_id(0) == 0)
    def _():
        copy.start()

    heads = bias_ref.shape[0]
    pairs = heads // 2
    lanes = dim // pairs
    row = Row(lengths_ref, place_ref, pl.program_id(0) + first, size)
    mask_ref[0] = jnp.where(row.own, 0.0, NEGATIVE).astype(BF)
    mask_ref[1] = jnp.where(row.alt, 0.0, NEGATIVE).astype(BF)
    store_group_masks(row, group_ref)
    gain1 = gains_ref[0:1, :].astype(F32)
    own = own_ref[0, 3].astype(F32)
    sides = by_side(place_ref, pair_ref[0], across_ref[0])
    for part, (source, slot) in enumerate(zip(sides, (row.slot_low, row.slot_high))):
        x = source.astype(F32)
        edge_ref[0, 4 + part] = where_tiles(slot, x * rms_scale(x) * gain1, own).astype(BF)
    edges = edge_ref[0, 4:].reshape(2 * size, dim)
    first_half = lax.broadcasted_iota(jnp.int32, (1, lanes), 1) < lanes // 2
    for index, weight_ref in enumerate((wk_ref, wv_ref)):
        value = dot_nn(edges, weight_ref[...]).astype(BF)
        edge_ref[0, 2 * index : 2 * index + 2] = value.reshape(2, size, dim)

    @pl.when(pl.program_id(0) == 0)
    def _():
        copy.wait()

    for pair in range(pairs):
        cols = slice(pair * lanes, (pair + 1) * lanes)
        keys, values = key_groups(own_ref, edge_ref, cols)
        halves = []
        for half in range(2):
            head = 2 * pair + half
            scores = dot_nt(keys, by_group(own_ref[0, 0, :, cols], group_ref, half))
            bias = jnp.maximum(
                bias_ref[head, :, :size] + mask_ref[0], bias_ref[head, :, size:] + mask_ref[1]
            )
            scores = scores + bias.astype(F32)
            peak = jnp.max(scores, axis=0, keepdims=True)
            powers = jnp.exp(scores - peak)
            inverse = 1.0 / jnp.sum(powers, axis=0, keepdims=True)
            probs = (powers * inverse).astype(BF)
            p_ref[0, head] = probs
            halves.append(dot_tn(probs, values))
        att_ref[0, :, cols] = fold_rows(row, first_half, halves).astype(BF)


def attend(first, earlier, lengths, place, pair, across, own, gains, wk, wv, bias):
    count, size, dim = pair.shape
    rows = own.shape[0]
    heads = bias.shape[0]
    constants = (gains, wk, wv, bias)
    shapes = ((6, size, dim), (heads, size, size), (size, dim))
    start = 2 + 3 + len(constants)
    return pl.pallas_call(
        functools.partial(attend_kernel, first),
        grid_spec=pltpu.PrefetchScalarGridSpec(
            num_scalar_prefetch=2,
            grid=(count,),
            in_specs=[row_spec((size, dim))] * 2
            + [row_spec((4, size, dim), first)]
            + [full(item.shape) for item in constants[:-1]]
            + [pl.BlockSpec(memory_space=pl.ANY)] * (1 + len(earlier)),
            out_specs=[row_spec(shape, first) for shape in shapes],
            scratch_shapes=[
                pltpu.VMEM((2, size, size), BF),
                pltpu.VMEM((2, 3, size, 2 * dim // heads), BF),
                pltpu.VMEM(bias.shape, BF),
                pltpu.SemaphoreType.DMA,
            ],
        ),
        out_shape=[jax.ShapeDtypeStruct((rows,) + shape, BF) for shape in shapes],
        input_output_aliases={start + index: index for index in range(len(earlier))},
        compiler_params=params(),
        cost_estimate=cost(count * size * dim * (4 * dim + 36 * size), count * size * dim * 40),
        name="attend_rows",
    )(lengths, place, pair, across, own, *constants, *earlier)


def forward_kernel(
    rows,
    lengths_ref,
    place_ref,
    x_ref,
    att_ref,
    gains_ref,
    wo_ref,
    win_ref,
    wout_ref,
    block_ref,
    pooled_ref,
    pre_ref,
    after_hbm,
    n2_hbm,
    after_low,
    n2_all,
    total_ref,
    sems,
):
    _, size, dim = x_ref.shape
    slots = pooled_ref.shape[1]
    toks = rows * size
    step = pl.program_id(0)
    copies = [
        pltpu.make_async_copy(after_low, after_hbm, sems.at[0]),
        pltpu.make_async_copy(n2_all, n2_hbm, sems.at[1]),
    ]

    @pl.when(step == 0)
    def _():
        mixed = dot_nn(att_ref[...].reshape(toks, dim), wo_ref[...])
        after = x_ref[...].reshape(toks, dim).astype(F32) + mixed
        after_low[...] = after.astype(BF)
        total_ref[...] = after
        n2_all[...] = (after * rms_scale(after) * gains_ref[1:2, :].astype(F32)).astype(BF)
        for copy in copies:
            copy.start()

    pre = dot_nn(n2_all[...], win_ref[...])
    square = pre * pre
    gate = 0.5 + 0.5 * jnp.tanh(pre * (GELU_A + (GELU_A * GELU_B) * square))
    pre_ref[...] = pre.astype(BF)
    total_ref[...] += dot_nn((pre * gate).astype(BF), wout_ref[...])

    @pl.when(step == pl.num_programs(0) - 1)
    def _():
        gainf = gains_ref[2:3, :].astype(F32)
        for row in range(rows):
            here = slice(row * size, (row + 1) * size)
            block = total_ref[here, :].astype(BF)
            block_ref[row] = block
            out = block.astype(F32)
            final = out * rms_scale(out) * gainf
            found = row_sentences(lengths_ref, place_ref, row, size)
            member = (lax.broadcasted_iota(jnp.int32, (slots, size), 0) == found).astype(BF)
            high_part, low_part = split_bf(final)
            pooled_ref[row] = dot_nn(member, high_part) + dot_nn(member, low_part)
        for copy in copies:
            copy.wait()


def by_side(place_ref, pair, across):
    odd = place_ref[0] % 2 == 1
    return jnp.where(odd, pair, across), jnp.where(odd, across, pair)


def key_groups(own_ref, edge_ref, cols):
    return [
        jnp.concatenate(
            [edge_ref[0, 2 * index, :, cols], own_ref[0, 1 + index, :, cols], edge_ref[0, 2 * index + 1, :, cols]],
            axis=1,
        )
        for index in range(2)
    ]


def forward(lengths, place, tokens, att, gains, wo, win, wout):
    rows, size, dim = tokens.shape
    slots = lengths.shape[1]
    hidden = win.shape[1]
    toks = rows * size
    constants = (tokens, att, gains, wo)
    anywhere = pl.BlockSpec(memory_space=pl.ANY)
    out_of = lambda shape, kind=BF: jax.ShapeDtypeStruct(shape, kind)
    return pl.pallas_call(
        functools.partial(forward_kernel, rows),
        grid_spec=pltpu.PrefetchScalarGridSpec(
            num_scalar_prefetch=2,
            grid=(hidden // dim,),
            in_specs=[full(item.shape) for item in constants]
            + [
                pl.BlockSpec((dim, dim), lambda step, *_: (0, step)),
                pl.BlockSpec((dim, dim), lambda step, *_: (step, 0)),
            ],
            out_specs=[
                full((rows, size, dim)),
                full((rows, slots, dim)),
                pl.BlockSpec((toks, dim), lambda step, *_: (0, step)),
                anywhere,
                anywhere,
            ],
            scratch_shapes=[
                pltpu.VMEM((toks, dim), BF),
                pltpu.VMEM((toks, dim), BF),
                pltpu.VMEM((toks, dim), F32),
                pltpu.SemaphoreType.DMA((2,)),
            ],
        ),
        out_shape=[
            out_of((rows, size, dim)),
            out_of((rows, slots, dim), F32),
            out_of((toks, hidden)),
            out_of((toks, dim)),
            out_of((toks, dim)),
        ],
        compiler_params=params(),
        cost_estimate=cost(toks * dim * (dim + 2 * hidden), toks * (hidden * 2 + dim * 20)),
        name="feed_forward",
    )(lengths, place, *constants, win, wout)


def store_split(core, value, refs, count, first=0):
    if len(refs) == 1:
        refs[0][first : first + value.shape[0], :] = value
        return
    groups = value.shape[0] // (2 * count)
    for group in range(groups):
        even = value[2 * group * count : (2 * group + 1) * count]
        odd = value[(2 * group + 1) * count : (2 * group + 2) * count]

        refs[0][group, first : first + count, :] = jnp.where(core == 0, even, odd)
        refs[1][group, first : first + count, :] = jnp.where(core == 0, odd, even)


def feed_back_kernel(
    rows,
    parts,
    lengths_ref,
    place_ref,
    block_ref,
    cot_ref,
    pool_ref,
    graw_ref,
    pooled_ref,
    gain_ref,
    pre_ref,
    win_ref,
    wout_ref,
    after_hbm,
    n2_hbm,
    att_hbm,
    wo_hbm,
    back_ref,
    gains_ref,
    *rest,
):
    split = len(rest) == 14
    per = 2 if split else 1
    in_refs, out_refs, small_refs = (rest[i * per : (i + 1) * per] for i in range(3))
    gout_ref, branch_ref, gn2_ref, after_ref, n2_ref, att_ref, wo_ref, sems = rest[3 * per :]
    _, size, dim = block_ref.shape
    toks = rows * size
    slots = pool_ref.shape[1]
    step = pl.program_id(0)
    tiles = pl.num_programs(0) - 1
    core = place_ref[1]
    copies = [
        pltpu.make_async_copy(n2_hbm, n2_ref, sems.at[0]),
        pltpu.make_async_copy(after_hbm, after_ref, sems.at[1]),
        pltpu.make_async_copy(att_hbm, att_ref, sems.at[2]),
        pltpu.make_async_copy(wo_hbm, wo_ref, sems.at[3]),
    ]

    @pl.when(step == 0)
    def _():
        for copy in copies:
            copy.start()
        gainf = gain_ref[2:3, :].astype(F32)
        gain_f = jnp.zeros((1, dim), F32)
        for row in range(rows):
            here = slice(row * size, (row + 1) * size)
            found = row_sentences(lengths_ref, place_ref, row, size)
            member = (lax.broadcasted_iota(jnp.int32, (slots, size), 0) == found).astype(BF)
            high_part, low_part = split_bf(pool_ref[row])
            g_final = dot_tn(member, high_part) + dot_tn(member, low_part)
            out = block_ref[row].astype(F32)
            scale = rms_scale(out)
            gain_f = gain_f + jnp.sum(g_final * out * scale, axis=0, keepdims=True)
            g_out = rms_back(out, scale, g_final * gainf) + cot_ref[row].astype(F32)
            gout_ref[here, :] = g_out
            branch_ref[here, :] = g_out.astype(BF)
        gains_ref[...] = jnp.zeros_like(gains_ref)
        gains_ref[0:1, :] = gain_f
        copies[0].wait()

    @pl.when(step < tiles)
    def _():
        g_hidden = dot_nt(branch_ref[...], wout_ref[...])
        pre = pre_ref[...].astype(F32)
        square = pre * pre
        gate = 0.5 + 0.5 * jnp.tanh(pre * (GELU_A + (GELU_A * GELU_B) * square))
        act = pre * gate
        value = dot_tn(branch_ref[...], act.astype(BF)).astype(BF)
        store_split(core, value, out_refs, dim // parts)
        slope = gate + act * (1.0 - gate) * (2 * GELU_A + (6 * GELU_A * GELU_B) * square)
        g_pre = (g_hidden * slope).astype(BF)
        value = dot_tn(g_pre, n2_ref[...]).astype(BF)
        store_split(core, value, in_refs, tiles * dim // parts)
        part = dot_nt(g_pre, win_ref[...])

        @pl.when(step == 0)
        def _():
            gn2_ref[...] = part

        @pl.when(step > 0)
        def _():
            gn2_ref[...] += part

    @pl.when(step == tiles)
    def _():
        for copy in copies[1:]:
            copy.wait()
        gain2 = gain_ref[1:2, :].astype(F32)
        gain_2 = jnp.zeros((1, dim), F32)
        for row in range(rows):
            here = slice(row * size, (row + 1) * size)
            after = after_ref[here, :].astype(F32)
            g_n2 = gn2_ref[here, :]
            scale = rms_scale(after)
            gain_2 = gain_2 + jnp.sum(g_n2 * after * scale, axis=0, keepdims=True)
            g_after = gout_ref[here, :] + rms_back(after, scale, g_n2 * gain2)
            back_ref[row, 1] = g_after.astype(BF)
            branch_ref[here, :] = g_after.astype(BF)
        gains_ref[1:2, :] = gain_2
        g_mix = dot_nt(branch_ref[...], wo_ref[...]).astype(BF)
        for row in range(rows):
            back_ref[row, 0] = g_mix[row * size : (row + 1) * size]
        value = dot_tn(branch_ref[...], att_ref[...].reshape(toks, dim)).astype(BF)
        store_split(core, value, small_refs, dim // parts)
        left_high, left_low = split_bf(jnp.where(place_ref[0] == 0, graw_ref[...], 0.0))
        right_high, right_low = split_bf(pooled_ref[...])
        value = dot_tn(left_high, right_high)
        value += dot_tn(left_high, right_low) + dot_tn(left_low, right_high)
        first = dim // parts if split else dim
        store_split(core, value.astype(BF), small_refs, dim // parts, first)


def feed_back(parts, lengths, place, block, after, cot, att, n2, pre, pool, graw, pooled, gains, weights):
    rows, size, dim = block.shape
    hidden = pre.shape[1]
    tiles = hidden // dim
    toks = rows * size
    wo, win, wout = weights
    split = (dim // parts) % 16 == 0 and dim % (2 * hidden // parts) == 0
    tile = lambda step: jnp.minimum(step, tiles - 1)
    if split:
        groups = parts // 2
        wide = hidden // parts
        inner = dim // (2 * wide)
        narrow = dim // parts
        in_specs = [pl.BlockSpec((inner, wide, dim), lambda step, *_: (tile(step), 0, 0))] * 2
        out_specs = [pl.BlockSpec((groups, narrow, dim), lambda step, *_: (0, tile(step), 0))] * 2
        small_specs = [full((groups, 2 * narrow, dim))] * 2
        shapes = [(groups, wide, dim)] * 2 + [(groups, tiles * narrow, dim)] * 2 + [(groups, 2 * narrow, dim)] * 2
    else:
        in_specs = [pl.BlockSpec((dim, dim), lambda step, *_: (tile(step), 0))]
        out_specs = [pl.BlockSpec((dim, dim), lambda step, *_: (tile(step), 0))]
        small_specs = [full((2 * dim, dim))]
        shapes = [(hidden, dim), (tiles * dim, dim), (2 * dim, dim)]
    constants = (block, cot, pool, graw, pooled, gains)
    outs = pl.pallas_call(
        functools.partial(feed_back_kernel, rows, parts),
        grid_spec=pltpu.PrefetchScalarGridSpec(
            num_scalar_prefetch=2,
            grid=(tiles + 1,),
            in_specs=[full(item.shape) for item in constants]
            + [
                pl.BlockSpec((toks, dim), lambda step, *_: (0, tile(step))),
                pl.BlockSpec((dim, dim), lambda step, *_: (0, tile(step))),
                pl.BlockSpec((dim, dim), lambda step, *_: (tile(step), 0)),
            ]
            + [pl.BlockSpec(memory_space=pl.ANY)] * 4,
            out_specs=[full((rows, 2, size, dim)), full((8, dim))]
            + in_specs
            + out_specs
            + small_specs,
            scratch_shapes=[
                pltpu.VMEM((toks, dim), F32),
                pltpu.VMEM((toks, dim), BF),
                pltpu.VMEM((toks, dim), F32),
                pltpu.VMEM((toks, dim), BF),
                pltpu.VMEM((toks, dim), BF),
                pltpu.VMEM((rows, size, dim), BF),
                pltpu.VMEM((dim, dim), BF),
                pltpu.SemaphoreType.DMA((4,)),
            ],
        ),
        out_shape=[
            jax.ShapeDtypeStruct((rows, 2, size, dim), BF),
            jax.ShapeDtypeStruct((8, dim), F32),
        ]
        + [jax.ShapeDtypeStruct(shape, BF) for shape in shapes],
        compiler_params=params(),
        cost_estimate=cost(
            toks * dim * (4 * hidden + 2 * dim), toks * (hidden * 4 + dim * 20) + 8 * hidden * dim
        ),
        name="feed_back",
    )(lengths, place, *constants, pre, win, wout, after, n2, att, wo)
    if split:
        mine, theirs = outs[2::2], outs[3::2]
    else:
        whole = [
            outs[2].reshape(parts, hidden // parts, dim),
            outs[3].reshape(tiles, parts, dim // parts, dim).transpose(1, 0, 2, 3),
            outs[4].reshape(2, parts, dim // parts, dim).transpose(1, 0, 2, 3),
        ]
        mine, theirs = split_core(whole)
    return outs[0], outs[1], mine, theirs


def split_core(blocks):
    core = (lax.axis_index("batch") % 2).astype(jnp.int32)
    pairs = [item.reshape((item.shape[0] // 2, 2, -1, item.shape[-1])) for item in blocks]
    pick = lambda item, place: lax.dynamic_index_in_dim(item, place, 1, keepdims=False)
    return [pick(item, core) for item in pairs], [pick(item, 1 - core) for item in pairs]


def attend_grad_kernel(parts, place_ref, n1_ref, own_ref, edge_hbm, n1_edge_hbm, *rest):
    refs, (edge_ref, n1_edge_ref, sems) = rest[:-3], rest[-3:]
    rows, _, size, dim = own_ref.shape
    step = pl.program_id(0)
    width = dim // parts if len(refs) == 2 else dim
    flat = lambda ref: ref[...].reshape(-1, dim)
    n1_copy = pltpu.make_async_copy(n1_edge_hbm.at[:, 4:6], n1_edge_ref, sems.at[0])
    copies = [
        pltpu.make_async_copy(
            edge_hbm.at[:, 3 + 2 * index : 5 + 2 * index], edge_ref.at[index], sems.at[1 + index]
        )
        for index in range(2)
    ]

    @pl.when(step == 0)
    def _():
        n1_copy.start()
        for copy in copies:
            copy.start()
        value = dot_tn(flat(own_ref), flat(n1_ref)).astype(BF)
        store_split(place_ref[1], value, refs, dim // parts, 0)
        n1_copy.wait()

    for index in range(2):

        @pl.when(step == 1 + index)
        def _():
            copies[index].wait()
            value = dot_tn(flat(own_ref), flat(n1_ref)) + dot_tn(flat(edge_ref.at[index]), flat(n1_edge_ref))
            store_split(place_ref[1], value.astype(BF), refs, dim // parts, (1 + index) * width)


def attend_grad(parts, place, own, edges, grads):
    rows, _, size, dim = own.shape
    narrow = dim // parts
    split = narrow % 16 == 0
    shape = (parts // 2, 3 * narrow, dim) if split else (3 * dim, dim)
    copies = 2 if split else 1
    outs = pl.pallas_call(
        functools.partial(attend_grad_kernel, parts),
        grid_spec=pltpu.PrefetchScalarGridSpec(
            num_scalar_prefetch=1,
            grid=(3,),
            in_specs=[
                pl.BlockSpec((rows, 1, size, dim), lambda step, *_: (0, 3, 0, 0)),
                pl.BlockSpec((rows, 1, size, dim), lambda step, *_: (0, step, 0, 0)),
                pl.BlockSpec(memory_space=pl.ANY),
                pl.BlockSpec(memory_space=pl.ANY),
            ],
            out_specs=[full(shape)] * copies,
            scratch_shapes=[
                pltpu.VMEM((2, rows, 2, size, dim), BF),
                pltpu.VMEM((rows, 2, size, dim), BF),
                pltpu.SemaphoreType.DMA((3,)),
            ],
        ),
        out_shape=[jax.ShapeDtypeStruct(shape, BF)] * copies,
        compiler_params=params(),
        cost_estimate=cost(rows * size * dim * dim * 7, rows * size * dim * 26),
        name="attend_grad",
    )(place, own, grads, grads, edges)
    if split:
        return outs[0], outs[1]
    mine, theirs = split_core([outs[0].reshape(3, parts, narrow, dim).transpose(1, 0, 2, 3)])
    return mine[0], theirs[0]


def attend_back_kernel(
    first,
    lengths_ref,
    place_ref,
    own_ref,
    pair_ref,
    across_ref,
    qkv_ref,
    edge_ref,
    p_ref,
    back_ref,
    gain_ref,
    wq_hbm,
    wk_hbm,
    wv_hbm,
    *rest,
):
    grad_ref, part_ref, to_pair_ref, to_across_ref, offset_ref, gains_ref = rest[-11:-5]
    mask_ref, group_ref, acc_ref, weight_ref, sems = rest[-5:]
    copies = [
        pltpu.make_async_copy(source, weight_ref.at[index], sems.at[index])
        for index, source in enumerate((wq_hbm, wk_hbm, wv_hbm))
    ]
    size, dim = own_ref.shape[1:]
    heads = p_ref.shape[1]
    pairs = heads // 2
    lanes = dim // pairs
    step = pl.program_id(0)
    row = Row(lengths_ref, place_ref, step + first, size)
    mask_ref[...] = row.own.astype(F32)

    @pl.when(step == 0)
    def _():
        for copy in copies:
            copy.start()
        acc_ref[...] = jnp.zeros_like(acc_ref)
        gains_ref[...] = jnp.zeros_like(gains_ref)

    first_half = lax.broadcasted_iota(jnp.int32, (1, lanes), 1) < lanes // 2
    store_group_masks(row, group_ref)
    half_size = size // 2
    for pair in range(pairs):
        cols = slice(pair * lanes, (pair + 1) * lanes)
        keys, values = key_groups(qkv_ref, edge_ref, cols)
        q_groups = [by_group(qkv_ref[0, 0, :, cols], group_ref, half) for half in range(2)]
        o_groups = [by_group(back_ref[0, 0, :, cols], group_ref, half) for half in range(2)]
        d_q, scores_pair = [], []
        for half in range(2):
            head = 2 * pair + half
            g_probs = dot_nt(values, o_groups[half])
            full_probs = p_ref[0, head].astype(F32)
            product = full_probs * g_probs
            inner = jnp.sum(product, axis=0, keepdims=True)
            g_scores = product - full_probs * inner
            on_own = g_scores * mask_ref[...]
            off_own = g_scores - on_own
            acc_ref[head, :, :half_size] += on_own[:half_size, :half_size] + on_own[half_size:, half_size:]
            acc_ref[head, :, half_size:size] += on_own[:half_size, half_size:] + off_own[half_size:, :half_size]
            acc_ref[head, :, size : size + half_size] += off_own[:half_size, :half_size] + off_own[half_size:, half_size:]
            acc_ref[head, :, size + half_size :] += off_own[:half_size, half_size:] + on_own[half_size:, :half_size]
            scores_pair.append(g_scores.astype(BF))
            d_q.append(dot_tn(scores_pair[-1], keys))
        grad_ref[0, 0, :, cols] = fold_rows(row, first_half, d_q).astype(BF)
        probs_pair = [p_ref[0, 2 * pair], p_ref[0, 2 * pair + 1]]
        for index, (left, right) in enumerate(((scores_pair, q_groups), (probs_pair, o_groups))):
            value = dot_nn(jnp.concatenate(left, axis=1), jnp.concatenate(right, axis=0)).astype(BF)
            grad_ref[0, 3 + 2 * index, :, cols] = value[:, :lanes]
            grad_ref[0, 1 + index, :, cols] = value[:, lanes : 2 * lanes]
            grad_ref[0, 4 + 2 * index, :, cols] = value[:, 2 * lanes :]

    @pl.when(step == 0)
    def _():
        for copy in copies:
            copy.wait()

    gain1 = gain_ref[0:1, :].astype(F32)
    g_whole = None
    for index in range(2):
        edge_grad = grad_ref[0, 3 + 2 * index : 5 + 2 * index].reshape(2 * size, dim)
        left = jnp.concatenate([edge_grad, grad_ref[0, 1 + index]], axis=0)
        term = dot_nt(left, weight_ref[1 + index])
        g_whole = term if g_whole is None else g_whole + term
    zero = jnp.zeros((size, dim), F32)
    g_low = where_tiles(row.slot_low, g_whole[:size], zero)
    g_high = where_tiles(row.slot_high, g_whole[size : 2 * size], zero)
    g_own = g_whole[2 * size :] + (g_whole[:size] - g_low) + (g_whole[size : 2 * size] - g_high)
    g_own = g_own + dot_nt(grad_ref[0, 0], weight_ref[0])
    gain_1 = jnp.zeros((1, dim), F32)
    low, high = by_side(place_ref, pair_ref[0], across_ref[0])
    results = []
    for source, g_norm in ((own_ref[0], g_own), (low, g_low), (high, g_high)):
        x = source.astype(F32)
        scale = rms_scale(x)
        gain_1 = gain_1 + jnp.sum(g_norm * x * scale, axis=0, keepdims=True)
        results.append(rms_back(x, scale, g_norm * gain1))
    part_ref[0] = (results[0] + back_ref[0, 1].astype(F32)).astype(BF)
    odd = place_ref[0] % 2 == 1
    to_pair_ref[0] = jnp.where(odd, results[1], results[2]).astype(BF)
    to_across_ref[0] = jnp.where(odd, results[2], results[1]).astype(BF)
    gains_ref[0:1, :] += gain_1

    @pl.when(step == pl.num_programs(0) - 1)
    def _():
        for head, rows in enumerate(fold_offsets([acc_ref[head] for head in range(heads)])):
            offset_ref[head] = rows


def attend_back(first, count, halo, earlier, lengths, place, x, low, high, own, edges, p, back, gains, weights):
    rows, size, dim = x.shape
    heads = p.shape[1]
    constants = (gains,) + tuple(weights)
    anywhere = pl.BlockSpec(memory_space=pl.ANY)
    start = 2 + 7 + len(constants)
    aliases = {start + index: index for index in range(len(earlier))}
    return pl.pallas_call(
        functools.partial(attend_back_kernel, first),
        grid_spec=pltpu.PrefetchScalarGridSpec(
            num_scalar_prefetch=2,
            grid=(count,),
            in_specs=[row_spec((size, dim), first)] * 3
            + [row_spec((3, size, dim), first), row_spec((4, size, dim), first)]
            + [row_spec((heads, size, size), first), row_spec((2, size, dim), first)]
            + [full(gains.shape)]
            + [anywhere] * (len(weights) + len(earlier)),
            out_specs=[
                row_spec((7, size, dim), first),
                row_spec((size, dim), first),
                row_spec((size, dim), first - halo[0]),
                row_spec((size, dim), first - halo[0]),
            ]
            + [full((heads, 8, 2 * size)), full((8, dim))],
            scratch_shapes=[
                pltpu.VMEM((size, size), F32),
                pltpu.VMEM((2, 3, size, 2 * dim // heads), BF),
                pltpu.VMEM((heads, size // 2, 2 * size), F32),
                pltpu.VMEM((3, dim, dim), BF),
                pltpu.SemaphoreType.DMA((3,)),
            ],
        ),
        out_shape=[
            jax.ShapeDtypeStruct((rows, 7, size, dim), BF),
            jax.ShapeDtypeStruct((rows, size, dim), BF),
            jax.ShapeDtypeStruct((halo[1], size, dim), BF),
            jax.ShapeDtypeStruct((halo[1], size, dim), BF),
            jax.ShapeDtypeStruct((heads, 8, 2 * size), F32),
            jax.ShapeDtypeStruct((8, dim), F32),
        ],
        input_output_aliases=aliases,
        compiler_params=params(),
        cost_estimate=cost(
            count * size * dim * (9 * dim + 128 * size), count * size * dim * 60
        ),
        name="attend_back_rows",
    )(lengths, place, x, low, high, own, edges, p, back, *constants, *earlier)


def flip(block, axis, bit):
    count = lax.axis_size(axis)
    return lax.ppermute(block, axis, [(i, i ^ bit) for i in range(count)])


def sum_along(block, axis):
    bit = 1
    while bit < lax.axis_size(axis):
        block = block + flip(block, axis, bit)
        bit *= 2
    return block


def bit_places(axis):
    return [1 << level for level in range((lax.axis_size(axis) - 1).bit_length())]


def gather_batch(block):
    place = lax.axis_index("batch")
    bits = bit_places("batch")
    gathered = block[None]
    for bit in reversed(bits):
        other = flip(gathered, "batch", bit)
        upper = (place & bit) > 0
        gathered = jnp.stack(
            [jnp.where(upper, other, gathered), jnp.where(upper, gathered, other)], axis=1
        )
        gathered = gathered.reshape((-1,) + block.shape)
    return gathered.reshape((-1,) + block.shape[1:])


def halve(block, bits, bit):
    axis = bits.index(bit)
    mine = ((lax.axis_index("batch") & bit) > 0).astype(jnp.int32)
    send = lax.dynamic_index_in_dim(block, 1 - mine, axis, keepdims=False)
    keep = lax.dynamic_index_in_dim(block, mine, axis, keepdims=False)
    return keep + flip(send, "batch", bit), [item for item in bits if item != bit]


def after(value, *others):
    return lax.optimization_barrier((value,) + tuple(others))[0]


def stage_kernel(groups, place_ref, *refs):
    ins = refs[: 2 * sum(len(group) for group in groups)]
    outs = refs[len(ins) :]
    taken = 0
    for index, group in enumerate(groups):
        first = 0
        for count in group:
            value = ins[2 * taken][0, 0, 0] + ins[2 * taken + 1][0, 0, 0]
            taken += 1
            for which in range(2):

                @pl.when(pl.program_id(0) == which)
                def _():
                    outs[2 * index + which][0, 0, first : first + count, :] = value

            first += count


def stage(place, groups, bits, pieces):
    columns = groups[0][0][0].shape[-1]
    lead = bits[0][0][0] * bits[0][0][1]
    if any(count % (16 * pieces) or first % count for group in groups for _, _, first, count in group):
        sends, keeps = [], []
        for index, group in enumerate(groups):
            before, behind = bits[index][0]
            total = jnp.concatenate(
                [(kept + arrived)[..., first : first + count, :].reshape(-1, count, columns)
                 for kept, arrived, first, count in group],
                axis=1,
            ).reshape(before, 2, behind, -1, columns)
            pick = lambda which: lax.dynamic_index_in_dim(total, which, 1, keepdims=False)
            sends.append(pick(1 - place[index]).reshape(lead, 1, -1, columns))
            keeps.append(pick(place[index]).reshape(lead, 1, -1, columns))
        return sends, keeps
    in_specs, operands, out_specs, shapes = [], [], [], []
    for index, group in enumerate(groups):
        before, behind = bits[index][0]
        total = 0

        def place_of(half, step, chunk, places, index=index, behind=behind):
            mine = places[index]
            where_at = jnp.where(half == 0, 1 - mine, mine)
            return step // behind, where_at, step % behind, chunk

        for kept, arrived, first, count in group:
            rows = count // pieces
            total += rows
            shape = (before, 2, behind) + kept.shape[-2:]

            def index_map(half, step, chunk, places, place_of=place_of, first=first, rows=rows):
                one, two, three, four = place_of(half, step, chunk, places)
                return one, two, three, four + first // rows, 0

            for item in (kept, arrived):
                in_specs.append(pl.BlockSpec((1, 1, 1, rows, columns), index_map))
                operands.append(item.reshape(shape))
        for which in range(2):

            def out_map(half, step, chunk, places, which=which):
                if which == 0:
                    step = jnp.where(half == 0, step, lead - 1)
                    chunk = jnp.where(half == 0, chunk, pieces - 1)
                else:
                    step = jnp.where(half == 1, step, 0)
                    chunk = jnp.where(half == 1, chunk, 0)
                return step, chunk, 0, 0

            out_specs.append(pl.BlockSpec((1, 1, total, columns), out_map))
            shapes.append(jax.ShapeDtypeStruct((lead, pieces, total, columns), BF))
    outs = pl.pallas_call(
        functools.partial(
            stage_kernel, [[count // pieces for _, _, _, count in group] for group in groups]
        ),
        grid_spec=pltpu.PrefetchScalarGridSpec(
            num_scalar_prefetch=1, grid=(2, lead, pieces), in_specs=in_specs, out_specs=out_specs
        ),
        out_shape=shapes,
        compiler_params=pltpu.CompilerParams(
            vmem_limit_bytes=VMEM_BYTES, dimension_semantics=("arbitrary",) * 3
        ),
        name="halving_stage",
    )(place, *operands)
    return outs[0::2], outs[1::2]


class BatchSum:
    def __init__(self, mine, theirs, streams):
        bits = bit_places("batch")
        arrived = [flip(item, "batch", bits[0]) for item in theirs]
        self.groups = [
            [(mine[item], arrived[item], first, rows) for item, first, rows in stream] for stream in streams
        ]
        self.bits = [bits[1:][::-1]] * len(streams)
        self.steps = len(bits) - 1
        self.done = 0

    def hold(self, *others):
        self.groups = [
            [(kept, after(arrived, *others), first, rows) for kept, arrived, first, rows in group]
            for group in self.groups
        ]

    def advance(self):
        moved, bits, places = [], [], []
        me = lax.axis_index("batch")
        for index, left in enumerate(self.bits):
            bit = left[::-1][index % len(left)]
            axis = left.index(bit)
            moved.append(bit)
            places.append(((me & bit) > 0).astype(jnp.int32))
            bits.append(((1 << axis, 1 << (len(left) - 1 - axis)),))
        sends, keeps = stage(jnp.stack(places), self.groups, bits, 1)
        self.groups = [
            [(keep, flip(send, "batch", bit), 0, keep.shape[2])]
            for keep, send, bit in zip(keeps, sends, moved)
        ]
        self.bits = [[item for item in left if item != bit] for left, bit in zip(self.bits, moved)]
        self.done += 1
        return sends

    def total(self):
        return [(kept + arrived).reshape(kept.shape[-2:]) for ((kept, arrived, _, _),) in self.groups]


def pack_kernel(tiles_rows, keep_a, come_a, keep_b, come_b, out_ref):
    groups, _, wide = out_ref.shape
    cols = wide // 2
    rows = tiles_rows // groups
    first = keep_a[...] + come_a[...]
    second = keep_b[...] + come_b[...]
    for group in range(groups):
        here = slice(group * cols, (group + 1) * cols)
        out_ref[group, :, :cols] = first[:, here]
        for part in range(groups):
            out_ref[group, part * rows : (part + 1) * rows, cols:] = second[
                group * rows : (group + 1) * rows, part * cols : (part + 1) * cols
            ]
        out_ref[group, tiles_rows:, cols:] = second[tiles_rows:, here]


def pack(stream_a, stream_b, tiles_rows, groups):
    (keep_a, come_a), (keep_b, come_b) = stream_a, stream_b
    rows, dim = keep_a.shape[-2:]
    flat = lambda item: item.reshape(rows, dim)
    shape = (groups, rows, 2 * dim // groups)
    if tiles_rows // groups % 16 == 0:
        return pl.pallas_call(
            functools.partial(pack_kernel, tiles_rows),
            out_shape=jax.ShapeDtypeStruct(shape, BF),
            compiler_params=pltpu.CompilerParams(vmem_limit_bytes=VMEM_BYTES),
            name="pack_places",
        )(flat(keep_a), flat(come_a), flat(keep_b), flat(come_b))
    first = flat(keep_a + come_a).reshape(rows, groups, -1).transpose(1, 0, 2)
    second = flat(keep_b + come_b)
    out = second[:tiles_rows].reshape(groups, -1, groups, dim // groups).transpose(0, 2, 1, 3)
    out = out.reshape(groups, tiles_rows, -1)
    last = second[tiles_rows:].reshape(-1, groups, dim // groups).transpose(1, 0, 2)
    return jnp.concatenate([first, jnp.concatenate([out, last], axis=1)], axis=2)


def columns_kernel(keep_a, come_a, keep_b, come_b, out_ref):
    groups, rows, cols = out_ref.shape
    half = keep_a.shape[0]
    first = keep_a[...] + come_a[...]
    second = keep_b[...] + come_b[...]
    for group in range(groups):
        here = slice(group * cols, (group + 1) * cols)
        out_ref[group, :half, :] = first[:, here]
        out_ref[group, half:, :] = second[:, here]


def pack_columns(streams, groups):
    rows, dim = streams[0][0].shape[-2:]
    pieces = [item.reshape(rows, dim) for keep, come in streams for item in (keep, come)]
    if rows % 16:
        total = jnp.concatenate([pieces[0] + pieces[1], pieces[2] + pieces[3]], axis=0)
        return total.reshape(2 * rows, groups, -1).transpose(1, 0, 2)
    return pl.pallas_call(
        columns_kernel,
        out_shape=jax.ShapeDtypeStruct((groups, 2 * rows, dim // groups), BF),
        compiler_params=pltpu.CompilerParams(vmem_limit_bytes=VMEM_BYTES),
        name="pack_columns",
    )(*pieces)


def split_dot(dot, left, right):
    return dot(left[0], right[0]) + (dot(left[0], right[1]) + dot(left[1], right[0]))


def embed_kernel(sum_ref, more_ref, count_ref, proj_ref, pooled_ref, emb_ref, inverse_ref):
    pooled = (sum_ref[...] + more_ref[...]) / count_ref[...]
    high, low = split_bf(pooled)
    raw = dot_nn(high, proj_ref[...]) + dot_nn(low, proj_ref[...])
    inverse = lax.rsqrt(jnp.sum(raw * raw, axis=-1, keepdims=True) + EPS)
    pooled_ref[...] = pooled
    emb_ref[...] = raw * inverse
    inverse_ref[...] = jnp.broadcast_to(inverse, inverse_ref.shape)


def embed(sums, more, counts, w_proj):
    own, dim = sums.shape
    shapes = ((own, dim), (own, dim), (own, LANES))
    return pl.pallas_call(
        embed_kernel,
        out_shape=[jax.ShapeDtypeStruct(shape, F32) for shape in shapes],
        compiler_params=pltpu.CompilerParams(vmem_limit_bytes=VMEM_BYTES),
        name="embed",
    )(sums, more, counts, w_proj)


def contrast_kernel(
    place_ref,
    own_ref,
    x_ref,
    y_ref,
    xy_ref,
    other_ref,
    inverse_ref,
    partner_ref,
    count_ref,
    proj_ref,
    loss_ref,
    graw_ref,
    pool_ref,
    all_ref,
    logit_ref,
):
    own, dim = own_ref.shape
    total = all_ref.shape[0]
    me = place_ref[0]
    rows_of = lambda place: pl.ds(pl.multiple_of(place * own, own), own)
    for step, ref in enumerate((own_ref, x_ref, y_ref, xy_ref)):
        place = jnp.bitwise_xor(me, 2 * step)
        all_ref[rows_of(place), :] = ref[...]
        all_ref[rows_of(jnp.bitwise_xor(place, 1)), :] = other_ref[step]
    everyone = split_bf(all_ref[...])
    logits = SHARPNESS * split_dot(dot_nt, everyone, everyone)
    row = lax.broadcasted_iota(jnp.int32, (total, total), 0)
    column = lax.broadcasted_iota(jnp.int32, (total, total), 1)
    logits = jnp.where(row == column, NEGATIVE, logits)
    logit_ref[...] = logits
    peak = jnp.max(logits, axis=0, keepdims=True)
    lse_all = peak + jnp.log(jnp.sum(jnp.exp(logits - peak), axis=0, keepdims=True))
    mine = logit_ref[rows_of(me), :]
    peak = jnp.max(mine, axis=1, keepdims=True)
    lse_own = peak + jnp.log(jnp.sum(jnp.exp(mine - peak), axis=1, keepdims=True))
    target = (lax.broadcasted_iota(jnp.int32, (own, total), 1) == partner_ref[...]).astype(F32)
    loss = lse_own - jnp.sum(jnp.where(target > 0, mine, 0.0), axis=1, keepdims=True)
    loss_ref[...] = jnp.broadcast_to(loss, loss_ref.shape)
    both = SHARPNESS * (jnp.exp(mine - lse_own) + jnp.exp(mine - lse_all) - 2.0 * target)
    grad = split_dot(dot_nn, split_bf(both), everyone)
    emb = own_ref[...]
    grad = inverse_ref[:, :1] * (grad - emb * jnp.sum(emb * grad, axis=1, keepdims=True))
    graw_ref[...] = grad
    high, low = split_bf(grad)
    pool_ref[...] = (dot_nt(high, proj_ref[...]) + dot_nt(low, proj_ref[...])) / count_ref[...]


def contrast_near(embedded, inverse, partner, counts, w_proj):
    own, dim = embedded.shape
    total = own * lax.axis_size("batch")
    parts = [embedded] + [flip(embedded, "batch", bits) for bits in (2, 4, 6)]
    other = flip(jnp.stack(parts), "batch", 1)
    me = lax.axis_index("batch").astype(jnp.int32).reshape(1)
    constants = (*parts, other, inverse, partner.reshape(own, 1), counts, w_proj)
    loss, graw, pool = pl.pallas_call(
        contrast_kernel,
        grid_spec=pltpu.PrefetchScalarGridSpec(
            num_scalar_prefetch=1,
            grid=(1,),
            in_specs=[full(item.shape) for item in constants],
            out_specs=[full((own, LANES)), full((own, dim)), full((own, dim))],
            scratch_shapes=[pltpu.VMEM((total, dim), F32), pltpu.VMEM((total, total), F32)],
        ),
        out_shape=[
            jax.ShapeDtypeStruct((own, LANES), F32),
            jax.ShapeDtypeStruct((own, dim), F32),
            jax.ShapeDtypeStruct((own, dim), F32),
        ],
        compiler_params=params(),
        name="contrast",
    )(me, *constants)
    return loss[:, 0], graw, pool


def finish_kernel(count, width, *refs):
    total = sum(ref[...].astype(F32) for ref in refs[:-count])
    for index, ref in enumerate(refs[-count:]):
        ref[...] = total[index * width : (index + 1) * width, :].T


def finish(pieces, count, width):
    cols = pieces[0].shape[1]
    return pl.pallas_call(
        functools.partial(finish_kernel, count, width),
        out_shape=[jax.ShapeDtypeStruct((cols, width), F32)] * count,
        compiler_params=pltpu.CompilerParams(vmem_limit_bytes=VMEM_BYTES),
        name="finish",
    )(*pieces)


def contrast(embedded, inv_norm, w_proj, partner):
    proj = w_proj.astype(F32)
    everyone = gather_batch(embedded)
    own_count = embedded.shape[0]
    total = everyone.shape[0]
    own_index = lax.axis_index("batch") * own_count + jnp.arange(own_count, dtype=jnp.int32)
    columns = jnp.arange(total, dtype=jnp.int32)

    def lse_of(rows, index):
        logits = SHARPNESS * jnp.einsum("nd,md->nm", rows, everyone, precision=HIGHEST)
        logits = jnp.where(columns[None, :] == index[:, None], NEGATIVE, logits)
        peak = jnp.max(logits, axis=-1, keepdims=True)
        return peak[:, 0] + jnp.log(jnp.sum(jnp.exp(logits - peak), axis=-1))

    if total <= 1024:
        lse_all = lse_of(everyone, columns)
    else:
        lse_all = lax.map(
            lambda pieces: lse_of(pieces[0], pieces[1]),
            (everyone.reshape(-1, 512, everyone.shape[1]), columns.reshape(-1, 512)),
        ).reshape(-1)
    logits = SHARPNESS * jnp.einsum("nd,md->nm", embedded, everyone, precision=HIGHEST)
    is_self = columns[None, :] == own_index[:, None]
    logits = jnp.where(is_self, NEGATIVE, logits)
    peak = jnp.max(logits, axis=-1, keepdims=True)
    lse_own = peak[:, 0] + jnp.log(jnp.sum(jnp.exp(logits - peak), axis=-1))
    is_target = columns[None, :] == partner[:, None]
    picked = jnp.sum(jnp.where(is_target, logits, 0.0), axis=-1)
    loss = lse_own - picked
    both = SHARPNESS * (
        jnp.exp(logits - lse_own[:, None])
        + jnp.exp(logits - lse_all[None, :])
        - 2.0 * is_target.astype(F32)
    )
    grad_emb = jnp.dot(both, everyone, precision=HIGHEST)
    grad_raw = inv_norm * (
        grad_emb - embedded * jnp.sum(embedded * grad_emb, axis=-1, keepdims=True)
    )
    grad_pooled = jnp.einsum("ne,de->nd", grad_raw, proj, precision=HIGHEST)
    return loss, grad_raw, grad_pooled


def shards(
    tokens,
    norm1_gain,
    w_query,
    w_key,
    w_value,
    rel_bias,
    w_output,
    norm2_gain,
    w_in,
    w_out,
    final_gain,
    w_proj,
    lengths,
    partner,
    cotangent,
):
    rows, size, dim = tokens.shape
    slots = lengths.shape[1]
    toks = rows * size
    seq_count = lax.axis_size("seq")
    seq_place = lax.axis_index("seq")
    place = seq_place.astype(jnp.int32).reshape(1)
    pairs = [(i, i ^ 1) for i in range(seq_count)]
    across = [(i, i - 1 if i % 2 == 0 else i + 1) for i in range(1, seq_count - 1)]
    gains = jnp.stack([norm1_gain, norm2_gain, final_gain])

    half_rows = rows // 2 if rows > 1 else rows
    bounds = [(first, min(first + half_rows, rows)) for first in range(0, rows, half_rows)]
    sides = []
    for first, last in bounds:
        piece = tokens[first:last]
        if sides:
            piece = after(piece, *sides[-1])
        sides.append((lax.ppermute(piece, "seq", pairs), lax.ppermute(piece, "seq", across)))
    bias = bias_tables(rel_bias, size)
    own = own_projections(tokens, norm1_gain.reshape(1, dim), (w_query, w_key, w_value))
    attended = ()
    for (first, _), (pair_part, across_part) in zip(bounds, sides):
        attended = tuple(
            attend(
                first, attended, lengths, place, pair_part, across_part, own, gains, w_key, w_value, bias
            )
        )
    edges, p, att = attended
    block, partial, pre, after_attn, n2 = forward(
        lengths, place, tokens, att, gains, w_output, w_in, w_out
    )
    x_pair, x_across = (
        jnp.concatenate([side[index] for side in sides], axis=0) for index in range(2)
    )
    counts = lengths.astype(F32).reshape(rows * slots, 1)
    partial = partial.reshape(rows * slots, dim)
    seq_bits = bit_places("seq")
    for bit in seq_bits[:-1]:
        partial = partial + flip(partial, "seq", bit)
    arrived = flip(partial, "seq", seq_bits[-1])
    partial = after(partial, x_pair, x_across)
    pooled, embedded, inverse = embed(partial, arrived, counts, w_proj)
    if lax.axis_size("batch") == 8:
        loss, grad_raw, pool_grad = contrast_near(embedded, inverse, partner, counts, w_proj)
    else:
        loss, grad_raw, grad_pooled = contrast(embedded, inverse[:, :1], w_proj, partner)
        pool_grad = grad_pooled / counts
    pool_grad = pool_grad.reshape(rows, slots, dim)
    batch_count = lax.axis_size("batch")
    place = jnp.stack([seq_place, lax.axis_index("batch") % 2]).astype(jnp.int32)

    back, gains_a, mine, theirs = feed_back(
        batch_count,
        lengths,
        place,
        block,
        after_attn,
        cotangent,
        att,
        n2,
        pre,
        pool_grad,
        grad_raw,
        pooled,
        gains,
        (w_output, w_in, w_out),
    )
    hidden = w_in.shape[1]
    width = dim // batch_count
    tiles = hidden // dim
    wide = hidden // batch_count
    feed_sum = BatchSum(
        mine,
        theirs,
        (((0, 0, wide), (2, 0, width)), ((1, 0, tiles * width), (2, width, width))),
    )
    segments = [(0, 1), (1, rows - 2), (rows - 1, 1)] if rows > 2 else [(0, rows)]
    halves, from_pair, from_across = [], [], []
    earlier = ()
    for first, count in segments:
        if halves and feed_sum.done < feed_sum.steps:
            place = after(place, *feed_sum.advance())
        halves.append(
            attend_back(
                first,
                count,
                (0, rows - 1) if first + count < rows else (first, count),
                earlier,
                lengths,
                place,
                tokens,
                x_pair,
                x_across,
                own,
                edges,
                p,
                back,
                gains,
                (w_query, w_key, w_value),
            )
        )
        feed_sum.hold(halves[-1][5])
        earlier = tuple(halves[-1][:4])
        if first + count >= rows - 1:
            from_pair.append(lax.ppermute(halves[-1][2], "seq", pairs))
            from_across.append(lax.ppermute(halves[-1][3], "seq", across))
            earlier = earlier[:2]
    grads, part = earlier
    while feed_sum.done < feed_sum.steps:
        place = after(place, *feed_sum.advance())

    feed_part = pack(
        *[(group[0][0], group[0][1]) for group in feed_sum.groups], tiles * width, seq_count
    )
    grad_rel = bias_grad([item[4] for item in halves], rel_bias.shape[0])
    gain1_grad = sum(item[5][0] for item in halves)
    small = jnp.concatenate([gain1_grad, gains_a[1], gains_a[0], grad_rel.reshape(-1)])
    small = jnp.pad(small, (0, -small.shape[0] % 1024)).reshape(-1, 128)
    batch_bits = bit_places("batch")
    arrived = flip(small, "seq", seq_bits[0])
    place = after(place, feed_part, small, *from_pair, *from_across)
    attend_mine, attend_theirs = attend_grad(batch_count, place, own, edges, grads)
    feed_done = lax.psum_scatter(feed_part, "seq", scatter_dimension=0, tiled=True)[0]
    half = 3 * width // 2
    attend_sum = BatchSum([attend_mine], [attend_theirs], (((0, 0, half),), ((0, half, 3 * width - half),)))
    small = after(small, attend_mine) + arrived
    arrived = flip(small, "batch", batch_bits[0])
    attend_sum.hold(arrived)
    for bit in batch_bits[1:]:
        sends = attend_sum.advance()
        small = after(small, *sends) + arrived
        arrived = flip(small, "batch", bit)
        attend_sum.hold(arrived)
    attend_parts = pack_columns([group[0][:2] for group in attend_sum.groups], seq_count)
    small = after(small, attend_parts) + arrived
    came = [lax.dynamic_index_in_dim(attend_parts, seq_place, 0, keepdims=False)]
    for distance in range(1, seq_count):
        route = [(i, (i + distance) % seq_count) for i in range(seq_count)]
        target = (seq_place + distance) % seq_count
        send = lax.dynamic_index_in_dim(attend_parts, target, 0, keepdims=False)
        came.append(lax.ppermute(send, "seq", route))
    sent = came[0]
    for bit in seq_bits[1:]:
        small = small + flip(small, "seq", bit)
    small = small.reshape(-1)
    gain_sums = [small[i * dim : (i + 1) * dim] for i in range(3)]
    rel_sum = small[3 * dim : 3 * dim + rel_bias.size].reshape(rel_bias.shape)

    grad_tokens = (
        after(part, sent).astype(F32)
        + jnp.concatenate(from_pair, axis=0).astype(F32)
        + jnp.concatenate(from_across, axis=0).astype(F32)
    )
    turn = lambda array: array.T.astype(F32)
    cols = dim // seq_count
    s_in = turn(feed_done[:wide, :cols])
    s_output = turn(feed_done[wide:, :cols])
    s_out = feed_done[:-width, cols:].reshape(seq_count, width, cols)
    s_out = s_out.transpose(0, 2, 1).reshape(dim, width).astype(F32)
    s_proj = turn(feed_done[-width:, cols:])
    came[0] = after(came[0], s_in, s_output, s_out, s_proj, grad_tokens)
    s_attend = finish(came, 3, width)
    return (
        block,
        embedded,
        loss,
        grad_tokens,
        gain_sums[0],
        s_attend[0],
        s_attend[1],
        s_attend[2],
        rel_sum,
        s_output,
        gain_sums[1],
        s_in,
        s_out,
        gain_sums[2],
        s_proj,
    )


def solution(mesh):
    tok = P("batch", "seq", None)
    mat = P("seq", "batch")
    return jax.shard_map(
        shards,
        mesh=mesh,
        in_specs=(tok,) + (P(),) * 11 + (P("batch", None), P("batch"), tok),
        out_specs=(
            tok,
            P("batch", None),
            P("batch"),
            tok,
            P(),
            mat,
            mat,
            mat,
            P(),
            mat,
            P(),
            mat,
            mat,
            P(),
            mat,
        ),
        check_vma=False,
    )
```
